32 devices in a mesh: fsdp: 8 (over z, x), tensor: 4 (over y, core).
Axes of the slice: x: 2, y: 2, z: 4, core: 2. Of those that a mesh axis runs over, the one named last changes fastest.
Arguments:
- tokens: bfloat16 [6144, 8192], P('fsdp'), may hold values from -6 to 6
- weight: bfloat16 [8192, 8192], P('fsdp', 'tensor'), may hold values from -0.0625 to 0.0625
- momentum: float32 [8192, 8192], P('fsdp', 'tensor'), may hold values from -700 to 700
- gradient: bfloat16 [8192, 8192], P('fsdp', 'tensor'), may hold values from -6 to 6
- probes: float32 [32, 8192], P(None, 'tensor'), may hold values from -6 to 6
Outputs:
- activations: float32 [6144, 8192], P('fsdp', 'tensor')
- momentum_out: float32 [8192, 8192], P('fsdp', 'tensor')
- krylov_scaled: float32 [96, 96], replicated
The draws below stay inside these ranges and needn't reach their ends.
All inputs are finite; a program needn't handle non-finite values.
Results may differ from the reference program's by a relative error of at most 0.0029.
Values may be sent and summed in bfloat16 or wider, within the bound.
No kernel may reach another device: no remote copies, remote signals or barrier semaphores. Data moves between devices by JAX's collectives and lax.ppermute only.
A program may use at most 192 MiB of HBM per device.

```python
import math
import jax
import jax.numpy as jnp
from jax import lax

D_IN = 8192
D_OUT = 8192
K = 32
STEPS = 3
POWER = 32
TOKENS = 6144


def draw_momentum(key, part):
    keys = jax.random.split(key, 3)
    row_scale = jnp.exp(jax.random.uniform(keys[0], (D_IN, 1), jnp.float32) * math.log(10.0))
    col_scale = jnp.exp(jax.random.uniform(keys[1], (1, D_OUT), jnp.float32) * math.log(10.0))
    row_place = jnp.arange(D_IN, dtype=jnp.float32).reshape(D_IN, 1) / D_IN
    col_place = jnp.arange(D_OUT, dtype=jnp.float32).reshape(1, D_OUT) / D_OUT
    row_ramp = jnp.exp(row_place * math.log(4.0))
    col_ramp = jnp.exp(col_place * math.log(4.0))
    noise = jax.random.truncated_normal(keys[2], -4.0, 4.0, (D_IN, D_OUT), jnp.float32)
    return 0.1 * noise * row_scale * col_scale * row_ramp * col_ramp


def shard_levels(key, dims, cuts, low, high):
    loudness = 1.0
    for axis_at, blocks in cuts:
        steps = jax.random.uniform(jax.random.fold_in(jax.random.fold_in(key, 6), axis_at), (blocks,), jnp.float32, low / len(cuts), high / len(cuts))
        loudness = loudness * jnp.repeat(jnp.exp(steps), dims[axis_at] // blocks).reshape((-1,) + (1,) * (len(dims) - 1 - axis_at))
    return loudness


def gaussian(stream_key, dims, width, bound, shards=(), kind=jnp.bfloat16):
    values = width * jax.random.normal(stream_key, dims, jnp.float32)
    if shards:
        values = values * shard_levels(stream_key, dims, shards, -0.22, 0.18)
    return jnp.clip(values, -bound, bound).astype(kind)


def setup_inputs(seed: int = 0) -> dict:
    key_list = jax.random.split(jax.random.key(seed), 6)
    tokens = gaussian(key_list[0], (TOKENS, D_IN), 1.0, 6.0, ((0, 8),))
    weight = gaussian(key_list[1], (D_IN, D_OUT), D_IN ** -0.5, 0.0625, ((0, 8), (1, 4)))
    momentum = draw_momentum(jax.random.fold_in(key_list[5], 71), 0)
    gradient = gaussian(key_list[3], (D_IN, D_OUT), 1.0, 6.0, ((0, 8), (1, 4)))
    probes = gaussian(key_list[4], (K, D_OUT), 1.0, 6.0, ((1, 4),), jnp.float32)
    return {"tokens": tokens, "weight": weight, "momentum": momentum, "gradient": gradient, "probes": probes}


highest = lax.Precision.HIGHEST
decay_factor = 0.9

def hdot(left, right):
    return jnp.dot(left.astype(jnp.float32), right.astype(jnp.float32), precision=highest, preferred_element_type=jnp.float32)

def orthonormal(block_mat, gram_mat):
    factor_low = jnp.linalg.cholesky(gram_mat)
    basis_next = jax.scipy.linalg.solve_triangular(factor_low, block_mat, lower=True)
    return (basis_next, factor_low)

def assemble(diag_blocks, low_factors):
    blk_width = diag_blocks[0].shape[0]
    total_size = len(diag_blocks) * blk_width
    krylov = jnp.zeros((total_size, total_size), jnp.float32)
    for position, diag_mat in enumerate(diag_blocks):
        first_at = position * blk_width
        krylov = krylov.at[first_at:first_at + blk_width, first_at:first_at + blk_width].set(diag_mat)
    for position, factor_low in enumerate(low_factors):
        first_at = position * blk_width
        second_at = first_at + blk_width
        krylov = krylov.at[second_at:second_at + blk_width, first_at:second_at].set(factor_low.T)
        krylov = krylov.at[first_at:second_at, second_at:second_at + blk_width].set(factor_low)
    return krylov

def top_value(krylov):

    def advance(position, vector):
        moved = hdot(krylov, vector)
        return moved / jnp.sqrt(jnp.sum(moved * moved))
    vector = lax.fori_loop(0, POWER, advance, jnp.ones((krylov.shape[0],), jnp.float32))
    return jnp.sum(vector * hdot(krylov, vector))

def reference(tokens, weight, momentum, gradient, probes):
    moment = decay_factor * momentum + gradient.astype(jnp.float32)
    basis_now, factor_first = orthonormal(probes, hdot(probes, probes.T))
    basis_prev = jnp.zeros_like(basis_now)
    low_prev = jnp.zeros((K, K), jnp.float32)
    diag_blocks = []
    low_factors = []
    for lanczos_step in range(STEPS):
        reduced = hdot(basis_now, moment.T)
        images = hdot(reduced, moment)
        diag_raw = hdot(basis_now, images.T)
        diag_mat = 0.5 * (diag_raw + diag_raw.T)
        diag_blocks.append(diag_mat)
        if lanczos_step + 1 < STEPS:
            residue = images - hdot(diag_mat, basis_now) - hdot(low_prev.T, basis_prev)
            basis_next, factor_low = orthonormal(residue, hdot(residue, residue.T))
            low_factors.append(factor_low)
            basis_prev, low_prev, basis_now = (basis_now, factor_low, basis_next)
    krylov = assemble(diag_blocks, low_factors)
    top = top_value(krylov)
    new_weight = (weight.astype(jnp.float32) - moment / jnp.sqrt(top)).astype(jnp.bfloat16)
    activations = jnp.dot(tokens.astype(jnp.float32), new_weight.astype(jnp.float32), preferred_element_type=jnp.float32)
    return (activations, moment, krylov / top)
```

```python
import functools

import jax
import jax.numpy as jnp
from jax import lax
from jax.experimental import pallas as pl
from jax.experimental.pallas import tpu as pltpu
from jax.sharding import PartitionSpec as P

DECAY = 0.9
SQUARINGS = 5
LANES = 128
CHUNKS = 4
EARLY = 2

HIGHEST = lax.Precision.HIGHEST
PARAMS = pltpu.CompilerParams(vmem_limit_bytes=24 * 1024 * 1024)
VMEM = pl.BlockSpec(memory_space=pltpu.VMEM)


def fdot(left, right):
    return lax.dot_general(
        left, right, (((1,), (0,)), ((), ())), precision=HIGHEST, preferred_element_type=jnp.float32
    )


def fdot_t(left, right):
    return lax.dot_general(
        left, right, (((1,), (1,)), ((), ())), precision=HIGHEST, preferred_element_type=jnp.float32
    )


def halves(values):
    high = values.astype(jnp.bfloat16)
    return high, (values - high.astype(jnp.float32)).astype(jnp.bfloat16)


def split_dot(stacked, mat, contract):
    rows = stacked.shape[0] // 2
    mat_high, mat_low = halves(mat)
    dims = (((1,), (contract,)), ((), ()))
    first = lax.dot_general(stacked, mat_high, dims, preferred_element_type=jnp.float32)
    second = lax.dot_general(stacked[:rows], mat_low, dims, preferred_element_type=jnp.float32)
    return first[:rows] + first[rows:] + second


def eliminate(gram, count):
    rows = lax.broadcasted_iota(jnp.int32, (count, LANES), 0)
    lanes = lax.broadcasted_iota(jnp.int32, (count, LANES), 1)
    aug = jnp.where(lanes < count, gram, jnp.where(lanes - count == rows, 1.0, 0.0))
    for step in range(count):
        pivot = aug[step : step + 1, step : step + 1]
        factor = jnp.where(rows > step, aug[:, step : step + 1] * (1.0 / pivot), 0.0)
        aug = aug - factor * aug[step : step + 1, :]
    pivots = jnp.sum(jnp.where(lanes == rows, aug, 0.0), axis=1, keepdims=True)
    aug = aug * (1.0 / jnp.sqrt(pivots))
    low_t = jnp.where((lanes >= rows) & (lanes < count), aug, 0.0)
    return low_t, aug[:, count : 2 * count]


def pad_lanes(square):
    return jnp.concatenate(
        [square, jnp.zeros((square.shape[0], LANES - square.shape[1]), jnp.float32)], axis=1
    )


def start_kernel(width, mom_ref, grad_ref, probes_ref, moment_ref, short_ref, pack_ref, stack_ref):
    at = pl.program_id(0)
    count = probes_ref.shape[0]
    height = mom_ref.shape[0]

    @pl.when(at == 0)
    def _():
        probes = probes_ref[...]
        high, low = halves(probes)
        stack_ref[:count] = high
        stack_ref[count:] = low
        pack_ref[:, width:] = pad_lanes(fdot_t(probes, probes))

    moment = DECAY * mom_ref[...] + grad_ref[...].astype(jnp.float32)
    moment_ref[...] = moment
    short_ref[...] = moment.astype(jnp.bfloat16)
    pack_ref[:, pl.ds(pl.multiple_of(at * height, height), height)] = split_dot(stack_ref[...], moment, 1)


def start_call(momentum, gradient, probes):
    depth, cols = momentum.shape
    count = probes.shape[0]
    height = min(256, depth)
    rows = pl.BlockSpec((height, cols), lambda i: (i, 0))
    return pl.pallas_call(
        functools.partial(start_kernel, depth),
        grid=(depth // height,),
        in_specs=[rows, rows, VMEM],
        out_specs=[rows, rows, VMEM],
        out_shape=[
            jax.ShapeDtypeStruct((depth, cols), jnp.float32),
            jax.ShapeDtypeStruct((depth, cols), jnp.bfloat16),
            jax.ShapeDtypeStruct((count, depth + LANES), jnp.float32),
        ],
        scratch_shapes=[pltpu.VMEM((2 * count, cols), jnp.bfloat16)],
        compiler_params=PARAMS,
    )(momentum, gradient, probes)


def images_kernel(own_ref, recv_ref, block_ref, moment_ref, pack_ref, basis_ref, low_ref, stack_ref):
    at = pl.program_id(0)
    count, cols = block_ref.shape
    depth = moment_ref.shape[0]
    width = moment_ref.shape[1]

    @pl.when(at == 0)
    def _():
        low_t, inverse = eliminate(own_ref[:, depth:] + recv_ref[:, depth:], count)
        low_ref[...] = low_t
        reduced = fdot(inverse, own_ref[:, :depth] + recv_ref[:, :depth])
        high, low = halves(reduced)
        stack_ref[:count] = high
        stack_ref[count:] = low
        pack_ref[:, cols:] = pad_lanes(fdot_t(reduced, reduced))
        basis_ref[...] = fdot(inverse, block_ref[...])

    pack_ref[:, pl.ds(pl.multiple_of(at * width, width), width)] = split_dot(stack_ref[...], moment_ref[...], 0)


def images_call(own, recv, block, moment):
    depth, cols = moment.shape
    count = block.shape[0]
    width = min(512, cols)
    return pl.pallas_call(
        images_kernel,
        grid=(cols // width,),
        in_specs=[VMEM, VMEM, VMEM, pl.BlockSpec((depth, width), lambda i: (0, i))],
        out_specs=[VMEM, VMEM, VMEM],
        out_shape=[
            jax.ShapeDtypeStruct((count, cols + LANES), jnp.float32),
            jax.ShapeDtypeStruct((count, cols), jnp.float32),
            jax.ShapeDtypeStruct((count, LANES), jnp.float32),
        ],
        scratch_shapes=[pltpu.VMEM((2 * count, depth), jnp.bfloat16)],
        compiler_params=PARAMS,
    )(own, recv, block, moment)


def reduced_kernel(has_prev, width, *refs):
    if has_prev:
        own_ref, recv_ref, basis_ref, prev_ref, low_ref, moment_ref = refs[:6]
        pack_ref, residue_ref, diag_ref, stack_ref = refs[6:]
    else:
        own_ref, recv_ref, basis_ref, moment_ref = refs[:4]
        pack_ref, residue_ref, diag_ref, stack_ref = refs[4:]
    at = pl.program_id(0)
    count, cols = basis_ref.shape
    height = moment_ref.shape[0]

    @pl.when(at == 0)
    def _():
        diag = (own_ref[:, cols:] + recv_ref[:, cols:])[:, :count]
        diag = 0.5 * (diag + diag.T)
        diag_ref[...] = pad_lanes(diag)
        residue = own_ref[:, :cols] + recv_ref[:, :cols] - fdot(diag, basis_ref[...])
        if has_prev:
            residue = residue - fdot(low_ref[:, :count], prev_ref[...])
        residue_ref[...] = residue
        high, low = halves(residue)
        stack_ref[:count] = high
        stack_ref[count:] = low
        pack_ref[:, width:] = pad_lanes(fdot_t(residue, residue))

    pack_ref[:, pl.ds(pl.multiple_of(at * height, height), height)] = split_dot(
        stack_ref[...], moment_ref[...], 1
    )


def reduced_call(own, recv, basis, prev, low, moment):
    depth, cols = moment.shape
    count = basis.shape[0]
    height = min(256, depth)
    has_prev = prev is not None
    operands = (own, recv, basis) + ((prev, low) if has_prev else ()) + (moment,)
    return pl.pallas_call(
        functools.partial(reduced_kernel, has_prev, depth),
        grid=(depth // height,),
        in_specs=[VMEM] * (len(operands) - 1) + [pl.BlockSpec((height, cols), lambda i: (i, 0))],
        out_specs=[VMEM, VMEM, VMEM],
        out_shape=[
            jax.ShapeDtypeStruct((count, depth + LANES), jnp.float32),
            jax.ShapeDtypeStruct((count, cols), jnp.float32),
            jax.ShapeDtypeStruct((count, LANES), jnp.float32),
        ],
        scratch_shapes=[pltpu.VMEM((2 * count, cols), jnp.bfloat16)],
        compiler_params=PARAMS,
    )(*operands)


def last_kernel(own_ref, recv_ref, diag_ref, low_ref):
    count = own_ref.shape[0]
    depth = own_ref.shape[1] - LANES
    low_t, inverse = eliminate(own_ref[:, depth:] + recv_ref[:, depth:], count)
    low_ref[...] = low_t
    reduced = fdot(inverse, own_ref[:, :depth] + recv_ref[:, :depth])
    diag_ref[...] = pad_lanes(fdot_t(reduced, reduced))


def last_call(own, recv):
    shape = jax.ShapeDtypeStruct((own.shape[0], LANES), jnp.float32)
    return pl.pallas_call(
        last_kernel,
        in_specs=[VMEM, VMEM],
        out_specs=[VMEM, VMEM],
        out_shape=[shape, shape],
        compiler_params=PARAMS,
    )(own, recv)


def top_kernel(steps, *refs):
    diag_refs = refs[:steps]
    low_refs = refs[steps : 2 * steps - 1]
    scaled_ref, rate_ref, krylov_ref = refs[2 * steps - 1 :]
    count = diag_refs[0].shape[0]
    size = steps * count
    krylov_ref[...] = jnp.zeros_like(krylov_ref)
    for place in range(steps):
        first = place * count
        diag = diag_refs[place][:, :count]
        krylov_ref[first : first + count, first : first + count] = 0.5 * (diag + diag.T)
        if place + 1 < steps:
            second = first + count
            low_t = low_refs[place][:, :count]
            krylov_ref[second : second + count, first:second] = low_t
            krylov_ref[first:second, second : second + count] = low_t.T
    krylov = krylov_ref[...]
    power = krylov * (1.0 / jnp.max(jnp.abs(krylov), keepdims=True))
    for _ in range(SQUARINGS):
        power = fdot(power, power)
        power = power * (1.0 / jnp.max(jnp.abs(power), keepdims=True))
    tall = jnp.sum(power, axis=1, keepdims=True)
    wide = jnp.sum(power, axis=0, keepdims=True)
    tall = tall * (1.0 / jnp.sqrt(jnp.sum(tall * tall, keepdims=True)))
    wide = wide * (1.0 / jnp.sqrt(jnp.sum(wide * wide, keepdims=True)))
    top = jnp.sum(krylov * tall * wide, keepdims=True)
    scaled_ref[...] = krylov[:size, :size] / top
    rate_ref[...] = jnp.broadcast_to(1.0 / jnp.sqrt(top), rate_ref.shape)


def top_call(diags, lows):
    steps = len(diags)
    count = diags[0].shape[0]
    size = steps * count
    padded = -(-size // LANES) * LANES
    return pl.pallas_call(
        functools.partial(top_kernel, steps),
        in_specs=[VMEM] * (2 * steps - 1),
        out_specs=[VMEM, VMEM],
        out_shape=[
            jax.ShapeDtypeStruct((size, size), jnp.float32),
            jax.ShapeDtypeStruct((8, LANES), jnp.float32),
        ],
        scratch_shapes=[pltpu.VMEM((padded, padded), jnp.float32)],
        compiler_params=PARAMS,
    )(*diags, *lows)


def swap(values, axis, size, bit):
    return lax.ppermute(values, axis, [(at, at ^ bit) for at in range(size)])


def butterfly(values, axis, size):
    bit = 1
    while 2 * bit < size:
        values = values + swap(values, axis, size, bit)
        bit *= 2
    return values, swap(values, axis, size, bit)


def gather(values, axis, size, count):
    parts = [values]
    bit = 1
    while bit < count:
        parts = parts + [swap(part, axis, size, bit) for part in parts]
        bit *= 2
    return parts


def dot32(left, right):
    return jnp.dot(left, right, preferred_element_type=jnp.float32)


def local(rows_n, cols_n, tokens, weight, momentum, gradient, probes):
    half = rows_n // 2
    place = lax.axis_index("fsdp")
    low_at = lax.rem(place, half)
    side = lax.div(place, half)
    column_at = lax.axis_index("tensor")
    num_rows = tokens.shape[0]
    depth, cols = weight.shape
    piece = num_rows // cols_n
    width = cols // CHUNKS

    def columns(values, of_side):
        blocks = [
            lax.dynamic_slice_in_dim(values, (of_side * half + (low_at ^ i)) * depth, depth, axis=1)
            for i in range(half)
        ]
        return jnp.concatenate(blocks, axis=1)

    sent = columns(lax.dynamic_slice_in_dim(tokens, column_at * piece, piece, axis=0), 1 - side)
    pieces = gather(swap(sent, "fsdp", rows_n, half), "tensor", cols_n, cols_n)
    near_tokens = columns(tokens, side)

    def early_gather(values, chunk):
        return jnp.concatenate(
            gather(values[:, chunk * width : (chunk + 1) * width], "fsdp", rows_n, half), axis=0
        )

    early_weight = [early_gather(weight, chunk) for chunk in range(EARLY)]

    moment, short, pack = start_call(momentum, gradient, probes)
    early_moment = [early_gather(short, chunk) for chunk in range(EARLY)]

    own, recv = butterfly(pack, "tensor", cols_n)
    pack, basis_1, _ = images_call(own, recv, probes, moment)
    own, recv = butterfly(pack, "fsdp", rows_n)
    pack, residue, diag_1 = reduced_call(own, recv, basis_1, None, None, moment)
    own, recv = butterfly(pack, "tensor", cols_n)
    pack, basis_2, low_1 = images_call(own, recv, residue, moment)
    own, recv = butterfly(pack, "fsdp", rows_n)
    pack, _, diag_2 = reduced_call(own, recv, basis_2, basis_1, low_1, moment)
    own, recv = butterfly(pack, "tensor", cols_n)
    diag_3, low_2 = last_call(own, recv)
    diag_3 = lax.psum(diag_3, "fsdp")
    scaled, rate = top_call([diag_1, diag_2, diag_3], [low_1, low_2])
    rate = rate[0, 0]

    far_tokens = jnp.zeros((num_rows, half * depth), tokens.dtype)
    for i, part in enumerate(pieces):
        far_tokens = lax.dynamic_update_slice_in_dim(far_tokens, part, (column_at ^ i) * piece, axis=0)

    results = []
    for chunk in range(CHUNKS):
        if chunk < EARLY:
            far = dot32(far_tokens, early_weight[chunk]) - rate * dot32(far_tokens, early_moment[chunk])
            far = swap(far.astype(jnp.bfloat16), "fsdp", rows_n, half)
            near = dot32(near_tokens, early_weight[chunk]) - rate * dot32(near_tokens, early_moment[chunk])
        else:
            at = slice(chunk * width, (chunk + 1) * width)
            stepped = (weight[:, at].astype(jnp.float32) - moment[:, at] * rate).astype(jnp.bfloat16)
            stepped = jnp.concatenate(gather(stepped, "fsdp", rows_n, half), axis=0)
            far = swap(dot32(far_tokens, stepped).astype(jnp.bfloat16), "fsdp", rows_n, half)
            near = dot32(near_tokens, stepped)
        results.append(near + far.astype(jnp.float32))
    return jnp.concatenate(results, axis=1), moment, scaled


def solution(mesh):
    return jax.shard_map(
        functools.partial(local, mesh.shape["fsdp"], mesh.shape["tensor"]),
        mesh=mesh,
        in_specs=(
            P("fsdp", None),
            P("fsdp", "tensor"),
            P("fsdp", "tensor"),
            P("fsdp", "tensor"),
            P(None, "tensor"),
        ),
        out_specs=(P("fsdp", "tensor"), P("fsdp", "tensor"), P()),
        check_vma=False,
    )
```

```python
import functools

import jax
import jax.numpy as jnp
from jax import lax
from jax.experimental import pallas as pl
from jax.experimental.pallas import tpu as pltpu
from jax.sharding import PartitionSpec as P

DECAY = 0.9
SQUARINGS = 5
LANES = 128
CHUNKS = 4
EARLY = 2

HIGHEST = lax.Precision.HIGHEST
PARAMS = pltpu.CompilerParams(vmem_limit_bytes=56 * 1024 * 1024)
SMALL = pltpu.CompilerParams(vmem_limit_bytes=16 * 1024 * 1024)
VMEM = pl.BlockSpec(memory_space=pltpu.VMEM)


def fdot(left, right):
    return lax.dot_general(
        left, right, (((1,), (0,)), ((), ())), precision=HIGHEST, preferred_element_type=jnp.float32
    )


def fdot_t(left, right):
    return lax.dot_general(
        left, right, (((1,), (1,)), ((), ())), precision=HIGHEST, preferred_element_type=jnp.float32
    )


def halves(values):
    high = values.astype(jnp.bfloat16)
    return high, (values - high.astype(jnp.float32)).astype(jnp.bfloat16)


def split_dot(stacked, mat, contract):
    rows = stacked.shape[0] // 2
    mat_high, mat_low = halves(mat)
    dims = (((1,), (contract,)), ((), ()))
    first = lax.dot_general(stacked, mat_high, dims, preferred_element_type=jnp.float32)
    second = lax.dot_general(stacked[:rows], mat_low, dims, preferred_element_type=jnp.float32)
    return first[:rows] + first[rows:] + second


def eliminate(gram, count):
    rows = lax.broadcasted_iota(jnp.int32, (count, LANES), 0)
    lanes = lax.broadcasted_iota(jnp.int32, (count, LANES), 1)
    aug = jnp.where(lanes < count, gram, jnp.where(lanes - count == rows, 1.0, 0.0))
    for step in range(count):
        pivot = aug[step : step + 1, step : step + 1]
        factor = jnp.where(rows > step, aug[:, step : step + 1] * (1.0 / pivot), 0.0)
        aug = aug - factor * aug[step : step + 1, :]
    pivots = jnp.sum(jnp.where(lanes == rows, aug, 0.0), axis=1, keepdims=True)
    aug = aug * (1.0 / jnp.sqrt(pivots))
    low_t = jnp.where((lanes >= rows) & (lanes < count), aug, 0.0)
    return low_t, aug[:, count : 2 * count]


def pad_lanes(square):
    return jnp.concatenate(
        [square, jnp.zeros((square.shape[0], LANES - square.shape[1]), jnp.float32)], axis=1
    )


def start_kernel(width, mom_ref, grad_ref, probes_ref, moment_ref, short_ref, pack_ref, stack_ref):
    at = pl.program_id(0)
    count = probes_ref.shape[0]
    height = mom_ref.shape[0]

    @pl.when(at == 0)
    def _():
        probes = probes_ref[...]
        high, low = halves(probes)
        stack_ref[:count] = high
        stack_ref[count:] = low
        pack_ref[:, width:] = pad_lanes(fdot_t(probes, probes))

    moment = DECAY * mom_ref[...] + grad_ref[...].astype(jnp.float32)
    moment_ref[...] = moment
    short_ref[...] = moment[:, : short_ref.shape[1]].astype(jnp.bfloat16)
    pack_ref[:, pl.ds(pl.multiple_of(at * height, height), height)] = split_dot(stack_ref[...], moment, 1)


def start_call(momentum, gradient, probes, early_cols):
    depth, cols = momentum.shape
    count = probes.shape[0]
    height = min(256, depth)
    rows = pl.BlockSpec((height, cols), lambda i: (i, 0))
    return pl.pallas_call(
        functools.partial(start_kernel, depth),
        grid=(depth // height,),
        in_specs=[rows, rows, VMEM],
        out_specs=[rows, pl.BlockSpec((height, early_cols), lambda i: (i, 0)), VMEM],
        out_shape=[
            jax.ShapeDtypeStruct((depth, cols), jnp.float32),
            jax.ShapeDtypeStruct((depth, early_cols), jnp.bfloat16),
            jax.ShapeDtypeStruct((count, depth + LANES), jnp.float32),
        ],
        scratch_shapes=[pltpu.VMEM((2 * count, cols), jnp.bfloat16)],
        compiler_params=PARAMS,
    )(momentum, gradient, probes)


def images_kernel(own_ref, recv_ref, block_ref, moment_ref, pack_ref, basis_ref, low_ref, stack_ref):
    at = pl.program_id(0)
    count, cols = block_ref.shape
    depth = moment_ref.shape[0]
    width = moment_ref.shape[1]

    @pl.when(at == 0)
    def _():
        low_t, inverse = eliminate(own_ref[:, depth:] + recv_ref[:, depth:], count)
        low_ref[...] = low_t
        reduced = fdot(inverse, own_ref[:, :depth] + recv_ref[:, :depth])
        high, low = halves(reduced)
        stack_ref[:count] = high
        stack_ref[count:] = low
        pack_ref[:, cols:] = pad_lanes(fdot_t(reduced, reduced))
        basis_ref[...] = fdot(inverse, block_ref[...])

    pack_ref[:, pl.ds(pl.multiple_of(at * width, width), width)] = split_dot(stack_ref[...], moment_ref[...], 0)


def images_call(own, recv, block, moment):
    depth, cols = moment.shape
    count = block.shape[0]
    width = min(512, cols)
    return pl.pallas_call(
        images_kernel,
        grid=(cols // width,),
        in_specs=[VMEM, VMEM, VMEM, pl.BlockSpec((depth, width), lambda i: (0, i))],
        out_specs=[VMEM, VMEM, VMEM],
        out_shape=[
            jax.ShapeDtypeStruct((count, cols + LANES), jnp.float32),
            jax.ShapeDtypeStruct((count, cols), jnp.float32),
            jax.ShapeDtypeStruct((count, LANES), jnp.float32),
        ],
        scratch_shapes=[pltpu.VMEM((2 * count, depth), jnp.bfloat16)],
        compiler_params=PARAMS,
    )(own, recv, block, moment)


def reduced_kernel(has_prev, width, *refs):
    if has_prev:
        own_ref, recv_ref, basis_ref, prev_ref, low_ref, moment_ref = refs[:6]
        pack_ref, residue_ref, diag_ref, stack_ref = refs[6:]
    else:
        own_ref, recv_ref, basis_ref, moment_ref = refs[:4]
        pack_ref, residue_ref, diag_ref, stack_ref = refs[4:]
    at = pl.program_id(0)
    count, cols = basis_ref.shape
    height = moment_ref.shape[0]

    @pl.when(at == 0)
    def _():
        diag = (own_ref[:, cols:] + recv_ref[:, cols:])[:, :count]
        diag = 0.5 * (diag + diag.T)
        diag_ref[...] = pad_lanes(diag)
        residue = own_ref[:, :cols] + recv_ref[:, :cols] - fdot(diag, basis_ref[...])
        if has_prev:
            residue = residue - fdot(low_ref[:, :count], prev_ref[...])
        residue_ref[...] = residue
        high, low = halves(residue)
        stack_ref[:count] = high
        stack_ref[count:] = low
        pack_ref[:, width:] = pad_lanes(fdot_t(residue, residue))

    pack_ref[:, pl.ds(pl.multiple_of(at * height, height), height)] = split_dot(
        stack_ref[...], moment_ref[...], 1
    )


def reduced_call(own, recv, basis, prev, low, moment):
    depth, cols = moment.shape
    count = basis.shape[0]
    height = min(256, depth)
    has_prev = prev is not None
    operands = (own, recv, basis) + ((prev, low) if has_prev else ()) + (moment,)
    return pl.pallas_call(
        functools.partial(reduced_kernel, has_prev, depth),
        grid=(depth // height,),
        in_specs=[VMEM] * (len(operands) - 1) + [pl.BlockSpec((height, cols), lambda i: (i, 0))],
        out_specs=[VMEM, VMEM, VMEM],
        out_shape=[
            jax.ShapeDtypeStruct((count, depth + LANES), jnp.float32),
            jax.ShapeDtypeStruct((count, cols), jnp.float32),
            jax.ShapeDtypeStruct((count, LANES), jnp.float32),
        ],
        scratch_shapes=[pltpu.VMEM((2 * count, cols), jnp.bfloat16)],
        compiler_params=PARAMS,
    )(*operands)


def last_kernel(own_ref, recv_ref, diag_ref, low_ref):
    count = own_ref.shape[0]
    depth = own_ref.shape[1] - LANES
    low_t, inverse = eliminate(own_ref[:, depth:] + recv_ref[:, depth:], count)
    low_ref[...] = low_t
    reduced = fdot(inverse, own_ref[:, :depth] + recv_ref[:, :depth])
    diag_ref[...] = pad_lanes(fdot_t(reduced, reduced))


def last_call(own, recv):
    shape = jax.ShapeDtypeStruct((own.shape[0], LANES), jnp.float32)
    return pl.pallas_call(
        last_kernel,
        in_specs=[VMEM, VMEM],
        out_specs=[VMEM, VMEM],
        out_shape=[shape, shape],
        compiler_params=PARAMS,
    )(own, recv)


def top_kernel(steps, *refs):
    diag_refs = refs[: steps + 1]
    low_refs = refs[steps + 1 : 2 * steps]
    scaled_ref, rate_ref, krylov_ref = refs[2 * steps :]
    count = diag_refs[0].shape[0]
    size = steps * count
    krylov_ref[...] = jnp.zeros_like(krylov_ref)
    for place in range(steps):
        first = place * count
        diag = diag_refs[place][:, :count]
        if place + 1 == steps:
            diag = diag + diag_refs[steps][:, :count]
        krylov_ref[first : first + count, first : first + count] = 0.5 * (diag + diag.T)
        if place + 1 < steps:
            second = first + count
            low_t = low_refs[place][:, :count]
            krylov_ref[second : second + count, first:second] = low_t
            krylov_ref[first:second, second : second + count] = low_t.T
    krylov = krylov_ref[...]
    power = krylov * (1.0 / jnp.max(jnp.abs(krylov), keepdims=True))
    for _ in range(SQUARINGS):
        power = fdot(power, power)
        power = power * (1.0 / jnp.max(jnp.abs(power), keepdims=True))
    tall = jnp.sum(power, axis=1, keepdims=True)
    wide = jnp.sum(power, axis=0, keepdims=True)
    tall = tall * (1.0 / jnp.sqrt(jnp.sum(tall * tall, keepdims=True)))
    wide = wide * (1.0 / jnp.sqrt(jnp.sum(wide * wide, keepdims=True)))
    top = jnp.sum(krylov * tall * wide, keepdims=True)
    scaled_ref[...] = krylov[:size, :size] / top
    rate_ref[...] = jnp.broadcast_to(1.0 / jnp.sqrt(top), rate_ref.shape)


def top_call(diags, lows):
    steps = len(lows) + 1
    count = diags[0].shape[0]
    size = steps * count
    padded = -(-size // LANES) * LANES
    return pl.pallas_call(
        functools.partial(top_kernel, steps),
        in_specs=[VMEM] * (2 * steps),
        out_specs=[VMEM, VMEM],
        out_shape=[
            jax.ShapeDtypeStruct((size, size), jnp.float32),
            jax.ShapeDtypeStruct((8, LANES), jnp.float32),
        ],
        scratch_shapes=[pltpu.VMEM((padded, padded), jnp.float32)],
        compiler_params=PARAMS,
    )(*diags, *lows)


def step_kernel(weight_ref, moment_ref, rate_ref, out_ref):
    stepped = weight_ref[...].astype(jnp.float32) - moment_ref[...] * rate_ref[:1, :1]
    out_ref[...] = stepped.astype(jnp.bfloat16)


def step_call(weight, moment, rate, chunk, width):
    depth = weight.shape[0]
    height = min(256, depth)
    block = pl.BlockSpec((height, width), lambda i: (i, chunk))
    return pl.pallas_call(
        step_kernel,
        grid=(depth // height,),
        in_specs=[block, block, VMEM],
        out_specs=pl.BlockSpec((height, width), lambda i: (i, 0)),
        out_shape=jax.ShapeDtypeStruct((depth, width), jnp.bfloat16),
        compiler_params=SMALL,
    )(weight, moment, rate)


def project_kernel(count, early, order_ref, *refs):
    tokens = refs[:count]
    weights = refs[count : 2 * count]
    out_ref, ready_ref = refs[-2:]
    depth = weights[0].shape[0]
    if early:
        moments = refs[2 * count : 3 * count]
        rate_ref = refs[3 * count]

        @pl.when(pl.program_id(0) == 0)
        def _():
            rate = rate_ref[:1, :1]
            for i in range(count):
                stepped = weights[i][...].astype(jnp.float32) - moments[i][...].astype(jnp.float32) * rate
                ready_ref[i * depth : (i + 1) * depth] = stepped.astype(jnp.bfloat16)

    total = jnp.zeros(out_ref.shape, jnp.float32)
    for i in range(count):
        block = ready_ref[i * depth : (i + 1) * depth] if early else weights[i][...]
        total = total + jnp.dot(tokens[i][...], block, preferred_element_type=jnp.float32)
    out_ref[...] = total.astype(out_ref.dtype)


def project_call(order, tokens, weights, moments, rate, chunk, width, out, out_chunk):
    count = len(weights)
    early = moments is not None
    depth = weights[0].shape[0]
    num_rows = tokens.shape[0]
    height = min(256, num_rows)

    def token_spec(i):
        return pl.BlockSpec((height, depth), lambda r, order_ref: (r, order_ref[i]))

    part = pl.BlockSpec((depth, width), lambda r, order_ref: (0, chunk), pipeline_mode=pl.Buffered(1))
    operands = [tokens] * count + list(weights)
    specs = [token_spec(i) for i in range(count)] + [part] * count
    if early:
        operands += list(moments) + [rate]
        specs += [part] * count + [VMEM]
    aliases = {}
    if out is None:
        dtype = jnp.bfloat16
        out_shape = jax.ShapeDtypeStruct((num_rows, width), dtype)
    elif isinstance(out, int):
        out_shape = jax.ShapeDtypeStruct((num_rows, out), jnp.float32)
    else:
        out_shape = jax.ShapeDtypeStruct(out.shape, out.dtype)
        operands.append(out)
        specs.append(pl.BlockSpec(memory_space=pl.ANY))
        aliases = {len(operands): 0}
    return pl.pallas_call(
        functools.partial(project_kernel, count, early),
        grid_spec=pltpu.PrefetchScalarGridSpec(
            num_scalar_prefetch=1,
            grid=(num_rows // height,),
            in_specs=specs,
            out_specs=pl.BlockSpec((height, width), lambda r, order_ref: (r, out_chunk)),
            scratch_shapes=[pltpu.VMEM((count * depth, width), jnp.bfloat16)],
        ),
        out_shape=out_shape,
        input_output_aliases=aliases,
        compiler_params=PARAMS,
        cost_estimate=pl.CostEstimate(
            flops=2 * num_rows * count * depth * width,
            bytes_accessed=2 * num_rows * count * depth + 4 * count * depth * width,
            transcendentals=0,
        ),
    )(order, *operands)


def add_kernel(old_ref, far_ref, out_ref):
    out_ref[...] = old_ref[...] + far_ref[...].astype(jnp.float32)


def add_call(out, far, chunk):
    num_rows, width = far.shape
    height = min(256, num_rows)
    block = pl.BlockSpec((height, width), lambda r: (r, chunk))
    return pl.pallas_call(
        add_kernel,
        grid=(num_rows // height,),
        in_specs=[block, pl.BlockSpec((height, width), lambda r: (r, 0))],
        out_specs=block,
        out_shape=jax.ShapeDtypeStruct(out.shape, out.dtype),
        input_output_aliases={0: 0},
        compiler_params=SMALL,
    )(out, far)


def swap(values, axis, size, bit):
    return lax.ppermute(values, axis, [(at, at ^ bit) for at in range(size)])


def butterfly(values, axis, size):
    bit = 1
    while 2 * bit < size:
        values = values + swap(values, axis, size, bit)
        bit *= 2
    return values, swap(values, axis, size, bit)


def offsets(count):
    found = [0]
    bit = count // 2
    while bit:
        found = found + [at ^ bit for at in found]
        bit //= 2
    return found


def gather(values, axis, size, count):
    parts = [values]
    bit = count // 2
    while bit:
        parts = parts + [swap(part, axis, size, bit) for part in parts]
        bit //= 2
    return parts


def local(rows_n, cols_n, tokens, weight, momentum, gradient, probes):
    half = rows_n // 2
    place = lax.axis_index("fsdp")
    low_at = lax.rem(place, half)
    side = lax.div(place, half)
    column_at = lax.axis_index("tensor")
    num_rows = tokens.shape[0]
    depth, cols = weight.shape
    piece = num_rows // cols_n
    width = cols // CHUNKS
    early_cols = EARLY * width

    mixed = jnp.stack([low_at ^ at for at in offsets(half)])
    near_order = side * half + mixed
    far_order = jnp.arange(half, dtype=jnp.int32)

    sent = lax.dynamic_slice_in_dim(tokens, column_at * piece, piece, axis=0)
    sent = jnp.concatenate(
        [
            lax.dynamic_slice_in_dim(sent, ((1 - side) * half + (low_at ^ at)) * depth, depth, axis=1)
            for at in offsets(half)
        ],
        axis=1,
    )
    pieces = [swap(sent, "fsdp", rows_n, half)]
    bit = 1
    while bit < cols_n:
        pieces = pieces + [swap(part, "tensor", cols_n, bit) for part in pieces]
        bit *= 2

    early_weight = gather(weight[:, :early_cols], "fsdp", rows_n, half)

    moment, short, pack = start_call(momentum, gradient, probes, early_cols)
    early_moment = gather(short, "fsdp", rows_n, half)

    own, recv = butterfly(pack, "tensor", cols_n)
    pack, basis_1, _ = images_call(own, recv, probes, moment)
    own, recv = butterfly(pack, "fsdp", rows_n)
    pack, residue, diag_1 = reduced_call(own, recv, basis_1, None, None, moment)
    own, recv = butterfly(pack, "tensor", cols_n)
    pack, basis_2, low_1 = images_call(own, recv, residue, moment)
    own, recv = butterfly(pack, "fsdp", rows_n)
    pack, _, diag_2 = reduced_call(own, recv, basis_2, basis_1, low_1, moment)
    own, recv = butterfly(pack, "tensor", cols_n)
    diag_3, low_2 = last_call(own, recv)
    own, recv = butterfly(diag_3, "fsdp", rows_n)
    scaled, rate = top_call([diag_1, diag_2, own, recv], [low_1, low_2])

    far_tokens = jnp.zeros((num_rows, half * depth), tokens.dtype)
    for i, part in enumerate(pieces):
        far_tokens = lax.dynamic_update_slice_in_dim(far_tokens, part, (column_at ^ i) * piece, axis=0)

    gathered = []
    for chunk in range(CHUNKS):
        if chunk < EARLY:
            gathered.append((early_weight, early_moment, rate, chunk, width))
        else:
            stepped = step_call(weight, moment, rate, chunk, width)
            gathered.append((gather(stepped, "fsdp", rows_n, half), None, None, 0, width))

    far = []
    for chunk in range(CHUNKS):
        partial = project_call(far_order, far_tokens, *gathered[chunk], None, 0)
        far.append(swap(partial, "fsdp", rows_n, half))
    out = cols
    for chunk in range(CHUNKS):
        out = project_call(near_order, tokens, *gathered[chunk], out, chunk)
        if chunk >= 1:
            out = add_call(out, far[chunk - 1], chunk - 1)
    out = add_call(out, far[-1], CHUNKS - 1)
    return out, moment, scaled


def solution(mesh):
    return jax.shard_map(
        functools.partial(local, mesh.shape["fsdp"], mesh.shape["tensor"]),
        mesh=mesh,
        in_specs=(
            P("fsdp", None),
            P("fsdp", "tensor"),
            P("fsdp", "tensor"),
            P("fsdp", "tensor"),
            P(None, "tensor"),
        ),
        out_specs=(P("fsdp", "tensor"), P("fsdp", "tensor"), P()),
        check_vma=False,
    )
```

```python
import functools

import jax
import jax.numpy as jnp
from jax import lax
from jax.experimental import pallas as pl
from jax.experimental.pallas import tpu as pltpu
from jax.sharding import PartitionSpec as P

DECAY = 0.9
SQUARINGS = 5
LANES = 128
CHUNKS = 4
EARLY = 1
PARTS = 2

HIGHEST = lax.Precision.HIGHEST
LARGE = pltpu.CompilerParams(vmem_limit_bytes=56 * 1024 * 1024)
PARAMS = pltpu.CompilerParams(vmem_limit_bytes=24 * 1024 * 1024)
VMEM = pl.BlockSpec(memory_space=pltpu.VMEM)
ANY = pl.BlockSpec(memory_space=pl.ANY)


def fdot(left, right):
    return lax.dot_general(
        left, right, (((1,), (0,)), ((), ())), precision=HIGHEST, preferred_element_type=jnp.float32
    )


def fdot_t(left, right):
    return lax.dot_general(
        left, right, (((1,), (1,)), ((), ())), precision=HIGHEST, preferred_element_type=jnp.float32
    )


def halves(values):
    high = values.astype(jnp.bfloat16)
    return high, (values - high.astype(jnp.float32)).astype(jnp.bfloat16)


def split_dot(stacked, mat, contract):
    rows = stacked.shape[0] // 2
    mat_high, mat_low = halves(mat)
    dims = (((1,), (contract,)), ((), ()))
    first = lax.dot_general(stacked, mat_high, dims, preferred_element_type=jnp.float32)
    second = lax.dot_general(stacked[:rows], mat_low, dims, preferred_element_type=jnp.float32)
    return first[:rows] + first[rows:] + second


def eliminate(gram, count):
    rows = lax.broadcasted_iota(jnp.int32, (count, LANES), 0)
    lanes = lax.broadcasted_iota(jnp.int32, (count, LANES), 1)
    aug = jnp.where(lanes < count, gram, jnp.where(lanes - count == rows, 1.0, 0.0))
    for step in range(count):
        pivot = aug[step : step + 1, step : step + 1]
        factor = jnp.where(rows > step, aug[:, step : step + 1] * (1.0 / pivot), 0.0)
        aug = aug - factor * aug[step : step + 1, :]
    pivots = jnp.sum(jnp.where(lanes == rows, aug, 0.0), axis=1, keepdims=True)
    aug = aug * (1.0 / jnp.sqrt(pivots))
    low_t = jnp.where((lanes >= rows) & (lanes < count), aug, 0.0)
    return low_t, aug[:, count : 2 * count]


def pad_lanes(square):
    return jnp.concatenate(
        [square, jnp.zeros((square.shape[0], LANES - square.shape[1]), jnp.float32)], axis=1
    )


def pick_kernel(num_tokens, order_ref, tokens_ref, weight_ref, *refs):
    outs, early_ref, sems = refs[:num_tokens], refs[num_tokens], refs[-1]
    depth = weight_ref.shape[0]
    copies = []
    for part, out in enumerate(outs):
        rows = out.shape[0]
        for i in range(out.shape[1] // depth):
            copies.append(
                pltpu.make_async_copy(
                    tokens_ref.at[
                        pl.ds(pl.multiple_of(order_ref[0] + part * rows, 16), rows),
                        pl.ds(pl.multiple_of(order_ref[1 + i] * depth, LANES), depth),
                    ],
                    out.at[:, i * depth : (i + 1) * depth],
                    sems.at[len(copies)],
                )
            )
    copies.append(
        pltpu.make_async_copy(weight_ref.at[:, : early_ref.shape[1]], early_ref, sems.at[len(copies)])
    )
    for copy in copies:
        copy.start()
    for copy in copies:
        copy.wait()


def pick_call(order, tokens, weight, rows, count, early_cols):
    depth = weight.shape[0]
    sent = jax.ShapeDtypeStruct((rows, count * depth), tokens.dtype)
    return pl.pallas_call(
        functools.partial(pick_kernel, PARTS),
        grid_spec=pltpu.PrefetchScalarGridSpec(
            num_scalar_prefetch=1,
            grid=(1,),
            in_specs=[ANY, ANY],
            out_specs=[ANY] * (PARTS + 1),
            scratch_shapes=[pltpu.SemaphoreType.DMA((PARTS * count + 1,))],
        ),
        out_shape=[sent] * PARTS + [jax.ShapeDtypeStruct((depth, early_cols), weight.dtype)],
        compiler_params=LARGE,
    )(order, tokens, weight)


def start_kernel(width, mom_ref, grad_ref, probes_ref, tie_ref, moment_ref, short_ref, pack_ref, stack_ref):
    at = pl.program_id(0)
    count = probes_ref.shape[0]
    height = mom_ref.shape[0]

    @pl.when(at == 0)
    def _():
        probes = probes_ref[...]
        high, low = halves(probes)
        stack_ref[:count] = high
        stack_ref[count:] = low
        pack_ref[:, width:] = pad_lanes(fdot_t(probes, probes))

    moment = DECAY * mom_ref[...] + grad_ref[...].astype(jnp.float32)
    moment_ref[...] = moment
    short_ref[...] = moment[:, : short_ref.shape[1]].astype(jnp.bfloat16)
    pack_ref[:, pl.ds(pl.multiple_of(at * height, height), height)] = split_dot(stack_ref[...], moment, 1)


def start_call(momentum, gradient, probes, tie, early_cols):
    depth, cols = momentum.shape
    count = probes.shape[0]
    height = min(256, depth)
    rows = pl.BlockSpec((height, cols), lambda i: (i, 0))
    return pl.pallas_call(
        functools.partial(start_kernel, depth),
        grid=(depth // height,),
        in_specs=[rows, rows, VMEM, ANY],
        out_specs=[rows, pl.BlockSpec((height, early_cols), lambda i: (i, 0)), VMEM],
        out_shape=[
            jax.ShapeDtypeStruct((depth, cols), jnp.float32),
            jax.ShapeDtypeStruct((depth, early_cols), jnp.bfloat16),
            jax.ShapeDtypeStruct((count, depth + LANES), jnp.float32),
        ],
        scratch_shapes=[pltpu.VMEM((2 * count, cols), jnp.bfloat16)],
        compiler_params=LARGE,
    )(momentum, gradient, probes, tie)


def gate_kernel(passed, own_ref, recv_ref, *refs):
    sum_ref = refs[-1 - passed]
    sum_ref[...] = own_ref[...] + recv_ref[...]


def gate_call(own, recv, gates=(), ties=()):
    shapes = [jax.ShapeDtypeStruct(at.shape, at.dtype) for at in (own, *gates)]
    first = 2 + len(ties)
    return pl.pallas_call(
        functools.partial(gate_kernel, len(gates)),
        in_specs=[VMEM, VMEM] + [ANY] * (len(gates) + len(ties)),
        out_specs=[VMEM] + [ANY] * len(gates),
        out_shape=shapes,
        input_output_aliases={first + i: 1 + i for i in range(len(gates))},
        compiler_params=PARAMS,
    )(own, recv, *ties, *gates)


def images_kernel(own_ref, recv_ref, block_ref, moment_ref, pack_ref, basis_ref, low_ref, stack_ref):
    at = pl.program_id(0)
    count, cols = block_ref.shape
    depth = moment_ref.shape[0]
    width = moment_ref.shape[1]

    @pl.when(at == 0)
    def _():
        low_t, inverse = eliminate(own_ref[:, depth:] + recv_ref[:, depth:], count)
        low_ref[...] = low_t
        reduced = fdot(inverse, own_ref[:, :depth] + recv_ref[:, :depth])
        high, low = halves(reduced)
        stack_ref[:count] = high
        stack_ref[count:] = low
        pack_ref[:, cols:] = pad_lanes(fdot_t(reduced, reduced))
        basis_ref[...] = fdot(inverse, block_ref[...])

    pack_ref[:, pl.ds(pl.multiple_of(at * width, width), width)] = split_dot(stack_ref[...], moment_ref[...], 0)


def images_call(own, recv, block, moment):
    depth, cols = moment.shape
    count = block.shape[0]
    width = min(512, cols)
    return pl.pallas_call(
        images_kernel,
        grid=(cols // width,),
        in_specs=[VMEM, VMEM, VMEM, pl.BlockSpec((depth, width), lambda i: (0, i))],
        out_specs=[VMEM, VMEM, VMEM],
        out_shape=[
            jax.ShapeDtypeStruct((count, cols + LANES), jnp.float32),
            jax.ShapeDtypeStruct((count, cols), jnp.float32),
            jax.ShapeDtypeStruct((count, LANES), jnp.float32),
        ],
        scratch_shapes=[pltpu.VMEM((2 * count, depth), jnp.bfloat16)],
        compiler_params=PARAMS,
    )(own, recv, block, moment)


def reduced_kernel(has_prev, passed, width, *refs):
    names = 5 if has_prev else 3
    own_ref, recv_ref, basis_ref = refs[:3]
    prev_ref, low_ref = refs[3:5] if has_prev else (None, None)
    moment_ref = refs[names]
    outs = refs[names + 1 + passed :]
    pack_ref, residue_ref, diag_ref = outs[:3]
    stack_ref = refs[-1]
    at = pl.program_id(0)
    count, cols = basis_ref.shape
    height = moment_ref.shape[0]

    @pl.when(at == 0)
    def _():
        diag = (own_ref[:, cols:] + recv_ref[:, cols:])[:, :count]
        diag = 0.5 * (diag + diag.T)
        diag_ref[...] = pad_lanes(diag)
        residue = own_ref[:, :cols] + recv_ref[:, :cols] - fdot(diag, basis_ref[...])
        if has_prev:
            residue = residue - fdot(low_ref[:, :count], prev_ref[...])
        residue_ref[...] = residue
        high, low = halves(residue)
        stack_ref[:count] = high
        stack_ref[count:] = low
        pack_ref[:, width:] = pad_lanes(fdot_t(residue, residue))

    moment = moment_ref[...]
    if passed:
        short_ref = outs[3]
        short_ref[...] = moment[:, : short_ref.shape[1]].astype(jnp.bfloat16)
    pack_ref[:, pl.ds(pl.multiple_of(at * height, height), height)] = split_dot(stack_ref[...], moment, 1)


def reduced_call(own, recv, basis, prev, low, moment, gates, early_cols):
    depth, cols = moment.shape
    count = basis.shape[0]
    height = min(256, depth)
    has_prev = prev is not None
    operands = (own, recv, basis) + ((prev, low) if has_prev else ()) + (moment,)
    out_specs = [VMEM, VMEM, VMEM]
    out_shape = [
        jax.ShapeDtypeStruct((count, depth + LANES), jnp.float32),
        jax.ShapeDtypeStruct((count, cols), jnp.float32),
        jax.ShapeDtypeStruct((count, LANES), jnp.float32),
    ]
    if gates:
        out_specs += [pl.BlockSpec((height, early_cols), lambda i: (i, 0))] + [ANY] * len(gates)
        out_shape += [jax.ShapeDtypeStruct((depth, early_cols), jnp.bfloat16)]
        out_shape += [jax.ShapeDtypeStruct(at.shape, at.dtype) for at in gates]
    return pl.pallas_call(
        functools.partial(reduced_kernel, has_prev, len(gates), depth),
        grid=(depth // height,),
        in_specs=[VMEM] * (len(operands) - 1)
        + [pl.BlockSpec((height, cols), lambda i: (i, 0))]
        + [ANY] * len(gates),
        out_specs=out_specs,
        out_shape=out_shape,
        input_output_aliases={len(operands) + i: 4 + i for i in range(len(gates))},
        scratch_shapes=[pltpu.VMEM((2 * count, cols), jnp.bfloat16)],
        compiler_params=PARAMS,
    )(*operands, *gates)


def last_kernel(own_ref, recv_ref, diag_ref, low_ref):
    count = own_ref.shape[0]
    depth = own_ref.shape[1] - LANES
    low_t, inverse = eliminate(own_ref[:, depth:] + recv_ref[:, depth:], count)
    low_ref[...] = low_t
    reduced = fdot(inverse, own_ref[:, :depth] + recv_ref[:, :depth])
    diag_ref[...] = pad_lanes(fdot_t(reduced, reduced))


def last_call(own, recv):
    shape = jax.ShapeDtypeStruct((own.shape[0], LANES), jnp.float32)
    return pl.pallas_call(
        last_kernel,
        in_specs=[VMEM, VMEM],
        out_specs=[VMEM, VMEM],
        out_shape=[shape, shape],
        compiler_params=PARAMS,
    )(own, recv)


def top_kernel(steps, *refs):
    diag_refs = refs[: steps + 1]
    low_refs = refs[steps + 1 : 2 * steps]
    scaled_ref, rate_ref, krylov_ref = refs[-3:]
    count = diag_refs[0].shape[0]
    size = steps * count
    krylov_ref[...] = jnp.zeros_like(krylov_ref)
    for place in range(steps):
        first = place * count
        diag = diag_refs[place][:, :count]
        if place + 1 == steps:
            diag = diag + diag_refs[steps][:, :count]
        krylov_ref[first : first + count, first : first + count] = 0.5 * (diag + diag.T)
        if place + 1 < steps:
            second = first + count
            low_t = low_refs[place][:, :count]
            krylov_ref[second : second + count, first:second] = low_t
            krylov_ref[first:second, second : second + count] = low_t.T
    krylov = krylov_ref[...]
    power = krylov * (1.0 / jnp.max(jnp.abs(krylov), keepdims=True))
    for _ in range(SQUARINGS):
        power = fdot(power, power)
        power = power * (1.0 / jnp.max(jnp.abs(power), keepdims=True))
    tall = jnp.sum(power, axis=1, keepdims=True)
    wide = jnp.sum(power, axis=0, keepdims=True)
    tall = tall * (1.0 / jnp.sqrt(jnp.sum(tall * tall, keepdims=True)))
    wide = wide * (1.0 / jnp.sqrt(jnp.sum(wide * wide, keepdims=True)))
    top = jnp.sum(krylov * tall * wide, keepdims=True)
    scaled_ref[...] = krylov[:size, :size] / top
    rate_ref[...] = jnp.broadcast_to(1.0 / jnp.sqrt(top), rate_ref.shape)


def top_call(diags, lows, ties):
    steps = len(lows) + 1
    count = diags[0].shape[0]
    size = steps * count
    padded = -(-size // LANES) * LANES
    return pl.pallas_call(
        functools.partial(top_kernel, steps),
        in_specs=[VMEM] * (2 * steps) + [ANY] * len(ties),
        out_specs=[VMEM, VMEM],
        out_shape=[
            jax.ShapeDtypeStruct((size, size), jnp.float32),
            jax.ShapeDtypeStruct((8, LANES), jnp.float32),
        ],
        scratch_shapes=[pltpu.VMEM((padded, padded), jnp.float32)],
        compiler_params=PARAMS,
    )(*diags, *lows, *ties)


def step_kernel(count, weight_ref, moment_ref, rate_ref, *out_refs):
    stepped = weight_ref[...].astype(jnp.float32) - moment_ref[...] * rate_ref[:1, :1]
    at = pl.program_id(1)
    for i in range(count):

        @pl.when(at == i)
        def _():
            out_refs[i][...] = stepped.astype(jnp.bfloat16)


def step_call(weight, moment, rate, first, width):
    depth, cols = weight.shape
    height = min(512, depth)
    count = cols // width - first
    block = pl.BlockSpec((height, width), lambda r, c: (r, first + c))
    out = pl.BlockSpec((height, width), lambda r, c: (r, 0))
    return pl.pallas_call(
        functools.partial(step_kernel, count),
        grid=(depth // height, count),
        in_specs=[block, block, VMEM],
        out_specs=[out] * count,
        out_shape=[jax.ShapeDtypeStruct((depth, width), jnp.bfloat16)] * count,
        compiler_params=LARGE,
    )(weight, moment, rate)


def project_kernel(far, pieces, count, early, in_place, ties, out_chunk, order_ref, *refs):
    tokens = refs[:pieces]
    refs = refs[pieces:]
    weights, refs = refs[:count], refs[count:]
    if early:
        moments, rate_ref, refs = refs[:count], refs[count], refs[count + 1 :]
    refs = refs[ties + (1 if in_place else 0) :]
    out_ref, tokens_buf, weight_buf, moment_buf, total_ref, result_ref, sems, out_sem = refs
    depth, width = weight_buf.shape[1:]
    copies = []
    for k in range(count):
        step = []
        for i in range(pieces):
            if far:
                rows = tokens[i].shape[0]
                source = tokens[i].at[:, k * depth : (k + 1) * depth]
                target = tokens_buf.at[k, pl.ds(pl.multiple_of(order_ref[i], 16), rows), :]
            else:
                source = tokens[i].at[:, pl.ds(pl.multiple_of(order_ref[k] * depth, LANES), depth)]
                target = tokens_buf.at[k]
            step.append(pltpu.make_async_copy(source, target, sems.at[k, i]))
        step.append(pltpu.make_async_copy(weights[k], weight_buf.at[k], sems.at[k, pieces]))
        if early:
            step.append(pltpu.make_async_copy(moments[k], moment_buf.at[k], sems.at[k, pieces + 1]))
        for copy in step:
            copy.start()
        copies.append(step)
    for k in range(count):
        for copy in copies[k]:
            copy.wait()
        block = weight_buf[k]
        if early:
            stepped = block.astype(jnp.float32) - moment_buf[k].astype(jnp.float32) * rate_ref[:1, :1]
            block = stepped.astype(jnp.bfloat16)
        part = jnp.dot(tokens_buf[k], block, preferred_element_type=jnp.float32)
        total_ref[...] = part if k == 0 else total_ref[...] + part
    if far:
        result_ref[...] = total_ref[...].astype(result_ref.dtype)
        copy = pltpu.make_async_copy(result_ref, out_ref, out_sem)
    else:
        copy = pltpu.make_async_copy(
            total_ref, out_ref.at[:, out_chunk * width : (out_chunk + 1) * width], out_sem
        )
    copy.start()
    copy.wait()


def project_call(far, order, tokens, weights, moments, rate, ties=(), out=None, cols=None, out_chunk=0):
    count = len(weights)
    early = moments is not None
    depth, width = weights[0].shape
    num_rows = sum(at.shape[0] for at in tokens)
    operands = list(tokens) + list(weights)
    specs = [ANY] * len(operands)
    if early:
        operands += list(moments) + [rate]
        specs += [ANY] * count + [VMEM]
    operands += list(ties)
    specs += [ANY] * len(ties)
    aliases = {}
    if far:
        out_shape = jax.ShapeDtypeStruct((num_rows, width), jnp.bfloat16)
    else:
        out_shape = jax.ShapeDtypeStruct((num_rows, cols), jnp.float32)
        if out is not None:
            operands.append(out)
            specs.append(ANY)
            aliases = {len(operands): 0}
    return pl.pallas_call(
        functools.partial(
            project_kernel, far, len(tokens), count, early, bool(aliases), len(ties), out_chunk
        ),
        grid_spec=pltpu.PrefetchScalarGridSpec(
            num_scalar_prefetch=1,
            grid=(1,),
            in_specs=specs,
            out_specs=ANY,
            scratch_shapes=[
                pltpu.VMEM((count, num_rows, depth), jnp.bfloat16),
                pltpu.VMEM((count, depth, width), jnp.bfloat16),
                pltpu.VMEM((count, depth, width) if early else (8, LANES), jnp.bfloat16),
                pltpu.VMEM((num_rows, width), jnp.float32),
                pltpu.VMEM((num_rows, width) if far else (8, LANES), jnp.bfloat16),
                pltpu.SemaphoreType.DMA((count, len(tokens) + 2)),
                pltpu.SemaphoreType.DMA,
            ],
        ),
        out_shape=out_shape,
        input_output_aliases=aliases,
        compiler_params=LARGE,
        cost_estimate=pl.CostEstimate(
            flops=2 * num_rows * count * depth * width,
            bytes_accessed=2 * num_rows * count * depth + 4 * count * depth * width,
            transcendentals=0,
        ),
    )(order, *operands)


def add_kernel(old_ref, far_ref, out_ref):
    out_ref[...] = old_ref[...] + far_ref[...].astype(jnp.float32)


def add_call(out, far, chunk):
    num_rows, width = far.shape
    height = min(256, num_rows)
    block = pl.BlockSpec((height, width), lambda r: (r, chunk))
    return pl.pallas_call(
        add_kernel,
        grid=(num_rows // height,),
        in_specs=[block, pl.BlockSpec((height, width), lambda r: (r, 0))],
        out_specs=block,
        out_shape=jax.ShapeDtypeStruct(out.shape, out.dtype),
        input_output_aliases={0: 0},
        compiler_params=LARGE,
    )(out, far)


def swap(values, axis, size, bit):
    return lax.ppermute(values, axis, [(at, at ^ bit) for at in range(size)])


def butterfly(values, axis, size):
    bit = 1
    while 2 * bit < size:
        values = values + swap(values, axis, size, bit)
        bit *= 2
    return values, swap(values, axis, size, bit)


def offsets(count):
    found = [0]
    bit = count // 2
    while bit:
        found = found + [at ^ bit for at in found]
        bit //= 2
    return found


def gather(values, axis, size, count):
    parts = [values]
    bit = count // 2
    while bit:
        parts = parts + [swap(part, axis, size, bit) for part in parts]
        bit //= 2
    return parts


def spread(piece, axis, size):
    parts = [piece]
    bit = 1
    while bit < size:
        parts = parts + [swap(part, axis, size, bit) for part in parts]
        bit *= 2
    return parts


def local(rows_n, cols_n, tokens, weight, momentum, gradient, probes):
    half = rows_n // 2
    far_bit, near_bit = half // 2, half // 4
    place = lax.axis_index("fsdp")
    low_at = lax.rem(place, half)
    side = lax.div(place, half)
    column_at = lax.axis_index("tensor")
    num_rows = tokens.shape[0]
    depth, cols = weight.shape
    rows = num_rows // cols_n // PARTS
    width = cols // CHUNKS
    early_cols = EARLY * width

    def fswap(values, bit):
        return swap(values, "fsdp", rows_n, bit)

    def complete(own, across, beside):
        parts = [own, across, beside, fswap(across, near_bit)]
        bit = near_bit // 2
        while bit:
            parts = parts + [fswap(part, bit) for part in parts]
            bit //= 2
        return parts

    def sum_over_rows(pack, gates, ties):
        passed = {}
        bit = 1
        while bit < half:
            pack, *passed[bit] = gate_call(pack, fswap(pack, bit), gates.get(bit, ()), ties.get(bit, ()))
            bit *= 2
        return pack, fswap(pack, half), passed

    mixed = jnp.stack([low_at ^ at for at in offsets(half)]).astype(jnp.int32)
    near_order = side * half + mixed
    pick_order = jnp.concatenate([(column_at * PARTS * rows)[None], (1 - side) * half + mixed])
    far_order = jnp.stack(
        [(column_at ^ i) * PARTS * rows + part * rows for part in range(PARTS) for i in range(cols_n)]
    ).astype(jnp.int32)

    sent_0, sent_1, weight_own = pick_call(pick_order, tokens, weight, rows, half, early_cols)
    moment, short_1, pack = start_call(momentum, gradient, probes, sent_0, early_cols)
    weight_beside = fswap(weight_own, near_bit)
    weight_across = fswap(weight_own, far_bit)
    tokens_0 = fswap(sent_0, half)

    own, recv = butterfly(pack, "tensor", cols_n)
    pack, basis_1, _ = images_call(own, recv, probes, moment)
    own, recv, passed = sum_over_rows(
        pack, {1: [weight_across, short_1], 2: [tokens_0]}, {1: [weight_beside]}
    )
    weight_across, short_1 = passed[1]
    weight_parts = complete(weight_own, weight_across, weight_beside)
    moment_beside = fswap(short_1, near_bit)
    token_parts = spread(passed[2][0], "tensor", cols_n)
    pack, residue, diag_1, short_2, sent_1 = reduced_call(
        own, recv, basis_1, None, None, moment, [sent_1], early_cols
    )
    moment_across = fswap(short_2, far_bit)
    tokens_1 = fswap(sent_1, half)

    own, recv = butterfly(pack, "tensor", cols_n)
    pack, basis_2, low_1 = images_call(own, recv, residue, moment)
    own, recv, passed = sum_over_rows(
        pack,
        {1: [moment_across], 2: [tokens_1]},
        {1: [*token_parts[1:], *weight_parts[3:], moment_beside]},
    )
    moment_parts = complete(short_1, passed[1][0], moment_beside)
    token_parts = token_parts + spread(passed[2][0], "tensor", cols_n)
    pack, _, diag_2 = reduced_call(own, recv, basis_2, basis_1, low_1, moment, [], early_cols)

    own, recv = butterfly(pack, "tensor", cols_n)
    diag_3, low_2 = last_call(own, recv)
    own, recv = butterfly(diag_3, "fsdp", rows_n)
    scaled, rate = top_call(
        [diag_1, diag_2, own, recv], [low_1, low_2], [*token_parts[cols_n + 1 :], *moment_parts[3:]]
    )

    stepped = step_call(weight, moment, rate, EARLY, width)
    gathered = [(weight_parts, moment_parts, rate)]
    gathered += [(gather(part, "fsdp", rows_n, half), None, None) for part in stepped]

    partial, far = [stepped[0]], []
    for chunk in range(CHUNKS):
        partial.append(project_call(True, far_order, token_parts, *gathered[chunk], ties=partial[-1:]))
        far.append(fswap(partial[-1], half))
    out = None
    for chunk in range(CHUNKS):
        out = project_call(
            False,
            near_order,
            [tokens],
            *gathered[chunk],
            ties=[partial[chunk + 1]],
            out=out,
            cols=cols,
            out_chunk=chunk,
        )
        if chunk:
            out = add_call(out, far[chunk - 1], chunk - 1)
    out = add_call(out, far[-1], CHUNKS - 1)
    return out, moment, scaled


def solution(mesh):
    return jax.shard_map(
        functools.partial(local, mesh.shape["fsdp"], mesh.shape["tensor"]),
        mesh=mesh,
        in_specs=(
            P("fsdp", None),
            P("fsdp", "tensor"),
            P("fsdp", "tensor"),
            P("fsdp", "tensor"),
            P(None, "tensor"),
        ),
        out_specs=(P("fsdp", "tensor"), P("fsdp", "tensor"), P()),
        check_vma=False,
    )
```

```python
import functools

import jax
import jax.numpy as jnp
from jax import lax
from jax.experimental import pallas as pl
from jax.experimental.pallas import tpu as pltpu
from jax.sharding import PartitionSpec as P

DECAY = 0.9
SQUARINGS = 5
LANES = 128
UNIT = 256
EARLY = (1, 1)
LATE = (2, 1, 1, 1, 1)
PARTS = 2

HIGHEST = lax.Precision.HIGHEST
LARGE = pltpu.CompilerParams(vmem_limit_bytes=53 * 1024 * 1024)
PARAMS = pltpu.CompilerParams(vmem_limit_bytes=24 * 1024 * 1024)
BRIEF = pl.CostEstimate(flops=0, bytes_accessed=0, transcendentals=0)
VMEM = pl.BlockSpec(memory_space=pltpu.VMEM)
ANY = pl.BlockSpec(memory_space=pl.ANY)


def fdot(left, right):
    return lax.dot_general(
        left, right, (((1,), (0,)), ((), ())), precision=HIGHEST, preferred_element_type=jnp.float32
    )


def fdot_t(left, right):
    return lax.dot_general(
        left, right, (((1,), (1,)), ((), ())), precision=HIGHEST, preferred_element_type=jnp.float32
    )


def halves(values):
    high = values.astype(jnp.bfloat16)
    return high, (values - high.astype(jnp.float32)).astype(jnp.bfloat16)


def split_dot(stacked, mat, contract):
    rows = stacked.shape[0] // 2
    mat_high, mat_low = halves(mat)
    dims = (((1,), (contract,)), ((), ()))
    first = lax.dot_general(stacked, mat_high, dims, preferred_element_type=jnp.float32)
    second = lax.dot_general(stacked[:rows], mat_low, dims, preferred_element_type=jnp.float32)
    return first[:rows] + first[rows:] + second


def eliminate(gram, count):
    rows = lax.broadcasted_iota(jnp.int32, (count, LANES), 0)
    lanes = lax.broadcasted_iota(jnp.int32, (count, LANES), 1)
    aug = jnp.where(lanes < count, gram, jnp.where(lanes - count == rows, 1.0, 0.0))
    for step in range(count):
        pivot = aug[step : step + 1, step : step + 1]
        factor = jnp.where(rows > step, aug[:, step : step + 1] * (1.0 / pivot), 0.0)
        aug = aug - factor * aug[step : step + 1, :]
    pivots = jnp.sum(jnp.where(lanes == rows, aug, 0.0), axis=1, keepdims=True)
    aug = aug * (1.0 / jnp.sqrt(pivots))
    low_t = jnp.where((lanes >= rows) & (lanes < count), aug, 0.0)
    return low_t, aug[:, count : 2 * count]


def pad_lanes(square):
    return jnp.concatenate(
        [square, jnp.zeros((square.shape[0], LANES - square.shape[1]), jnp.float32)], axis=1
    )


def pick_kernel(order_ref, token_0, token_1, weight_ref, sent_0, sent_1, early_ref):
    sent_0[...] = token_0[...]
    sent_1[...] = token_1[...]
    early_ref[...] = weight_ref[...]


def pick_call(order, tokens, weight, rows, count, early_cols):
    depth = weight.shape[0]
    height = depth // count
    sent = jax.ShapeDtypeStruct((rows, count * depth), tokens.dtype)
    weight_spec = pl.BlockSpec((height, early_cols), lambda i, order_ref: (i, 0))
    sent_spec = pl.BlockSpec((rows, depth), lambda i, order_ref: (0, i))
    return pl.pallas_call(
        pick_kernel,
        grid_spec=pltpu.PrefetchScalarGridSpec(
            num_scalar_prefetch=1,
            grid=(count,),
            in_specs=[
                pl.BlockSpec((rows, depth), lambda i, order_ref: (order_ref[0], order_ref[1 + i])),
                pl.BlockSpec((rows, depth), lambda i, order_ref: (order_ref[0] + 1, order_ref[1 + i])),
                weight_spec,
            ],
            out_specs=[sent_spec, sent_spec, weight_spec],
        ),
        out_shape=[sent, sent, jax.ShapeDtypeStruct((depth, early_cols), weight.dtype)],
        compiler_params=LARGE,
        cost_estimate=BRIEF,
    )(order, tokens, tokens, weight)


def start_kernel(width, mom_ref, grad_ref, probes_ref, tie_ref, moment_ref, short_ref, pack_ref, stack_ref):
    at = pl.program_id(0)
    count = probes_ref.shape[0]
    height = mom_ref.shape[0]

    @pl.when(at == 0)
    def _():
        probes = probes_ref[...]
        high, low = halves(probes)
        stack_ref[:count] = high
        stack_ref[count:] = low
        pack_ref[:, width:] = pad_lanes(fdot_t(probes, probes))

    moment = DECAY * mom_ref[...] + grad_ref[...].astype(jnp.float32)
    moment_ref[...] = moment
    short_ref[...] = moment[:, : short_ref.shape[1]].astype(jnp.bfloat16)
    pack_ref[:, pl.ds(pl.multiple_of(at * height, height), height)] = split_dot(stack_ref[...], moment, 1)


def start_call(momentum, gradient, probes, tie, early_cols):
    depth, cols = momentum.shape
    count = probes.shape[0]
    height = min(256, depth)
    rows = pl.BlockSpec((height, cols), lambda i: (i, 0))
    return pl.pallas_call(
        functools.partial(start_kernel, depth),
        grid=(depth // height,),
        in_specs=[rows, rows, VMEM, ANY],
        out_specs=[rows, pl.BlockSpec((height, early_cols), lambda i: (i, 0)), VMEM],
        out_shape=[
            jax.ShapeDtypeStruct((depth, cols), jnp.float32),
            jax.ShapeDtypeStruct((depth, early_cols), jnp.bfloat16),
            jax.ShapeDtypeStruct((count, depth + LANES), jnp.float32),
        ],
        scratch_shapes=[pltpu.VMEM((2 * count, cols), jnp.bfloat16)],
        compiler_params=LARGE,
        cost_estimate=BRIEF,
    )(momentum, gradient, probes, tie)


def gate_kernel(passed, own_ref, recv_ref, *refs):
    sum_ref = refs[-1 - passed]
    sum_ref[...] = own_ref[...] + recv_ref[...]


def gate_call(own, recv, gates=(), ties=()):
    shapes = [jax.ShapeDtypeStruct(at.shape, at.dtype) for at in (own, *gates)]
    first = 2 + len(ties)
    return pl.pallas_call(
        functools.partial(gate_kernel, len(gates)),
        in_specs=[VMEM, VMEM] + [ANY] * (len(gates) + len(ties)),
        out_specs=[VMEM] + [ANY] * len(gates),
        out_shape=shapes,
        input_output_aliases={first + i: 1 + i for i in range(len(gates))},
        compiler_params=LARGE,
        cost_estimate=BRIEF,
    )(own, recv, *ties, *gates)


def pass_kernel(value_ref, tie_ref, out_ref):
    pass


def pass_call(value, tie):
    return pl.pallas_call(
        pass_kernel,
        in_specs=[ANY, ANY],
        out_specs=ANY,
        out_shape=jax.ShapeDtypeStruct(value.shape, value.dtype),
        input_output_aliases={0: 0},
        compiler_params=LARGE,
        cost_estimate=BRIEF,
    )(value, tie)


def images_kernel(
    own_ref, recv_ref, block_ref, moment_ref, pack_ref, basis_ref, low_ref, held_ref, stack_ref, sems
):
    count, cols = block_ref.shape
    blocks, depth, width = held_ref.shape
    copies = [
        pltpu.make_async_copy(
            moment_ref.at[:, at * width : (at + 1) * width], held_ref.at[at], sems.at[at]
        )
        for at in range(blocks)
    ]
    for copy in copies:
        copy.start()
    low_t, inverse = eliminate(own_ref[:, depth:] + recv_ref[:, depth:], count)
    low_ref[...] = low_t
    reduced = fdot(inverse, own_ref[:, :depth] + recv_ref[:, :depth])
    high, low = halves(reduced)
    stack_ref[:count] = high
    stack_ref[count:] = low
    pack_ref[:, cols:] = pad_lanes(fdot_t(reduced, reduced))
    basis_ref[...] = fdot(inverse, block_ref[...])
    for at, copy in enumerate(copies):
        copy.wait()
        pack_ref[:, at * width : (at + 1) * width] = split_dot(stack_ref[...], held_ref[at], 0)


def images_call(own, recv, block, moment):
    depth, cols = moment.shape
    count = block.shape[0]
    width = min(512, cols)
    return pl.pallas_call(
        images_kernel,
        in_specs=[VMEM, VMEM, VMEM, ANY],
        out_specs=[VMEM, VMEM, VMEM],
        out_shape=[
            jax.ShapeDtypeStruct((count, cols + LANES), jnp.float32),
            jax.ShapeDtypeStruct((count, cols), jnp.float32),
            jax.ShapeDtypeStruct((count, LANES), jnp.float32),
        ],
        scratch_shapes=[
            pltpu.VMEM((cols // width, depth, width), jnp.float32),
            pltpu.VMEM((2 * count, depth), jnp.bfloat16),
            pltpu.SemaphoreType.DMA((cols // width,)),
        ],
        compiler_params=LARGE,
        cost_estimate=BRIEF,
    )(own, recv, block, moment)


def reduced_kernel(has_prev, passed, *refs):
    names = 5 if has_prev else 3
    own_ref, recv_ref, basis_ref = refs[:3]
    prev_ref, low_ref = refs[3:5] if has_prev else (None, None)
    moment_ref = refs[names]
    outs = refs[names + 1 + passed :]
    pack_ref, residue_ref, diag_ref = outs[:3]
    held_ref, sems = refs[-2:]
    count, cols = basis_ref.shape
    blocks, height = held_ref.shape[:2]
    copies = [
        pltpu.make_async_copy(moment_ref.at[at * height : (at + 1) * height], held_ref.at[at], sems.at[at])
        for at in range(blocks)
    ]
    for copy in copies:
        copy.start()
    diag = (own_ref[:, cols:] + recv_ref[:, cols:])[:, :count]
    diag = 0.5 * (diag + diag.T)
    diag_ref[...] = pad_lanes(diag)
    residue = own_ref[:, :cols] + recv_ref[:, :cols] - fdot(diag, basis_ref[...])
    if has_prev:
        residue = residue - fdot(low_ref[:, :count], prev_ref[...])
    residue_ref[...] = residue
    stacked = jnp.concatenate(halves(residue), axis=0)
    pack_ref[:, blocks * height :] = pad_lanes(fdot_t(residue, residue))
    for at, copy in enumerate(copies):
        copy.wait()
        moment = held_ref[at]
        if passed:
            short_ref = outs[3]
            short_ref[at * height : (at + 1) * height] = moment[:, : short_ref.shape[1]].astype(jnp.bfloat16)
        pack_ref[:, at * height : (at + 1) * height] = split_dot(stacked, moment, 1)


def reduced_call(own, recv, basis, prev, low, moment, gates, early_cols):
    depth, cols = moment.shape
    count = basis.shape[0]
    height = min(256, depth)
    has_prev = prev is not None
    operands = (own, recv, basis) + ((prev, low) if has_prev else ()) + (moment,)
    out_specs = [VMEM, VMEM, VMEM]
    out_shape = [
        jax.ShapeDtypeStruct((count, depth + LANES), jnp.float32),
        jax.ShapeDtypeStruct((count, cols), jnp.float32),
        jax.ShapeDtypeStruct((count, LANES), jnp.float32),
    ]
    if gates:
        out_specs += [VMEM] + [ANY] * len(gates)
        out_shape += [jax.ShapeDtypeStruct((depth, early_cols), jnp.bfloat16)]
        out_shape += [jax.ShapeDtypeStruct(at.shape, at.dtype) for at in gates]
    return pl.pallas_call(
        functools.partial(reduced_kernel, has_prev, len(gates)),
        in_specs=[VMEM] * (len(operands) - 1) + [ANY] * (1 + len(gates)),
        out_specs=out_specs,
        out_shape=out_shape,
        input_output_aliases={len(operands) + i: 4 + i for i in range(len(gates))},
        scratch_shapes=[
            pltpu.VMEM((depth // height, height, cols), jnp.float32),
            pltpu.SemaphoreType.DMA((depth // height,)),
        ],
        compiler_params=LARGE,
        cost_estimate=BRIEF,
    )(*operands, *gates)


def last_kernel(passed, own_ref, recv_ref, *refs):
    diag_ref, low_ref = refs[passed : passed + 2]
    count = own_ref.shape[0]
    depth = own_ref.shape[1] - LANES
    low_t, inverse = eliminate(own_ref[:, depth:] + recv_ref[:, depth:], count)
    low_ref[...] = low_t
    reduced = fdot(inverse, own_ref[:, :depth] + recv_ref[:, :depth])
    diag_ref[...] = pad_lanes(fdot_t(reduced, reduced))


def last_call(own, recv, gates):
    shape = jax.ShapeDtypeStruct((own.shape[0], LANES), jnp.float32)
    return pl.pallas_call(
        functools.partial(last_kernel, len(gates)),
        in_specs=[VMEM, VMEM] + [ANY] * len(gates),
        out_specs=[VMEM, VMEM] + [ANY] * len(gates),
        out_shape=[shape, shape] + [jax.ShapeDtypeStruct(at.shape, at.dtype) for at in gates],
        input_output_aliases={2 + i: 2 + i for i in range(len(gates))},
        compiler_params=LARGE,
        cost_estimate=BRIEF,
    )(own, recv, *gates)


def top_kernel(steps, *refs):
    diag_refs = refs[: steps + 1]
    low_refs = refs[steps + 1 : 2 * steps]
    scaled_ref, rate_ref, krylov_ref = refs[-3:]
    count = diag_refs[0].shape[0]
    size = steps * count
    krylov_ref[...] = jnp.zeros_like(krylov_ref)
    for place in range(steps):
        first = place * count
        diag = diag_refs[place][:, :count]
        if place + 1 == steps:
            diag = diag + diag_refs[steps][:, :count]
        krylov_ref[first : first + count, first : first + count] = 0.5 * (diag + diag.T)
        if place + 1 < steps:
            second = first + count
            low_t = low_refs[place][:, :count]
            krylov_ref[second : second + count, first:second] = low_t
            krylov_ref[first:second, second : second + count] = low_t.T
    krylov = krylov_ref[...]
    power = krylov * (1.0 / jnp.max(jnp.abs(krylov), keepdims=True))
    for _ in range(SQUARINGS):
        power = fdot(power, power)
        power = power * (1.0 / jnp.max(jnp.abs(power), keepdims=True))
    tall = jnp.sum(power, axis=1, keepdims=True)
    wide = jnp.sum(power, axis=0, keepdims=True)
    tall = tall * (1.0 / jnp.sqrt(jnp.sum(tall * tall, keepdims=True)))
    wide = wide * (1.0 / jnp.sqrt(jnp.sum(wide * wide, keepdims=True)))
    top = jnp.sum(krylov * tall * wide, keepdims=True)
    scaled_ref[...] = krylov[:size, :size] / top
    rate_ref[...] = jnp.broadcast_to(1.0 / jnp.sqrt(top), rate_ref.shape)


def top_call(diags, lows, ties):
    steps = len(lows) + 1
    count = diags[0].shape[0]
    size = steps * count
    padded = -(-size // LANES) * LANES
    return pl.pallas_call(
        functools.partial(top_kernel, steps),
        in_specs=[VMEM] * (2 * steps) + [ANY] * len(ties),
        out_specs=[VMEM, VMEM],
        out_shape=[
            jax.ShapeDtypeStruct((size, size), jnp.float32),
            jax.ShapeDtypeStruct((8, LANES), jnp.float32),
        ],
        scratch_shapes=[pltpu.VMEM((padded, padded), jnp.float32)],
        compiler_params=PARAMS,
        cost_estimate=BRIEF,
    )(*diags, *lows, *ties)


def step_kernel(weight_ref, moment_ref, rate_ref, tie_ref, out_ref):
    stepped = weight_ref[...].astype(jnp.float32) - moment_ref[...] * rate_ref[:1, :1]
    out_ref[...] = stepped.astype(jnp.bfloat16)


def step_call(weight, moment, rate, first, width, tie):
    depth = weight.shape[0]
    height = min(512, depth)
    block = pl.BlockSpec((height, width), lambda r: (r, first // width))
    return pl.pallas_call(
        step_kernel,
        grid=(depth // height,),
        in_specs=[block, block, VMEM, ANY],
        out_specs=pl.BlockSpec((height, width), lambda r: (r, 0)),
        out_shape=jax.ShapeDtypeStruct((depth, width), jnp.bfloat16),
        compiler_params=LARGE,
        cost_estimate=BRIEF,
    )(weight, moment, rate, tie)


def project_kernel(far, pieces, count, early, in_place, ties, first, order_ref, *refs):
    tokens = refs[:pieces]
    refs = refs[pieces:]
    weights, refs = refs[:count], refs[count:]
    if early:
        moments, rate_ref, refs = refs[:count], refs[count], refs[count + 1 :]
    refs = refs[ties + (1 if in_place else 0) :]
    if not far:
        refs[1][...] = jnp.zeros(refs[1].shape, jnp.float32)
        refs = refs[:1] + refs[2:]
    out_ref, tokens_buf, weight_buf, moment_buf, total_ref, result_ref, sems, out_sem = refs
    depth, width = weight_buf.shape[1:]
    copies = []
    for k in range(count):
        step = []
        for i in range(pieces):
            if far:
                rows = tokens[i].shape[0]
                source = tokens[i].at[:, k * depth : (k + 1) * depth]
                target = tokens_buf.at[k, pl.ds(pl.multiple_of(order_ref[i], 16), rows), :]
            else:
                source = tokens[i].at[:, pl.ds(pl.multiple_of(order_ref[k] * depth, LANES), depth)]
                target = tokens_buf.at[k]
            step.append(pltpu.make_async_copy(source, target, sems.at[k, i]))
        at = slice(first, first + width) if early else slice(None)
        step.append(pltpu.make_async_copy(weights[k].at[:, at], weight_buf.at[k], sems.at[k, pieces]))
        if early:
            step.append(
                pltpu.make_async_copy(moments[k].at[:, at], moment_buf.at[k], sems.at[k, pieces + 1])
            )
        for copy in step:
            copy.start()
        copies.append(step)
    for k in range(count):
        for copy in copies[k]:
            copy.wait()
        block = weight_buf[k]
        if early:
            stepped = block.astype(jnp.float32) - moment_buf[k].astype(jnp.float32) * rate_ref[:1, :1]
            block = stepped.astype(jnp.bfloat16)
        part = jnp.dot(tokens_buf[k], block, preferred_element_type=jnp.float32)
        total_ref[...] = part if k == 0 else total_ref[...] + part
    if far:
        result_ref[...] = total_ref[...].astype(result_ref.dtype)
        copy = pltpu.make_async_copy(result_ref, out_ref, out_sem)
    else:
        copy = pltpu.make_async_copy(total_ref, out_ref.at[:, first : first + width], out_sem)
    copy.start()
    copy.wait()


def project_call(far, order, tokens, first, width, weights, moments, rate, ties=(), out=None, cols=None):
    count = len(weights)
    early = moments is not None
    depth = weights[0].shape[0]
    num_rows = sum(at.shape[0] for at in tokens)
    operands = list(tokens) + list(weights)
    specs = [ANY] * len(operands)
    if early:
        operands += list(moments) + [rate]
        specs += [ANY] * count + [VMEM]
    operands += list(ties)
    specs += [ANY] * len(ties)
    aliases = {}
    if far:
        out_shape = jax.ShapeDtypeStruct((num_rows, width), jnp.bfloat16)
    else:
        out_shape = [
            jax.ShapeDtypeStruct((num_rows, cols), jnp.float32),
            jax.ShapeDtypeStruct((8, LANES), jnp.float32),
        ]
        if out is not None:
            operands.append(out)
            specs.append(ANY)
            aliases = {len(operands): 0}
    return pl.pallas_call(
        functools.partial(
            project_kernel, far, len(tokens), count, early, bool(aliases), len(ties), first
        ),
        grid_spec=pltpu.PrefetchScalarGridSpec(
            num_scalar_prefetch=1,
            grid=(1,),
            in_specs=specs,
            out_specs=ANY if far else [ANY, VMEM],
            scratch_shapes=[
                pltpu.VMEM((count, num_rows, depth), jnp.bfloat16),
                pltpu.VMEM((count, depth, width), jnp.bfloat16),
                pltpu.VMEM((count, depth, width) if early else (8, LANES), jnp.bfloat16),
                pltpu.VMEM((num_rows, width), jnp.float32),
                pltpu.VMEM((num_rows, width) if far else (8, LANES), jnp.bfloat16),
                pltpu.SemaphoreType.DMA((count, len(tokens) + 2)),
                pltpu.SemaphoreType.DMA,
            ],
        ),
        out_shape=out_shape,
        input_output_aliases=aliases,
        compiler_params=LARGE,
        cost_estimate=BRIEF,
    )(order, *operands)


def add_kernel(old_ref, far_ref, out_ref):
    out_ref[...] = old_ref[...] + far_ref[...].astype(jnp.float32)


def add_call(out, far, first):
    num_rows, width = far.shape
    block = pl.BlockSpec((num_rows, UNIT), lambda c: (0, first // UNIT + c))
    return pl.pallas_call(
        add_kernel,
        grid=(width // UNIT,),
        in_specs=[block, pl.BlockSpec((num_rows, UNIT), lambda c: (0, c))],
        out_specs=block,
        out_shape=jax.ShapeDtypeStruct(out.shape, out.dtype),
        input_output_aliases={0: 0},
        compiler_params=LARGE,
        cost_estimate=BRIEF,
    )(out, far)


def swap(values, axis, size, bit):
    return lax.ppermute(values, axis, [(at, at ^ bit) for at in range(size)])


def butterfly(values, axis, size):
    bit = 1
    while 2 * bit < size:
        values = values + swap(values, axis, size, bit)
        bit *= 2
    return values, swap(values, axis, size, bit)


def offsets(count):
    found = [0]
    bit = count // 2
    while bit:
        found = found + [at ^ bit for at in found]
        bit //= 2
    return found


def spread(piece, axis, size):
    parts = [piece]
    bit = 1
    while bit < size:
        parts = parts + [swap(part, axis, size, bit) for part in parts]
        bit *= 2
    return parts


def local(rows_n, cols_n, tokens, weight, momentum, gradient, probes):
    half = rows_n // 2
    far_bit, near_bit = half // 2, half // 4
    place = lax.axis_index("fsdp")
    low_at = lax.rem(place, half)
    side = lax.div(place, half)
    column_at = lax.axis_index("tensor")
    num_rows = tokens.shape[0]
    depth, cols = weight.shape
    rows = num_rows // cols_n // PARTS
    unit = cols // (sum(EARLY) + sum(LATE))
    early_cols = sum(EARLY) * unit

    def fswap(values, bit):
        return swap(values, "fsdp", rows_n, bit)

    def complete(own, across, beside):
        parts = [own, across, beside, fswap(across, near_bit)]
        bit = near_bit // 2
        while bit:
            parts = parts + [fswap(part, bit) for part in parts]
            bit //= 2
        return parts

    def sum_over_rows(pack, gates, ties):
        passed = {}
        bit = 1
        while bit < half:
            pack, *passed[bit] = gate_call(pack, fswap(pack, bit), gates.get(bit, ()), ties.get(bit, ()))
            bit *= 2
        return pack, fswap(pack, half), passed

    mixed = jnp.stack([low_at ^ at for at in offsets(half)]).astype(jnp.int32)
    near_order = side * half + mixed
    pick_order = jnp.concatenate([(column_at * PARTS)[None], (1 - side) * half + mixed])
    far_order = jnp.stack(
        [(column_at ^ i) * PARTS * rows + part * rows for part in range(PARTS) for i in range(cols_n)]
    ).astype(jnp.int32)

    sent_0, sent_1, weight_own = pick_call(pick_order, tokens, weight, rows, half, early_cols)
    moment, short_1, pack = start_call(momentum, gradient, probes, sent_0, early_cols)
    weight_beside = fswap(weight_own, near_bit)
    weight_across = fswap(weight_own, far_bit)
    tokens_0 = fswap(sent_0, half)

    own, recv = butterfly(pack, "tensor", cols_n)
    pack, basis_1, _ = images_call(own, recv, probes, moment)
    own, recv, passed = sum_over_rows(
        pack, {1: [weight_across, short_1], 2: [tokens_0]}, {1: [weight_beside]}
    )
    weight_across, short_1 = passed[1]
    weight_parts = complete(weight_own, weight_across, weight_beside)
    moment_beside = fswap(short_1, near_bit)
    token_parts = spread(passed[2][0], "tensor", cols_n)
    pack, residue, diag_1, short_2, sent_1 = reduced_call(
        own, recv, basis_1, None, None, moment, [sent_1], early_cols
    )
    moment_across = fswap(short_2, far_bit)
    tokens_1 = fswap(sent_1, half)

    own, recv = butterfly(pack, "tensor", cols_n)
    pack, basis_2, low_1 = images_call(own, recv, residue, moment)
    own, recv, passed = sum_over_rows(
        pack,
        {1: [moment_across], 2: [tokens_1]},
        {1: [*token_parts[1:], *weight_parts[3:], moment_beside]},
    )
    moment_parts = complete(short_1, passed[1][0], moment_beside)
    token_1 = passed[2][0]
    token_1_beside = swap(token_1, "tensor", cols_n, 1)
    token_1_across = swap(token_1, "tensor", cols_n, 2)
    pack, _, diag_2 = reduced_call(own, recv, basis_2, basis_1, low_1, moment, [], early_cols)

    own, recv = butterfly(pack, "tensor", cols_n)
    diag_3, low_2, token_1_beside = last_call(own, recv, [token_1_beside])
    token_parts += [token_1, token_1_beside, token_1_across, swap(token_1_beside, "tensor", cols_n, 2)]
    own, recv = butterfly(diag_3, "fsdp", rows_n)
    scaled, rate = top_call(
        [diag_1, diag_2, own, recv], [low_1, low_2], [*token_parts[cols_n + 2 :], *moment_parts[3:]]
    )

    firsts, widths = [0], []
    for size in EARLY + LATE:
        widths.append(size * unit)
        firsts.append(firsts[-1] + size * unit)
    num_early = len(EARLY)
    gathered = [(weight_parts, moment_parts, rate)] * num_early
    out, partial, far = None, [], []

    def send(chunk, tie):
        ties = [tie] + far[chunk - num_early : chunk - num_early + 1] * (chunk >= num_early)
        partial.append(
            project_call(
                True, far_order, token_parts, firsts[chunk], widths[chunk], *gathered[chunk], ties=ties
            )
        )
        far.append(fswap(partial[-1], half))

    def keep(chunk, out, tie):
        return project_call(
            False,
            near_order,
            [tokens],
            firsts[chunk],
            widths[chunk],
            *gathered[chunk],
            ties=[tie],
            out=out,
            cols=cols,
        )

    def step(chunk, tie):
        own = step_call(weight, moment, rate, firsts[chunk], widths[chunk], tie)
        return own, fswap(own, near_bit), fswap(own, far_bit)

    own, beside, across = step(num_early, rate)
    send(0, own)
    for chunk in range(1, num_early):
        send(chunk, partial[-1])
    for chunk in range(num_early):
        out, token = keep(chunk, out, partial[-1] if chunk == 0 else token)
    for chunk in range(num_early, len(widths)):
        across = pass_call(across, partial[-1])
        gathered.append((complete(own, across, beside), None, None))
        if chunk + 1 < len(widths):
            own, beside, across = step(chunk + 1, token)
        send(chunk, partial[-1])
        out = add_call(out, far[chunk - num_early], firsts[chunk - num_early])
        out, token = keep(chunk, out, partial[-1])
    for chunk in range(len(widths) - num_early, len(widths)):
        out = add_call(out, far[chunk], firsts[chunk])
    return out, moment, scaled


def solution(mesh):
    return jax.shard_map(
        functools.partial(local, mesh.shape["fsdp"], mesh.shape["tensor"]),
        mesh=mesh,
        in_specs=(
            P("fsdp", None),
            P("fsdp", "tensor"),
            P("fsdp", "tensor"),
            P("fsdp", "tensor"),
            P(None, "tensor"),
        ),
        out_specs=(P("fsdp", "tensor"), P("fsdp", "tensor"), P()),
        check_vma=False,
    )
```

```python
import functools

import jax
import jax.numpy as jnp
from jax import lax
from jax.experimental import pallas as pl
from jax.experimental.pallas import tpu as pltpu
from jax.sharding import PartitionSpec as P

DECAY = 0.9
SQUARINGS = 5
LANES = 128
UNIT = 256
EARLY = (2,)
LATE = (2, 2, 1, 1)
PARTS = 2
PIECES = 2

HIGHEST = lax.Precision.HIGHEST
LARGE = pltpu.CompilerParams(vmem_limit_bytes=53 * 1024 * 1024)
PARAMS = pltpu.CompilerParams(vmem_limit_bytes=24 * 1024 * 1024)
BRIEF = pl.CostEstimate(flops=0, bytes_accessed=0, transcendentals=0)
VMEM = pl.BlockSpec(memory_space=pltpu.VMEM)
ANY = pl.BlockSpec(memory_space=pl.ANY)


def fdot(left, right):
    return lax.dot_general(
        left, right, (((1,), (0,)), ((), ())), precision=HIGHEST, preferred_element_type=jnp.float32
    )


def fdot_t(left, right):
    return lax.dot_general(
        left, right, (((1,), (1,)), ((), ())), precision=HIGHEST, preferred_element_type=jnp.float32
    )


def halves(values):
    high = values.astype(jnp.bfloat16)
    return high, (values - high.astype(jnp.float32)).astype(jnp.bfloat16)


def split_dot(stacked, mat, contract):
    rows = stacked.shape[0] // 2
    mat_high, mat_low = halves(mat)
    dims = (((1,), (contract,)), ((), ()))
    first = lax.dot_general(stacked, mat_high, dims, preferred_element_type=jnp.float32)
    second = lax.dot_general(stacked[:rows], mat_low, dims, preferred_element_type=jnp.float32)
    return first[:rows] + first[rows:] + second


def eliminate(gram, count):
    rows = lax.broadcasted_iota(jnp.int32, (count, LANES), 0)
    lanes = lax.broadcasted_iota(jnp.int32, (count, LANES), 1)
    aug = jnp.where(lanes < count, gram, jnp.where(lanes - count == rows, 1.0, 0.0))
    for step in range(count):
        pivot = aug[step : step + 1, step : step + 1]
        factor = jnp.where(rows > step, aug[:, step : step + 1] * (1.0 / pivot), 0.0)
        aug = aug - factor * aug[step : step + 1, :]
    pivots = jnp.sum(jnp.where(lanes == rows, aug, 0.0), axis=1, keepdims=True)
    aug = aug * (1.0 / jnp.sqrt(pivots))
    low_t = jnp.where((lanes >= rows) & (lanes < count), aug, 0.0)
    return low_t, aug[:, count : 2 * count]


def pad_lanes(square):
    return jnp.concatenate(
        [square, jnp.zeros((square.shape[0], LANES - square.shape[1]), jnp.float32)], axis=1
    )


def pick_kernel(order_ref, token_0, token_1, weight_ref, sent_0, sent_1, early_ref):
    sent_0[...] = token_0[...]
    sent_1[...] = token_1[...]
    early_ref[...] = weight_ref[...]


def pick_call(order, tokens, weight, rows, count, early_cols):
    depth = weight.shape[0]
    height = depth // count
    sent = jax.ShapeDtypeStruct((rows, count * depth), tokens.dtype)
    weight_spec = pl.BlockSpec((height, early_cols), lambda i, order_ref: (i, 0))
    sent_spec = pl.BlockSpec((rows, depth), lambda i, order_ref: (0, i))
    return pl.pallas_call(
        pick_kernel,
        grid_spec=pltpu.PrefetchScalarGridSpec(
            num_scalar_prefetch=1,
            grid=(count,),
            in_specs=[
                pl.BlockSpec((rows, depth), lambda i, order_ref: (order_ref[0], order_ref[1 + i])),
                pl.BlockSpec((rows, depth), lambda i, order_ref: (order_ref[0] + 1, order_ref[1 + i])),
                weight_spec,
            ],
            out_specs=[sent_spec, sent_spec, weight_spec],
        ),
        out_shape=[sent, sent, jax.ShapeDtypeStruct((depth, early_cols), weight.dtype)],
        compiler_params=LARGE,
    )(order, tokens, tokens, weight)


def start_kernel(width, mom_ref, grad_ref, probes_ref, tie_ref, moment_ref, short_ref, pack_ref, stack_ref):
    at = pl.program_id(0)
    count = probes_ref.shape[0]
    height = mom_ref.shape[0]

    @pl.when(at == 0)
    def _():
        probes = probes_ref[...]
        high, low = halves(probes)
        stack_ref[:count] = high
        stack_ref[count:] = low
        pack_ref[:, width:] = pad_lanes(fdot_t(probes, probes))

    moment = DECAY * mom_ref[...] + grad_ref[...].astype(jnp.float32)
    moment_ref[...] = moment
    short_ref[...] = moment[:, : short_ref.shape[1]].astype(jnp.bfloat16)
    pack_ref[:, pl.ds(pl.multiple_of(at * height, height), height)] = split_dot(stack_ref[...], moment, 1)


def start_call(momentum, gradient, probes, tie, early_cols):
    depth, cols = momentum.shape
    count = probes.shape[0]
    height = min(256, depth)
    rows = pl.BlockSpec((height, cols), lambda i: (i, 0))
    return pl.pallas_call(
        functools.partial(start_kernel, depth),
        grid=(depth // height,),
        in_specs=[rows, rows, VMEM, ANY],
        out_specs=[rows, pl.BlockSpec((height, early_cols), lambda i: (i, 0)), VMEM],
        out_shape=[
            jax.ShapeDtypeStruct((depth, cols), jnp.float32),
            jax.ShapeDtypeStruct((depth, early_cols), jnp.bfloat16),
            jax.ShapeDtypeStruct((count, depth + LANES), jnp.float32),
        ],
        scratch_shapes=[pltpu.VMEM((2 * count, cols), jnp.bfloat16)],
        compiler_params=LARGE,
    )(momentum, gradient, probes, tie)


def gate_kernel(passed, own_ref, recv_ref, *refs):
    sum_ref = refs[-1 - passed]
    sum_ref[...] = own_ref[...] + recv_ref[...]


def gate_call(own, recv, gates=(), ties=()):
    shapes = [jax.ShapeDtypeStruct(at.shape, at.dtype) for at in (own, *gates)]
    first = 2 + len(ties)
    return pl.pallas_call(
        functools.partial(gate_kernel, len(gates)),
        in_specs=[VMEM, VMEM] + [ANY] * (len(gates) + len(ties)),
        out_specs=[VMEM] + [ANY] * len(gates),
        out_shape=shapes,
        input_output_aliases={first + i: 1 + i for i in range(len(gates))},
        compiler_params=PARAMS,
    )(own, recv, *ties, *gates)


def pass_kernel(*refs):
    pass


def pass_call(values, tie):
    return pl.pallas_call(
        pass_kernel,
        in_specs=[ANY] * (len(values) + 1),
        out_specs=[ANY] * len(values),
        out_shape=[jax.ShapeDtypeStruct(at.shape, at.dtype) for at in values],
        input_output_aliases={i: i for i in range(len(values))},
        compiler_params=PARAMS,
        cost_estimate=BRIEF,
    )(*values, tie)


def images_blocked(own_ref, recv_ref, block_ref, moment_ref, pack_ref, basis_ref, low_ref, stack_ref):
    at = pl.program_id(0)
    count, cols = block_ref.shape
    depth = moment_ref.shape[0]
    width = moment_ref.shape[1]

    @pl.when(at == 0)
    def _():
        low_t, inverse = eliminate(own_ref[:, depth:] + recv_ref[:, depth:], count)
        low_ref[...] = low_t
        reduced = fdot(inverse, own_ref[:, :depth] + recv_ref[:, :depth])
        high, low = halves(reduced)
        stack_ref[:count] = high
        stack_ref[count:] = low
        pack_ref[:, cols:] = pad_lanes(fdot_t(reduced, reduced))
        basis_ref[...] = fdot(inverse, block_ref[...])

    pack_ref[:, pl.ds(pl.multiple_of(at * width, width), width)] = split_dot(stack_ref[...], moment_ref[...], 0)


def images_kernel(
    own_ref, recv_ref, block_ref, moment_ref, pack_ref, basis_ref, low_ref, held_ref, stack_ref, sems
):
    count, cols = block_ref.shape
    blocks, depth, width = held_ref.shape
    copies = [
        pltpu.make_async_copy(
            moment_ref.at[:, at * width : (at + 1) * width], held_ref.at[at], sems.at[at]
        )
        for at in range(blocks)
    ]
    for copy in copies:
        copy.start()
    low_t, inverse = eliminate(own_ref[:, depth:] + recv_ref[:, depth:], count)
    low_ref[...] = low_t
    reduced = fdot(inverse, own_ref[:, :depth] + recv_ref[:, :depth])
    high, low = halves(reduced)
    stack_ref[:count] = high
    stack_ref[count:] = low
    pack_ref[:, cols:] = pad_lanes(fdot_t(reduced, reduced))
    basis_ref[...] = fdot(inverse, block_ref[...])
    for at, copy in enumerate(copies):
        copy.wait()
        pack_ref[:, at * width : (at + 1) * width] = split_dot(stack_ref[...], held_ref[at], 0)


def images_call(own, recv, block, moment, fetch):
    depth, cols = moment.shape
    count = block.shape[0]
    width = min(512, cols)
    stack = pltpu.VMEM((2 * count, depth), jnp.bfloat16)
    held = [
        pltpu.VMEM((cols // width, depth, width), jnp.float32),
        stack,
        pltpu.SemaphoreType.DMA((cols // width,)),
    ]
    return pl.pallas_call(
        images_kernel if fetch else images_blocked,
        grid=(1 if fetch else cols // width,),
        in_specs=[VMEM, VMEM, VMEM, ANY if fetch else pl.BlockSpec((depth, width), lambda i: (0, i))],
        out_specs=[VMEM, VMEM, VMEM],
        out_shape=[
            jax.ShapeDtypeStruct((count, cols + LANES), jnp.float32),
            jax.ShapeDtypeStruct((count, cols), jnp.float32),
            jax.ShapeDtypeStruct((count, LANES), jnp.float32),
        ],
        scratch_shapes=held if fetch else [stack],
        compiler_params=LARGE if fetch else PARAMS,
    )(own, recv, block, moment)


def reduced_kernel(has_prev, passed, width, *refs):
    names = 5 if has_prev else 3
    own_ref, recv_ref, basis_ref = refs[:3]
    prev_ref, low_ref = refs[3:5] if has_prev else (None, None)
    moment_ref = refs[names]
    outs = refs[names + 1 + passed :]
    pack_ref, residue_ref, diag_ref = outs[:3]
    stack_ref = refs[-1]
    at = pl.program_id(0)
    count, cols = basis_ref.shape
    height = moment_ref.shape[0]

    @pl.when(at == 0)
    def _():
        diag = (own_ref[:, cols:] + recv_ref[:, cols:])[:, :count]
        diag = 0.5 * (diag + diag.T)
        diag_ref[...] = pad_lanes(diag)
        residue = own_ref[:, :cols] + recv_ref[:, :cols] - fdot(diag, basis_ref[...])
        if has_prev:
            residue = residue - fdot(low_ref[:, :count], prev_ref[...])
        residue_ref[...] = residue
        high, low = halves(residue)
        stack_ref[:count] = high
        stack_ref[count:] = low
        pack_ref[:, width:] = pad_lanes(fdot_t(residue, residue))

    moment = moment_ref[...]
    if passed:
        short_ref = outs[3]
        short_ref[...] = moment[:, : short_ref.shape[1]].astype(jnp.bfloat16)
    pack_ref[:, pl.ds(pl.multiple_of(at * height, height), height)] = split_dot(stack_ref[...], moment, 1)


def reduced_call(own, recv, basis, prev, low, moment, gates, early_cols):
    depth, cols = moment.shape
    count = basis.shape[0]
    height = min(256, depth)
    has_prev = prev is not None
    operands = (own, recv, basis) + ((prev, low) if has_prev else ()) + (moment,)
    out_specs = [VMEM, VMEM, VMEM]
    out_shape = [
        jax.ShapeDtypeStruct((count, depth + LANES), jnp.float32),
        jax.ShapeDtypeStruct((count, cols), jnp.float32),
        jax.ShapeDtypeStruct((count, LANES), jnp.float32),
    ]
    if gates:
        out_specs += [pl.BlockSpec((height, early_cols), lambda i: (i, 0))] + [ANY] * len(gates)
        out_shape += [jax.ShapeDtypeStruct((depth, early_cols), jnp.bfloat16)]
        out_shape += [jax.ShapeDtypeStruct(at.shape, at.dtype) for at in gates]
    return pl.pallas_call(
        functools.partial(reduced_kernel, has_prev, len(gates), depth),
        grid=(depth // height,),
        in_specs=[VMEM] * (len(operands) - 1)
        + [pl.BlockSpec((height, cols), lambda i: (i, 0))]
        + [ANY] * len(gates),
        out_specs=out_specs,
        out_shape=out_shape,
        input_output_aliases={len(operands) + i: 4 + i for i in range(len(gates))},
        scratch_shapes=[pltpu.VMEM((2 * count, cols), jnp.bfloat16)],
        compiler_params=PARAMS,
    )(*operands, *gates)


def last_kernel(passed, own_ref, recv_ref, *refs):
    diag_ref, low_ref = refs[passed : passed + 2]
    count = own_ref.shape[0]
    depth = own_ref.shape[1] - LANES
    low_t, inverse = eliminate(own_ref[:, depth:] + recv_ref[:, depth:], count)
    low_ref[...] = low_t
    reduced = fdot(inverse, own_ref[:, :depth] + recv_ref[:, :depth])
    diag_ref[...] = pad_lanes(fdot_t(reduced, reduced))


def last_call(own, recv, gates, ties):
    shape = jax.ShapeDtypeStruct((own.shape[0], LANES), jnp.float32)
    return pl.pallas_call(
        functools.partial(last_kernel, len(gates) + len(ties)),
        in_specs=[VMEM, VMEM] + [ANY] * (len(gates) + len(ties)),
        out_specs=[VMEM, VMEM] + [ANY] * len(gates),
        out_shape=[shape, shape] + [jax.ShapeDtypeStruct(at.shape, at.dtype) for at in gates],
        input_output_aliases={2 + i: 2 + i for i in range(len(gates))},
        compiler_params=PARAMS,
    )(own, recv, *gates, *ties)


def top_kernel(steps, *refs):
    diag_refs = refs[: steps + 1]
    low_refs = refs[steps + 1 : 2 * steps]
    scaled_ref, rate_ref, krylov_ref = refs[-3:]
    count = diag_refs[0].shape[0]
    size = steps * count
    krylov_ref[...] = jnp.zeros_like(krylov_ref)
    for place in range(steps):
        first = place * count
        diag = diag_refs[place][:, :count]
        if place + 1 == steps:
            diag = diag + diag_refs[steps][:, :count]
        krylov_ref[first : first + count, first : first + count] = 0.5 * (diag + diag.T)
        if place + 1 < steps:
            second = first + count
            low_t = low_refs[place][:, :count]
            krylov_ref[second : second + count, first:second] = low_t
            krylov_ref[first:second, second : second + count] = low_t.T
    krylov = krylov_ref[...]
    power = krylov * (1.0 / jnp.max(jnp.abs(krylov), keepdims=True))
    for _ in range(SQUARINGS):
        power = fdot(power, power)
        power = power * (1.0 / jnp.max(jnp.abs(power), keepdims=True))
    tall = jnp.sum(power, axis=1, keepdims=True)
    wide = jnp.sum(power, axis=0, keepdims=True)
    tall = tall * (1.0 / jnp.sqrt(jnp.sum(tall * tall, keepdims=True)))
    wide = wide * (1.0 / jnp.sqrt(jnp.sum(wide * wide, keepdims=True)))
    top = jnp.sum(krylov * tall * wide, keepdims=True)
    scaled_ref[...] = krylov[:size, :size] / top
    rate_ref[...] = jnp.broadcast_to(1.0 / jnp.sqrt(top), rate_ref.shape)


def top_call(diags, lows, ties):
    steps = len(lows) + 1
    count = diags[0].shape[0]
    size = steps * count
    padded = -(-size // LANES) * LANES
    return pl.pallas_call(
        functools.partial(top_kernel, steps),
        in_specs=[VMEM] * (2 * steps) + [ANY] * len(ties),
        out_specs=[VMEM, VMEM],
        out_shape=[
            jax.ShapeDtypeStruct((size, size), jnp.float32),
            jax.ShapeDtypeStruct((8, LANES), jnp.float32),
        ],
        scratch_shapes=[pltpu.VMEM((padded, padded), jnp.float32)],
        compiler_params=PARAMS,
    )(*diags, *lows, *ties)


def step_kernel(weight_ref, moment_ref, rate_ref, tie_ref, *out_refs):
    stepped = weight_ref[...].astype(jnp.float32) - moment_ref[...] * rate_ref[:1, :1]
    width = out_refs[0].shape[1]
    for i, out_ref in enumerate(out_refs):
        out_ref[...] = stepped[:, i * width : (i + 1) * width].astype(jnp.bfloat16)


def step_call(weight, moment, rate, first, width, tie):
    depth = weight.shape[0]
    height = min(512, depth)
    part = width // PIECES
    block = pl.BlockSpec((height, width), lambda r: (r, first // width))
    return pl.pallas_call(
        step_kernel,
        grid=(depth // height,),
        in_specs=[block, block, VMEM, ANY],
        out_specs=[pl.BlockSpec((height, part), lambda r: (r, 0))] * PIECES,
        out_shape=[jax.ShapeDtypeStruct((depth, part), jnp.bfloat16)] * PIECES,
        compiler_params=LARGE,
        cost_estimate=BRIEF,
    )(weight, moment, rate, tie)


def project_kernel(far, pieces, count, early, in_place, ties, first, order_ref, *refs):
    tokens = refs[:pieces]
    refs = refs[pieces:]
    split = 1 if early else PIECES
    weights, refs = refs[: split * count], refs[split * count :]
    if early:
        moments, rate_ref, refs = refs[:count], refs[count], refs[count + 1 :]
    refs = refs[ties + (1 if in_place else 0) :]
    if not far:
        refs[1][...] = jnp.zeros(refs[1].shape, jnp.float32)
        refs = refs[:1] + refs[2:]
    out_ref, tokens_buf, weight_buf, moment_buf, total_ref, result_ref, sems, out_sem = refs
    depth, width = weight_buf.shape[1:]
    copies = []
    for k in range(count):
        step = []
        for i in range(pieces):
            if far:
                rows = tokens[i].shape[0]
                source = tokens[i].at[:, k * depth : (k + 1) * depth]
                target = tokens_buf.at[k, pl.ds(pl.multiple_of(order_ref[i], 16), rows), :]
            else:
                source = tokens[i].at[:, pl.ds(pl.multiple_of(order_ref[k] * depth, LANES), depth)]
                target = tokens_buf.at[k]
            step.append(pltpu.make_async_copy(source, target, sems.at[k, i]))
        if early:
            at = slice(first, first + width)
            step.append(pltpu.make_async_copy(weights[k].at[:, at], weight_buf.at[k], sems.at[k, pieces]))
            step.append(
                pltpu.make_async_copy(moments[k].at[:, at], moment_buf.at[k], sems.at[k, pieces + 1])
            )
        else:
            part = width // PIECES
            for i in range(PIECES):
                target = weight_buf.at[k, :, i * part : (i + 1) * part]
                step.append(
                    pltpu.make_async_copy(weights[k * PIECES + i], target, sems.at[k, pieces + i])
                )
        for copy in step:
            copy.start()
        copies.append(step)
    for k in range(count):
        for copy in copies[k]:
            copy.wait()
        block = weight_buf[k]
        if early:
            stepped = block.astype(jnp.float32) - moment_buf[k].astype(jnp.float32) * rate_ref[:1, :1]
            block = stepped.astype(jnp.bfloat16)
        part = jnp.dot(tokens_buf[k], block, preferred_element_type=jnp.float32)
        total_ref[...] = part if k == 0 else total_ref[...] + part
    if far:
        result_ref[...] = total_ref[...].astype(result_ref.dtype)
        copy = pltpu.make_async_copy(result_ref, out_ref, out_sem)
    else:
        copy = pltpu.make_async_copy(total_ref, out_ref.at[:, first : first + width], out_sem)
    copy.start()
    copy.wait()


def project_call(far, order, tokens, first, width, weights, moments, rate, ties=(), out=None, cols=None):
    early = moments is not None
    count = len(weights) // (1 if early else PIECES)
    depth = weights[0].shape[0]
    num_rows = sum(at.shape[0] for at in tokens)
    operands = list(tokens) + list(weights)
    specs = [ANY] * len(operands)
    if early:
        operands += list(moments) + [rate]
        specs += [ANY] * count + [VMEM]
    operands += list(ties)
    specs += [ANY] * len(ties)
    aliases = {}
    if far:
        out_shape = jax.ShapeDtypeStruct((num_rows, width), jnp.bfloat16)
    else:
        out_shape = [
            jax.ShapeDtypeStruct((num_rows, cols), jnp.float32),
            jax.ShapeDtypeStruct((8, LANES), jnp.float32),
        ]
        if out is not None:
            operands.append(out)
            specs.append(ANY)
            aliases = {len(operands): 0}
    return pl.pallas_call(
        functools.partial(
            project_kernel, far, len(tokens), count, early, bool(aliases), len(ties), first
        ),
        grid_spec=pltpu.PrefetchScalarGridSpec(
            num_scalar_prefetch=1,
            grid=(1,),
            in_specs=specs,
            out_specs=ANY if far else [ANY, VMEM],
            scratch_shapes=[
                pltpu.VMEM((count, num_rows, depth), jnp.bfloat16),
                pltpu.VMEM((count, depth, width), jnp.bfloat16),
                pltpu.VMEM((count, depth, width) if early else (8, LANES), jnp.bfloat16),
                pltpu.VMEM((num_rows, width), jnp.float32),
                pltpu.VMEM((num_rows, width) if far else (8, LANES), jnp.bfloat16),
                pltpu.SemaphoreType.DMA((count, len(tokens) + max(2, PIECES))),
                pltpu.SemaphoreType.DMA,
            ],
        ),
        out_shape=out_shape,
        input_output_aliases=aliases,
        compiler_params=LARGE,
        cost_estimate=BRIEF,
    )(order, *operands)


def add_kernel(old_ref, far_ref, out_ref):
    out_ref[...] = old_ref[...] + far_ref[...].astype(jnp.float32)


def add_call(out, far, first):
    num_rows, width = far.shape
    block = pl.BlockSpec((num_rows, UNIT), lambda c: (0, first // UNIT + c))
    return pl.pallas_call(
        add_kernel,
        grid=(width // UNIT,),
        in_specs=[block, pl.BlockSpec((num_rows, UNIT), lambda c: (0, c))],
        out_specs=block,
        out_shape=jax.ShapeDtypeStruct(out.shape, out.dtype),
        input_output_aliases={0: 0},
        compiler_params=LARGE,
        cost_estimate=BRIEF,
    )(out, far)


def swap(values, axis, size, bit):
    return lax.ppermute(values, axis, [(at, at ^ bit) for at in range(size)])


def butterfly(values, axis, size):
    bit = 1
    while 2 * bit < size:
        values = values + swap(values, axis, size, bit)
        bit *= 2
    return values, swap(values, axis, size, bit)


def offsets(count):
    found = [0]
    bit = count // 2
    while bit:
        found = found + [at ^ bit for at in found]
        bit //= 2
    return found


def spread(piece, axis, size):
    parts = [piece]
    bit = 1
    while bit < size:
        parts = parts + [swap(part, axis, size, bit) for part in parts]
        bit *= 2
    return parts


def local(rows_n, cols_n, tokens, weight, momentum, gradient, probes):
    half = rows_n // 2
    far_bit, near_bit = half // 2, half // 4
    place = lax.axis_index("fsdp")
    low_at = lax.rem(place, half)
    side = lax.div(place, half)
    column_at = lax.axis_index("tensor")
    num_rows = tokens.shape[0]
    depth, cols = weight.shape
    rows = num_rows // cols_n // PARTS
    unit = cols // (sum(EARLY) + sum(LATE))
    early_cols = sum(EARLY) * unit

    def fswap(values, bit):
        return swap(values, "fsdp", rows_n, bit)

    def complete(own, across, beside):
        parts = [own, across, beside, fswap(across, near_bit)]
        bit = near_bit // 2
        while bit:
            parts = parts + [fswap(part, bit) for part in parts]
            bit //= 2
        return parts

    def sum_over_rows(pack, gates, ties):
        passed = {}
        bit = 1
        while bit < half:
            pack, *passed[bit] = gate_call(pack, fswap(pack, bit), gates.get(bit, ()), ties.get(bit, ()))
            bit *= 2
        return pack, fswap(pack, half), passed

    mixed = jnp.stack([low_at ^ at for at in offsets(half)]).astype(jnp.int32)
    near_order = side * half + mixed
    pick_order = jnp.concatenate([(column_at * PARTS)[None], (1 - side) * half + mixed])
    far_order = jnp.stack(
        [(column_at ^ i) * PARTS * rows + part * rows for part in range(PARTS) for i in range(cols_n)]
    ).astype(jnp.int32)

    sent_0, sent_1, weight_own = pick_call(pick_order, tokens, weight, rows, half, early_cols)
    moment, short_1, pack = start_call(momentum, gradient, probes, sent_0, early_cols)
    weight_beside = fswap(weight_own, near_bit)
    weight_across = fswap(weight_own, far_bit)
    tokens_0 = fswap(sent_0, half)

    own, recv = butterfly(pack, "tensor", cols_n)
    pack, basis_1, _ = images_call(own, recv, probes, moment, True)
    own, recv, passed = sum_over_rows(
        pack, {1: [weight_across, short_1], 2: [tokens_0]}, {1: [weight_beside]}
    )
    weight_across, short_1 = passed[1]
    weight_parts = complete(weight_own, weight_across, weight_beside)
    moment_beside = fswap(short_1, near_bit)
    token_parts = spread(passed[2][0], "tensor", cols_n)
    pack, residue, diag_1, short_2, sent_1 = reduced_call(
        own, recv, basis_1, None, None, moment, [sent_1], early_cols
    )
    moment_across = fswap(short_2, far_bit)
    tokens_1 = fswap(sent_1, half)

    own, recv = butterfly(pack, "tensor", cols_n)
    pack, basis_2, low_1 = images_call(own, recv, residue, moment, False)
    own, recv, passed = sum_over_rows(
        pack,
        {1: [moment_across], 2: [tokens_1]},
        {1: [*token_parts[1:], *weight_parts[3:], moment_beside]},
    )
    moment_parts = complete(short_1, passed[1][0], moment_beside)
    token_1 = passed[2][0]
    token_1_beside = swap(token_1, "tensor", cols_n, 1)
    token_1_across = swap(token_1, "tensor", cols_n, 2)
    pack, _, diag_2 = reduced_call(own, recv, basis_2, basis_1, low_1, moment, [], early_cols)

    own, recv = butterfly(pack, "tensor", cols_n)
    diag_3, low_2, token_1_beside = last_call(
        own, recv, [token_1_beside], [token_1_across, *moment_parts[3:]]
    )
    token_parts += [token_1, token_1_beside, token_1_across, swap(token_1_beside, "tensor", cols_n, 2)]
    own, recv = butterfly(diag_3, "fsdp", rows_n)
    scaled, rate = top_call(
        [diag_1, diag_2, own, recv], [low_1, low_2], [token_parts[-1]]
    )

    firsts, widths = [0], []
    for size in EARLY + LATE:
        widths.append(size * unit)
        firsts.append(firsts[-1] + size * unit)
    num_early = len(EARLY)
    gathered = [(weight_parts, moment_parts, rate)] * num_early
    out, partial, far = None, [], []

    def send(chunk, *ties):
        ties = [*ties] + far[chunk - num_early : chunk - num_early + 1] * (chunk >= num_early)
        partial.append(
            project_call(
                True, far_order, token_parts, firsts[chunk], widths[chunk], *gathered[chunk], ties=ties
            )
        )
        far.append(fswap(partial[-1], half))

    def keep(chunk, out, tie):
        return project_call(
            False,
            near_order,
            [tokens],
            firsts[chunk],
            widths[chunk],
            *gathered[chunk],
            ties=[tie],
            out=out,
            cols=cols,
        )

    def step(chunk, tie):
        own = step_call(weight, moment, rate, firsts[chunk], widths[chunk], tie)
        return own, [fswap(at, near_bit) for at in own], [fswap(at, far_bit) for at in own]

    own, beside, across = step(num_early, rate)
    send(0, own[0])
    for chunk in range(1, num_early):
        send(chunk, partial[-1])
    for chunk in range(num_early):
        out, token = keep(chunk, out, partial[-1] if chunk == 0 else token)
    for chunk in range(num_early, len(widths)):
        across = pass_call(across, partial[-1])
        pieces = [complete(*at) for at in zip(own, across, beside)]
        gathered.append(([piece[k] for k in range(half) for piece in pieces], None, None))
        if chunk + 1 < len(widths):
            own, beside, across = step(chunk + 1, token)
            send(chunk, partial[-1], own[0])
        else:
            send(chunk, partial[-1])
        out = add_call(out, far[chunk - num_early], firsts[chunk - num_early])
        out, token = keep(chunk, out, partial[-1])
    for chunk in range(len(widths) - num_early, len(widths)):
        out = add_call(out, far[chunk], firsts[chunk])
    return out, moment, scaled


def solution(mesh):
    return jax.shard_map(
        functools.partial(local, mesh.shape["fsdp"], mesh.shape["tensor"]),
        mesh=mesh,
        in_specs=(
            P("fsdp", None),
            P("fsdp", "tensor"),
            P("fsdp", "tensor"),
            P("fsdp", "tensor"),
            P(None, "tensor"),
        ),
        out_specs=(P("fsdp", "tensor"), P("fsdp", "tensor"), P()),
        check_vma=False,
    )
```

```python
import functools

import jax
import jax.numpy as jnp
from jax import lax
from jax.experimental import pallas as pl
from jax.experimental.pallas import tpu as pltpu
from jax.sharding import PartitionSpec as P

DECAY = 0.9
SQUARINGS = 5
LANES = 128
UNIT = 256
EARLY = (2,)
LATE = (2, 2, 1, 1)
PARTS = 2
PIECES = 2

HIGHEST = lax.Precision.HIGHEST
LARGE = pltpu.CompilerParams(vmem_limit_bytes=53 * 1024 * 1024)
PARAMS = pltpu.CompilerParams(vmem_limit_bytes=24 * 1024 * 1024)
BRIEF = pl.CostEstimate(flops=0, bytes_accessed=0, transcendentals=0)
VMEM = pl.BlockSpec(memory_space=pltpu.VMEM)
ANY = pl.BlockSpec(memory_space=pl.ANY)


def fdot(left, right):
    return lax.dot_general(
        left, right, (((1,), (0,)), ((), ())), precision=HIGHEST, preferred_element_type=jnp.float32
    )


def fdot_t(left, right):
    return lax.dot_general(
        left, right, (((1,), (1,)), ((), ())), precision=HIGHEST, preferred_element_type=jnp.float32
    )


def halves(values):
    high = values.astype(jnp.bfloat16)
    return high, (values - high.astype(jnp.float32)).astype(jnp.bfloat16)


def split_dot(stacked, mat, contract):
    rows = stacked.shape[0] // 2
    mat_high, mat_low = halves(mat)
    dims = (((1,), (contract,)), ((), ()))
    first = lax.dot_general(stacked, mat_high, dims, preferred_element_type=jnp.float32)
    second = lax.dot_general(stacked[:rows], mat_low, dims, preferred_element_type=jnp.float32)
    return first[:rows] + first[rows:] + second


def eliminate(gram, count):
    rows = lax.broadcasted_iota(jnp.int32, (count, LANES), 0)
    lanes = lax.broadcasted_iota(jnp.int32, (count, LANES), 1)
    aug = jnp.where(lanes < count, gram, jnp.where(lanes - count == rows, 1.0, 0.0))
    for step in range(count):
        pivot = aug[step : step + 1, step : step + 1]
        factor = jnp.where(rows > step, aug[:, step : step + 1] * (1.0 / pivot), 0.0)
        aug = aug - factor * aug[step : step + 1, :]
    pivots = jnp.sum(jnp.where(lanes == rows, aug, 0.0), axis=1, keepdims=True)
    aug = aug * (1.0 / jnp.sqrt(pivots))
    low_t = jnp.where((lanes >= rows) & (lanes < count), aug, 0.0)
    return low_t, aug[:, count : 2 * count]


def pad_lanes(square):
    return jnp.concatenate(
        [square, jnp.zeros((square.shape[0], LANES - square.shape[1]), jnp.float32)], axis=1
    )


def pick_kernel(order_ref, token_0, token_1, weight_ref, sent_0, sent_1, early_ref):
    sent_0[...] = token_0[...]
    sent_1[...] = token_1[...]
    early_ref[...] = weight_ref[...]


def pick_call(order, tokens, weight, rows, count, early_cols):
    depth = weight.shape[0]
    height = depth // count
    sent = jax.ShapeDtypeStruct((rows, count * depth), tokens.dtype)
    weight_spec = pl.BlockSpec((height, early_cols), lambda i, order_ref: (i, 0))
    sent_spec = pl.BlockSpec((rows, depth), lambda i, order_ref: (0, i))
    return pl.pallas_call(
        pick_kernel,
        grid_spec=pltpu.PrefetchScalarGridSpec(
            num_scalar_prefetch=1,
            grid=(count,),
            in_specs=[
                pl.BlockSpec((rows, depth), lambda i, order_ref: (order_ref[0], order_ref[1 + i])),
                pl.BlockSpec((rows, depth), lambda i, order_ref: (order_ref[0] + 1, order_ref[1 + i])),
                weight_spec,
            ],
            out_specs=[sent_spec, sent_spec, weight_spec],
        ),
        out_shape=[sent, sent, jax.ShapeDtypeStruct((depth, early_cols), weight.dtype)],
        compiler_params=LARGE,
    )(order, tokens, tokens, weight)


def start_kernel(width, mom_ref, grad_ref, probes_ref, tie_ref, moment_ref, short_ref, pack_ref, stack_ref):
    at = pl.program_id(0)
    count = probes_ref.shape[0]
    height = mom_ref.shape[0]

    @pl.when(at == 0)
    def _():
        probes = probes_ref[...]
        high, low = halves(probes)
        stack_ref[:count] = high
        stack_ref[count:] = low
        pack_ref[:, width:] = pad_lanes(fdot_t(probes, probes))

    moment = DECAY * mom_ref[...] + grad_ref[...].astype(jnp.float32)
    moment_ref[...] = moment
    short_ref[...] = moment[:, : short_ref.shape[1]].astype(jnp.bfloat16)
    pack_ref[:, pl.ds(pl.multiple_of(at * height, height), height)] = split_dot(stack_ref[...], moment, 1)


def start_call(momentum, gradient, probes, tie, early_cols):
    depth, cols = momentum.shape
    count = probes.shape[0]
    height = min(256, depth)
    rows = pl.BlockSpec((height, cols), lambda i: (i, 0))
    return pl.pallas_call(
        functools.partial(start_kernel, depth),
        grid=(depth // height,),
        in_specs=[rows, rows, VMEM, ANY],
        out_specs=[rows, pl.BlockSpec((height, early_cols), lambda i: (i, 0)), VMEM],
        out_shape=[
            jax.ShapeDtypeStruct((depth, cols), jnp.float32),
            jax.ShapeDtypeStruct((depth, early_cols), jnp.bfloat16),
            jax.ShapeDtypeStruct((count, depth + LANES), jnp.float32),
        ],
        scratch_shapes=[pltpu.VMEM((2 * count, cols), jnp.bfloat16)],
        compiler_params=LARGE,
    )(momentum, gradient, probes, tie)


def gate_kernel(passed, own_ref, recv_ref, *refs):
    sum_ref = refs[-1 - passed]
    sum_ref[...] = own_ref[...] + recv_ref[...]


def gate_call(own, recv, gates=(), ties=()):
    shapes = [jax.ShapeDtypeStruct(at.shape, at.dtype) for at in (own, *gates)]
    first = 2 + len(ties)
    return pl.pallas_call(
        functools.partial(gate_kernel, len(gates)),
        in_specs=[VMEM, VMEM] + [ANY] * (len(gates) + len(ties)),
        out_specs=[VMEM] + [ANY] * len(gates),
        out_shape=shapes,
        input_output_aliases={first + i: 1 + i for i in range(len(gates))},
        compiler_params=PARAMS,
    )(own, recv, *ties, *gates)


def pass_kernel(*refs):
    pass


def pass_call(values, ties):
    return pl.pallas_call(
        pass_kernel,
        in_specs=[ANY] * (len(values) + len(ties)),
        out_specs=[ANY] * len(values),
        out_shape=[jax.ShapeDtypeStruct(at.shape, at.dtype) for at in values],
        input_output_aliases={i: i for i in range(len(values))},
        compiler_params=LARGE,
        cost_estimate=BRIEF,
    )(*values, *ties)


def images_blocked(own_ref, recv_ref, block_ref, moment_ref, pack_ref, basis_ref, low_ref, stack_ref):
    at = pl.program_id(0)
    count, cols = block_ref.shape
    depth = moment_ref.shape[0]
    width = moment_ref.shape[1]

    @pl.when(at == 0)
    def _():
        low_t, inverse = eliminate(own_ref[:, depth:] + recv_ref[:, depth:], count)
        low_ref[...] = low_t
        reduced = fdot(inverse, own_ref[:, :depth] + recv_ref[:, :depth])
        high, low = halves(reduced)
        stack_ref[:count] = high
        stack_ref[count:] = low
        pack_ref[:, cols:] = pad_lanes(fdot_t(reduced, reduced))
        basis_ref[...] = fdot(inverse, block_ref[...])

    pack_ref[:, pl.ds(pl.multiple_of(at * width, width), width)] = split_dot(stack_ref[...], moment_ref[...], 0)


def images_kernel(
    own_ref, recv_ref, block_ref, moment_ref, pack_ref, basis_ref, low_ref, held_ref, stack_ref, sems
):
    count, cols = block_ref.shape
    blocks, depth, width = held_ref.shape
    copies = [
        pltpu.make_async_copy(
            moment_ref.at[:, at * width : (at + 1) * width], held_ref.at[at], sems.at[at]
        )
        for at in range(blocks)
    ]
    for copy in copies:
        copy.start()
    low_t, inverse = eliminate(own_ref[:, depth:] + recv_ref[:, depth:], count)
    low_ref[...] = low_t
    reduced = fdot(inverse, own_ref[:, :depth] + recv_ref[:, :depth])
    high, low = halves(reduced)
    stack_ref[:count] = high
    stack_ref[count:] = low
    pack_ref[:, cols:] = pad_lanes(fdot_t(reduced, reduced))
    basis_ref[...] = fdot(inverse, block_ref[...])
    for at, copy in enumerate(copies):
        copy.wait()
        pack_ref[:, at * width : (at + 1) * width] = split_dot(stack_ref[...], held_ref[at], 0)


def images_call(own, recv, block, moment, fetch):
    depth, cols = moment.shape
    count = block.shape[0]
    width = min(512, cols)
    stack = pltpu.VMEM((2 * count, depth), jnp.bfloat16)
    held = [
        pltpu.VMEM((cols // width, depth, width), jnp.float32),
        stack,
        pltpu.SemaphoreType.DMA((cols // width,)),
    ]
    return pl.pallas_call(
        images_kernel if fetch else images_blocked,
        grid=(1 if fetch else cols // width,),
        in_specs=[VMEM, VMEM, VMEM, ANY if fetch else pl.BlockSpec((depth, width), lambda i: (0, i))],
        out_specs=[VMEM, VMEM, VMEM],
        out_shape=[
            jax.ShapeDtypeStruct((count, cols + LANES), jnp.float32),
            jax.ShapeDtypeStruct((count, cols), jnp.float32),
            jax.ShapeDtypeStruct((count, LANES), jnp.float32),
        ],
        scratch_shapes=held if fetch else [stack],
        compiler_params=LARGE if fetch else PARAMS,
    )(own, recv, block, moment)


def reduced_kernel(has_prev, passed, width, *refs):
    names = 5 if has_prev else 3
    own_ref, recv_ref, basis_ref = refs[:3]
    prev_ref, low_ref = refs[3:5] if has_prev else (None, None)
    moment_ref = refs[names]
    outs = refs[names + 1 + passed :]
    pack_ref, residue_ref, diag_ref = outs[:3]
    stack_ref = refs[-1]
    at = pl.program_id(0)
    count, cols = basis_ref.shape
    height = moment_ref.shape[0]

    @pl.when(at == 0)
    def _():
        diag = (own_ref[:, cols:] + recv_ref[:, cols:])[:, :count]
        diag = 0.5 * (diag + diag.T)
        diag_ref[...] = pad_lanes(diag)
        residue = own_ref[:, :cols] + recv_ref[:, :cols] - fdot(diag, basis_ref[...])
        if has_prev:
            residue = residue - fdot(low_ref[:, :count], prev_ref[...])
        residue_ref[...] = residue
        high, low = halves(residue)
        stack_ref[:count] = high
        stack_ref[count:] = low
        pack_ref[:, width:] = pad_lanes(fdot_t(residue, residue))

    moment = moment_ref[...]
    if passed:
        short_ref = outs[3]
        short_ref[...] = moment[:, : short_ref.shape[1]].astype(jnp.bfloat16)
    pack_ref[:, pl.ds(pl.multiple_of(at * height, height), height)] = split_dot(stack_ref[...], moment, 1)


def reduced_call(own, recv, basis, prev, low, moment, gates, early_cols):
    depth, cols = moment.shape
    count = basis.shape[0]
    height = min(256, depth)
    has_prev = prev is not None
    operands = (own, recv, basis) + ((prev, low) if has_prev else ()) + (moment,)
    out_specs = [VMEM, VMEM, VMEM]
    out_shape = [
        jax.ShapeDtypeStruct((count, depth + LANES), jnp.float32),
        jax.ShapeDtypeStruct((count, cols), jnp.float32),
        jax.ShapeDtypeStruct((count, LANES), jnp.float32),
    ]
    if gates:
        out_specs += [pl.BlockSpec((height, early_cols), lambda i: (i, 0))] + [ANY] * len(gates)
        out_shape += [jax.ShapeDtypeStruct((depth, early_cols), jnp.bfloat16)]
        out_shape += [jax.ShapeDtypeStruct(at.shape, at.dtype) for at in gates]
    return pl.pallas_call(
        functools.partial(reduced_kernel, has_prev, len(gates), depth),
        grid=(depth // height,),
        in_specs=[VMEM] * (len(operands) - 1)
        + [pl.BlockSpec((height, cols), lambda i: (i, 0))]
        + [ANY] * len(gates),
        out_specs=out_specs,
        out_shape=out_shape,
        input_output_aliases={len(operands) + i: 4 + i for i in range(len(gates))},
        scratch_shapes=[pltpu.VMEM((2 * count, cols), jnp.bfloat16)],
        compiler_params=PARAMS,
    )(*operands, *gates)


def last_kernel(passed, own_ref, recv_ref, *refs):
    diag_ref, low_ref = refs[passed : passed + 2]
    count = own_ref.shape[0]
    depth = own_ref.shape[1] - LANES
    low_t, inverse = eliminate(own_ref[:, depth:] + recv_ref[:, depth:], count)
    low_ref[...] = low_t
    reduced = fdot(inverse, own_ref[:, :depth] + recv_ref[:, :depth])
    diag_ref[...] = pad_lanes(fdot_t(reduced, reduced))


def last_call(own, recv, gates, ties):
    shape = jax.ShapeDtypeStruct((own.shape[0], LANES), jnp.float32)
    return pl.pallas_call(
        functools.partial(last_kernel, len(gates) + len(ties)),
        in_specs=[VMEM, VMEM] + [ANY] * (len(gates) + len(ties)),
        out_specs=[VMEM, VMEM] + [ANY] * len(gates),
        out_shape=[shape, shape] + [jax.ShapeDtypeStruct(at.shape, at.dtype) for at in gates],
        input_output_aliases={2 + i: 2 + i for i in range(len(gates))},
        compiler_params=PARAMS,
    )(own, recv, *gates, *ties)


def top_kernel(steps, *refs):
    diag_refs = refs[: steps + 1]
    low_refs = refs[steps + 1 : 2 * steps]
    scaled_ref, rate_ref, krylov_ref = refs[-3:]
    count = diag_refs[0].shape[0]
    size = steps * count
    krylov_ref[...] = jnp.zeros_like(krylov_ref)
    for place in range(steps):
        first = place * count
        diag = diag_refs[place][:, :count]
        if place + 1 == steps:
            diag = diag + diag_refs[steps][:, :count]
        krylov_ref[first : first + count, first : first + count] = 0.5 * (diag + diag.T)
        if place + 1 < steps:
            second = first + count
            low_t = low_refs[place][:, :count]
            krylov_ref[second : second + count, first:second] = low_t
            krylov_ref[first:second, second : second + count] = low_t.T
    krylov = krylov_ref[...]
    power = krylov * (1.0 / jnp.max(jnp.abs(krylov), keepdims=True))
    for _ in range(SQUARINGS):
        power = fdot(power, power)
        power = power * (1.0 / jnp.max(jnp.abs(power), keepdims=True))
    tall = jnp.sum(power, axis=1, keepdims=True)
    wide = jnp.sum(power, axis=0, keepdims=True)
    tall = tall * (1.0 / jnp.sqrt(jnp.sum(tall * tall, keepdims=True)))
    wide = wide * (1.0 / jnp.sqrt(jnp.sum(wide * wide, keepdims=True)))
    top = jnp.sum(krylov * tall * wide, keepdims=True)
    scaled_ref[...] = krylov[:size, :size] / top
    rate_ref[...] = jnp.broadcast_to(1.0 / jnp.sqrt(top), rate_ref.shape)


def top_call(diags, lows, ties):
    steps = len(lows) + 1
    count = diags[0].shape[0]
    size = steps * count
    padded = -(-size // LANES) * LANES
    return pl.pallas_call(
        functools.partial(top_kernel, steps),
        in_specs=[VMEM] * (2 * steps) + [ANY] * len(ties),
        out_specs=[VMEM, VMEM],
        out_shape=[
            jax.ShapeDtypeStruct((size, size), jnp.float32),
            jax.ShapeDtypeStruct((8, LANES), jnp.float32),
        ],
        scratch_shapes=[pltpu.VMEM((padded, padded), jnp.float32)],
        compiler_params=PARAMS,
    )(*diags, *lows, *ties)


def step_kernel(weight_ref, moment_ref, rate_ref, tie_ref, *out_refs):
    stepped = weight_ref[...].astype(jnp.float32) - moment_ref[...] * rate_ref[:1, :1]
    width = out_refs[0].shape[1]
    for i, out_ref in enumerate(out_refs):
        out_ref[...] = stepped[:, i * width : (i + 1) * width].astype(jnp.bfloat16)


def step_call(weight, moment, rate, first, width, tie):
    depth = weight.shape[0]
    height = min(512, depth)
    part = width // PIECES
    block = pl.BlockSpec((height, width), lambda r: (r, first // width))
    return pl.pallas_call(
        step_kernel,
        grid=(depth // height,),
        in_specs=[block, block, VMEM, ANY],
        out_specs=[pl.BlockSpec((height, part), lambda r: (r, 0))] * PIECES,
        out_shape=[jax.ShapeDtypeStruct((depth, part), jnp.bfloat16)] * PIECES,
        compiler_params=LARGE,
        cost_estimate=BRIEF,
    )(weight, moment, rate, tie)


def project_kernel(far, pieces, count, early, in_place, ties, first, order_ref, *refs):
    tokens = refs[:pieces]
    refs = refs[pieces:]
    split = 1 if early else PIECES
    weights, refs = refs[: split * count], refs[split * count :]
    if early:
        moments, rate_ref, refs = refs[:count], refs[count], refs[count + 1 :]
    refs = refs[ties + (1 if in_place else 0) :]
    if not far:
        refs[1][...] = jnp.zeros(refs[1].shape, jnp.float32)
        refs = refs[:1] + refs[2:]
    out_ref, tokens_buf, weight_buf, moment_buf, total_ref, result_ref, sems, out_sem = refs
    depth, width = weight_buf.shape[1:]
    copies = []
    for k in range(count):
        step = []
        for i in range(pieces):
            if far:
                rows = tokens[i].shape[0]
                source = tokens[i].at[:, k * depth : (k + 1) * depth]
                target = tokens_buf.at[k, pl.ds(pl.multiple_of(order_ref[i], 16), rows), :]
            else:
                source = tokens[i].at[:, pl.ds(pl.multiple_of(order_ref[k] * depth, LANES), depth)]
                target = tokens_buf.at[k]
            step.append(pltpu.make_async_copy(source, target, sems.at[k, i]))
        if early:
            at = slice(first, first + width)
            step.append(pltpu.make_async_copy(weights[k].at[:, at], weight_buf.at[k], sems.at[k, pieces]))
            step.append(
                pltpu.make_async_copy(moments[k].at[:, at], moment_buf.at[k], sems.at[k, pieces + 1])
            )
        else:
            part = width // PIECES
            for i in range(PIECES):
                target = weight_buf.at[k, :, i * part : (i + 1) * part]
                step.append(
                    pltpu.make_async_copy(weights[k * PIECES + i], target, sems.at[k, pieces + i])
                )
        for copy in step:
            copy.start()
        copies.append(step)
    for k in range(count):
        for copy in copies[k]:
            copy.wait()
        block = weight_buf[k]
        if early:
            stepped = block.astype(jnp.float32) - moment_buf[k].astype(jnp.float32) * rate_ref[:1, :1]
            block = stepped.astype(jnp.bfloat16)
        part = jnp.dot(tokens_buf[k], block, preferred_element_type=jnp.float32)
        total_ref[...] = part if k == 0 else total_ref[...] + part
    if far:
        result_ref[...] = total_ref[...].astype(result_ref.dtype)
        copy = pltpu.make_async_copy(result_ref, out_ref, out_sem)
    else:
        copy = pltpu.make_async_copy(total_ref, out_ref.at[:, first : first + width], out_sem)
    copy.start()
    copy.wait()


def project_call(far, order, tokens, first, width, weights, moments, rate, ties=(), out=None, cols=None):
    early = moments is not None
    count = len(weights) // (1 if early else PIECES)
    depth = weights[0].shape[0]
    num_rows = sum(at.shape[0] for at in tokens)
    operands = list(tokens) + list(weights)
    specs = [ANY] * len(operands)
    if early:
        operands += list(moments) + [rate]
        specs += [ANY] * count + [VMEM]
    operands += list(ties)
    specs += [ANY] * len(ties)
    aliases = {}
    if far:
        out_shape = jax.ShapeDtypeStruct((num_rows, width), jnp.bfloat16)
    else:
        out_shape = [
            jax.ShapeDtypeStruct((num_rows, cols), jnp.float32),
            jax.ShapeDtypeStruct((8, LANES), jnp.float32),
        ]
        if out is not None:
            operands.append(out)
            specs.append(ANY)
            aliases = {len(operands): 0}
    return pl.pallas_call(
        functools.partial(
            project_kernel, far, len(tokens), count, early, bool(aliases), len(ties), first
        ),
        grid_spec=pltpu.PrefetchScalarGridSpec(
            num_scalar_prefetch=1,
            grid=(1,),
            in_specs=specs,
            out_specs=ANY if far else [ANY, VMEM],
            scratch_shapes=[
                pltpu.VMEM((count, num_rows, depth), jnp.bfloat16),
                pltpu.VMEM((count, depth, width), jnp.bfloat16),
                pltpu.VMEM((count, depth, width) if early else (8, LANES), jnp.bfloat16),
                pltpu.VMEM((num_rows, width), jnp.float32),
                pltpu.VMEM((num_rows, width) if far else (8, LANES), jnp.bfloat16),
                pltpu.SemaphoreType.DMA((count, len(tokens) + max(2, PIECES))),
                pltpu.SemaphoreType.DMA,
            ],
        ),
        out_shape=out_shape,
        input_output_aliases=aliases,
        compiler_params=LARGE,
        cost_estimate=BRIEF,
    )(order, *operands)


def add_kernel(old_ref, far_ref, out_ref):
    out_ref[...] = old_ref[...] + far_ref[...].astype(jnp.float32)


def add_call(out, far, first):
    num_rows, width = far.shape
    block = pl.BlockSpec((num_rows, UNIT), lambda c: (0, first // UNIT + c))
    return pl.pallas_call(
        add_kernel,
        grid=(width // UNIT,),
        in_specs=[block, pl.BlockSpec((num_rows, UNIT), lambda c: (0, c))],
        out_specs=block,
        out_shape=jax.ShapeDtypeStruct(out.shape, out.dtype),
        input_output_aliases={0: 0},
        compiler_params=LARGE,
        cost_estimate=BRIEF,
    )(out, far)


def swap(values, axis, size, bit):
    return lax.ppermute(values, axis, [(at, at ^ bit) for at in range(size)])


def butterfly(values, axis, size):
    bit = 1
    while 2 * bit < size:
        values = values + swap(values, axis, size, bit)
        bit *= 2
    return values, swap(values, axis, size, bit)


def offsets(count):
    found = [0]
    bit = count // 2
    while bit:
        found = found + [at ^ bit for at in found]
        bit //= 2
    return found


def spread(piece, axis, size):
    parts = [piece]
    bit = 1
    while bit < size:
        parts = parts + [swap(part, axis, size, bit) for part in parts]
        bit *= 2
    return parts


def local(rows_n, cols_n, tokens, weight, momentum, gradient, probes):
    half = rows_n // 2
    far_bit, near_bit = half // 2, half // 4
    place = lax.axis_index("fsdp")
    low_at = lax.rem(place, half)
    side = lax.div(place, half)
    column_at = lax.axis_index("tensor")
    num_rows = tokens.shape[0]
    depth, cols = weight.shape
    rows = num_rows // cols_n // PARTS
    unit = cols // (sum(EARLY) + sum(LATE))
    early_cols = sum(EARLY) * unit

    def fswap(values, bit):
        return swap(values, "fsdp", rows_n, bit)

    def complete(own, across, beside):
        parts = [own, across, beside, fswap(across, near_bit)]
        bit = near_bit // 2
        while bit:
            parts = parts + [fswap(part, bit) for part in parts]
            bit //= 2
        return parts

    def sum_over_rows(pack, gates, ties):
        passed = {}
        bit = 1
        while bit < half:
            pack, *passed[bit] = gate_call(pack, fswap(pack, bit), gates.get(bit, ()), ties.get(bit, ()))
            bit *= 2
        return pack, fswap(pack, half), passed

    mixed = jnp.stack([low_at ^ at for at in offsets(half)]).astype(jnp.int32)
    near_order = side * half + mixed
    pick_order = jnp.concatenate([(column_at * PARTS)[None], (1 - side) * half + mixed])
    far_order = jnp.stack(
        [(column_at ^ i) * PARTS * rows + part * rows for part in range(PARTS) for i in range(cols_n)]
    ).astype(jnp.int32)

    sent_0, sent_1, weight_own = pick_call(pick_order, tokens, weight, rows, half, early_cols)
    moment, short_1, pack = start_call(momentum, gradient, probes, sent_0, early_cols)
    weight_beside = fswap(weight_own, near_bit)
    weight_across = fswap(weight_own, far_bit)
    tokens_0 = fswap(sent_0, half)

    own, recv = butterfly(pack, "tensor", cols_n)
    pack, basis_1, _ = images_call(own, recv, probes, moment, True)
    own, recv, passed = sum_over_rows(
        pack, {1: [short_1], 2: [weight_across, tokens_0]}, {2: [weight_beside]}
    )
    short_1, = passed[1]
    weight_across, tokens_0 = passed[2]
    weight_parts = complete(weight_own, weight_across, weight_beside)
    moment_beside = fswap(short_1, near_bit)
    token_parts = spread(tokens_0, "tensor", cols_n)
    pack, residue, diag_1, short_2, sent_1 = reduced_call(
        own, recv, basis_1, None, None, moment, [sent_1], early_cols
    )
    moment_across = fswap(short_2, far_bit)
    tokens_1 = fswap(sent_1, half)

    own, recv = butterfly(pack, "tensor", cols_n)
    pack, basis_2, low_1 = images_call(own, recv, residue, moment, False)
    own, recv, passed = sum_over_rows(
        pack,
        {1: [moment_across], 2: [tokens_1]},
        {1: [*weight_parts[3:], moment_beside], 2: token_parts[1:]},
    )
    moment_across, = passed[1]
    token_1, = passed[2]
    moment_parts = complete(short_1, moment_across, moment_beside)
    token_1_beside = swap(token_1, "tensor", cols_n, 1)
    token_1_across = swap(token_1, "tensor", cols_n, 2)
    pack, _, diag_2 = reduced_call(own, recv, basis_2, basis_1, low_1, moment, [], early_cols)

    own, recv = butterfly(pack, "tensor", cols_n)
    diag_3, low_2, token_1_beside = last_call(
        own, recv, [token_1_beside], [token_1_across, *moment_parts[3:]]
    )
    token_parts += [token_1, token_1_beside, token_1_across, swap(token_1_beside, "tensor", cols_n, 2)]
    own, recv = butterfly(diag_3, "fsdp", rows_n)
    scaled, rate = top_call(
        [diag_1, diag_2, own, recv], [low_1, low_2], []
    )

    firsts, widths = [0], []
    for size in EARLY + LATE:
        widths.append(size * unit)
        firsts.append(firsts[-1] + size * unit)
    num_early = len(EARLY)
    gathered = [(weight_parts, moment_parts, rate)] * num_early
    out, partial, far = None, [], []

    def send(chunk, *ties):
        ties = [*ties] + far[chunk - num_early : chunk - num_early + 1] * (chunk >= num_early)
        partial.append(
            project_call(
                True, far_order, token_parts, firsts[chunk], widths[chunk], *gathered[chunk], ties=ties
            )
        )
        far.append(fswap(partial[-1], half))

    def keep(chunk, out, tie):
        return project_call(
            False,
            near_order,
            [tokens],
            firsts[chunk],
            widths[chunk],
            *gathered[chunk],
            ties=[tie],
            out=out,
            cols=cols,
        )

    total = len(widths)
    own, across, beside = {}, {}, {}

    def step(chunk, tie):
        own[chunk] = step_call(weight, moment, rate, firsts[chunk], widths[chunk], tie)
        across[chunk] = [fswap(at, far_bit) for at in own[chunk]]
        beside[chunk] = [fswap(at, near_bit) for at in own[chunk]]

    step(num_early, rate)
    if num_early + 1 < total:
        step(num_early + 1, own[num_early][0])
    send(0, own[min(num_early + 1, total - 1)][0])
    for chunk in range(1, num_early):
        send(chunk, partial[-1])
    for chunk in range(num_early):
        out, token = keep(chunk, out, partial[-1] if chunk == 0 else token)
    for chunk in range(num_early, total):
        ahead = [*beside[chunk], *across.get(chunk + 1, ())] if chunk > num_early else []
        passed = pass_call(across[chunk], [partial[-1], *ahead])
        pieces = [complete(*at) for at in zip(own[chunk], passed, beside[chunk])]
        gathered.append(([piece[k] for k in range(half) for piece in pieces], None, None))
        if chunk + 2 < total:
            step(chunk + 2, token)
            send(chunk, partial[-1], own[chunk + 2][0])
        else:
            send(chunk, partial[-1], token)
        out = add_call(out, far[chunk - num_early], firsts[chunk - num_early])
        out, token = keep(chunk, out, partial[-1])
    for chunk in range(total - num_early, total):
        out = add_call(out, far[chunk], firsts[chunk])
    return out, moment, scaled


def solution(mesh):
    return jax.shard_map(
        functools.partial(local, mesh.shape["fsdp"], mesh.shape["tensor"]),
        mesh=mesh,
        in_specs=(
            P("fsdp", None),
            P("fsdp", "tensor"),
            P("fsdp", "tensor"),
            P("fsdp", "tensor"),
            P(None, "tensor"),
        ),
        out_specs=(P("fsdp", "tensor"), P("fsdp", "tensor"), P()),
        check_vma=False,
    )
```

```python
import functools

import jax
import jax.numpy as jnp
from jax import lax
from jax.experimental import pallas as pl
from jax.experimental.pallas import tpu as pltpu
from jax.sharding import PartitionSpec as P

DECAY = 0.9
SQUARINGS = 5
LANES = 128
UNIT = 256
EARLY = (2,)
LATE = (2, 2, 1, 1)
PARTS = 2

HIGHEST = lax.Precision.HIGHEST
LARGE = pltpu.CompilerParams(vmem_limit_bytes=53 * 1024 * 1024)
PARAMS = pltpu.CompilerParams(vmem_limit_bytes=24 * 1024 * 1024)
BRIEF = pl.CostEstimate(flops=0, bytes_accessed=0, transcendentals=0)
VMEM = pl.BlockSpec(memory_space=pltpu.VMEM)
ANY = pl.BlockSpec(memory_space=pl.ANY)


def fdot(left, right):
    return lax.dot_general(
        left, right, (((1,), (0,)), ((), ())), precision=HIGHEST, preferred_element_type=jnp.float32
    )


def fdot_t(left, right):
    return lax.dot_general(
        left, right, (((1,), (1,)), ((), ())), precision=HIGHEST, preferred_element_type=jnp.float32
    )


def halves(values):
    high = values.astype(jnp.bfloat16)
    return high, (values - high.astype(jnp.float32)).astype(jnp.bfloat16)


def split_dot(stacked, mat, contract):
    rows = stacked.shape[0] // 2
    mat_high, mat_low = halves(mat)
    dims = (((1,), (contract,)), ((), ()))
    first = lax.dot_general(stacked, mat_high, dims, preferred_element_type=jnp.float32)
    second = lax.dot_general(stacked[:rows], mat_low, dims, preferred_element_type=jnp.float32)
    return first[:rows] + first[rows:] + second


def eliminate(gram, count):
    rows = lax.broadcasted_iota(jnp.int32, (count, LANES), 0)
    lanes = lax.broadcasted_iota(jnp.int32, (count, LANES), 1)
    aug = jnp.where(lanes < count, gram, jnp.where(lanes - count == rows, 1.0, 0.0))
    for step in range(count):
        pivot = aug[step : step + 1, step : step + 1]
        factor = jnp.where(rows > step, aug[:, step : step + 1] * (1.0 / pivot), 0.0)
        aug = aug - factor * aug[step : step + 1, :]
    pivots = jnp.sum(jnp.where(lanes == rows, aug, 0.0), axis=1, keepdims=True)
    aug = aug * (1.0 / jnp.sqrt(pivots))
    low_t = jnp.where((lanes >= rows) & (lanes < count), aug, 0.0)
    return low_t, aug[:, count : 2 * count]


def pad_lanes(square):
    return jnp.concatenate(
        [square, jnp.zeros((square.shape[0], LANES - square.shape[1]), jnp.float32)], axis=1
    )


def pick_kernel(order_ref, token_0, token_1, weight_ref, sent_0, sent_1, early_ref):
    sent_0[...] = token_0[...]
    sent_1[...] = token_1[...]
    early_ref[...] = weight_ref[...]


def pick_call(order, tokens, weight, rows, count, early_cols):
    depth = weight.shape[0]
    height = depth // count
    sent = jax.ShapeDtypeStruct((rows, count * depth), tokens.dtype)
    weight_spec = pl.BlockSpec((height, early_cols), lambda i, order_ref: (i, 0))
    sent_spec = pl.BlockSpec((rows, depth), lambda i, order_ref: (0, i))
    return pl.pallas_call(
        pick_kernel,
        grid_spec=pltpu.PrefetchScalarGridSpec(
            num_scalar_prefetch=1,
            grid=(count,),
            in_specs=[
                pl.BlockSpec((rows, depth), lambda i, order_ref: (order_ref[0], order_ref[1 + i])),
                pl.BlockSpec((rows, depth), lambda i, order_ref: (order_ref[0] + 1, order_ref[1 + i])),
                weight_spec,
            ],
            out_specs=[sent_spec, sent_spec, weight_spec],
        ),
        out_shape=[sent, sent, jax.ShapeDtypeStruct((depth, early_cols), weight.dtype)],
        compiler_params=LARGE,
    )(order, tokens, tokens, weight)


def start_kernel(width, mom_ref, grad_ref, probes_ref, tie_ref, moment_ref, short_ref, pack_ref, stack_ref):
    at = pl.program_id(0)
    count = probes_ref.shape[0]
    height = mom_ref.shape[0]

    @pl.when(at == 0)
    def _():
        probes = probes_ref[...]
        high, low = halves(probes)
        stack_ref[:count] = high
        stack_ref[count:] = low
        pack_ref[:, width:] = pad_lanes(fdot_t(probes, probes))

    moment = DECAY * mom_ref[...] + grad_ref[...].astype(jnp.float32)
    moment_ref[...] = moment
    short_ref[...] = moment[:, : short_ref.shape[1]].astype(jnp.bfloat16)
    pack_ref[:, pl.ds(pl.multiple_of(at * height, height), height)] = split_dot(stack_ref[...], moment, 1)


def start_call(momentum, gradient, probes, tie, early_cols):
    depth, cols = momentum.shape
    count = probes.shape[0]
    height = min(256, depth)
    rows = pl.BlockSpec((height, cols), lambda i: (i, 0))
    return pl.pallas_call(
        functools.partial(start_kernel, depth),
        grid=(depth // height,),
        in_specs=[rows, rows, VMEM, ANY],
        out_specs=[rows, pl.BlockSpec((height, early_cols), lambda i: (i, 0)), VMEM],
        out_shape=[
            jax.ShapeDtypeStruct((depth, cols), jnp.float32),
            jax.ShapeDtypeStruct((depth, early_cols), jnp.bfloat16),
            jax.ShapeDtypeStruct((count, depth + LANES), jnp.float32),
        ],
        scratch_shapes=[pltpu.VMEM((2 * count, cols), jnp.bfloat16)],
        compiler_params=LARGE,
    )(momentum, gradient, probes, tie)


def gate_kernel(passed, own_ref, recv_ref, *refs):
    sum_ref = refs[-1 - passed]
    sum_ref[...] = own_ref[...] + recv_ref[...]


def gate_call(own, recv, gates=(), ties=()):
    shapes = [jax.ShapeDtypeStruct(at.shape, at.dtype) for at in (own, *gates)]
    first = 2 + len(ties)
    return pl.pallas_call(
        functools.partial(gate_kernel, len(gates)),
        in_specs=[VMEM, VMEM] + [ANY] * (len(gates) + len(ties)),
        out_specs=[VMEM] + [ANY] * len(gates),
        out_shape=shapes,
        input_output_aliases={first + i: 1 + i for i in range(len(gates))},
        compiler_params=PARAMS,
    )(own, recv, *ties, *gates)


def pass_kernel(*refs):
    pass


def pass_call(values, ties):
    return pl.pallas_call(
        pass_kernel,
        in_specs=[ANY] * (len(values) + len(ties)),
        out_specs=[ANY] * len(values),
        out_shape=[jax.ShapeDtypeStruct(at.shape, at.dtype) for at in values],
        input_output_aliases={i: i for i in range(len(values))},
        compiler_params=LARGE,
        cost_estimate=BRIEF,
    )(*values, *ties)


def images_blocked(own_ref, recv_ref, block_ref, moment_ref, *refs):
    pack_ref, basis_ref, low_ref, stack_ref = refs[-4:]
    at = pl.program_id(0)
    count, cols = block_ref.shape
    depth = moment_ref.shape[0]
    width = moment_ref.shape[1]

    @pl.when(at == 0)
    def _():
        low_t, inverse = eliminate(own_ref[:, depth:] + recv_ref[:, depth:], count)
        low_ref[...] = low_t
        reduced = fdot(inverse, own_ref[:, :depth] + recv_ref[:, :depth])
        high, low = halves(reduced)
        stack_ref[:count] = high
        stack_ref[count:] = low
        pack_ref[:, cols:] = pad_lanes(fdot_t(reduced, reduced))
        basis_ref[...] = fdot(inverse, block_ref[...])

    pack_ref[:, pl.ds(pl.multiple_of(at * width, width), width)] = split_dot(stack_ref[...], moment_ref[...], 0)


def images_kernel(
    own_ref, recv_ref, block_ref, moment_ref, pack_ref, basis_ref, low_ref, held_ref, stack_ref, sems
):
    count, cols = block_ref.shape
    blocks, depth, width = held_ref.shape
    copies = [
        pltpu.make_async_copy(
            moment_ref.at[:, at * width : (at + 1) * width], held_ref.at[at], sems.at[at]
        )
        for at in range(blocks)
    ]
    for copy in copies:
        copy.start()
    low_t, inverse = eliminate(own_ref[:, depth:] + recv_ref[:, depth:], count)
    low_ref[...] = low_t
    reduced = fdot(inverse, own_ref[:, :depth] + recv_ref[:, :depth])
    high, low = halves(reduced)
    stack_ref[:count] = high
    stack_ref[count:] = low
    pack_ref[:, cols:] = pad_lanes(fdot_t(reduced, reduced))
    basis_ref[...] = fdot(inverse, block_ref[...])
    for at, copy in enumerate(copies):
        copy.wait()
        pack_ref[:, at * width : (at + 1) * width] = split_dot(stack_ref[...], held_ref[at], 0)


def images_call(own, recv, block, moment, fetch, ties=()):
    depth, cols = moment.shape
    count = block.shape[0]
    width = min(512, cols)
    stack = pltpu.VMEM((2 * count, depth), jnp.bfloat16)
    held = [
        pltpu.VMEM((cols // width, depth, width), jnp.float32),
        stack,
        pltpu.SemaphoreType.DMA((cols // width,)),
    ]
    return pl.pallas_call(
        images_kernel if fetch else images_blocked,
        grid=(1 if fetch else cols // width,),
        in_specs=[VMEM, VMEM, VMEM, ANY if fetch else pl.BlockSpec((depth, width), lambda i: (0, i))]
        + [ANY] * len(ties),
        out_specs=[VMEM, VMEM, VMEM],
        out_shape=[
            jax.ShapeDtypeStruct((count, cols + LANES), jnp.float32),
            jax.ShapeDtypeStruct((count, cols), jnp.float32),
            jax.ShapeDtypeStruct((count, LANES), jnp.float32),
        ],
        scratch_shapes=held if fetch else [stack],
        compiler_params=LARGE if fetch else PARAMS,
    )(own, recv, block, moment, *ties)


def reduced_kernel(has_prev, passed, width, *refs):
    names = 5 if has_prev else 3
    own_ref, recv_ref, basis_ref = refs[:3]
    prev_ref, low_ref = refs[3:5] if has_prev else (None, None)
    moment_ref = refs[names]
    outs = refs[names + 1 + passed :]
    pack_ref, residue_ref, diag_ref = outs[:3]
    stack_ref = refs[-1]
    at = pl.program_id(0)
    count, cols = basis_ref.shape
    height = moment_ref.shape[0]

    @pl.when(at == 0)
    def _():
        diag = (own_ref[:, cols:] + recv_ref[:, cols:])[:, :count]
        diag = 0.5 * (diag + diag.T)
        diag_ref[...] = pad_lanes(diag)
        residue = own_ref[:, :cols] + recv_ref[:, :cols] - fdot(diag, basis_ref[...])
        if has_prev:
            residue = residue - fdot(low_ref[:, :count], prev_ref[...])
        residue_ref[...] = residue
        high, low = halves(residue)
        stack_ref[:count] = high
        stack_ref[count:] = low
        pack_ref[:, width:] = pad_lanes(fdot_t(residue, residue))

    moment = moment_ref[...]
    if passed:
        short_ref = outs[3]
        short_ref[...] = moment[:, : short_ref.shape[1]].astype(jnp.bfloat16)
    pack_ref[:, pl.ds(pl.multiple_of(at * height, height), height)] = split_dot(stack_ref[...], moment, 1)


def reduced_call(own, recv, basis, prev, low, moment, gates, early_cols):
    depth, cols = moment.shape
    count = basis.shape[0]
    height = min(256, depth)
    has_prev = prev is not None
    operands = (own, recv, basis) + ((prev, low) if has_prev else ()) + (moment,)
    out_specs = [VMEM, VMEM, VMEM]
    out_shape = [
        jax.ShapeDtypeStruct((count, depth + LANES), jnp.float32),
        jax.ShapeDtypeStruct((count, cols), jnp.float32),
        jax.ShapeDtypeStruct((count, LANES), jnp.float32),
    ]
    if gates:
        out_specs += [pl.BlockSpec((height, early_cols), lambda i: (i, 0))] + [ANY] * len(gates)
        out_shape += [jax.ShapeDtypeStruct((depth, early_cols), jnp.bfloat16)]
        out_shape += [jax.ShapeDtypeStruct(at.shape, at.dtype) for at in gates]
    return pl.pallas_call(
        functools.partial(reduced_kernel, has_prev, len(gates), depth),
        grid=(depth // height,),
        in_specs=[VMEM] * (len(operands) - 1)
        + [pl.BlockSpec((height, cols), lambda i: (i, 0))]
        + [ANY] * len(gates),
        out_specs=out_specs,
        out_shape=out_shape,
        input_output_aliases={len(operands) + i: 4 + i for i in range(len(gates))},
        scratch_shapes=[pltpu.VMEM((2 * count, cols), jnp.bfloat16)],
        compiler_params=PARAMS,
    )(*operands, *gates)


def last_kernel(passed, own_ref, recv_ref, *refs):
    diag_ref, low_ref = refs[passed : passed + 2]
    count = own_ref.shape[0]
    depth = own_ref.shape[1] - LANES
    low_t, inverse = eliminate(own_ref[:, depth:] + recv_ref[:, depth:], count)
    low_ref[...] = low_t
    reduced = fdot(inverse, own_ref[:, :depth] + recv_ref[:, :depth])
    diag_ref[...] = pad_lanes(fdot_t(reduced, reduced))


def last_call(own, recv, gates, ties):
    shape = jax.ShapeDtypeStruct((own.shape[0], LANES), jnp.float32)
    return pl.pallas_call(
        functools.partial(last_kernel, len(gates) + len(ties)),
        in_specs=[VMEM, VMEM] + [ANY] * (len(gates) + len(ties)),
        out_specs=[VMEM, VMEM] + [ANY] * len(gates),
        out_shape=[shape, shape] + [jax.ShapeDtypeStruct(at.shape, at.dtype) for at in gates],
        input_output_aliases={2 + i: 2 + i for i in range(len(gates))},
        compiler_params=PARAMS,
    )(own, recv, *gates, *ties)


def top_kernel(steps, *refs):
    diag_refs = refs[: steps + 1]
    low_refs = refs[steps + 1 : 2 * steps]
    scaled_ref, rate_ref, krylov_ref = refs[-3:]
    count = diag_refs[0].shape[0]
    size = steps * count
    krylov_ref[...] = jnp.zeros_like(krylov_ref)
    for place in range(steps):
        first = place * count
        diag = diag_refs[place][:, :count]
        if place + 1 == steps:
            diag = diag + diag_refs[steps][:, :count]
        krylov_ref[first : first + count, first : first + count] = 0.5 * (diag + diag.T)
        if place + 1 < steps:
            second = first + count
            low_t = low_refs[place][:, :count]
            krylov_ref[second : second + count, first:second] = low_t
            krylov_ref[first:second, second : second + count] = low_t.T
    krylov = krylov_ref[...]
    power = krylov * (1.0 / jnp.max(jnp.abs(krylov), keepdims=True))
    for _ in range(SQUARINGS):
        power = fdot(power, power)
        power = power * (1.0 / jnp.max(jnp.abs(power), keepdims=True))
    tall = jnp.sum(power, axis=1, keepdims=True)
    wide = jnp.sum(power, axis=0, keepdims=True)
    tall = tall * (1.0 / jnp.sqrt(jnp.sum(tall * tall, keepdims=True)))
    wide = wide * (1.0 / jnp.sqrt(jnp.sum(wide * wide, keepdims=True)))
    top = jnp.sum(krylov * tall * wide, keepdims=True)
    scaled_ref[...] = krylov[:size, :size] / top
    rate_ref[...] = jnp.broadcast_to(1.0 / jnp.sqrt(top), rate_ref.shape)


def top_call(diags, lows, ties):
    steps = len(lows) + 1
    count = diags[0].shape[0]
    size = steps * count
    padded = -(-size // LANES) * LANES
    return pl.pallas_call(
        functools.partial(top_kernel, steps),
        in_specs=[VMEM] * (2 * steps) + [ANY] * len(ties),
        out_specs=[VMEM, VMEM],
        out_shape=[
            jax.ShapeDtypeStruct((size, size), jnp.float32),
            jax.ShapeDtypeStruct((8, LANES), jnp.float32),
        ],
        scratch_shapes=[pltpu.VMEM((padded, padded), jnp.float32)],
        compiler_params=PARAMS,
    )(*diags, *lows, *ties)


def step_kernel(weight_ref, moment_ref, rate_ref, tie_ref, *out_refs):
    stepped = weight_ref[...].astype(jnp.float32) - moment_ref[...] * rate_ref[:1, :1]
    width = out_refs[0].shape[1]
    for i, out_ref in enumerate(out_refs):
        out_ref[...] = stepped[:, i * width : (i + 1) * width].astype(jnp.bfloat16)


def step_call(weight, moment, rate, first, width, tie):
    depth = weight.shape[0]
    height = min(512, depth)
    block = pl.BlockSpec((height, width), lambda r: (r, first // width))
    return pl.pallas_call(
        step_kernel,
        grid=(depth // height,),
        in_specs=[block, block, VMEM, ANY],
        out_specs=[pl.BlockSpec((height, UNIT), lambda r: (r, 0))] * (width // UNIT),
        out_shape=[jax.ShapeDtypeStruct((depth, UNIT), jnp.bfloat16)] * (width // UNIT),
        compiler_params=LARGE,
        cost_estimate=BRIEF,
    )(weight, moment, rate, tie)


def project_kernel(far, pieces, count, split, early, in_place, ties, first, order_ref, *refs):
    tokens = refs[:pieces]
    refs = refs[pieces:]
    weights, refs = refs[: split * count], refs[split * count :]
    if early:
        moments, rate_ref, refs = refs[:count], refs[count], refs[count + 1 :]
    refs = refs[ties + (1 if in_place else 0) :]
    if not far:
        refs[1][...] = jnp.zeros(refs[1].shape, jnp.float32)
        refs = refs[:1] + refs[2:]
    out_ref, tokens_buf, weight_buf, moment_buf, total_ref, result_ref, sems, out_sem = refs
    depth, width = weight_buf.shape[1:]
    copies = []
    for k in range(count):
        step = []
        for i in range(pieces):
            if far:
                rows = tokens[i].shape[0]
                source = tokens[i].at[:, k * depth : (k + 1) * depth]
                target = tokens_buf.at[k, pl.ds(pl.multiple_of(order_ref[i], 16), rows), :]
            else:
                source = tokens[i].at[:, pl.ds(pl.multiple_of(order_ref[k] * depth, LANES), depth)]
                target = tokens_buf.at[k]
            step.append(pltpu.make_async_copy(source, target, sems.at[k, i]))
        if early:
            at = slice(first, first + width)
            step.append(pltpu.make_async_copy(weights[k].at[:, at], weight_buf.at[k], sems.at[k, pieces]))
            step.append(
                pltpu.make_async_copy(moments[k].at[:, at], moment_buf.at[k], sems.at[k, pieces + 1])
            )
        else:
            for i in range(split):
                target = weight_buf.at[k, :, i * UNIT : (i + 1) * UNIT]
                step.append(
                    pltpu.make_async_copy(weights[k * split + i], target, sems.at[k, pieces + i])
                )
        for copy in step:
            copy.start()
        copies.append(step)
    for k in range(count):
        for copy in copies[k]:
            copy.wait()
        block = weight_buf[k]
        if early:
            stepped = block.astype(jnp.float32) - moment_buf[k].astype(jnp.float32) * rate_ref[:1, :1]
            block = stepped.astype(jnp.bfloat16)
        part = jnp.dot(tokens_buf[k], block, preferred_element_type=jnp.float32)
        total_ref[...] = part if k == 0 else total_ref[...] + part
    if far:
        result_ref[...] = total_ref[...].astype(result_ref.dtype)
        copy = pltpu.make_async_copy(result_ref, out_ref, out_sem)
    else:
        copy = pltpu.make_async_copy(total_ref, out_ref.at[:, first : first + width], out_sem)
    copy.start()
    copy.wait()


def project_call(far, order, tokens, first, width, weights, moments, rate, ties=(), out=None, cols=None):
    early = moments is not None
    split = 1 if early else width // UNIT
    count = len(weights) // split
    depth = weights[0].shape[0]
    num_rows = sum(at.shape[0] for at in tokens)
    operands = list(tokens) + list(weights)
    specs = [ANY] * len(operands)
    if early:
        operands += list(moments) + [rate]
        specs += [ANY] * count + [VMEM]
    operands += list(ties)
    specs += [ANY] * len(ties)
    aliases = {}
    if far:
        out_shape = jax.ShapeDtypeStruct((num_rows, width), jnp.bfloat16)
    else:
        out_shape = [
            jax.ShapeDtypeStruct((num_rows, cols), jnp.float32),
            jax.ShapeDtypeStruct((8, LANES), jnp.float32),
        ]
        if out is not None:
            operands.append(out)
            specs.append(ANY)
            aliases = {len(operands): 0}
    return pl.pallas_call(
        functools.partial(
            project_kernel, far, len(tokens), count, split, early, bool(aliases), len(ties), first
        ),
        grid_spec=pltpu.PrefetchScalarGridSpec(
            num_scalar_prefetch=1,
            grid=(1,),
            in_specs=specs,
            out_specs=ANY if far else [ANY, VMEM],
            scratch_shapes=[
                pltpu.VMEM((count, num_rows, depth), jnp.bfloat16),
                pltpu.VMEM((count, depth, width), jnp.bfloat16),
                pltpu.VMEM((count, depth, width) if early else (8, LANES), jnp.bfloat16),
                pltpu.VMEM((num_rows, width), jnp.float32),
                pltpu.VMEM((num_rows, width) if far else (8, LANES), jnp.bfloat16),
                pltpu.SemaphoreType.DMA((count, len(tokens) + max(2, split))),
                pltpu.SemaphoreType.DMA,
            ],
        ),
        out_shape=out_shape,
        input_output_aliases=aliases,
        compiler_params=LARGE,
        cost_estimate=BRIEF,
    )(order, *operands)


def add_kernel(old_ref, far_ref, out_ref):
    out_ref[...] = old_ref[...] + far_ref[...].astype(jnp.float32)


def add_call(out, far, first):
    num_rows, width = far.shape
    block = pl.BlockSpec((num_rows, UNIT), lambda c: (0, first // UNIT + c))
    return pl.pallas_call(
        add_kernel,
        grid=(width // UNIT,),
        in_specs=[block, pl.BlockSpec((num_rows, UNIT), lambda c: (0, c))],
        out_specs=block,
        out_shape=jax.ShapeDtypeStruct(out.shape, out.dtype),
        input_output_aliases={0: 0},
        compiler_params=LARGE,
        cost_estimate=BRIEF,
    )(out, far)


def swap(values, axis, size, bit):
    return lax.ppermute(values, axis, [(at, at ^ bit) for at in range(size)])


def butterfly(values, axis, size):
    bit = 1
    while 2 * bit < size:
        values = values + swap(values, axis, size, bit)
        bit *= 2
    return values, swap(values, axis, size, bit)


def offsets(count):
    found = [0]
    bit = count // 2
    while bit:
        found = found + [at ^ bit for at in found]
        bit //= 2
    return found


def spread(piece, axis, size):
    parts = [piece]
    bit = 1
    while bit < size:
        parts = parts + [swap(part, axis, size, bit) for part in parts]
        bit *= 2
    return parts


def local(rows_n, cols_n, tokens, weight, momentum, gradient, probes):
    half = rows_n // 2
    far_bit, near_bit = half // 2, half // 4
    place = lax.axis_index("fsdp")
    low_at = lax.rem(place, half)
    side = lax.div(place, half)
    column_at = lax.axis_index("tensor")
    num_rows = tokens.shape[0]
    depth, cols = weight.shape
    rows = num_rows // cols_n // PARTS
    unit = cols // (sum(EARLY) + sum(LATE))
    early_cols = sum(EARLY) * unit

    def fswap(values, bit):
        return swap(values, "fsdp", rows_n, bit)

    def complete(own, across, beside):
        parts = [own, across, beside, fswap(across, near_bit)]
        bit = near_bit // 2
        while bit:
            parts = parts + [fswap(part, bit) for part in parts]
            bit //= 2
        return parts

    def sum_over_rows(pack, gates, ties):
        passed = {}
        bit = 1
        while bit < half:
            pack, *passed[bit] = gate_call(pack, fswap(pack, bit), gates.get(bit, ()), ties.get(bit, ()))
            bit *= 2
        return pack, fswap(pack, half), passed

    mixed = jnp.stack([low_at ^ at for at in offsets(half)]).astype(jnp.int32)
    near_order = side * half + mixed
    pick_order = jnp.concatenate([(column_at * PARTS)[None], (1 - side) * half + mixed])
    far_order = jnp.stack(
        [(column_at ^ i) * PARTS * rows + part * rows for part in range(PARTS) for i in range(cols_n)]
    ).astype(jnp.int32)

    sent_0, sent_1, weight_own = pick_call(pick_order, tokens, weight, rows, half, early_cols)
    moment, short_1, pack = start_call(momentum, gradient, probes, sent_0, early_cols)
    weight_beside = fswap(weight_own, near_bit)
    weight_across = fswap(weight_own, far_bit)
    tokens_0 = fswap(sent_0, half)

    own, recv = butterfly(pack, "tensor", cols_n)
    pack, basis_1, _ = images_call(own, recv, probes, moment, True)
    own, recv, passed = sum_over_rows(
        pack, {1: [short_1, tokens_0], 2: [weight_across]}, {2: [weight_beside]}
    )
    short_1, tokens_0 = passed[1]
    weight_across, = passed[2]
    weight_parts = complete(weight_own, weight_across, weight_beside)
    moment_beside = fswap(short_1, near_bit)
    token_parts = spread(tokens_0, "tensor", cols_n)
    pack, residue, diag_1, short_2, sent_1 = reduced_call(
        own, recv, basis_1, None, None, moment, [sent_1], early_cols
    )
    moment_across = fswap(short_2, far_bit)
    tokens_1 = fswap(sent_1, half)

    own, recv = butterfly(pack, "tensor", cols_n)
    pack, basis_2, low_1 = images_call(own, recv, residue, moment, False, weight_parts[3:])
    own, recv, passed = sum_over_rows(
        pack,
        {1: [moment_across, tokens_1]},
        {1: [moment_beside], 2: token_parts[1:]},
    )
    moment_across, token_1 = passed[1]
    moment_parts = complete(short_1, moment_across, moment_beside)
    token_1_beside = swap(token_1, "tensor", cols_n, 1)
    token_1_across = swap(token_1, "tensor", cols_n, 2)
    pack, _, diag_2 = reduced_call(own, recv, basis_2, basis_1, low_1, moment, [], early_cols)

    own, recv = butterfly(pack, "tensor", cols_n)
    diag_3, low_2, token_1_beside = last_call(
        own, recv, [token_1_beside], [token_1_across, *moment_parts[3:]]
    )
    token_parts += [token_1, token_1_beside, token_1_across, swap(token_1_beside, "tensor", cols_n, 2)]
    own, recv = butterfly(diag_3, "fsdp", rows_n)
    scaled, rate = top_call(
        [diag_1, diag_2, own, recv], [low_1, low_2], []
    )

    firsts, widths = [0], []
    for size in EARLY + LATE:
        widths.append(size * unit)
        firsts.append(firsts[-1] + size * unit)
    num_early = len(EARLY)
    gathered = [(weight_parts, moment_parts, rate)] * num_early
    out, partial, far = None, [], []

    def send(chunk, *ties):
        ties = [*ties] + far[chunk - num_early : chunk - num_early + 1] * (chunk >= num_early)
        partial.append(
            project_call(
                True, far_order, token_parts, firsts[chunk], widths[chunk], *gathered[chunk], ties=ties
            )
        )
        far.append(fswap(partial[-1], half))

    def keep(chunk, out, tie):
        return project_call(
            False,
            near_order,
            [tokens],
            firsts[chunk],
            widths[chunk],
            *gathered[chunk],
            ties=[tie],
            out=out,
            cols=cols,
        )

    total = len(widths)
    own, across, beside = {}, {}, {}

    def step(chunk, tie):
        own[chunk] = step_call(weight, moment, rate, firsts[chunk], widths[chunk], tie)
        across[chunk] = [fswap(at, far_bit) for at in own[chunk]]
        beside[chunk] = [fswap(at, near_bit) for at in own[chunk]]

    step(num_early, rate)
    send(0, own[num_early][0])
    for chunk in range(1, num_early):
        send(chunk, partial[-1])
    for chunk in range(num_early):
        out, token = keep(chunk, out, partial[-1] if chunk == 0 else token)
    for chunk in range(num_early, total):
        ahead = beside[chunk] + (across.get(chunk + 1, []) if chunk > num_early else [])
        passed = pass_call(across[chunk], [partial[-1], *ahead])
        pieces = [complete(*at) for at in zip(own[chunk], passed, beside[chunk])]
        gathered.append(([piece[k] for k in range(half) for piece in pieces], None, None))
        if chunk == num_early and chunk + 1 < total:
            step(chunk + 1, passed[0])
        if chunk + 2 < total:
            step(chunk + 2, token)
            send(chunk, partial[-1], own[chunk + 2][0])
        else:
            send(chunk, partial[-1], token)
        out = add_call(out, far[chunk - num_early], firsts[chunk - num_early])
        out, token = keep(chunk, out, partial[-1])
    for chunk in range(total - num_early, total):
        out = add_call(out, far[chunk], firsts[chunk])
    return out, moment, scaled


def solution(mesh):
    return jax.shard_map(
        functools.partial(local, mesh.shape["fsdp"], mesh.shape["tensor"]),
        mesh=mesh,
        in_specs=(
            P("fsdp", None),
            P("fsdp", "tensor"),
            P("fsdp", "tensor"),
            P("fsdp", "tensor"),
            P(None, "tensor"),
        ),
        out_specs=(P("fsdp", "tensor"), P("fsdp", "tensor"), P()),
        check_vma=False,
    )
```

```python
import functools

import jax
import jax.numpy as jnp
from jax import lax
from jax.experimental import pallas as pl
from jax.experimental.pallas import tpu as pltpu
from jax.sharding import PartitionSpec as P

DECAY = 0.9
SQUARINGS = 5
LANES = 128
UNIT = 256
EARLY = (2,)
LATE = (2, 2, 1, 1)
PARTS = (2, 1)

HIGHEST = lax.Precision.HIGHEST
LARGE = pltpu.CompilerParams(vmem_limit_bytes=53 * 1024 * 1024)
PARAMS = pltpu.CompilerParams(vmem_limit_bytes=24 * 1024 * 1024)
BRIEF = pl.CostEstimate(flops=0, bytes_accessed=0, transcendentals=0)
VMEM = pl.BlockSpec(memory_space=pltpu.VMEM)
ANY = pl.BlockSpec(memory_space=pl.ANY)


def fdot(left, right):
    return lax.dot_general(
        left, right, (((1,), (0,)), ((), ())), precision=HIGHEST, preferred_element_type=jnp.float32
    )


def fdot_t(left, right):
    return lax.dot_general(
        left, right, (((1,), (1,)), ((), ())), precision=HIGHEST, preferred_element_type=jnp.float32
    )


def halves(values):
    high = values.astype(jnp.bfloat16)
    return high, (values - high.astype(jnp.float32)).astype(jnp.bfloat16)


def split_dot(stacked, mat, contract):
    rows = stacked.shape[0] // 2
    mat_high, mat_low = halves(mat)
    dims = (((1,), (contract,)), ((), ()))
    first = lax.dot_general(stacked, mat_high, dims, preferred_element_type=jnp.float32)
    second = lax.dot_general(stacked[:rows], mat_low, dims, preferred_element_type=jnp.float32)
    return first[:rows] + first[rows:] + second


def eliminate(gram, count):
    rows = lax.broadcasted_iota(jnp.int32, (count, LANES), 0)
    lanes = lax.broadcasted_iota(jnp.int32, (count, LANES), 1)
    aug = jnp.where(lanes < count, gram, jnp.where(lanes - count == rows, 1.0, 0.0))
    for step in range(count):
        pivot = aug[step : step + 1, step : step + 1]
        factor = jnp.where(rows > step, aug[:, step : step + 1] * (1.0 / pivot), 0.0)
        aug = aug - factor * aug[step : step + 1, :]
    pivots = jnp.sum(jnp.where(lanes == rows, aug, 0.0), axis=1, keepdims=True)
    aug = aug * (1.0 / jnp.sqrt(pivots))
    low_t = jnp.where((lanes >= rows) & (lanes < count), aug, 0.0)
    return low_t, aug[:, count : 2 * count]


def pad_lanes(square):
    return jnp.concatenate(
        [square, jnp.zeros((square.shape[0], LANES - square.shape[1]), jnp.float32)], axis=1
    )


def pick_kernel(split, order_ref, *refs):
    tokens = refs[: sum(split)]
    weight_ref, *sent, early_ref = refs[sum(split) :]
    for out in sent:
        rows = tokens[0].shape[0]
        for i in range(out.shape[0] // rows):
            out[i * rows : (i + 1) * rows] = tokens[i][...]
        tokens = tokens[out.shape[0] // rows :]
    early_ref[...] = weight_ref[...]


def pick_call(order, tokens, weight, rows, count, early_cols):
    depth = weight.shape[0]
    height = depth // count

    def token_spec(i):
        return pl.BlockSpec((rows, depth), lambda c, order_ref: (order_ref[0] + i, order_ref[1 + c]))

    weight_spec = pl.BlockSpec((height, early_cols), lambda c, order_ref: (c, 0))
    return pl.pallas_call(
        functools.partial(pick_kernel, PARTS),
        grid_spec=pltpu.PrefetchScalarGridSpec(
            num_scalar_prefetch=1,
            grid=(count,),
            in_specs=[token_spec(i) for i in range(sum(PARTS))] + [weight_spec],
            out_specs=[pl.BlockSpec((part * rows, depth), lambda c, order_ref: (0, c)) for part in PARTS]
            + [weight_spec],
        ),
        out_shape=[jax.ShapeDtypeStruct((part * rows, count * depth), tokens.dtype) for part in PARTS]
        + [jax.ShapeDtypeStruct((depth, early_cols), weight.dtype)],
        compiler_params=LARGE,
    )(order, *[tokens] * sum(PARTS), weight)


def start_kernel(width, mom_ref, grad_ref, probes_ref, tie_ref, moment_ref, short_ref, pack_ref, stack_ref):
    at = pl.program_id(0)
    count = probes_ref.shape[0]
    height = mom_ref.shape[0]

    @pl.when(at == 0)
    def _():
        probes = probes_ref[...]
        high, low = halves(probes)
        stack_ref[:count] = high
        stack_ref[count:] = low
        pack_ref[:, width:] = pad_lanes(fdot_t(probes, probes))

    moment = DECAY * mom_ref[...] + grad_ref[...].astype(jnp.float32)
    moment_ref[...] = moment
    short_ref[...] = moment[:, : short_ref.shape[1]].astype(jnp.bfloat16)
    pack_ref[:, pl.ds(pl.multiple_of(at * height, height), height)] = split_dot(stack_ref[...], moment, 1)


def start_call(momentum, gradient, probes, tie, early_cols):
    depth, cols = momentum.shape
    count = probes.shape[0]
    height = min(256, depth)
    rows = pl.BlockSpec((height, cols), lambda i: (i, 0))
    return pl.pallas_call(
        functools.partial(start_kernel, depth),
        grid=(depth // height,),
        in_specs=[rows, rows, VMEM, ANY],
        out_specs=[rows, pl.BlockSpec((height, early_cols), lambda i: (i, 0)), VMEM],
        out_shape=[
            jax.ShapeDtypeStruct((depth, cols), jnp.float32),
            jax.ShapeDtypeStruct((depth, early_cols), jnp.bfloat16),
            jax.ShapeDtypeStruct((count, depth + LANES), jnp.float32),
        ],
        scratch_shapes=[pltpu.VMEM((2 * count, cols), jnp.bfloat16)],
        compiler_params=LARGE,
    )(momentum, gradient, probes, tie)


def gate_kernel(passed, own_ref, recv_ref, *refs):
    sum_ref = refs[-1 - passed]
    sum_ref[...] = own_ref[...] + recv_ref[...]


def gate_call(own, recv, gates=(), ties=()):
    shapes = [jax.ShapeDtypeStruct(at.shape, at.dtype) for at in (own, *gates)]
    first = 2 + len(ties)
    return pl.pallas_call(
        functools.partial(gate_kernel, len(gates)),
        in_specs=[VMEM, VMEM] + [ANY] * (len(gates) + len(ties)),
        out_specs=[VMEM] + [ANY] * len(gates),
        out_shape=shapes,
        input_output_aliases={first + i: 1 + i for i in range(len(gates))},
        compiler_params=PARAMS,
    )(own, recv, *ties, *gates)


def pass_kernel(*refs):
    pass


def pass_call(values, ties):
    return pl.pallas_call(
        pass_kernel,
        in_specs=[ANY] * (len(values) + len(ties)),
        out_specs=[ANY] * len(values),
        out_shape=[jax.ShapeDtypeStruct(at.shape, at.dtype) for at in values],
        input_output_aliases={i: i for i in range(len(values))},
        compiler_params=LARGE,
        cost_estimate=BRIEF,
    )(*values, *ties)


def images_blocked(own_ref, recv_ref, block_ref, moment_ref, *refs):
    pack_ref, basis_ref, low_ref, stack_ref = refs[-4:]
    at = pl.program_id(0)
    count, cols = block_ref.shape
    depth = moment_ref.shape[0]
    width = moment_ref.shape[1]

    @pl.when(at == 0)
    def _():
        low_t, inverse = eliminate(own_ref[:, depth:] + recv_ref[:, depth:], count)
        low_ref[...] = low_t
        reduced = fdot(inverse, own_ref[:, :depth] + recv_ref[:, :depth])
        high, low = halves(reduced)
        stack_ref[:count] = high
        stack_ref[count:] = low
        pack_ref[:, cols:] = pad_lanes(fdot_t(reduced, reduced))
        basis_ref[...] = fdot(inverse, block_ref[...])

    pack_ref[:, pl.ds(pl.multiple_of(at * width, width), width)] = split_dot(stack_ref[...], moment_ref[...], 0)


def images_kernel(
    own_ref, recv_ref, block_ref, moment_ref, pack_ref, basis_ref, low_ref, held_ref, stack_ref, sems
):
    count, cols = block_ref.shape
    blocks, depth, width = held_ref.shape
    copies = [
        pltpu.make_async_copy(
            moment_ref.at[:, at * width : (at + 1) * width], held_ref.at[at], sems.at[at]
        )
        for at in range(blocks)
    ]
    for copy in copies:
        copy.start()
    low_t, inverse = eliminate(own_ref[:, depth:] + recv_ref[:, depth:], count)
    low_ref[...] = low_t
    reduced = fdot(inverse, own_ref[:, :depth] + recv_ref[:, :depth])
    high, low = halves(reduced)
    stack_ref[:count] = high
    stack_ref[count:] = low
    pack_ref[:, cols:] = pad_lanes(fdot_t(reduced, reduced))
    basis_ref[...] = fdot(inverse, block_ref[...])
    for at, copy in enumerate(copies):
        copy.wait()
        pack_ref[:, at * width : (at + 1) * width] = split_dot(stack_ref[...], held_ref[at], 0)


def images_call(own, recv, block, moment, fetch, ties=()):
    depth, cols = moment.shape
    count = block.shape[0]
    width = min(512, cols)
    stack = pltpu.VMEM((2 * count, depth), jnp.bfloat16)
    held = [
        pltpu.VMEM((cols // width, depth, width), jnp.float32),
        stack,
        pltpu.SemaphoreType.DMA((cols // width,)),
    ]
    return pl.pallas_call(
        images_kernel if fetch else images_blocked,
        grid=(1 if fetch else cols // width,),
        in_specs=[VMEM, VMEM, VMEM, ANY if fetch else pl.BlockSpec((depth, width), lambda i: (0, i))]
        + [ANY] * len(ties),
        out_specs=[VMEM, VMEM, VMEM],
        out_shape=[
            jax.ShapeDtypeStruct((count, cols + LANES), jnp.float32),
            jax.ShapeDtypeStruct((count, cols), jnp.float32),
            jax.ShapeDtypeStruct((count, LANES), jnp.float32),
        ],
        scratch_shapes=held if fetch else [stack],
        compiler_params=LARGE if fetch else PARAMS,
    )(own, recv, block, moment, *ties)


def reduced_kernel(has_prev, passed, ties, width, *refs):
    names = 5 if has_prev else 3
    own_ref, recv_ref, basis_ref = refs[:3]
    prev_ref, low_ref = refs[3:5] if has_prev else (None, None)
    moment_ref = refs[names]
    outs = refs[names + 1 + passed + ties :]
    pack_ref, residue_ref, diag_ref = outs[:3]
    stack_ref = refs[-1]
    at = pl.program_id(0)
    count, cols = basis_ref.shape
    height = moment_ref.shape[0]

    @pl.when(at == 0)
    def _():
        diag = (own_ref[:, cols:] + recv_ref[:, cols:])[:, :count]
        diag = 0.5 * (diag + diag.T)
        diag_ref[...] = pad_lanes(diag)
        residue = own_ref[:, :cols] + recv_ref[:, :cols] - fdot(diag, basis_ref[...])
        if has_prev:
            residue = residue - fdot(low_ref[:, :count], prev_ref[...])
        residue_ref[...] = residue
        high, low = halves(residue)
        stack_ref[:count] = high
        stack_ref[count:] = low
        pack_ref[:, width:] = pad_lanes(fdot_t(residue, residue))

    moment = moment_ref[...]
    if passed:
        short_ref = outs[3]
        short_ref[...] = moment[:, : short_ref.shape[1]].astype(jnp.bfloat16)
    pack_ref[:, pl.ds(pl.multiple_of(at * height, height), height)] = split_dot(stack_ref[...], moment, 1)


def reduced_call(own, recv, basis, prev, low, moment, gates, ties, early_cols):
    depth, cols = moment.shape
    count = basis.shape[0]
    height = min(256, depth)
    has_prev = prev is not None
    operands = (own, recv, basis) + ((prev, low) if has_prev else ()) + (moment,)
    out_specs = [VMEM, VMEM, VMEM]
    out_shape = [
        jax.ShapeDtypeStruct((count, depth + LANES), jnp.float32),
        jax.ShapeDtypeStruct((count, cols), jnp.float32),
        jax.ShapeDtypeStruct((count, LANES), jnp.float32),
    ]
    if gates:
        out_specs += [pl.BlockSpec((height, early_cols), lambda i: (i, 0))] + [ANY] * len(gates)
        out_shape += [jax.ShapeDtypeStruct((depth, early_cols), jnp.bfloat16)]
        out_shape += [jax.ShapeDtypeStruct(at.shape, at.dtype) for at in gates]
    return pl.pallas_call(
        functools.partial(reduced_kernel, has_prev, len(gates), len(ties), depth),
        grid=(depth // height,),
        in_specs=[VMEM] * (len(operands) - 1)
        + [pl.BlockSpec((height, cols), lambda i: (i, 0))]
        + [ANY] * (len(gates) + len(ties)),
        out_specs=out_specs,
        out_shape=out_shape,
        input_output_aliases={len(operands) + i: 4 + i for i in range(len(gates))},
        scratch_shapes=[pltpu.VMEM((2 * count, cols), jnp.bfloat16)],
        compiler_params=PARAMS,
    )(*operands, *gates, *ties)


def last_kernel(passed, own_ref, recv_ref, *refs):
    diag_ref, low_ref = refs[passed : passed + 2]
    count = own_ref.shape[0]
    depth = own_ref.shape[1] - LANES
    low_t, inverse = eliminate(own_ref[:, depth:] + recv_ref[:, depth:], count)
    low_ref[...] = low_t
    reduced = fdot(inverse, own_ref[:, :depth] + recv_ref[:, :depth])
    diag_ref[...] = pad_lanes(fdot_t(reduced, reduced))


def last_call(own, recv, gates, ties):
    shape = jax.ShapeDtypeStruct((own.shape[0], LANES), jnp.float32)
    return pl.pallas_call(
        functools.partial(last_kernel, len(gates) + len(ties)),
        in_specs=[VMEM, VMEM] + [ANY] * (len(gates) + len(ties)),
        out_specs=[VMEM, VMEM] + [ANY] * len(gates),
        out_shape=[shape, shape] + [jax.ShapeDtypeStruct(at.shape, at.dtype) for at in gates],
        input_output_aliases={2 + i: 2 + i for i in range(len(gates))},
        compiler_params=PARAMS,
    )(own, recv, *gates, *ties)


def top_kernel(steps, *refs):
    diag_refs = refs[: steps + 1]
    low_refs = refs[steps + 1 : 2 * steps]
    scaled_ref, rate_ref, krylov_ref = refs[-3:]
    count = diag_refs[0].shape[0]
    size = steps * count
    krylov_ref[...] = jnp.zeros_like(krylov_ref)
    for place in range(steps):
        first = place * count
        diag = diag_refs[place][:, :count]
        if place + 1 == steps:
            diag = diag + diag_refs[steps][:, :count]
        krylov_ref[first : first + count, first : first + count] = 0.5 * (diag + diag.T)
        if place + 1 < steps:
            second = first + count
            low_t = low_refs[place][:, :count]
            krylov_ref[second : second + count, first:second] = low_t
            krylov_ref[first:second, second : second + count] = low_t.T
    krylov = krylov_ref[...]
    power = krylov * (1.0 / jnp.max(jnp.abs(krylov), keepdims=True))
    for _ in range(SQUARINGS):
        power = fdot(power, power)
        power = power * (1.0 / jnp.max(jnp.abs(power), keepdims=True))
    tall = jnp.sum(power, axis=1, keepdims=True)
    wide = jnp.sum(power, axis=0, keepdims=True)
    tall = tall * (1.0 / jnp.sqrt(jnp.sum(tall * tall, keepdims=True)))
    wide = wide * (1.0 / jnp.sqrt(jnp.sum(wide * wide, keepdims=True)))
    top = jnp.sum(krylov * tall * wide, keepdims=True)
    scaled_ref[...] = krylov[:size, :size] / top
    rate_ref[...] = jnp.broadcast_to(1.0 / jnp.sqrt(top), rate_ref.shape)


def top_call(diags, lows, ties):
    steps = len(lows) + 1
    count = diags[0].shape[0]
    size = steps * count
    padded = -(-size // LANES) * LANES
    return pl.pallas_call(
        functools.partial(top_kernel, steps),
        in_specs=[VMEM] * (2 * steps) + [ANY] * len(ties),
        out_specs=[VMEM, VMEM],
        out_shape=[
            jax.ShapeDtypeStruct((size, size), jnp.float32),
            jax.ShapeDtypeStruct((8, LANES), jnp.float32),
        ],
        scratch_shapes=[pltpu.VMEM((padded, padded), jnp.float32)],
        compiler_params=PARAMS,
    )(*diags, *lows, *ties)


def step_kernel(weight_ref, moment_ref, rate_ref, tie_ref, out_ref):
    stepped = weight_ref[...].astype(jnp.float32) - moment_ref[...] * rate_ref[:1, :1]
    out_ref[...] = stepped.astype(jnp.bfloat16)


def step_call(weight, moment, rate, first, width, tie):
    depth = weight.shape[0]
    height = min(512, depth)
    block = pl.BlockSpec((height, width), lambda r: (r, first // width))
    return pl.pallas_call(
        step_kernel,
        grid=(depth // height,),
        in_specs=[block, block, VMEM, ANY],
        out_specs=pl.BlockSpec((height, width), lambda r: (r, 0)),
        out_shape=jax.ShapeDtypeStruct((depth, width), jnp.bfloat16),
        compiler_params=LARGE,
        cost_estimate=BRIEF,
    )(weight, moment, rate, tie)


def project_kernel(far, pieces, count, early, in_place, ties, first, order_ref, *refs):
    tokens = refs[:pieces]
    refs = refs[pieces:]
    weights, refs = refs[:count], refs[count:]
    if early:
        moments, rate_ref, refs = refs[:count], refs[count], refs[count + 1 :]
    refs = refs[ties + (1 if in_place else 0) :]
    if not far:
        refs[1][...] = jnp.zeros(refs[1].shape, jnp.float32)
        refs = refs[:1] + refs[2:]
    out_ref, tokens_buf, weight_buf, moment_buf, total_ref, result_ref, sems, out_sem = refs
    depth, width = weight_buf.shape[1:]
    copies = []
    for k in range(count):
        step = []
        for i in range(pieces):
            if far:
                rows = tokens[i].shape[0]
                source = tokens[i].at[:, k * depth : (k + 1) * depth]
                target = tokens_buf.at[k, pl.ds(pl.multiple_of(order_ref[i], 16), rows), :]
            else:
                source = tokens[i].at[:, pl.ds(pl.multiple_of(order_ref[k] * depth, LANES), depth)]
                target = tokens_buf.at[k]
            step.append(pltpu.make_async_copy(source, target, sems.at[k, i]))
        if early:
            at = slice(first, first + width)
            step.append(pltpu.make_async_copy(weights[k].at[:, at], weight_buf.at[k], sems.at[k, pieces]))
            step.append(
                pltpu.make_async_copy(moments[k].at[:, at], moment_buf.at[k], sems.at[k, pieces + 1])
            )
        else:
            step.append(pltpu.make_async_copy(weights[k], weight_buf.at[k], sems.at[k, pieces]))
        for copy in step:
            copy.start()
        copies.append(step)
    for k in range(count):
        for copy in copies[k]:
            copy.wait()
        block = weight_buf[k]
        if early:
            stepped = block.astype(jnp.float32) - moment_buf[k].astype(jnp.float32) * rate_ref[:1, :1]
            block = stepped.astype(jnp.bfloat16)
        part = jnp.dot(tokens_buf[k], block, preferred_element_type=jnp.float32)
        total_ref[...] = part if k == 0 else total_ref[...] + part
    if far:
        result_ref[...] = total_ref[...].astype(result_ref.dtype)
        copy = pltpu.make_async_copy(result_ref, out_ref, out_sem)
    else:
        copy = pltpu.make_async_copy(total_ref, out_ref.at[:, first : first + width], out_sem)
    copy.start()
    copy.wait()


def project_call(far, order, tokens, first, width, weights, moments, rate, ties=(), out=None, cols=None):
    early = moments is not None
    count = len(weights)
    depth = weights[0].shape[0]
    num_rows = sum(at.shape[0] for at in tokens)
    operands = list(tokens) + list(weights)
    specs = [ANY] * len(operands)
    if early:
        operands += list(moments) + [rate]
        specs += [ANY] * count + [VMEM]
    operands += list(ties)
    specs += [ANY] * len(ties)
    aliases = {}
    if far:
        out_shape = jax.ShapeDtypeStruct((num_rows, width), jnp.bfloat16)
    else:
        out_shape = [
            jax.ShapeDtypeStruct((num_rows, cols), jnp.float32),
            jax.ShapeDtypeStruct((8, LANES), jnp.float32),
        ]
        if out is not None:
            operands.append(out)
            specs.append(ANY)
            aliases = {len(operands): 0}
    return pl.pallas_call(
        functools.partial(
            project_kernel, far, len(tokens), count, early, bool(aliases), len(ties), first
        ),
        grid_spec=pltpu.PrefetchScalarGridSpec(
            num_scalar_prefetch=1,
            grid=(1,),
            in_specs=specs,
            out_specs=ANY if far else [ANY, VMEM],
            scratch_shapes=[
                pltpu.VMEM((count, num_rows, depth), jnp.bfloat16),
                pltpu.VMEM((count, depth, width), jnp.bfloat16),
                pltpu.VMEM((count, depth, width) if early else (8, LANES), jnp.bfloat16),
                pltpu.VMEM((num_rows, width), jnp.float32),
                pltpu.VMEM((num_rows, width) if far else (8, LANES), jnp.bfloat16),
                pltpu.SemaphoreType.DMA((count, len(tokens) + 2)),
                pltpu.SemaphoreType.DMA,
            ],
        ),
        out_shape=out_shape,
        input_output_aliases=aliases,
        compiler_params=LARGE,
        cost_estimate=BRIEF,
    )(order, *operands)


def add_kernel(old_ref, far_ref, out_ref):
    out_ref[...] = old_ref[...] + far_ref[...].astype(jnp.float32)


def add_call(out, far, first):
    num_rows, width = far.shape
    block = pl.BlockSpec((num_rows, UNIT), lambda c: (0, first // UNIT + c))
    return pl.pallas_call(
        add_kernel,
        grid=(width // UNIT,),
        in_specs=[block, pl.BlockSpec((num_rows, UNIT), lambda c: (0, c))],
        out_specs=block,
        out_shape=jax.ShapeDtypeStruct(out.shape, out.dtype),
        input_output_aliases={0: 0},
        compiler_params=LARGE,
        cost_estimate=BRIEF,
    )(out, far)


def swap(values, axis, size, bit):
    return lax.ppermute(values, axis, [(at, at ^ bit) for at in range(size)])


def butterfly(values, axis, size):
    bit = 1
    while 2 * bit < size:
        values = values + swap(values, axis, size, bit)
        bit *= 2
    return values, swap(values, axis, size, bit)


def offsets(count):
    found = [0]
    bit = count // 2
    while bit:
        found = found + [at ^ bit for at in found]
        bit //= 2
    return found


def spread(piece, axis, size):
    parts = [piece]
    bit = 1
    while bit < size:
        parts = parts + [swap(part, axis, size, bit) for part in parts]
        bit *= 2
    return parts


def local(rows_n, cols_n, tokens, weight, momentum, gradient, probes):
    half = rows_n // 2
    far_bit, near_bit = half // 2, half // 4
    place = lax.axis_index("fsdp")
    low_at = lax.rem(place, half)
    side = lax.div(place, half)
    column_at = lax.axis_index("tensor")
    num_rows = tokens.shape[0]
    depth, cols = weight.shape
    rows = num_rows // cols_n // sum(PARTS)
    unit = cols // (sum(EARLY) + sum(LATE))
    early_cols = sum(EARLY) * unit

    def fswap(values, bit):
        return swap(values, "fsdp", rows_n, bit)

    def complete(own, across, beside):
        parts = [own, across, beside, fswap(across, near_bit)]
        bit = near_bit // 2
        while bit:
            parts = parts + [fswap(part, bit) for part in parts]
            bit //= 2
        return parts

    def sum_over_rows(pack, gates, ties):
        passed = {}
        bit = 1
        while bit < half:
            pack, *passed[bit] = gate_call(pack, fswap(pack, bit), gates.get(bit, ()), ties.get(bit, ()))
            bit *= 2
        return pack, fswap(pack, half), passed

    mixed = jnp.stack([low_at ^ at for at in offsets(half)]).astype(jnp.int32)
    near_order = side * half + mixed
    pick_order = jnp.concatenate([(column_at * sum(PARTS))[None], (1 - side) * half + mixed])
    far_order = jnp.stack(
        [((column_at ^ i) * sum(PARTS) + part) * rows for part in (0, PARTS[0]) for i in range(cols_n)]
    ).astype(jnp.int32)

    sent_0, sent_1, weight_own = pick_call(pick_order, tokens, weight, rows, half, early_cols)
    moment, short_1, pack = start_call(momentum, gradient, probes, sent_0, early_cols)
    weight_beside = fswap(weight_own, near_bit)
    weight_across = fswap(weight_own, far_bit)
    tokens_0 = fswap(sent_0, half)

    own, recv = butterfly(pack, "tensor", cols_n)
    pack, basis_1, _ = images_call(own, recv, probes, moment, True)
    own, recv, passed = sum_over_rows(
        pack, {1: [short_1], 2: [weight_across, tokens_0]}, {2: [weight_beside]}
    )
    short_1, = passed[1]
    weight_across, tokens_0 = passed[2]
    weight_parts = complete(weight_own, weight_across, weight_beside)
    moment_beside = fswap(short_1, near_bit)
    token_parts = spread(tokens_0, "tensor", cols_n)
    pack, residue, diag_1, short_2, sent_1 = reduced_call(
        own, recv, basis_1, None, None, moment, [sent_1], [moment_beside], early_cols
    )
    moment_across = fswap(short_2, far_bit)
    tokens_1 = fswap(sent_1, half)

    own, recv = butterfly(pack, "tensor", cols_n)
    pack, basis_2, low_1 = images_call(own, recv, residue, moment, False, weight_parts[3:])
    own, recv, passed = sum_over_rows(
        pack,
        {1: [moment_across, tokens_1]},
        {2: token_parts[1:]},
    )
    moment_across, token_1 = passed[1]
    moment_parts = complete(short_1, moment_across, moment_beside)
    token_1_beside = swap(token_1, "tensor", cols_n, 1)
    token_1_across = swap(token_1, "tensor", cols_n, 2)
    pack, _, diag_2 = reduced_call(own, recv, basis_2, basis_1, low_1, moment, [], [], early_cols)

    own, recv = butterfly(pack, "tensor", cols_n)
    diag_3, low_2, token_1_beside = last_call(
        own, recv, [token_1_beside], [token_1_across, *moment_parts[3:]]
    )
    token_parts += [token_1, token_1_beside, token_1_across, swap(token_1_beside, "tensor", cols_n, 2)]
    own, recv = butterfly(diag_3, "fsdp", rows_n)
    scaled, rate = top_call(
        [diag_1, diag_2, own, recv], [low_1, low_2], token_parts[-1:]
    )

    firsts, widths = [0], []
    for size in EARLY + LATE:
        widths.append(size * unit)
        firsts.append(firsts[-1] + size * unit)
    num_early = len(EARLY)
    gathered = [(weight_parts, moment_parts, rate)] * num_early
    out, partial, far = None, [], []

    def send(chunk, *ties):
        ties = [*ties] + far[chunk - num_early : chunk - num_early + 1] * (chunk >= num_early)
        partial.append(
            project_call(
                True, far_order, token_parts, firsts[chunk], widths[chunk], *gathered[chunk], ties=ties
            )
        )
        far.append(fswap(partial[-1], half))

    def keep(chunk, out, tie):
        return project_call(
            False,
            near_order,
            [tokens],
            firsts[chunk],
            widths[chunk],
            *gathered[chunk],
            ties=[tie],
            out=out,
            cols=cols,
        )

    total = len(widths)
    own, across, beside = {}, {}, {}

    def step(chunk, tie):
        own[chunk] = step_call(weight, moment, rate, firsts[chunk], widths[chunk], tie)
        across[chunk] = fswap(own[chunk], far_bit)
        beside[chunk] = fswap(own[chunk], near_bit)

    step(num_early, rate)
    send(0, own[num_early])
    for chunk in range(1, num_early):
        send(chunk, partial[-1])
    for chunk in range(num_early):
        out, token = keep(chunk, out, partial[-1] if chunk == 0 else token)
    for chunk in range(num_early, total):
        ahead = [across[chunk + 1]] if chunk > num_early and chunk + 1 < total else []
        passed, = pass_call([across[chunk]], [partial[-1], beside[chunk], *ahead])
        gathered.append((complete(own[chunk], passed, beside[chunk]), None, None))
        if chunk == num_early and chunk + 1 < total:
            step(chunk + 1, passed)
        if chunk + 2 < total:
            step(chunk + 2, token)
            send(chunk, partial[-1], own[chunk + 2])
        else:
            send(chunk, partial[-1], token)
        out = add_call(out, far[chunk - num_early], firsts[chunk - num_early])
        out, token = keep(chunk, out, partial[-1])
    for chunk in range(total - num_early, total):
        out = add_call(out, far[chunk], firsts[chunk])
    return out, moment, scaled


def solution(mesh):
    return jax.shard_map(
        functools.partial(local, mesh.shape["fsdp"], mesh.shape["tensor"]),
        mesh=mesh,
        in_specs=(
            P("fsdp", None),
            P("fsdp", "tensor"),
            P("fsdp", "tensor"),
            P("fsdp", "tensor"),
            P(None, "tensor"),
        ),
        out_specs=(P("fsdp", "tensor"), P("fsdp", "tensor"), P()),
        check_vma=False,
    )
```

```python
import functools

import jax
import jax.numpy as jnp
from jax import lax
from jax.experimental import pallas as pl
from jax.experimental.pallas import tpu as pltpu
from jax.sharding import PartitionSpec as P

DECAY = 0.9
SQUARINGS = 5
LANES = 128
UNIT = 256
EARLY = (2,)
LATE = (2, 2, 1, 1)
PARTS = 2

HIGHEST = lax.Precision.HIGHEST
LARGE = pltpu.CompilerParams(vmem_limit_bytes=53 * 1024 * 1024)
PARAMS = pltpu.CompilerParams(vmem_limit_bytes=24 * 1024 * 1024)
BRIEF = pl.CostEstimate(flops=0, bytes_accessed=0, transcendentals=0)
VMEM = pl.BlockSpec(memory_space=pltpu.VMEM)
ANY = pl.BlockSpec(memory_space=pl.ANY)


def fdot(left, right):
    return lax.dot_general(
        left, right, (((1,), (0,)), ((), ())), precision=HIGHEST, preferred_element_type=jnp.float32
    )


def fdot_t(left, right):
    return lax.dot_general(
        left, right, (((1,), (1,)), ((), ())), precision=HIGHEST, preferred_element_type=jnp.float32
    )


def halves(values):
    high = values.astype(jnp.bfloat16)
    return high, (values - high.astype(jnp.float32)).astype(jnp.bfloat16)


def split_dot(stacked, mat, contract):
    rows = stacked.shape[0] // 2
    mat_high, mat_low = halves(mat)
    dims = (((1,), (contract,)), ((), ()))
    first = lax.dot_general(stacked, mat_high, dims, preferred_element_type=jnp.float32)
    second = lax.dot_general(stacked[:rows], mat_low, dims, preferred_element_type=jnp.float32)
    return first[:rows] + first[rows:] + second


def eliminate(gram, count):
    rows = lax.broadcasted_iota(jnp.int32, (count, LANES), 0)
    lanes = lax.broadcasted_iota(jnp.int32, (count, LANES), 1)
    aug = jnp.where(lanes < count, gram, jnp.where(lanes - count == rows, 1.0, 0.0))
    for step in range(count):
        pivot = aug[step : step + 1, step : step + 1]
        factor = jnp.where(rows > step, aug[:, step : step + 1] * (1.0 / pivot), 0.0)
        aug = aug - factor * aug[step : step + 1, :]
    pivots = jnp.sum(jnp.where(lanes == rows, aug, 0.0), axis=1, keepdims=True)
    aug = aug * (1.0 / jnp.sqrt(pivots))
    low_t = jnp.where((lanes >= rows) & (lanes < count), aug, 0.0)
    return low_t, aug[:, count : 2 * count]


def pad_lanes(square):
    return jnp.concatenate(
        [square, jnp.zeros((square.shape[0], LANES - square.shape[1]), jnp.float32)], axis=1
    )


def pick_kernel(order_ref, token_0, token_1, weight_ref, sent_0, sent_1, early_ref):
    sent_0[...] = token_0[...]
    sent_1[...] = token_1[...]
    early_ref[...] = weight_ref[...]


def pick_call(order, tokens, weight, rows, count, early_cols):
    depth = weight.shape[0]
    height = depth // count
    sent = jax.ShapeDtypeStruct((rows, count * depth), tokens.dtype)
    weight_spec = pl.BlockSpec((height, early_cols), lambda i, order_ref: (i, 0))
    sent_spec = pl.BlockSpec((rows, depth), lambda i, order_ref: (0, i))
    return pl.pallas_call(
        pick_kernel,
        grid_spec=pltpu.PrefetchScalarGridSpec(
            num_scalar_prefetch=1,
            grid=(count,),
            in_specs=[
                pl.BlockSpec((rows, depth), lambda i, order_ref: (order_ref[0], order_ref[1 + i])),
                pl.BlockSpec((rows, depth), lambda i, order_ref: (order_ref[0] + 1, order_ref[1 + i])),
                weight_spec,
            ],
            out_specs=[sent_spec, sent_spec, weight_spec],
        ),
        out_shape=[sent, sent, jax.ShapeDtypeStruct((depth, early_cols), weight.dtype)],
        compiler_params=LARGE,
    )(order, tokens, tokens, weight)


def start_kernel(width, mom_ref, grad_ref, probes_ref, tie_ref, moment_ref, short_ref, pack_ref, stack_ref):
    at = pl.program_id(0)
    count = probes_ref.shape[0]
    height = mom_ref.shape[0]

    @pl.when(at == 0)
    def _():
        probes = probes_ref[...]
        high, low = halves(probes)
        stack_ref[:count] = high
        stack_ref[count:] = low
        pack_ref[:, width:] = pad_lanes(fdot_t(probes, probes))

    moment = DECAY * mom_ref[...] + grad_ref[...].astype(jnp.float32)
    moment_ref[...] = moment
    short_ref[...] = moment[:, : short_ref.shape[1]].astype(jnp.bfloat16)
    pack_ref[:, pl.ds(pl.multiple_of(at * height, height), height)] = split_dot(stack_ref[...], moment, 1)


def start_call(momentum, gradient, probes, tie, early_cols):
    depth, cols = momentum.shape
    count = probes.shape[0]
    height = min(256, depth)
    rows = pl.BlockSpec((height, cols), lambda i: (i, 0))
    return pl.pallas_call(
        functools.partial(start_kernel, depth),
        grid=(depth // height,),
        in_specs=[rows, rows, VMEM, ANY],
        out_specs=[rows, pl.BlockSpec((height, early_cols), lambda i: (i, 0)), VMEM],
        out_shape=[
            jax.ShapeDtypeStruct((depth, cols), jnp.float32),
            jax.ShapeDtypeStruct((depth, early_cols), jnp.bfloat16),
            jax.ShapeDtypeStruct((count, depth + LANES), jnp.float32),
        ],
        scratch_shapes=[pltpu.VMEM((2 * count, cols), jnp.bfloat16)],
        compiler_params=LARGE,
    )(momentum, gradient, probes, tie)


def gate_kernel(passed, own_ref, recv_ref, *refs):
    sum_ref = refs[-1 - passed]
    sum_ref[...] = own_ref[...] + recv_ref[...]


def gate_call(own, recv, gates=(), ties=()):
    shapes = [jax.ShapeDtypeStruct(at.shape, at.dtype) for at in (own, *gates)]
    first = 2 + len(ties)
    return pl.pallas_call(
        functools.partial(gate_kernel, len(gates)),
        in_specs=[VMEM, VMEM] + [ANY] * (len(gates) + len(ties)),
        out_specs=[VMEM] + [ANY] * len(gates),
        out_shape=shapes,
        input_output_aliases={first + i: 1 + i for i in range(len(gates))},
        compiler_params=PARAMS,
    )(own, recv, *ties, *gates)


def pass_kernel(*refs):
    pass


def pass_call(values, ties):
    return pl.pallas_call(
        pass_kernel,
        in_specs=[ANY] * (len(values) + len(ties)),
        out_specs=[ANY] * len(values),
        out_shape=[jax.ShapeDtypeStruct(at.shape, at.dtype) for at in values],
        input_output_aliases={i: i for i in range(len(values))},
        compiler_params=LARGE,
        cost_estimate=BRIEF,
    )(*values, *ties)


def images_blocked(own_ref, recv_ref, block_ref, moment_ref, *refs):
    pack_ref, basis_ref, low_ref, stack_ref = refs[-4:]
    at = pl.program_id(0)
    count, cols = block_ref.shape
    depth = moment_ref.shape[0]
    width = moment_ref.shape[1]

    @pl.when(at == 0)
    def _():
        low_t, inverse = eliminate(own_ref[:, depth:] + recv_ref[:, depth:], count)
        low_ref[...] = low_t
        reduced = fdot(inverse, own_ref[:, :depth] + recv_ref[:, :depth])
        high, low = halves(reduced)
        stack_ref[:count] = high
        stack_ref[count:] = low
        pack_ref[:, cols:] = pad_lanes(fdot_t(reduced, reduced))
        basis_ref[...] = fdot(inverse, block_ref[...])

    pack_ref[:, pl.ds(pl.multiple_of(at * width, width), width)] = split_dot(stack_ref[...], moment_ref[...], 0)


def images_kernel(
    own_ref, recv_ref, block_ref, moment_ref, pack_ref, basis_ref, low_ref, held_ref, stack_ref, sems
):
    count, cols = block_ref.shape
    blocks, depth, width = held_ref.shape
    copies = [
        pltpu.make_async_copy(
            moment_ref.at[:, at * width : (at + 1) * width], held_ref.at[at], sems.at[at]
        )
        for at in range(blocks)
    ]
    for copy in copies:
        copy.start()
    low_t, inverse = eliminate(own_ref[:, depth:] + recv_ref[:, depth:], count)
    low_ref[...] = low_t
    reduced = fdot(inverse, own_ref[:, :depth] + recv_ref[:, :depth])
    high, low = halves(reduced)
    stack_ref[:count] = high
    stack_ref[count:] = low
    pack_ref[:, cols:] = pad_lanes(fdot_t(reduced, reduced))
    basis_ref[...] = fdot(inverse, block_ref[...])
    for at, copy in enumerate(copies):
        copy.wait()
        pack_ref[:, at * width : (at + 1) * width] = split_dot(stack_ref[...], held_ref[at], 0)


def images_call(own, recv, block, moment, fetch, ties=()):
    depth, cols = moment.shape
    count = block.shape[0]
    width = min(512, cols)
    stack = pltpu.VMEM((2 * count, depth), jnp.bfloat16)
    held = [
        pltpu.VMEM((cols // width, depth, width), jnp.float32),
        stack,
        pltpu.SemaphoreType.DMA((cols // width,)),
    ]
    return pl.pallas_call(
        images_kernel if fetch else images_blocked,
        grid=(1 if fetch else cols // width,),
        in_specs=[VMEM, VMEM, VMEM, ANY if fetch else pl.BlockSpec((depth, width), lambda i: (0, i))]
        + [ANY] * len(ties),
        out_specs=[VMEM, VMEM, VMEM],
        out_shape=[
            jax.ShapeDtypeStruct((count, cols + LANES), jnp.float32),
            jax.ShapeDtypeStruct((count, cols), jnp.float32),
            jax.ShapeDtypeStruct((count, LANES), jnp.float32),
        ],
        scratch_shapes=held if fetch else [stack],
        compiler_params=LARGE if fetch else PARAMS,
    )(own, recv, block, moment, *ties)


def reduced_kernel(has_prev, passed, width, *refs):
    names = 5 if has_prev else 3
    own_ref, recv_ref, basis_ref = refs[:3]
    prev_ref, low_ref = refs[3:5] if has_prev else (None, None)
    moment_ref = refs[names]
    outs = refs[names + 1 + passed :]
    pack_ref, residue_ref, diag_ref = outs[:3]
    stack_ref = refs[-1]
    at = pl.program_id(0)
    count, cols = basis_ref.shape
    height = moment_ref.shape[0]

    @pl.when(at == 0)
    def _():
        diag = (own_ref[:, cols:] + recv_ref[:, cols:])[:, :count]
        diag = 0.5 * (diag + diag.T)
        diag_ref[...] = pad_lanes(diag)
        residue = own_ref[:, :cols] + recv_ref[:, :cols] - fdot(diag, basis_ref[...])
        if has_prev:
            residue = residue - fdot(low_ref[:, :count], prev_ref[...])
        residue_ref[...] = residue
        high, low = halves(residue)
        stack_ref[:count] = high
        stack_ref[count:] = low
        pack_ref[:, width:] = pad_lanes(fdot_t(residue, residue))

    moment = moment_ref[...]
    if passed:
        short_ref = outs[3]
        short_ref[...] = moment[:, : short_ref.shape[1]].astype(jnp.bfloat16)
    pack_ref[:, pl.ds(pl.multiple_of(at * height, height), height)] = split_dot(stack_ref[...], moment, 1)


def reduced_call(own, recv, basis, prev, low, moment, gates, early_cols):
    depth, cols = moment.shape
    count = basis.shape[0]
    height = min(256, depth)
    has_prev = prev is not None
    operands = (own, recv, basis) + ((prev, low) if has_prev else ()) + (moment,)
    out_specs = [VMEM, VMEM, VMEM]
    out_shape = [
        jax.ShapeDtypeStruct((count, depth + LANES), jnp.float32),
        jax.ShapeDtypeStruct((count, cols), jnp.float32),
        jax.ShapeDtypeStruct((count, LANES), jnp.float32),
    ]
    if gates:
        out_specs += [pl.BlockSpec((height, early_cols), lambda i: (i, 0))] + [ANY] * len(gates)
        out_shape += [jax.ShapeDtypeStruct((depth, early_cols), jnp.bfloat16)]
        out_shape += [jax.ShapeDtypeStruct(at.shape, at.dtype) for at in gates]
    return pl.pallas_call(
        functools.partial(reduced_kernel, has_prev, len(gates), depth),
        grid=(depth // height,),
        in_specs=[VMEM] * (len(operands) - 1)
        + [pl.BlockSpec((height, cols), lambda i: (i, 0))]
        + [ANY] * len(gates),
        out_specs=out_specs,
        out_shape=out_shape,
        input_output_aliases={len(operands) + i: 4 + i for i in range(len(gates))},
        scratch_shapes=[pltpu.VMEM((2 * count, cols), jnp.bfloat16)],
        compiler_params=PARAMS,
    )(*operands, *gates)


def last_kernel(passed, own_ref, recv_ref, *refs):
    diag_ref, low_ref = refs[passed : passed + 2]
    count = own_ref.shape[0]
    depth = own_ref.shape[1] - LANES
    low_t, inverse = eliminate(own_ref[:, depth:] + recv_ref[:, depth:], count)
    low_ref[...] = low_t
    reduced = fdot(inverse, own_ref[:, :depth] + recv_ref[:, :depth])
    diag_ref[...] = pad_lanes(fdot_t(reduced, reduced))


def last_call(own, recv, gates, ties):
    shape = jax.ShapeDtypeStruct((own.shape[0], LANES), jnp.float32)
    return pl.pallas_call(
        functools.partial(last_kernel, len(gates) + len(ties)),
        in_specs=[VMEM, VMEM] + [ANY] * (len(gates) + len(ties)),
        out_specs=[VMEM, VMEM] + [ANY] * len(gates),
        out_shape=[shape, shape] + [jax.ShapeDtypeStruct(at.shape, at.dtype) for at in gates],
        input_output_aliases={2 + i: 2 + i for i in range(len(gates))},
        compiler_params=PARAMS,
    )(own, recv, *gates, *ties)


def top_kernel(steps, *refs):
    diag_refs = refs[: steps + 1]
    low_refs = refs[steps + 1 : 2 * steps]
    scaled_ref, rate_ref, krylov_ref = refs[-3:]
    count = diag_refs[0].shape[0]
    size = steps * count
    krylov_ref[...] = jnp.zeros_like(krylov_ref)
    for place in range(steps):
        first = place * count
        diag = diag_refs[place][:, :count]
        if place + 1 == steps:
            diag = diag + diag_refs[steps][:, :count]
        krylov_ref[first : first + count, first : first + count] = 0.5 * (diag + diag.T)
        if place + 1 < steps:
            second = first + count
            low_t = low_refs[place][:, :count]
            krylov_ref[second : second + count, first:second] = low_t
            krylov_ref[first:second, second : second + count] = low_t.T
    krylov = krylov_ref[...]
    power = krylov * (1.0 / jnp.max(jnp.abs(krylov), keepdims=True))
    for _ in range(SQUARINGS):
        power = fdot(power, power)
        power = power * (1.0 / jnp.max(jnp.abs(power), keepdims=True))
    tall = jnp.sum(power, axis=1, keepdims=True)
    wide = jnp.sum(power, axis=0, keepdims=True)
    tall = tall * (1.0 / jnp.sqrt(jnp.sum(tall * tall, keepdims=True)))
    wide = wide * (1.0 / jnp.sqrt(jnp.sum(wide * wide, keepdims=True)))
    top = jnp.sum(krylov * tall * wide, keepdims=True)
    scaled_ref[...] = krylov[:size, :size] / top
    rate_ref[...] = jnp.broadcast_to(1.0 / jnp.sqrt(top), rate_ref.shape)


def top_call(diags, lows, ties):
    steps = len(lows) + 1
    count = diags[0].shape[0]
    size = steps * count
    padded = -(-size // LANES) * LANES
    return pl.pallas_call(
        functools.partial(top_kernel, steps),
        in_specs=[VMEM] * (2 * steps) + [ANY] * len(ties),
        out_specs=[VMEM, VMEM],
        out_shape=[
            jax.ShapeDtypeStruct((size, size), jnp.float32),
            jax.ShapeDtypeStruct((8, LANES), jnp.float32),
        ],
        scratch_shapes=[pltpu.VMEM((padded, padded), jnp.float32)],
        compiler_params=PARAMS,
    )(*diags, *lows, *ties)


def step_kernel(weight_ref, moment_ref, rate_ref, tie_ref, *out_refs):
    stepped = weight_ref[...].astype(jnp.float32) - moment_ref[...] * rate_ref[:1, :1]
    width = out_refs[0].shape[1]
    for i, out_ref in enumerate(out_refs):
        out_ref[...] = stepped[:, i * width : (i + 1) * width].astype(jnp.bfloat16)


def step_call(weight, moment, rate, first, width, tie):
    depth = weight.shape[0]
    height = min(512, depth)
    block = pl.BlockSpec((height, width), lambda r: (r, first // width))
    return pl.pallas_call(
        step_kernel,
        grid=(depth // height,),
        in_specs=[block, block, VMEM, ANY],
        out_specs=[pl.BlockSpec((height, UNIT), lambda r: (r, 0))] * (width // UNIT),
        out_shape=[jax.ShapeDtypeStruct((depth, UNIT), jnp.bfloat16)] * (width // UNIT),
        compiler_params=LARGE,
        cost_estimate=BRIEF,
    )(weight, moment, rate, tie)


def project_kernel(far, pieces, count, split, early, in_place, ties, first, order_ref, *refs):
    tokens = refs[:pieces]
    refs = refs[pieces:]
    weights, refs = refs[: split * count], refs[split * count :]
    if early:
        moments, rate_ref, refs = refs[:count], refs[count], refs[count + 1 :]
    refs = refs[ties + (1 if in_place else 0) :]
    if not far:
        refs[1][...] = jnp.zeros(refs[1].shape, jnp.float32)
        refs = refs[:1] + refs[2:]
    out_ref, tokens_buf, weight_buf, moment_buf, total_ref, result_ref, sems, out_sem = refs
    depth, width = weight_buf.shape[1:]
    copies = []
    for k in range(count):
        step = []
        for i in range(pieces):
            if far:
                rows = tokens[i].shape[0]
                source = tokens[i].at[:, k * depth : (k + 1) * depth]
                target = tokens_buf.at[k, pl.ds(pl.multiple_of(order_ref[i], 16), rows), :]
            else:
                source = tokens[i].at[:, pl.ds(pl.multiple_of(order_ref[k] * depth, LANES), depth)]
                target = tokens_buf.at[k]
            step.append(pltpu.make_async_copy(source, target, sems.at[k, i]))
        if early:
            at = slice(first, first + width)
            step.append(pltpu.make_async_copy(weights[k].at[:, at], weight_buf.at[k], sems.at[k, pieces]))
            step.append(
                pltpu.make_async_copy(moments[k].at[:, at], moment_buf.at[k], sems.at[k, pieces + 1])
            )
        else:
            for i in range(split):
                target = weight_buf.at[k, :, i * UNIT : (i + 1) * UNIT]
                step.append(
                    pltpu.make_async_copy(weights[k * split + i], target, sems.at[k, pieces + i])
                )
        for copy in step:
            copy.start()
        copies.append(step)
    for k in range(count):
        for copy in copies[k]:
            copy.wait()
        block = weight_buf[k]
        if early:
            stepped = block.astype(jnp.float32) - moment_buf[k].astype(jnp.float32) * rate_ref[:1, :1]
            block = stepped.astype(jnp.bfloat16)
        part = jnp.dot(tokens_buf[k], block, preferred_element_type=jnp.float32)
        total_ref[...] = part if k == 0 else total_ref[...] + part
    if far:
        result_ref[...] = total_ref[...].astype(result_ref.dtype)
        copy = pltpu.make_async_copy(result_ref, out_ref, out_sem)
    else:
        copy = pltpu.make_async_copy(total_ref, out_ref.at[:, first : first + width], out_sem)
    copy.start()
    copy.wait()


def project_call(far, order, tokens, first, width, weights, moments, rate, ties=(), out=None, cols=None):
    early = moments is not None
    split = 1 if early else width // UNIT
    count = len(weights) // split
    depth = weights[0].shape[0]
    num_rows = sum(at.shape[0] for at in tokens)
    operands = list(tokens) + list(weights)
    specs = [ANY] * len(operands)
    if early:
        operands += list(moments) + [rate]
        specs += [ANY] * count + [VMEM]
    operands += list(ties)
    specs += [ANY] * len(ties)
    aliases = {}
    if far:
        out_shape = jax.ShapeDtypeStruct((num_rows, width), jnp.bfloat16)
    else:
        out_shape = [
            jax.ShapeDtypeStruct((num_rows, cols), jnp.float32),
            jax.ShapeDtypeStruct((8, LANES), jnp.float32),
        ]
        if out is not None:
            operands.append(out)
            specs.append(ANY)
            aliases = {len(operands): 0}
    return pl.pallas_call(
        functools.partial(
            project_kernel, far, len(tokens), count, split, early, bool(aliases), len(ties), first
        ),
        grid_spec=pltpu.PrefetchScalarGridSpec(
            num_scalar_prefetch=1,
            grid=(1,),
            in_specs=specs,
            out_specs=ANY if far else [ANY, VMEM],
            scratch_shapes=[
                pltpu.VMEM((count, num_rows, depth), jnp.bfloat16),
                pltpu.VMEM((count, depth, width), jnp.bfloat16),
                pltpu.VMEM((count, depth, width) if early else (8, LANES), jnp.bfloat16),
                pltpu.VMEM((num_rows, width), jnp.float32),
                pltpu.VMEM((num_rows, width) if far else (8, LANES), jnp.bfloat16),
                pltpu.SemaphoreType.DMA((count, len(tokens) + max(2, split))),
                pltpu.SemaphoreType.DMA,
            ],
        ),
        out_shape=out_shape,
        input_output_aliases=aliases,
        compiler_params=LARGE,
        cost_estimate=BRIEF,
    )(order, *operands)


def add_kernel(old_ref, far_ref, out_ref):
    out_ref[...] = old_ref[...] + far_ref[...].astype(jnp.float32)


def add_call(out, far, first):
    num_rows, width = far.shape
    block = pl.BlockSpec((num_rows, UNIT), lambda c: (0, first // UNIT + c))
    return pl.pallas_call(
        add_kernel,
        grid=(width // UNIT,),
        in_specs=[block, pl.BlockSpec((num_rows, UNIT), lambda c: (0, c))],
        out_specs=block,
        out_shape=jax.ShapeDtypeStruct(out.shape, out.dtype),
        input_output_aliases={0: 0},
        compiler_params=LARGE,
        cost_estimate=BRIEF,
    )(out, far)


def swap(values, axis, size, bit):
    return lax.ppermute(values, axis, [(at, at ^ bit) for at in range(size)])


def butterfly(values, axis, size):
    bit = 1
    while 2 * bit < size:
        values = values + swap(values, axis, size, bit)
        bit *= 2
    return values, swap(values, axis, size, bit)


def offsets(count):
    found = [0]
    bit = count // 2
    while bit:
        found = found + [at ^ bit for at in found]
        bit //= 2
    return found


def spread(piece, axis, size):
    parts = [piece]
    bit = 1
    while bit < size:
        parts = parts + [swap(part, axis, size, bit) for part in parts]
        bit *= 2
    return parts


def local(rows_n, cols_n, tokens, weight, momentum, gradient, probes):
    half = rows_n // 2
    far_bit, near_bit = half // 2, half // 4
    place = lax.axis_index("fsdp")
    low_at = lax.rem(place, half)
    side = lax.div(place, half)
    column_at = lax.axis_index("tensor")
    num_rows = tokens.shape[0]
    depth, cols = weight.shape
    rows = num_rows // cols_n // PARTS
    unit = cols // (sum(EARLY) + sum(LATE))
    early_cols = sum(EARLY) * unit

    def fswap(values, bit):
        return swap(values, "fsdp", rows_n, bit)

    def complete(own, across, beside):
        parts = [own, across, beside, fswap(across, near_bit)]
        bit = near_bit // 2
        while bit:
            parts = parts + [fswap(part, bit) for part in parts]
            bit //= 2
        return parts

    def sum_over_rows(pack, gates, ties):
        passed = {}
        bit = 1
        while bit < half:
            pack, *passed[bit] = gate_call(pack, fswap(pack, bit), gates.get(bit, ()), ties.get(bit, ()))
            bit *= 2
        return pack, fswap(pack, half), passed

    mixed = jnp.stack([low_at ^ at for at in offsets(half)]).astype(jnp.int32)
    near_order = side * half + mixed
    pick_order = jnp.concatenate([(column_at * PARTS)[None], (1 - side) * half + mixed])
    far_order = jnp.stack(
        [(column_at ^ i) * PARTS * rows + part * rows for part in range(PARTS) for i in range(cols_n)]
    ).astype(jnp.int32)

    sent_0, sent_1, weight_own = pick_call(pick_order, tokens, weight, rows, half, early_cols)
    moment, short_1, pack = start_call(momentum, gradient, probes, sent_0, early_cols)
    weight_beside = fswap(weight_own, near_bit)
    weight_across = fswap(weight_own, far_bit)
    tokens_0 = fswap(sent_0, half)

    own, recv = butterfly(pack, "tensor", cols_n)
    pack, basis_1, _ = images_call(own, recv, probes, moment, True)
    own, recv, passed = sum_over_rows(
        pack, {1: [short_1, tokens_0], 2: [weight_across]}, {2: [weight_beside]}
    )
    short_1, tokens_0 = passed[1]
    weight_across, = passed[2]
    weight_parts = complete(weight_own, weight_across, weight_beside)
    moment_beside = fswap(short_1, near_bit)
    token_parts = spread(tokens_0, "tensor", cols_n)
    pack, residue, diag_1, short_2, sent_1 = reduced_call(
        own, recv, basis_1, None, None, moment, [sent_1], early_cols
    )
    moment_across = fswap(short_2, far_bit)
    tokens_1 = fswap(sent_1, half)

    own, recv = butterfly(pack, "tensor", cols_n)
    pack, basis_2, low_1 = images_call(own, recv, residue, moment, False, weight_parts[3:])
    own, recv, passed = sum_over_rows(
        pack,
        {1: [moment_across, tokens_1]},
        {1: [moment_beside], 2: token_parts[1:]},
    )
    moment_across, token_1 = passed[1]
    moment_parts = complete(short_1, moment_across, moment_beside)
    token_1_beside = swap(token_1, "tensor", cols_n, 1)
    token_1_across = swap(token_1, "tensor", cols_n, 2)
    pack, _, diag_2 = reduced_call(own, recv, basis_2, basis_1, low_1, moment, [], early_cols)

    own, recv = butterfly(pack, "tensor", cols_n)
    diag_3, low_2, token_1_beside = last_call(
        own, recv, [token_1_beside], [token_1_across, *moment_parts[3:]]
    )
    token_parts += [token_1, token_1_beside, token_1_across, swap(token_1_beside, "tensor", cols_n, 2)]
    own, recv = butterfly(diag_3, "fsdp", rows_n)
    scaled, rate = top_call(
        [diag_1, diag_2, own, recv], [low_1, low_2], []
    )

    firsts, widths = [0], []
    for size in EARLY + LATE:
        widths.append(size * unit)
        firsts.append(firsts[-1] + size * unit)
    num_early = len(EARLY)
    gathered = [(weight_parts, moment_parts, rate)] * num_early
    out, partial, far = None, [], []

    def send(chunk, *ties):
        partial.append(
            project_call(
                True, far_order, token_parts, firsts[chunk], widths[chunk], *gathered[chunk], ties=ties
            )
        )
        far.append(fswap(partial[-1], half))

    def keep(chunk, out, tie):
        return project_call(
            False,
            near_order,
            [tokens],
            firsts[chunk],
            widths[chunk],
            *gathered[chunk],
            ties=[tie],
            out=out,
            cols=cols,
        )

    total = len(widths)
    own, across, beside = {}, {}, {}

    def step(chunk, tie):
        own[chunk] = step_call(weight, moment, rate, firsts[chunk], widths[chunk], tie)
        across[chunk] = [fswap(at, far_bit) for at in own[chunk]]
        beside[chunk] = [fswap(at, near_bit) for at in own[chunk]]

    step(num_early, rate)
    send(0, own[num_early][0])
    for chunk in range(1, num_early):
        send(chunk, partial[-1])
    tokens_kept = []
    for chunk in range(num_early):
        out, token = keep(chunk, out, partial[-1] if chunk == 0 else token)
        tokens_kept.append(token)
    for chunk in range(num_early, total):
        passed = pass_call(across[chunk], [partial[-1], *beside[chunk]])
        pieces = [complete(*at) for at in zip(own[chunk], passed, beside[chunk])]
        gathered.append(([piece[k] for k in range(half) for piece in pieces], None, None))
        if chunk == num_early and chunk + 1 < total:
            step(chunk + 1, passed[0])
        if chunk + 2 < total:
            step(chunk + 2, tokens_kept[-1])
            send(chunk, partial[-1], own[chunk + 2][0], far[chunk - num_early])
        elif chunk + 1 < total:
            send(chunk, partial[-1])
        else:
            send(chunk, partial[-1], tokens_kept[-2], far[chunk - num_early - 1])
        out = add_call(out, far[chunk - num_early], firsts[chunk - num_early])
        out, token = keep(chunk, out, partial[-1])
        tokens_kept.append(token)
    for chunk in range(total - num_early, total):
        out = add_call(out, far[chunk], firsts[chunk])
    return out, moment, scaled


def solution(mesh):
    return jax.shard_map(
        functools.partial(local, mesh.shape["fsdp"], mesh.shape["tensor"]),
        mesh=mesh,
        in_specs=(
            P("fsdp", None),
            P("fsdp", "tensor"),
            P("fsdp", "tensor"),
            P("fsdp", "tensor"),
            P(None, "tensor"),
        ),
        out_specs=(P("fsdp", "tensor"), P("fsdp", "tensor"), P()),
        check_vma=False,
    )
```

```python
import functools

import jax
import jax.numpy as jnp
from jax import lax
from jax.experimental import pallas as pl
from jax.experimental.pallas import tpu as pltpu
from jax.sharding import PartitionSpec as P

DECAY = 0.9
SQUARINGS = 5
LANES = 128
UNIT = 256
EARLY = (2,)
LATE = (2, 2, 1, 1)
PARTS = 2

HIGHEST = lax.Precision.HIGHEST
LARGE = pltpu.CompilerParams(vmem_limit_bytes=53 * 1024 * 1024)
PARAMS = pltpu.CompilerParams(vmem_limit_bytes=24 * 1024 * 1024)
BRIEF = pl.CostEstimate(flops=0, bytes_accessed=0, transcendentals=0)
VMEM = pl.BlockSpec(memory_space=pltpu.VMEM)
ANY = pl.BlockSpec(memory_space=pl.ANY)


def fdot(left, right):
    return lax.dot_general(
        left, right, (((1,), (0,)), ((), ())), precision=HIGHEST, preferred_element_type=jnp.float32
    )


def fdot_t(left, right):
    return lax.dot_general(
        left, right, (((1,), (1,)), ((), ())), precision=HIGHEST, preferred_element_type=jnp.float32
    )


def halves(values):
    high = values.astype(jnp.bfloat16)
    return high, (values - high.astype(jnp.float32)).astype(jnp.bfloat16)


def split_dot(stacked, mat, contract):
    rows = stacked.shape[0] // 2
    mat_high, mat_low = halves(mat)
    dims = (((1,), (contract,)), ((), ()))
    first = lax.dot_general(stacked, mat_high, dims, preferred_element_type=jnp.float32)
    second = lax.dot_general(stacked[:rows], mat_low, dims, preferred_element_type=jnp.float32)
    return first[:rows] + first[rows:] + second


def eliminate(gram, count):
    rows = lax.broadcasted_iota(jnp.int32, (count, LANES), 0)
    lanes = lax.broadcasted_iota(jnp.int32, (count, LANES), 1)
    aug = jnp.where(lanes < count, gram, jnp.where(lanes - count == rows, 1.0, 0.0))
    for step in range(count):
        pivot = aug[step : step + 1, step : step + 1]
        factor = jnp.where(rows > step, aug[:, step : step + 1] * (1.0 / pivot), 0.0)
        aug = aug - factor * aug[step : step + 1, :]
    pivots = jnp.sum(jnp.where(lanes == rows, aug, 0.0), axis=1, keepdims=True)
    aug = aug * (1.0 / jnp.sqrt(pivots))
    low_t = jnp.where((lanes >= rows) & (lanes < count), aug, 0.0)
    return low_t, aug[:, count : 2 * count]


def pad_lanes(square):
    return jnp.concatenate(
        [square, jnp.zeros((square.shape[0], LANES - square.shape[1]), jnp.float32)], axis=1
    )


def pick_kernel(order_ref, token_0, token_1, weight_ref, sent_0, sent_1, early_ref):
    sent_0[...] = token_0[...]
    sent_1[...] = token_1[...]
    early_ref[...] = weight_ref[...]


def pick_call(order, tokens, weight, rows, count, early_cols):
    depth = weight.shape[0]
    height = depth // count
    sent = jax.ShapeDtypeStruct((rows, count * depth), tokens.dtype)
    weight_spec = pl.BlockSpec((height, early_cols), lambda i, order_ref: (i, 0))
    sent_spec = pl.BlockSpec((rows, depth), lambda i, order_ref: (0, i))
    return pl.pallas_call(
        pick_kernel,
        grid_spec=pltpu.PrefetchScalarGridSpec(
            num_scalar_prefetch=1,
            grid=(count,),
            in_specs=[
                pl.BlockSpec((rows, depth), lambda i, order_ref: (order_ref[0], order_ref[1 + i])),
                pl.BlockSpec((rows, depth), lambda i, order_ref: (order_ref[0] + 1, order_ref[1 + i])),
                weight_spec,
            ],
            out_specs=[sent_spec, sent_spec, weight_spec],
        ),
        out_shape=[sent, sent, jax.ShapeDtypeStruct((depth, early_cols), weight.dtype)],
        compiler_params=LARGE,
    )(order, tokens, tokens, weight)


def start_kernel(width, mom_ref, grad_ref, probes_ref, tie_ref, moment_ref, short_ref, pack_ref, stack_ref):
    at = pl.program_id(0)
    count = probes_ref.shape[0]
    height = mom_ref.shape[0]

    @pl.when(at == 0)
    def _():
        probes = probes_ref[...]
        high, low = halves(probes)
        stack_ref[:count] = high
        stack_ref[count:] = low
        pack_ref[:, width:] = pad_lanes(fdot_t(probes, probes))

    moment = DECAY * mom_ref[...] + grad_ref[...].astype(jnp.float32)
    moment_ref[...] = moment
    short_ref[...] = moment[:, : short_ref.shape[1]].astype(jnp.bfloat16)
    pack_ref[:, pl.ds(pl.multiple_of(at * height, height), height)] = split_dot(stack_ref[...], moment, 1)


def start_call(momentum, gradient, probes, tie, early_cols):
    depth, cols = momentum.shape
    count = probes.shape[0]
    height = min(256, depth)
    rows = pl.BlockSpec((height, cols), lambda i: (i, 0))
    return pl.pallas_call(
        functools.partial(start_kernel, depth),
        grid=(depth // height,),
        in_specs=[rows, rows, VMEM, ANY],
        out_specs=[rows, pl.BlockSpec((height, early_cols), lambda i: (i, 0)), VMEM],
        out_shape=[
            jax.ShapeDtypeStruct((depth, cols), jnp.float32),
            jax.ShapeDtypeStruct((depth, early_cols), jnp.bfloat16),
            jax.ShapeDtypeStruct((count, depth + LANES), jnp.float32),
        ],
        scratch_shapes=[pltpu.VMEM((2 * count, cols), jnp.bfloat16)],
        compiler_params=LARGE,
    )(momentum, gradient, probes, tie)


def gate_kernel(passed, own_ref, recv_ref, *refs):
    sum_ref = refs[-1 - passed]
    sum_ref[...] = own_ref[...] + recv_ref[...]


def gate_call(own, recv, gates=(), ties=()):
    shapes = [jax.ShapeDtypeStruct(at.shape, at.dtype) for at in (own, *gates)]
    first = 2 + len(ties)
    return pl.pallas_call(
        functools.partial(gate_kernel, len(gates)),
        in_specs=[VMEM, VMEM] + [ANY] * (len(gates) + len(ties)),
        out_specs=[VMEM] + [ANY] * len(gates),
        out_shape=shapes,
        input_output_aliases={first + i: 1 + i for i in range(len(gates))},
        compiler_params=PARAMS,
    )(own, recv, *ties, *gates)


def pass_kernel(*refs):
    pass


def pass_call(values, ties):
    return pl.pallas_call(
        pass_kernel,
        in_specs=[ANY] * (len(values) + len(ties)),
        out_specs=[ANY] * len(values),
        out_shape=[jax.ShapeDtypeStruct(at.shape, at.dtype) for at in values],
        input_output_aliases={i: i for i in range(len(values))},
        compiler_params=LARGE,
        cost_estimate=BRIEF,
    )(*values, *ties)


def images_blocked(own_ref, recv_ref, block_ref, moment_ref, *refs):
    pack_ref, basis_ref, low_ref, stack_ref = refs[-4:]
    at = pl.program_id(0)
    count, cols = block_ref.shape
    depth = moment_ref.shape[0]
    width = moment_ref.shape[1]

    @pl.when(at == 0)
    def _():
        low_t, inverse = eliminate(own_ref[:, depth:] + recv_ref[:, depth:], count)
        low_ref[...] = low_t
        reduced = fdot(inverse, own_ref[:, :depth] + recv_ref[:, :depth])
        high, low = halves(reduced)
        stack_ref[:count] = high
        stack_ref[count:] = low
        pack_ref[:, cols:] = pad_lanes(fdot_t(reduced, reduced))
        basis_ref[...] = fdot(inverse, block_ref[...])

    pack_ref[:, pl.ds(pl.multiple_of(at * width, width), width)] = split_dot(stack_ref[...], moment_ref[...], 0)


def images_kernel(
    own_ref, recv_ref, block_ref, moment_ref, pack_ref, basis_ref, low_ref, held_ref, stack_ref, sems
):
    count, cols = block_ref.shape
    blocks, depth, width = held_ref.shape
    copies = [
        pltpu.make_async_copy(
            moment_ref.at[:, at * width : (at + 1) * width], held_ref.at[at], sems.at[at]
        )
        for at in range(blocks)
    ]
    for copy in copies:
        copy.start()
    low_t, inverse = eliminate(own_ref[:, depth:] + recv_ref[:, depth:], count)
    low_ref[...] = low_t
    reduced = fdot(inverse, own_ref[:, :depth] + recv_ref[:, :depth])
    high, low = halves(reduced)
    stack_ref[:count] = high
    stack_ref[count:] = low
    pack_ref[:, cols:] = pad_lanes(fdot_t(reduced, reduced))
    basis_ref[...] = fdot(inverse, block_ref[...])
    for at, copy in enumerate(copies):
        copy.wait()
        pack_ref[:, at * width : (at + 1) * width] = split_dot(stack_ref[...], held_ref[at], 0)


def images_call(own, recv, block, moment, fetch, ties=()):
    depth, cols = moment.shape
    count = block.shape[0]
    width = min(512, cols)
    stack = pltpu.VMEM((2 * count, depth), jnp.bfloat16)
    held = [
        pltpu.VMEM((cols // width, depth, width), jnp.float32),
        stack,
        pltpu.SemaphoreType.DMA((cols // width,)),
    ]
    return pl.pallas_call(
        images_kernel if fetch else images_blocked,
        grid=(1 if fetch else cols // width,),
        in_specs=[VMEM, VMEM, VMEM, ANY if fetch else pl.BlockSpec((depth, width), lambda i: (0, i))]
        + [ANY] * len(ties),
        out_specs=[VMEM, VMEM, VMEM],
        out_shape=[
            jax.ShapeDtypeStruct((count, cols + LANES), jnp.float32),
            jax.ShapeDtypeStruct((count, cols), jnp.float32),
            jax.ShapeDtypeStruct((count, LANES), jnp.float32),
        ],
        scratch_shapes=held if fetch else [stack],
        compiler_params=LARGE if fetch else PARAMS,
    )(own, recv, block, moment, *ties)


def reduced_kernel(has_prev, emit, passed, width, *refs):
    names = 5 if has_prev else 3
    own_ref, recv_ref, basis_ref = refs[:3]
    prev_ref, low_ref = refs[3:5] if has_prev else (None, None)
    moment_ref = refs[names]
    outs = refs[names + 1 + passed :]
    pack_ref, residue_ref, diag_ref = outs[:3]
    stack_ref = refs[-1]
    at = pl.program_id(0)
    count, cols = basis_ref.shape
    height = moment_ref.shape[0]

    @pl.when(at == 0)
    def _():
        diag = (own_ref[:, cols:] + recv_ref[:, cols:])[:, :count]
        diag = 0.5 * (diag + diag.T)
        diag_ref[...] = pad_lanes(diag)
        residue = own_ref[:, :cols] + recv_ref[:, :cols] - fdot(diag, basis_ref[...])
        if has_prev:
            residue = residue - fdot(low_ref[:, :count], prev_ref[...])
        residue_ref[...] = residue
        high, low = halves(residue)
        stack_ref[:count] = high
        stack_ref[count:] = low
        pack_ref[:, width:] = pad_lanes(fdot_t(residue, residue))

    moment = moment_ref[...]
    if emit:
        short_ref = outs[3]
        short_ref[...] = moment[:, : short_ref.shape[1]].astype(jnp.bfloat16)
    pack_ref[:, pl.ds(pl.multiple_of(at * height, height), height)] = split_dot(stack_ref[...], moment, 1)


def reduced_call(own, recv, basis, prev, low, moment, gates, early_cols):
    depth, cols = moment.shape
    count = basis.shape[0]
    height = min(256, depth)
    has_prev = prev is not None
    operands = (own, recv, basis) + ((prev, low) if has_prev else ()) + (moment,)
    out_specs = [VMEM, VMEM, VMEM]
    out_shape = [
        jax.ShapeDtypeStruct((count, depth + LANES), jnp.float32),
        jax.ShapeDtypeStruct((count, cols), jnp.float32),
        jax.ShapeDtypeStruct((count, LANES), jnp.float32),
    ]
    if early_cols:
        out_specs.append(pl.BlockSpec((height, early_cols), lambda i: (i, 0)))
        out_shape.append(jax.ShapeDtypeStruct((depth, early_cols), jnp.bfloat16))
    first = len(out_specs)
    out_specs += [ANY] * len(gates)
    out_shape += [jax.ShapeDtypeStruct(at.shape, at.dtype) for at in gates]
    return pl.pallas_call(
        functools.partial(reduced_kernel, has_prev, bool(early_cols), len(gates), depth),
        grid=(depth // height,),
        in_specs=[VMEM] * (len(operands) - 1)
        + [pl.BlockSpec((height, cols), lambda i: (i, 0))]
        + [ANY] * len(gates),
        out_specs=out_specs,
        out_shape=out_shape,
        input_output_aliases={len(operands) + i: first + i for i in range(len(gates))},
        scratch_shapes=[pltpu.VMEM((2 * count, cols), jnp.bfloat16)],
        compiler_params=PARAMS,
    )(*operands, *gates)


def last_kernel(passed, own_ref, recv_ref, *refs):
    diag_ref, low_ref = refs[passed : passed + 2]
    count = own_ref.shape[0]
    depth = own_ref.shape[1] - LANES
    low_t, inverse = eliminate(own_ref[:, depth:] + recv_ref[:, depth:], count)
    low_ref[...] = low_t
    reduced = fdot(inverse, own_ref[:, :depth] + recv_ref[:, :depth])
    diag_ref[...] = pad_lanes(fdot_t(reduced, reduced))


def last_call(own, recv, gates, ties):
    shape = jax.ShapeDtypeStruct((own.shape[0], LANES), jnp.float32)
    return pl.pallas_call(
        functools.partial(last_kernel, len(gates) + len(ties)),
        in_specs=[VMEM, VMEM] + [ANY] * (len(gates) + len(ties)),
        out_specs=[VMEM, VMEM] + [ANY] * len(gates),
        out_shape=[shape, shape] + [jax.ShapeDtypeStruct(at.shape, at.dtype) for at in gates],
        input_output_aliases={2 + i: 2 + i for i in range(len(gates))},
        compiler_params=PARAMS,
    )(own, recv, *gates, *ties)


def top_kernel(steps, *refs):
    diag_refs = refs[: steps + 1]
    low_refs = refs[steps + 1 : 2 * steps]
    scaled_ref, rate_ref, krylov_ref = refs[-3:]
    count = diag_refs[0].shape[0]
    size = steps * count
    krylov_ref[...] = jnp.zeros_like(krylov_ref)
    for place in range(steps):
        first = place * count
        diag = diag_refs[place][:, :count]
        if place + 1 == steps:
            diag = diag + diag_refs[steps][:, :count]
        krylov_ref[first : first + count, first : first + count] = 0.5 * (diag + diag.T)
        if place + 1 < steps:
            second = first + count
            low_t = low_refs[place][:, :count]
            krylov_ref[second : second + count, first:second] = low_t
            krylov_ref[first:second, second : second + count] = low_t.T
    krylov = krylov_ref[...]
    power = krylov * (1.0 / jnp.max(jnp.abs(krylov), keepdims=True))
    for _ in range(SQUARINGS):
        power = fdot(power, power)
        power = power * (1.0 / jnp.max(jnp.abs(power), keepdims=True))
    tall = jnp.sum(power, axis=1, keepdims=True)
    wide = jnp.sum(power, axis=0, keepdims=True)
    tall = tall * (1.0 / jnp.sqrt(jnp.sum(tall * tall, keepdims=True)))
    wide = wide * (1.0 / jnp.sqrt(jnp.sum(wide * wide, keepdims=True)))
    top = jnp.sum(krylov * tall * wide, keepdims=True)
    scaled_ref[...] = krylov[:size, :size] / top
    rate_ref[...] = jnp.broadcast_to(1.0 / jnp.sqrt(top), rate_ref.shape)


def top_call(diags, lows, ties):
    steps = len(lows) + 1
    count = diags[0].shape[0]
    size = steps * count
    padded = -(-size // LANES) * LANES
    return pl.pallas_call(
        functools.partial(top_kernel, steps),
        in_specs=[VMEM] * (2 * steps) + [ANY] * len(ties),
        out_specs=[VMEM, VMEM],
        out_shape=[
            jax.ShapeDtypeStruct((size, size), jnp.float32),
            jax.ShapeDtypeStruct((8, LANES), jnp.float32),
        ],
        scratch_shapes=[pltpu.VMEM((padded, padded), jnp.float32)],
        compiler_params=PARAMS,
    )(*diags, *lows, *ties)


def step_kernel(weight_ref, moment_ref, rate_ref, tie_ref, *out_refs):
    stepped = weight_ref[...].astype(jnp.float32) - moment_ref[...] * rate_ref[:1, :1]
    width = out_refs[0].shape[1]
    for i, out_ref in enumerate(out_refs):
        out_ref[...] = stepped[:, i * width : (i + 1) * width].astype(jnp.bfloat16)


def step_call(weight, moment, rate, first, width, tie):
    depth = weight.shape[0]
    height = min(512, depth)
    block = pl.BlockSpec((height, width), lambda r: (r, first // width))
    return pl.pallas_call(
        step_kernel,
        grid=(depth // height,),
        in_specs=[block, block, VMEM, ANY],
        out_specs=[pl.BlockSpec((height, UNIT), lambda r: (r, 0))] * (width // UNIT),
        out_shape=[jax.ShapeDtypeStruct((depth, UNIT), jnp.bfloat16)] * (width // UNIT),
        compiler_params=LARGE,
        cost_estimate=BRIEF,
    )(weight, moment, rate, tie)


def project_kernel(far, pieces, count, split, early, in_place, ties, first, order_ref, *refs):
    tokens = refs[:pieces]
    refs = refs[pieces:]
    weights, refs = refs[: split * count], refs[split * count :]
    if early:
        moments, rate_ref, refs = refs[:count], refs[count], refs[count + 1 :]
    refs = refs[ties + (1 if in_place else 0) :]
    if not far:
        refs[1][...] = jnp.zeros(refs[1].shape, jnp.float32)
        refs = refs[:1] + refs[2:]
    out_ref, tokens_buf, weight_buf, moment_buf, total_ref, result_ref, sems, out_sem = refs
    depth, width = weight_buf.shape[1:]
    copies = []
    for k in range(count):
        step = []
        for i in range(pieces):
            if far:
                rows = tokens[i].shape[0]
                source = tokens[i].at[:, k * depth : (k + 1) * depth]
                target = tokens_buf.at[k, pl.ds(pl.multiple_of(order_ref[i], 16), rows), :]
            else:
                source = tokens[i].at[:, pl.ds(pl.multiple_of(order_ref[k] * depth, LANES), depth)]
                target = tokens_buf.at[k]
            step.append(pltpu.make_async_copy(source, target, sems.at[k, i]))
        if early:
            at = slice(first, first + width)
            step.append(pltpu.make_async_copy(weights[k].at[:, at], weight_buf.at[k], sems.at[k, pieces]))
            step.append(
                pltpu.make_async_copy(moments[k].at[:, at], moment_buf.at[k], sems.at[k, pieces + 1])
            )
        else:
            for i in range(split):
                target = weight_buf.at[k, :, i * UNIT : (i + 1) * UNIT]
                step.append(
                    pltpu.make_async_copy(weights[k * split + i], target, sems.at[k, pieces + i])
                )
        for copy in step:
            copy.start()
        copies.append(step)
    for k in range(count):
        for copy in copies[k]:
            copy.wait()
        block = weight_buf[k]
        if early:
            stepped = block.astype(jnp.float32) - moment_buf[k].astype(jnp.float32) * rate_ref[:1, :1]
            block = stepped.astype(jnp.bfloat16)
        part = jnp.dot(tokens_buf[k], block, preferred_element_type=jnp.float32)
        total_ref[...] = part if k == 0 else total_ref[...] + part
    if far:
        result_ref[...] = total_ref[...].astype(result_ref.dtype)
        copy = pltpu.make_async_copy(result_ref, out_ref, out_sem)
    else:
        copy = pltpu.make_async_copy(total_ref, out_ref.at[:, first : first + width], out_sem)
    copy.start()
    copy.wait()


def project_call(far, order, tokens, first, width, weights, moments, rate, ties=(), out=None, cols=None):
    early = moments is not None
    split = 1 if early else width // UNIT
    count = len(weights) // split
    depth = weights[0].shape[0]
    num_rows = sum(at.shape[0] for at in tokens)
    operands = list(tokens) + list(weights)
    specs = [ANY] * len(operands)
    if early:
        operands += list(moments) + [rate]
        specs += [ANY] * count + [VMEM]
    operands += list(ties)
    specs += [ANY] * len(ties)
    aliases = {}
    if far:
        out_shape = jax.ShapeDtypeStruct((num_rows, width), jnp.bfloat16)
    else:
        out_shape = [
            jax.ShapeDtypeStruct((num_rows, cols), jnp.float32),
            jax.ShapeDtypeStruct((8, LANES), jnp.float32),
        ]
        if out is not None:
            operands.append(out)
            specs.append(ANY)
            aliases = {len(operands): 0}
    return pl.pallas_call(
        functools.partial(
            project_kernel, far, len(tokens), count, split, early, bool(aliases), len(ties), first
        ),
        grid_spec=pltpu.PrefetchScalarGridSpec(
            num_scalar_prefetch=1,
            grid=(1,),
            in_specs=specs,
            out_specs=ANY if far else [ANY, VMEM],
            scratch_shapes=[
                pltpu.VMEM((count, num_rows, depth), jnp.bfloat16),
                pltpu.VMEM((count, depth, width), jnp.bfloat16),
                pltpu.VMEM((count, depth, width) if early else (8, LANES), jnp.bfloat16),
                pltpu.VMEM((num_rows, width), jnp.float32),
                pltpu.VMEM((num_rows, width) if far else (8, LANES), jnp.bfloat16),
                pltpu.SemaphoreType.DMA((count, len(tokens) + max(2, split))),
                pltpu.SemaphoreType.DMA,
            ],
        ),
        out_shape=out_shape,
        input_output_aliases=aliases,
        compiler_params=LARGE,
        cost_estimate=BRIEF,
    )(order, *operands)


def add_kernel(old_ref, far_ref, out_ref):
    out_ref[...] = old_ref[...] + far_ref[...].astype(jnp.float32)


def add_call(out, far, first):
    num_rows, width = far.shape
    block = pl.BlockSpec((num_rows, UNIT), lambda c: (0, first // UNIT + c))
    return pl.pallas_call(
        add_kernel,
        grid=(width // UNIT,),
        in_specs=[block, pl.BlockSpec((num_rows, UNIT), lambda c: (0, c))],
        out_specs=block,
        out_shape=jax.ShapeDtypeStruct(out.shape, out.dtype),
        input_output_aliases={0: 0},
        compiler_params=LARGE,
        cost_estimate=BRIEF,
    )(out, far)


def swap(values, axis, size, bit):
    return lax.ppermute(values, axis, [(at, at ^ bit) for at in range(size)])


def butterfly(values, axis, size):
    bit = 1
    while 2 * bit < size:
        values = values + swap(values, axis, size, bit)
        bit *= 2
    return values, swap(values, axis, size, bit)


def offsets(count):
    found = [0]
    bit = count // 2
    while bit:
        found = found + [at ^ bit for at in found]
        bit //= 2
    return found


def spread(piece, axis, size):
    parts = [piece]
    bit = 1
    while bit < size:
        parts = parts + [swap(part, axis, size, bit) for part in parts]
        bit *= 2
    return parts


def local(rows_n, cols_n, tokens, weight, momentum, gradient, probes):
    half = rows_n // 2
    far_bit, near_bit = half // 2, half // 4
    place = lax.axis_index("fsdp")
    low_at = lax.rem(place, half)
    side = lax.div(place, half)
    column_at = lax.axis_index("tensor")
    num_rows = tokens.shape[0]
    depth, cols = weight.shape
    rows = num_rows // cols_n // PARTS
    unit = cols // (sum(EARLY) + sum(LATE))
    early_cols = sum(EARLY) * unit

    def fswap(values, bit):
        return swap(values, "fsdp", rows_n, bit)

    def complete(own, across, beside):
        parts = [own, across, beside, fswap(across, near_bit)]
        bit = near_bit // 2
        while bit:
            parts = parts + [fswap(part, bit) for part in parts]
            bit //= 2
        return parts

    def sum_over_rows(pack, gates, ties):
        passed = {}
        bit = 1
        while bit < half:
            pack, *passed[bit] = gate_call(pack, fswap(pack, bit), gates.get(bit, ()), ties.get(bit, ()))
            bit *= 2
        return pack, fswap(pack, half), passed

    mixed = jnp.stack([low_at ^ at for at in offsets(half)]).astype(jnp.int32)
    near_order = side * half + mixed
    pick_order = jnp.concatenate([(column_at * PARTS)[None], (1 - side) * half + mixed])
    far_order = jnp.stack(
        [(column_at ^ i) * PARTS * rows + part * rows for part in range(PARTS) for i in range(cols_n)]
    ).astype(jnp.int32)

    sent_0, sent_1, weight_own = pick_call(pick_order, tokens, weight, rows, half, early_cols)
    moment, short_1, pack = start_call(momentum, gradient, probes, sent_0, early_cols)
    weight_beside = fswap(weight_own, near_bit)
    weight_across = fswap(weight_own, far_bit)
    tokens_0 = fswap(sent_0, half)

    own, recv = butterfly(pack, "tensor", cols_n)
    pack, basis_1, _ = images_call(own, recv, probes, moment, True)
    own, recv, passed = sum_over_rows(
        pack, {1: [short_1, tokens_0], 2: [weight_across]}, {2: [weight_beside]}
    )
    short_1, tokens_0 = passed[1]
    weight_across, = passed[2]
    weight_parts = complete(weight_own, weight_across, weight_beside)
    moment_beside = fswap(short_1, near_bit)
    token_parts = spread(tokens_0, "tensor", cols_n)
    pack, residue, diag_1, short_2, sent_1 = reduced_call(
        own, recv, basis_1, None, None, moment, [sent_1], early_cols
    )
    moment_across = fswap(short_2, far_bit)
    tokens_1 = fswap(sent_1, half)

    own, recv = butterfly(pack, "tensor", cols_n)
    pack, basis_2, low_1 = images_call(
        own, recv, residue, moment, False, [weight_parts[3], moment_beside]
    )
    own, recv, passed = sum_over_rows(pack, {1: [moment_across]}, {2: token_parts[1:]})
    moment_parts = complete(short_1, passed[1][0], moment_beside)
    pack, _, diag_2, token_1 = reduced_call(own, recv, basis_2, basis_1, low_1, moment, [tokens_1], 0)
    token_1_beside = swap(token_1, "tensor", cols_n, 1)
    token_1_across = swap(token_1, "tensor", cols_n, 2)

    own, recv = butterfly(pack, "tensor", cols_n)
    diag_3, low_2, token_1_beside = last_call(
        own, recv, [token_1_beside], [token_1_across, moment_parts[3]]
    )
    token_parts += [token_1, token_1_beside, token_1_across, swap(token_1_beside, "tensor", cols_n, 2)]
    own, recv = butterfly(diag_3, "fsdp", rows_n)
    scaled, rate = top_call(
        [diag_1, diag_2, own, recv], [low_1, low_2], token_parts[-1:]
    )

    firsts, widths = [0], []
    for size in EARLY + LATE:
        widths.append(size * unit)
        firsts.append(firsts[-1] + size * unit)
    num_early = len(EARLY)
    gathered = [(weight_parts, moment_parts, rate)] * num_early
    out, partial, far = None, [], []

    def send(chunk, *ties):
        partial.append(
            project_call(
                True, far_order, token_parts, firsts[chunk], widths[chunk], *gathered[chunk], ties=ties
            )
        )
        far.append(fswap(partial[-1], half))

    def keep(chunk, out, tie):
        return project_call(
            False,
            near_order,
            [tokens],
            firsts[chunk],
            widths[chunk],
            *gathered[chunk],
            ties=[tie],
            out=out,
            cols=cols,
        )

    total = len(widths)
    own, across, beside = {}, {}, {}

    def step(chunk, tie):
        own[chunk] = step_call(weight, moment, rate, firsts[chunk], widths[chunk], tie)
        across[chunk] = [fswap(at, far_bit) for at in own[chunk]]
        beside[chunk] = [fswap(at, near_bit) for at in own[chunk]]

    step(num_early, rate)
    send(0, own[num_early][0])
    for chunk in range(1, num_early):
        send(chunk, partial[-1])
    tokens_kept = []
    for chunk in range(num_early):
        out, token = keep(chunk, out, partial[-1] if chunk == 0 else token)
        tokens_kept.append(token)
    for chunk in range(num_early, total):
        ahead = across[chunk + 1] if chunk == total - 2 else []
        passed = pass_call(across[chunk], [partial[-1], *beside[chunk], *ahead])
        pieces = [complete(*at) for at in zip(own[chunk], passed, beside[chunk])]
        gathered.append(([piece[k] for k in range(half) for piece in pieces], None, None))
        if chunk == num_early and chunk + 1 < total:
            step(chunk + 1, passed[0])
        if chunk + 2 < total:
            step(chunk + 2, tokens_kept[-1])
            send(chunk, partial[-1], own[chunk + 2][0], far[chunk - num_early])
        elif chunk + 1 < total:
            send(chunk, partial[-1])
        else:
            send(chunk, partial[-1], tokens_kept[-2], far[chunk - num_early - 1])
        out = add_call(out, far[chunk - num_early], firsts[chunk - num_early])
        out, token = keep(chunk, out, partial[-1])
        tokens_kept.append(token)
    for chunk in range(total - num_early, total):
        out = add_call(out, far[chunk], firsts[chunk])
    return out, moment, scaled


def solution(mesh):
    return jax.shard_map(
        functools.partial(local, mesh.shape["fsdp"], mesh.shape["tensor"]),
        mesh=mesh,
        in_specs=(
            P("fsdp", None),
            P("fsdp", "tensor"),
            P("fsdp", "tensor"),
            P("fsdp", "tensor"),
            P(None, "tensor"),
        ),
        out_specs=(P("fsdp", "tensor"), P("fsdp", "tensor"), P()),
        check_vma=False,
    )
```

```python
import functools

import jax
import jax.numpy as jnp
from jax import lax
from jax.experimental import pallas as pl
from jax.experimental.pallas import tpu as pltpu
from jax.sharding import PartitionSpec as P

DECAY = 0.9
SQUARINGS = 5
LANES = 128
UNIT = 256
EARLY = (2,)
LATE = (2, 2, 2)
PARTS = 2

HIGHEST = lax.Precision.HIGHEST
LARGE = pltpu.CompilerParams(vmem_limit_bytes=53 * 1024 * 1024)
PARAMS = pltpu.CompilerParams(vmem_limit_bytes=24 * 1024 * 1024)
BRIEF = pl.CostEstimate(flops=0, bytes_accessed=0, transcendentals=0)
VMEM = pl.BlockSpec(memory_space=pltpu.VMEM)
ANY = pl.BlockSpec(memory_space=pl.ANY)


def fdot(left, right):
    return lax.dot_general(
        left, right, (((1,), (0,)), ((), ())), precision=HIGHEST, preferred_element_type=jnp.float32
    )


def fdot_t(left, right):
    return lax.dot_general(
        left, right, (((1,), (1,)), ((), ())), precision=HIGHEST, preferred_element_type=jnp.float32
    )


def halves(values):
    high = values.astype(jnp.bfloat16)
    return high, (values - high.astype(jnp.float32)).astype(jnp.bfloat16)


def split_dot(stacked, mat, contract):
    rows = stacked.shape[0] // 2
    mat_high, mat_low = halves(mat)
    dims = (((1,), (contract,)), ((), ()))
    first = lax.dot_general(stacked, mat_high, dims, preferred_element_type=jnp.float32)
    second = lax.dot_general(stacked[:rows], mat_low, dims, preferred_element_type=jnp.float32)
    return first[:rows] + first[rows:] + second


def eliminate(gram, count):
    rows = lax.broadcasted_iota(jnp.int32, (count, LANES), 0)
    lanes = lax.broadcasted_iota(jnp.int32, (count, LANES), 1)
    aug = jnp.where(lanes < count, gram, jnp.where(lanes - count == rows, 1.0, 0.0))
    for step in range(count):
        pivot = aug[step : step + 1, step : step + 1]
        factor = jnp.where(rows > step, aug[:, step : step + 1] * (1.0 / pivot), 0.0)
        aug = aug - factor * aug[step : step + 1, :]
    pivots = jnp.sum(jnp.where(lanes == rows, aug, 0.0), axis=1, keepdims=True)
    aug = aug * (1.0 / jnp.sqrt(pivots))
    low_t = jnp.where((lanes >= rows) & (lanes < count), aug, 0.0)
    return low_t, aug[:, count : 2 * count]


def pad_lanes(square):
    return jnp.concatenate(
        [square, jnp.zeros((square.shape[0], LANES - square.shape[1]), jnp.float32)], axis=1
    )


def pick_kernel(order_ref, token_0, token_1, weight_ref, sent_0, sent_1, early_ref):
    sent_0[...] = token_0[...]
    sent_1[...] = token_1[...]
    early_ref[...] = weight_ref[...]


def pick_call(order, tokens, weight, rows, count, early_cols):
    depth = weight.shape[0]
    height = depth // count
    sent = jax.ShapeDtypeStruct((rows, count * depth), tokens.dtype)
    weight_spec = pl.BlockSpec((height, early_cols), lambda i, order_ref: (i, 0))
    sent_spec = pl.BlockSpec((rows, depth), lambda i, order_ref: (0, i))
    return pl.pallas_call(
        pick_kernel,
        grid_spec=pltpu.PrefetchScalarGridSpec(
            num_scalar_prefetch=1,
            grid=(count,),
            in_specs=[
                pl.BlockSpec((rows, depth), lambda i, order_ref: (order_ref[0], order_ref[1 + i])),
                pl.BlockSpec((rows, depth), lambda i, order_ref: (order_ref[0] + 1, order_ref[1 + i])),
                weight_spec,
            ],
            out_specs=[sent_spec, sent_spec, weight_spec],
        ),
        out_shape=[sent, sent, jax.ShapeDtypeStruct((depth, early_cols), weight.dtype)],
        compiler_params=LARGE,
    )(order, tokens, tokens, weight)


def start_kernel(width, mom_ref, grad_ref, probes_ref, tie_ref, moment_ref, short_ref, pack_ref, stack_ref):
    at = pl.program_id(0)
    count = probes_ref.shape[0]
    height = mom_ref.shape[0]

    @pl.when(at == 0)
    def _():
        probes = probes_ref[...]
        high, low = halves(probes)
        stack_ref[:count] = high
        stack_ref[count:] = low
        pack_ref[:, width:] = pad_lanes(fdot_t(probes, probes))

    moment = DECAY * mom_ref[...] + grad_ref[...].astype(jnp.float32)
    moment_ref[...] = moment
    short_ref[...] = moment[:, : short_ref.shape[1]].astype(jnp.bfloat16)
    pack_ref[:, pl.ds(pl.multiple_of(at * height, height), height)] = split_dot(stack_ref[...], moment, 1)


def start_call(momentum, gradient, probes, tie, early_cols):
    depth, cols = momentum.shape
    count = probes.shape[0]
    height = min(256, depth)
    rows = pl.BlockSpec((height, cols), lambda i: (i, 0))
    return pl.pallas_call(
        functools.partial(start_kernel, depth),
        grid=(depth // height,),
        in_specs=[rows, rows, VMEM, ANY],
        out_specs=[rows, pl.BlockSpec((height, early_cols), lambda i: (i, 0)), VMEM],
        out_shape=[
            jax.ShapeDtypeStruct((depth, cols), jnp.float32),
            jax.ShapeDtypeStruct((depth, early_cols), jnp.bfloat16),
            jax.ShapeDtypeStruct((count, depth + LANES), jnp.float32),
        ],
        scratch_shapes=[pltpu.VMEM((2 * count, cols), jnp.bfloat16)],
        compiler_params=LARGE,
    )(momentum, gradient, probes, tie)


def gate_kernel(passed, own_ref, recv_ref, *refs):
    sum_ref = refs[-1 - passed]
    sum_ref[...] = own_ref[...] + recv_ref[...]


def gate_call(own, recv, gates=(), ties=()):
    shapes = [jax.ShapeDtypeStruct(at.shape, at.dtype) for at in (own, *gates)]
    first = 2 + len(ties)
    return pl.pallas_call(
        functools.partial(gate_kernel, len(gates)),
        in_specs=[VMEM, VMEM] + [ANY] * (len(gates) + len(ties)),
        out_specs=[VMEM] + [ANY] * len(gates),
        out_shape=shapes,
        input_output_aliases={first + i: 1 + i for i in range(len(gates))},
        compiler_params=PARAMS,
    )(own, recv, *ties, *gates)


def pass_kernel(*refs):
    pass


def pass_call(values, ties):
    return pl.pallas_call(
        pass_kernel,
        in_specs=[ANY] * (len(values) + len(ties)),
        out_specs=[ANY] * len(values),
        out_shape=[jax.ShapeDtypeStruct(at.shape, at.dtype) for at in values],
        input_output_aliases={i: i for i in range(len(values))},
        compiler_params=LARGE,
        cost_estimate=BRIEF,
    )(*values, *ties)


def images_blocked(own_ref, recv_ref, block_ref, moment_ref, *refs):
    pack_ref, basis_ref, low_ref, stack_ref = refs[-4:]
    at = pl.program_id(0)
    count, cols = block_ref.shape
    depth = moment_ref.shape[0]
    width = moment_ref.shape[1]

    @pl.when(at == 0)
    def _():
        low_t, inverse = eliminate(own_ref[:, depth:] + recv_ref[:, depth:], count)
        low_ref[...] = low_t
        reduced = fdot(inverse, own_ref[:, :depth] + recv_ref[:, :depth])
        high, low = halves(reduced)
        stack_ref[:count] = high
        stack_ref[count:] = low
        pack_ref[:, cols:] = pad_lanes(fdot_t(reduced, reduced))
        basis_ref[...] = fdot(inverse, block_ref[...])

    pack_ref[:, pl.ds(pl.multiple_of(at * width, width), width)] = split_dot(stack_ref[...], moment_ref[...], 0)


def images_kernel(
    own_ref, recv_ref, block_ref, moment_ref, pack_ref, basis_ref, low_ref, held_ref, stack_ref, sems
):
    count, cols = block_ref.shape
    blocks, depth, width = held_ref.shape
    copies = [
        pltpu.make_async_copy(
            moment_ref.at[:, at * width : (at + 1) * width], held_ref.at[at], sems.at[at]
        )
        for at in range(blocks)
    ]
    for copy in copies:
        copy.start()
    low_t, inverse = eliminate(own_ref[:, depth:] + recv_ref[:, depth:], count)
    low_ref[...] = low_t
    reduced = fdot(inverse, own_ref[:, :depth] + recv_ref[:, :depth])
    high, low = halves(reduced)
    stack_ref[:count] = high
    stack_ref[count:] = low
    pack_ref[:, cols:] = pad_lanes(fdot_t(reduced, reduced))
    basis_ref[...] = fdot(inverse, block_ref[...])
    for at, copy in enumerate(copies):
        copy.wait()
        pack_ref[:, at * width : (at + 1) * width] = split_dot(stack_ref[...], held_ref[at], 0)


def images_call(own, recv, block, moment, fetch, ties=()):
    depth, cols = moment.shape
    count = block.shape[0]
    width = min(512, cols)
    stack = pltpu.VMEM((2 * count, depth), jnp.bfloat16)
    held = [
        pltpu.VMEM((cols // width, depth, width), jnp.float32),
        stack,
        pltpu.SemaphoreType.DMA((cols // width,)),
    ]
    return pl.pallas_call(
        images_kernel if fetch else images_blocked,
        grid=(1 if fetch else cols // width,),
        in_specs=[VMEM, VMEM, VMEM, ANY if fetch else pl.BlockSpec((depth, width), lambda i: (0, i))]
        + [ANY] * len(ties),
        out_specs=[VMEM, VMEM, VMEM],
        out_shape=[
            jax.ShapeDtypeStruct((count, cols + LANES), jnp.float32),
            jax.ShapeDtypeStruct((count, cols), jnp.float32),
            jax.ShapeDtypeStruct((count, LANES), jnp.float32),
        ],
        scratch_shapes=held if fetch else [stack],
        compiler_params=LARGE if fetch else PARAMS,
    )(own, recv, block, moment, *ties)


def reduced_kernel(has_prev, passed, width, *refs):
    names = 5 if has_prev else 3
    own_ref, recv_ref, basis_ref = refs[:3]
    prev_ref, low_ref = refs[3:5] if has_prev else (None, None)
    moment_ref = refs[names]
    outs = refs[names + 1 + passed :]
    pack_ref, residue_ref, diag_ref = outs[:3]
    stack_ref = refs[-1]
    at = pl.program_id(0)
    count, cols = basis_ref.shape
    height = moment_ref.shape[0]

    @pl.when(at == 0)
    def _():
        diag = (own_ref[:, cols:] + recv_ref[:, cols:])[:, :count]
        diag = 0.5 * (diag + diag.T)
        diag_ref[...] = pad_lanes(diag)
        residue = own_ref[:, :cols] + recv_ref[:, :cols] - fdot(diag, basis_ref[...])
        if has_prev:
            residue = residue - fdot(low_ref[:, :count], prev_ref[...])
        residue_ref[...] = residue
        high, low = halves(residue)
        stack_ref[:count] = high
        stack_ref[count:] = low
        pack_ref[:, width:] = pad_lanes(fdot_t(residue, residue))

    moment = moment_ref[...]
    if passed:
        short_ref = outs[3]
        short_ref[...] = moment[:, : short_ref.shape[1]].astype(jnp.bfloat16)
    pack_ref[:, pl.ds(pl.multiple_of(at * height, height), height)] = split_dot(stack_ref[...], moment, 1)


def reduced_call(own, recv, basis, prev, low, moment, gates, early_cols):
    depth, cols = moment.shape
    count = basis.shape[0]
    height = min(256, depth)
    has_prev = prev is not None
    operands = (own, recv, basis) + ((prev, low) if has_prev else ()) + (moment,)
    out_specs = [VMEM, VMEM, VMEM]
    out_shape = [
        jax.ShapeDtypeStruct((count, depth + LANES), jnp.float32),
        jax.ShapeDtypeStruct((count, cols), jnp.float32),
        jax.ShapeDtypeStruct((count, LANES), jnp.float32),
    ]
    if gates:
        out_specs += [pl.BlockSpec((height, early_cols), lambda i: (i, 0))] + [ANY] * len(gates)
        out_shape += [jax.ShapeDtypeStruct((depth, early_cols), jnp.bfloat16)]
        out_shape += [jax.ShapeDtypeStruct(at.shape, at.dtype) for at in gates]
    return pl.pallas_call(
        functools.partial(reduced_kernel, has_prev, len(gates), depth),
        grid=(depth // height,),
        in_specs=[VMEM] * (len(operands) - 1)
        + [pl.BlockSpec((height, cols), lambda i: (i, 0))]
        + [ANY] * len(gates),
        out_specs=out_specs,
        out_shape=out_shape,
        input_output_aliases={len(operands) + i: 4 + i for i in range(len(gates))},
        scratch_shapes=[pltpu.VMEM((2 * count, cols), jnp.bfloat16)],
        compiler_params=PARAMS,
    )(*operands, *gates)


def last_kernel(passed, own_ref, recv_ref, *refs):
    diag_ref, low_ref = refs[passed : passed + 2]
    count = own_ref.shape[0]
    depth = own_ref.shape[1] - LANES
    low_t, inverse = eliminate(own_ref[:, depth:] + recv_ref[:, depth:], count)
    low_ref[...] = low_t
    reduced = fdot(inverse, own_ref[:, :depth] + recv_ref[:, :depth])
    diag_ref[...] = pad_lanes(fdot_t(reduced, reduced))


def last_call(own, recv, gates, ties):
    shape = jax.ShapeDtypeStruct((own.shape[0], LANES), jnp.float32)
    return pl.pallas_call(
        functools.partial(last_kernel, len(gates) + len(ties)),
        in_specs=[VMEM, VMEM] + [ANY] * (len(gates) + len(ties)),
        out_specs=[VMEM, VMEM] + [ANY] * len(gates),
        out_shape=[shape, shape] + [jax.ShapeDtypeStruct(at.shape, at.dtype) for at in gates],
        input_output_aliases={2 + i: 2 + i for i in range(len(gates))},
        compiler_params=PARAMS,
    )(own, recv, *gates, *ties)


def top_kernel(steps, *refs):
    diag_refs = refs[: steps + 1]
    low_refs = refs[steps + 1 : 2 * steps]
    scaled_ref, rate_ref, krylov_ref = refs[-3:]
    count = diag_refs[0].shape[0]
    size = steps * count
    krylov_ref[...] = jnp.zeros_like(krylov_ref)
    for place in range(steps):
        first = place * count
        diag = diag_refs[place][:, :count]
        if place + 1 == steps:
            diag = diag + diag_refs[steps][:, :count]
        krylov_ref[first : first + count, first : first + count] = 0.5 * (diag + diag.T)
        if place + 1 < steps:
            second = first + count
            low_t = low_refs[place][:, :count]
            krylov_ref[second : second + count, first:second] = low_t
            krylov_ref[first:second, second : second + count] = low_t.T
    krylov = krylov_ref[...]
    power = krylov * (1.0 / jnp.max(jnp.abs(krylov), keepdims=True))
    for _ in range(SQUARINGS):
        power = fdot(power, power)
        power = power * (1.0 / jnp.max(jnp.abs(power), keepdims=True))
    tall = jnp.sum(power, axis=1, keepdims=True)
    wide = jnp.sum(power, axis=0, keepdims=True)
    tall = tall * (1.0 / jnp.sqrt(jnp.sum(tall * tall, keepdims=True)))
    wide = wide * (1.0 / jnp.sqrt(jnp.sum(wide * wide, keepdims=True)))
    top = jnp.sum(krylov * tall * wide, keepdims=True)
    scaled_ref[...] = krylov[:size, :size] / top
    rate_ref[...] = jnp.broadcast_to(1.0 / jnp.sqrt(top), rate_ref.shape)


def top_call(diags, lows, ties):
    steps = len(lows) + 1
    count = diags[0].shape[0]
    size = steps * count
    padded = -(-size // LANES) * LANES
    return pl.pallas_call(
        functools.partial(top_kernel, steps),
        in_specs=[VMEM] * (2 * steps) + [ANY] * len(ties),
        out_specs=[VMEM, VMEM],
        out_shape=[
            jax.ShapeDtypeStruct((size, size), jnp.float32),
            jax.ShapeDtypeStruct((8, LANES), jnp.float32),
        ],
        scratch_shapes=[pltpu.VMEM((padded, padded), jnp.float32)],
        compiler_params=PARAMS,
    )(*diags, *lows, *ties)


def step_kernel(ties, weight_ref, moment_ref, rate_ref, *refs):
    stepped = weight_ref[...].astype(jnp.float32) - moment_ref[...] * rate_ref[:1, :1]
    for i, out_ref in enumerate(refs[ties:]):
        out_ref[...] = stepped[:, i * UNIT : (i + 1) * UNIT].astype(jnp.bfloat16)


def step_call(weight, moment, rate, first, width, ties):
    depth = weight.shape[0]
    height = min(512, depth)
    block = pl.BlockSpec((height, width), lambda r: (r, first // width))
    return pl.pallas_call(
        functools.partial(step_kernel, len(ties)),
        grid=(depth // height,),
        in_specs=[block, block, VMEM] + [ANY] * len(ties),
        out_specs=[pl.BlockSpec((height, UNIT), lambda r: (r, 0))] * (width // UNIT),
        out_shape=[jax.ShapeDtypeStruct((depth, UNIT), jnp.bfloat16)] * (width // UNIT),
        compiler_params=LARGE,
        cost_estimate=BRIEF,
    )(weight, moment, rate, *ties)


def project_kernel(far, pieces, count, split, early, in_place, ties, first, order_ref, *refs):
    tokens = refs[:pieces]
    refs = refs[pieces:]
    weights, refs = refs[: split * count], refs[split * count :]
    if early:
        moments, rate_ref, refs = refs[:count], refs[count], refs[count + 1 :]
    refs = refs[ties + (1 if in_place else 0) :]
    if not far:
        refs[1][...] = jnp.zeros(refs[1].shape, jnp.float32)
        refs = refs[:1] + refs[2:]
    out_ref, tokens_buf, weight_buf, moment_buf, total_ref, result_ref, sems, out_sem = refs
    depth, width = weight_buf.shape[1:]
    copies = []
    for k in range(count):
        step = []
        for i in range(pieces):
            if far:
                rows = tokens[i].shape[0]
                source = tokens[i].at[:, k * depth : (k + 1) * depth]
                target = tokens_buf.at[k, pl.ds(pl.multiple_of(order_ref[i], 16), rows), :]
            else:
                source = tokens[i].at[:, pl.ds(pl.multiple_of(order_ref[k] * depth, LANES), depth)]
                target = tokens_buf.at[k]
            step.append(pltpu.make_async_copy(source, target, sems.at[k, i]))
        if early:
            at = slice(first, first + width)
            step.append(pltpu.make_async_copy(weights[k].at[:, at], weight_buf.at[k], sems.at[k, pieces]))
            step.append(
                pltpu.make_async_copy(moments[k].at[:, at], moment_buf.at[k], sems.at[k, pieces + 1])
            )
        else:
            for i in range(split):
                target = weight_buf.at[k, :, i * UNIT : (i + 1) * UNIT]
                step.append(
                    pltpu.make_async_copy(weights[k * split + i], target, sems.at[k, pieces + i])
                )
        for copy in step:
            copy.start()
        copies.append(step)
    for k in range(count):
        for copy in copies[k]:
            copy.wait()
        block = weight_buf[k]
        if early:
            stepped = block.astype(jnp.float32) - moment_buf[k].astype(jnp.float32) * rate_ref[:1, :1]
            block = stepped.astype(jnp.bfloat16)
        part = jnp.dot(tokens_buf[k], block, preferred_element_type=jnp.float32)
        total_ref[...] = part if k == 0 else total_ref[...] + part
    if far:
        result_ref[...] = total_ref[...].astype(result_ref.dtype)
        copy = pltpu.make_async_copy(result_ref, out_ref, out_sem)
    else:
        copy = pltpu.make_async_copy(total_ref, out_ref.at[:, first : first + width], out_sem)
    copy.start()
    copy.wait()


def project_call(far, order, tokens, first, width, weights, moments, rate, ties=(), out=None, cols=None):
    early = moments is not None
    split = 1 if early else width // UNIT
    count = len(weights) // split
    depth = weights[0].shape[0]
    num_rows = sum(at.shape[0] for at in tokens)
    operands = list(tokens) + list(weights)
    specs = [ANY] * len(operands)
    if early:
        operands += list(moments) + [rate]
        specs += [ANY] * count + [VMEM]
    operands += list(ties)
    specs += [ANY] * len(ties)
    aliases = {}
    if far:
        out_shape = jax.ShapeDtypeStruct((num_rows, width), jnp.bfloat16)
    else:
        out_shape = [
            jax.ShapeDtypeStruct((num_rows, cols), jnp.float32),
            jax.ShapeDtypeStruct((8, LANES), jnp.float32),
        ]
        if out is not None:
            operands.append(out)
            specs.append(ANY)
            aliases = {len(operands): 0}
    return pl.pallas_call(
        functools.partial(
            project_kernel, far, len(tokens), count, split, early, bool(aliases), len(ties), first
        ),
        grid_spec=pltpu.PrefetchScalarGridSpec(
            num_scalar_prefetch=1,
            grid=(1,),
            in_specs=specs,
            out_specs=ANY if far else [ANY, VMEM],
            scratch_shapes=[
                pltpu.VMEM((count, num_rows, depth), jnp.bfloat16),
                pltpu.VMEM((count, depth, width), jnp.bfloat16),
                pltpu.VMEM((count, depth, width) if early else (8, LANES), jnp.bfloat16),
                pltpu.VMEM((num_rows, width), jnp.float32),
                pltpu.VMEM((num_rows, width) if far else (8, LANES), jnp.bfloat16),
                pltpu.SemaphoreType.DMA((count, len(tokens) + max(2, split))),
                pltpu.SemaphoreType.DMA,
            ],
        ),
        out_shape=out_shape,
        input_output_aliases=aliases,
        compiler_params=LARGE,
        cost_estimate=BRIEF,
    )(order, *operands)


def add_kernel(old_ref, far_ref, out_ref):
    out_ref[...] = old_ref[...] + far_ref[...].astype(jnp.float32)


def add_call(out, far, first):
    num_rows, width = far.shape
    block = pl.BlockSpec((num_rows, UNIT), lambda c: (0, first // UNIT + c))
    return pl.pallas_call(
        add_kernel,
        grid=(width // UNIT,),
        in_specs=[block, pl.BlockSpec((num_rows, UNIT), lambda c: (0, c))],
        out_specs=block,
        out_shape=jax.ShapeDtypeStruct(out.shape, out.dtype),
        input_output_aliases={0: 0},
        compiler_params=LARGE,
        cost_estimate=BRIEF,
    )(out, far)


def swap(values, axis, size, bit):
    return lax.ppermute(values, axis, [(at, at ^ bit) for at in range(size)])


def butterfly(values, axis, size):
    bit = 1
    while 2 * bit < size:
        values = values + swap(values, axis, size, bit)
        bit *= 2
    return values, swap(values, axis, size, bit)


def offsets(count):
    found = [0]
    bit = count // 2
    while bit:
        found = found + [at ^ bit for at in found]
        bit //= 2
    return found


def spread(piece, axis, size):
    parts = [piece]
    bit = 1
    while bit < size:
        parts = parts + [swap(part, axis, size, bit) for part in parts]
        bit *= 2
    return parts


def local(rows_n, cols_n, tokens, weight, momentum, gradient, probes):
    half = rows_n // 2
    far_bit, near_bit = half // 2, half // 4
    place = lax.axis_index("fsdp")
    low_at = lax.rem(place, half)
    side = lax.div(place, half)
    column_at = lax.axis_index("tensor")
    num_rows = tokens.shape[0]
    depth, cols = weight.shape
    rows = num_rows // cols_n // PARTS
    unit = cols // (sum(EARLY) + sum(LATE))
    early_cols = sum(EARLY) * unit

    def fswap(values, bit):
        return swap(values, "fsdp", rows_n, bit)

    def complete(own, across, beside):
        parts = [own, across, beside, fswap(across, near_bit)]
        bit = near_bit // 2
        while bit:
            parts = parts + [fswap(part, bit) for part in parts]
            bit //= 2
        return parts

    def sum_over_rows(pack, gates, ties):
        passed = {}
        bit = 1
        while bit < half:
            pack, *passed[bit] = gate_call(pack, fswap(pack, bit), gates.get(bit, ()), ties.get(bit, ()))
            bit *= 2
        return pack, fswap(pack, half), passed

    mixed = jnp.stack([low_at ^ at for at in offsets(half)]).astype(jnp.int32)
    near_order = side * half + mixed
    pick_order = jnp.concatenate([(column_at * PARTS)[None], (1 - side) * half + mixed])
    far_order = jnp.stack(
        [(column_at ^ i) * PARTS * rows + part * rows for part in range(PARTS) for i in range(cols_n)]
    ).astype(jnp.int32)

    sent_0, sent_1, weight_own = pick_call(pick_order, tokens, weight, rows, half, early_cols)
    moment, short_1, pack = start_call(momentum, gradient, probes, sent_0, early_cols)
    weight_beside = fswap(weight_own, near_bit)
    weight_across = fswap(weight_own, far_bit)
    tokens_0 = fswap(sent_0, half)

    own, recv = butterfly(pack, "tensor", cols_n)
    pack, basis_1, _ = images_call(own, recv, probes, moment, True)
    own, recv, passed = sum_over_rows(
        pack, {1: [short_1, tokens_0], 2: [weight_across]}, {2: [weight_beside]}
    )
    short_1, tokens_0 = passed[1]
    weight_across, = passed[2]
    weight_parts = complete(weight_own, weight_across, weight_beside)
    moment_beside = fswap(short_1, near_bit)
    token_parts = spread(tokens_0, "tensor", cols_n)
    pack, residue, diag_1, short_2, sent_1 = reduced_call(
        own, recv, basis_1, None, None, moment, [sent_1], early_cols
    )
    moment_across = fswap(short_2, far_bit)
    tokens_1 = fswap(sent_1, half)

    own, recv = butterfly(pack, "tensor", cols_n)
    pack, basis_2, low_1 = images_call(own, recv, residue, moment, False, weight_parts[3:])
    own, recv, passed = sum_over_rows(
        pack,
        {1: [moment_across, tokens_1]},
        {1: [moment_beside], 2: token_parts[1:]},
    )
    moment_across, token_1 = passed[1]
    moment_parts = complete(short_1, moment_across, moment_beside)
    token_1_beside = swap(token_1, "tensor", cols_n, 1)
    token_1_across = swap(token_1, "tensor", cols_n, 2)
    pack, _, diag_2 = reduced_call(own, recv, basis_2, basis_1, low_1, moment, [], early_cols)

    own, recv = butterfly(pack, "tensor", cols_n)
    diag_3, low_2, token_1_beside = last_call(
        own, recv, [token_1_beside], [token_1_across, *moment_parts[3:]]
    )
    token_parts += [token_1, token_1_beside, token_1_across, swap(token_1_beside, "tensor", cols_n, 2)]
    own, recv = butterfly(diag_3, "fsdp", rows_n)
    scaled, rate = top_call(
        [diag_1, diag_2, own, recv], [low_1, low_2], []
    )

    firsts, widths = [0], []
    for size in EARLY + LATE:
        widths.append(size * unit)
        firsts.append(firsts[-1] + size * unit)
    num_early = len(EARLY)
    gathered = [(weight_parts, moment_parts, rate)] * num_early
    out, partial, far = None, [], []

    def send(weights, first, width, *ties):
        partial.append(project_call(True, far_order, token_parts, first, width, *weights, ties=ties))
        far.append(fswap(partial[-1], half))

    def keep(chunk, out, tie):
        return project_call(
            False,
            near_order,
            [tokens],
            firsts[chunk],
            widths[chunk],
            *gathered[chunk],
            ties=[tie],
            out=out,
            cols=cols,
        )

    total = len(widths)
    own, across, beside = {}, {}, {}

    def step(chunk, *ties):
        own[chunk] = step_call(weight, moment, rate, firsts[chunk], widths[chunk], ties)
        across[chunk] = [fswap(at, far_bit) for at in own[chunk]]
        beside[chunk] = [fswap(at, near_bit) for at in own[chunk]]

    step(num_early, rate)
    tie = own[num_early][0]
    for chunk in range(num_early):
        send(gathered[chunk], firsts[chunk], widths[chunk], tie)
        tie = partial[-1]
    kept = []
    for chunk in range(num_early):
        out, token = keep(chunk, out, kept[-1] if kept else partial[-1])
        kept.append(token)
    for chunk in range(num_early, total):
        passed = pass_call(across[chunk], [partial[-1], *beside[chunk]])
        pieces = [complete(*at) for at in zip(own[chunk], passed, beside[chunk])]
        gathered.append(([piece[k] for k in range(half) for piece in pieces], None, None))
        if chunk + 1 < total:
            step(chunk + 1, kept[-1], passed[0])
            send(
                gathered[chunk], firsts[chunk], widths[chunk], partial[-1], own[chunk + 1][0], far[chunk - 1]
            )
            out = add_call(out, far[chunk - 1], firsts[chunk - 1])
            out, token = keep(chunk, out, partial[-1])
            kept.append(token)
    last_sent = partial[-1]
    for i, piece in enumerate(pieces):
        ties = [last_sent, kept[-1]] + far[total - 2 : total - 1] * (i > 0)
        send((piece, None, None), firsts[total - 1] + i * unit, unit, *ties)
    out = add_call(out, far[total - 2], firsts[total - 2])
    out, _ = keep(total - 1, out, partial[-1])
    for i in range(len(pieces)):
        out = add_call(out, far[total - 1 + i], firsts[total - 1] + i * unit)
    return out, moment, scaled


def solution(mesh):
    return jax.shard_map(
        functools.partial(local, mesh.shape["fsdp"], mesh.shape["tensor"]),
        mesh=mesh,
        in_specs=(
            P("fsdp", None),
            P("fsdp", "tensor"),
            P("fsdp", "tensor"),
            P("fsdp", "tensor"),
            P(None, "tensor"),
        ),
        out_specs=(P("fsdp", "tensor"), P("fsdp", "tensor"), P()),
        check_vma=False,
    )
```

```python
import functools

import jax
import jax.numpy as jnp
from jax import lax
from jax.experimental import pallas as pl
from jax.experimental.pallas import tpu as pltpu
from jax.sharding import PartitionSpec as P

DECAY = 0.9
SQUARINGS = 5
LANES = 128
UNIT = 256
EARLY = (2,)
LATE = (2, 2, 2)
PARTS = 2

HIGHEST = lax.Precision.HIGHEST
LARGE = pltpu.CompilerParams(vmem_limit_bytes=53 * 1024 * 1024)
PARAMS = pltpu.CompilerParams(vmem_limit_bytes=24 * 1024 * 1024)
BRIEF = pl.CostEstimate(flops=0, bytes_accessed=0, transcendentals=0)
VMEM = pl.BlockSpec(memory_space=pltpu.VMEM)
ANY = pl.BlockSpec(memory_space=pl.ANY)


def fdot(left, right):
    return lax.dot_general(
        left, right, (((1,), (0,)), ((), ())), precision=HIGHEST, preferred_element_type=jnp.float32
    )


def fdot_t(left, right):
    return lax.dot_general(
        left, right, (((1,), (1,)), ((), ())), precision=HIGHEST, preferred_element_type=jnp.float32
    )


def halves(values):
    high = values.astype(jnp.bfloat16)
    return high, (values - high.astype(jnp.float32)).astype(jnp.bfloat16)


def split_dot(stacked, mat, contract):
    rows = stacked.shape[0] // 2
    mat_high, mat_low = halves(mat)
    dims = (((1,), (contract,)), ((), ()))
    first = lax.dot_general(stacked, mat_high, dims, preferred_element_type=jnp.float32)
    second = lax.dot_general(stacked[:rows], mat_low, dims, preferred_element_type=jnp.float32)
    return first[:rows] + first[rows:] + second


def eliminate(gram, count):
    rows = lax.broadcasted_iota(jnp.int32, (count, LANES), 0)
    lanes = lax.broadcasted_iota(jnp.int32, (count, LANES), 1)
    aug = jnp.where(lanes < count, gram, jnp.where(lanes - count == rows, 1.0, 0.0))
    for step in range(count):
        pivot = aug[step : step + 1, step : step + 1]
        factor = jnp.where(rows > step, aug[:, step : step + 1] * (1.0 / pivot), 0.0)
        aug = aug - factor * aug[step : step + 1, :]
    pivots = jnp.sum(jnp.where(lanes == rows, aug, 0.0), axis=1, keepdims=True)
    aug = aug * (1.0 / jnp.sqrt(pivots))
    low_t = jnp.where((lanes >= rows) & (lanes < count), aug, 0.0)
    return low_t, aug[:, count : 2 * count]


def pad_lanes(square):
    return jnp.concatenate(
        [square, jnp.zeros((square.shape[0], LANES - square.shape[1]), jnp.float32)], axis=1
    )


def pick_kernel(order_ref, token_0, token_1, weight_ref, sent_0, sent_1, early_ref):
    sent_0[...] = token_0[...]
    sent_1[...] = token_1[...]
    early_ref[...] = weight_ref[...]


def pick_call(order, tokens, weight, rows, count, early_cols):
    depth = weight.shape[0]
    height = depth // count
    sent = jax.ShapeDtypeStruct((rows, count * depth), tokens.dtype)
    weight_spec = pl.BlockSpec((height, early_cols), lambda i, order_ref: (i, 0))
    sent_spec = pl.BlockSpec((rows, depth), lambda i, order_ref: (0, i))
    return pl.pallas_call(
        pick_kernel,
        grid_spec=pltpu.PrefetchScalarGridSpec(
            num_scalar_prefetch=1,
            grid=(count,),
            in_specs=[
                pl.BlockSpec((rows, depth), lambda i, order_ref: (order_ref[0], order_ref[1 + i])),
                pl.BlockSpec((rows, depth), lambda i, order_ref: (order_ref[0] + 1, order_ref[1 + i])),
                weight_spec,
            ],
            out_specs=[sent_spec, sent_spec, weight_spec],
        ),
        out_shape=[sent, sent, jax.ShapeDtypeStruct((depth, early_cols), weight.dtype)],
        compiler_params=LARGE,
    )(order, tokens, tokens, weight)


def start_kernel(width, mom_ref, grad_ref, probes_ref, tie_ref, moment_ref, short_ref, pack_ref, stack_ref):
    at = pl.program_id(0)
    count = probes_ref.shape[0]
    height = mom_ref.shape[0]

    @pl.when(at == 0)
    def _():
        probes = probes_ref[...]
        high, low = halves(probes)
        stack_ref[:count] = high
        stack_ref[count:] = low
        pack_ref[:, width:] = pad_lanes(fdot_t(probes, probes))

    moment = DECAY * mom_ref[...] + grad_ref[...].astype(jnp.float32)
    moment_ref[...] = moment
    short_ref[...] = moment[:, : short_ref.shape[1]].astype(jnp.bfloat16)
    pack_ref[:, pl.ds(pl.multiple_of(at * height, height), height)] = split_dot(stack_ref[...], moment, 1)


def start_call(momentum, gradient, probes, tie, early_cols):
    depth, cols = momentum.shape
    count = probes.shape[0]
    height = min(256, depth)
    rows = pl.BlockSpec((height, cols), lambda i: (i, 0))
    return pl.pallas_call(
        functools.partial(start_kernel, depth),
        grid=(depth // height,),
        in_specs=[rows, rows, VMEM, ANY],
        out_specs=[rows, pl.BlockSpec((height, early_cols), lambda i: (i, 0)), VMEM],
        out_shape=[
            jax.ShapeDtypeStruct((depth, cols), jnp.float32),
            jax.ShapeDtypeStruct((depth, early_cols), jnp.bfloat16),
            jax.ShapeDtypeStruct((count, depth + LANES), jnp.float32),
        ],
        scratch_shapes=[pltpu.VMEM((2 * count, cols), jnp.bfloat16)],
        compiler_params=LARGE,
    )(momentum, gradient, probes, tie)


def gate_kernel(passed, own_ref, recv_ref, *refs):
    sum_ref = refs[-1 - passed]
    sum_ref[...] = own_ref[...] + recv_ref[...]


def gate_call(own, recv, gates=(), ties=()):
    shapes = [jax.ShapeDtypeStruct(at.shape, at.dtype) for at in (own, *gates)]
    first = 2 + len(ties)
    return pl.pallas_call(
        functools.partial(gate_kernel, len(gates)),
        in_specs=[VMEM, VMEM] + [ANY] * (len(gates) + len(ties)),
        out_specs=[VMEM] + [ANY] * len(gates),
        out_shape=shapes,
        input_output_aliases={first + i: 1 + i for i in range(len(gates))},
        compiler_params=PARAMS,
    )(own, recv, *ties, *gates)


def pass_kernel(*refs):
    pass


def pass_call(values, ties):
    return pl.pallas_call(
        pass_kernel,
        in_specs=[ANY] * (len(values) + len(ties)),
        out_specs=[ANY] * len(values),
        out_shape=[jax.ShapeDtypeStruct(at.shape, at.dtype) for at in values],
        input_output_aliases={i: i for i in range(len(values))},
        compiler_params=LARGE,
        cost_estimate=BRIEF,
    )(*values, *ties)


def merge_kernel(count, *refs):
    first = 0
    for value_ref in refs[:count]:
        width = value_ref.shape[1]
        refs[-1][:, first : first + width] = value_ref[...]
        first += width


def merge_call(values, ties):
    depth = values[0][0].shape[0]
    height = min(512, depth)
    cols = sum(width for _, _, width in values)

    def spec(first, width):
        return pl.BlockSpec((height, width), lambda r: (r, first // width))

    return pl.pallas_call(
        functools.partial(merge_kernel, len(values)),
        grid=(depth // height,),
        in_specs=[spec(first, width) for _, first, width in values] + [ANY] * len(ties),
        out_specs=spec(0, cols),
        out_shape=jax.ShapeDtypeStruct((depth, cols), values[0][0].dtype),
        compiler_params=LARGE,
        cost_estimate=BRIEF,
    )(*[array for array, _, _ in values], *ties)


def images_blocked(own_ref, recv_ref, block_ref, moment_ref, *refs):
    pack_ref, basis_ref, low_ref, stack_ref = refs[-4:]
    at = pl.program_id(0)
    count, cols = block_ref.shape
    depth = moment_ref.shape[0]
    width = moment_ref.shape[1]

    @pl.when(at == 0)
    def _():
        low_t, inverse = eliminate(own_ref[:, depth:] + recv_ref[:, depth:], count)
        low_ref[...] = low_t
        reduced = fdot(inverse, own_ref[:, :depth] + recv_ref[:, :depth])
        high, low = halves(reduced)
        stack_ref[:count] = high
        stack_ref[count:] = low
        pack_ref[:, cols:] = pad_lanes(fdot_t(reduced, reduced))
        basis_ref[...] = fdot(inverse, block_ref[...])

    pack_ref[:, pl.ds(pl.multiple_of(at * width, width), width)] = split_dot(stack_ref[...], moment_ref[...], 0)


def images_kernel(
    own_ref, recv_ref, block_ref, moment_ref, pack_ref, basis_ref, low_ref, held_ref, stack_ref, sems
):
    count, cols = block_ref.shape
    blocks, depth, width = held_ref.shape
    copies = [
        pltpu.make_async_copy(
            moment_ref.at[:, at * width : (at + 1) * width], held_ref.at[at], sems.at[at]
        )
        for at in range(blocks)
    ]
    for copy in copies:
        copy.start()
    low_t, inverse = eliminate(own_ref[:, depth:] + recv_ref[:, depth:], count)
    low_ref[...] = low_t
    reduced = fdot(inverse, own_ref[:, :depth] + recv_ref[:, :depth])
    high, low = halves(reduced)
    stack_ref[:count] = high
    stack_ref[count:] = low
    pack_ref[:, cols:] = pad_lanes(fdot_t(reduced, reduced))
    basis_ref[...] = fdot(inverse, block_ref[...])
    for at, copy in enumerate(copies):
        copy.wait()
        pack_ref[:, at * width : (at + 1) * width] = split_dot(stack_ref[...], held_ref[at], 0)


def images_call(own, recv, block, moment, fetch, ties=()):
    depth, cols = moment.shape
    count = block.shape[0]
    width = min(512, cols)
    stack = pltpu.VMEM((2 * count, depth), jnp.bfloat16)
    held = [
        pltpu.VMEM((cols // width, depth, width), jnp.float32),
        stack,
        pltpu.SemaphoreType.DMA((cols // width,)),
    ]
    return pl.pallas_call(
        images_kernel if fetch else images_blocked,
        grid=(1 if fetch else cols // width,),
        in_specs=[VMEM, VMEM, VMEM, ANY if fetch else pl.BlockSpec((depth, width), lambda i: (0, i))]
        + [ANY] * len(ties),
        out_specs=[VMEM, VMEM, VMEM],
        out_shape=[
            jax.ShapeDtypeStruct((count, cols + LANES), jnp.float32),
            jax.ShapeDtypeStruct((count, cols), jnp.float32),
            jax.ShapeDtypeStruct((count, LANES), jnp.float32),
        ],
        scratch_shapes=held if fetch else [stack],
        compiler_params=LARGE if fetch else PARAMS,
    )(own, recv, block, moment, *ties)


def reduced_kernel(has_prev, passed, width, *refs):
    names = 5 if has_prev else 3
    own_ref, recv_ref, basis_ref = refs[:3]
    prev_ref, low_ref = refs[3:5] if has_prev else (None, None)
    moment_ref = refs[names]
    outs = refs[names + 1 + passed :]
    pack_ref, residue_ref, diag_ref = outs[:3]
    stack_ref = refs[-1]
    at = pl.program_id(0)
    count, cols = basis_ref.shape
    height = moment_ref.shape[0]

    @pl.when(at == 0)
    def _():
        diag = (own_ref[:, cols:] + recv_ref[:, cols:])[:, :count]
        diag = 0.5 * (diag + diag.T)
        diag_ref[...] = pad_lanes(diag)
        residue = own_ref[:, :cols] + recv_ref[:, :cols] - fdot(diag, basis_ref[...])
        if has_prev:
            residue = residue - fdot(low_ref[:, :count], prev_ref[...])
        residue_ref[...] = residue
        high, low = halves(residue)
        stack_ref[:count] = high
        stack_ref[count:] = low
        pack_ref[:, width:] = pad_lanes(fdot_t(residue, residue))

    moment = moment_ref[...]
    if passed:
        short_ref = outs[3]
        short_ref[...] = moment[:, : short_ref.shape[1]].astype(jnp.bfloat16)
    pack_ref[:, pl.ds(pl.multiple_of(at * height, height), height)] = split_dot(stack_ref[...], moment, 1)


def reduced_call(own, recv, basis, prev, low, moment, gates, early_cols):
    depth, cols = moment.shape
    count = basis.shape[0]
    height = min(256, depth)
    has_prev = prev is not None
    operands = (own, recv, basis) + ((prev, low) if has_prev else ()) + (moment,)
    out_specs = [VMEM, VMEM, VMEM]
    out_shape = [
        jax.ShapeDtypeStruct((count, depth + LANES), jnp.float32),
        jax.ShapeDtypeStruct((count, cols), jnp.float32),
        jax.ShapeDtypeStruct((count, LANES), jnp.float32),
    ]
    if gates:
        out_specs += [pl.BlockSpec((height, early_cols), lambda i: (i, 0))] + [ANY] * len(gates)
        out_shape += [jax.ShapeDtypeStruct((depth, early_cols), jnp.bfloat16)]
        out_shape += [jax.ShapeDtypeStruct(at.shape, at.dtype) for at in gates]
    return pl.pallas_call(
        functools.partial(reduced_kernel, has_prev, len(gates), depth),
        grid=(depth // height,),
        in_specs=[VMEM] * (len(operands) - 1)
        + [pl.BlockSpec((height, cols), lambda i: (i, 0))]
        + [ANY] * len(gates),
        out_specs=out_specs,
        out_shape=out_shape,
        input_output_aliases={len(operands) + i: 4 + i for i in range(len(gates))},
        scratch_shapes=[pltpu.VMEM((2 * count, cols), jnp.bfloat16)],
        compiler_params=PARAMS,
    )(*operands, *gates)


def last_kernel(passed, own_ref, recv_ref, *refs):
    diag_ref, low_ref = refs[passed : passed + 2]
    count = own_ref.shape[0]
    depth = own_ref.shape[1] - LANES
    low_t, inverse = eliminate(own_ref[:, depth:] + recv_ref[:, depth:], count)
    low_ref[...] = low_t
    reduced = fdot(inverse, own_ref[:, :depth] + recv_ref[:, :depth])
    diag_ref[...] = pad_lanes(fdot_t(reduced, reduced))


def last_call(own, recv, gates, ties):
    shape = jax.ShapeDtypeStruct((own.shape[0], LANES), jnp.float32)
    return pl.pallas_call(
        functools.partial(last_kernel, len(gates) + len(ties)),
        in_specs=[VMEM, VMEM] + [ANY] * (len(gates) + len(ties)),
        out_specs=[VMEM, VMEM] + [ANY] * len(gates),
        out_shape=[shape, shape] + [jax.ShapeDtypeStruct(at.shape, at.dtype) for at in gates],
        input_output_aliases={2 + i: 2 + i for i in range(len(gates))},
        compiler_params=PARAMS,
    )(own, recv, *gates, *ties)


def top_kernel(steps, *refs):
    diag_refs = refs[: steps + 1]
    low_refs = refs[steps + 1 : 2 * steps]
    scaled_ref, rate_ref, krylov_ref = refs[-3:]
    count = diag_refs[0].shape[0]
    size = steps * count
    krylov_ref[...] = jnp.zeros_like(krylov_ref)
    for place in range(steps):
        first = place * count
        diag = diag_refs[place][:, :count]
        if place + 1 == steps:
            diag = diag + diag_refs[steps][:, :count]
        krylov_ref[first : first + count, first : first + count] = 0.5 * (diag + diag.T)
        if place + 1 < steps:
            second = first + count
            low_t = low_refs[place][:, :count]
            krylov_ref[second : second + count, first:second] = low_t
            krylov_ref[first:second, second : second + count] = low_t.T
    krylov = krylov_ref[...]
    power = krylov * (1.0 / jnp.max(jnp.abs(krylov), keepdims=True))
    for _ in range(SQUARINGS):
        power = fdot(power, power)
        power = power * (1.0 / jnp.max(jnp.abs(power), keepdims=True))
    tall = jnp.sum(power, axis=1, keepdims=True)
    wide = jnp.sum(power, axis=0, keepdims=True)
    tall = tall * (1.0 / jnp.sqrt(jnp.sum(tall * tall, keepdims=True)))
    wide = wide * (1.0 / jnp.sqrt(jnp.sum(wide * wide, keepdims=True)))
    top = jnp.sum(krylov * tall * wide, keepdims=True)
    scaled_ref[...] = krylov[:size, :size] / top
    rate_ref[...] = jnp.broadcast_to(1.0 / jnp.sqrt(top), rate_ref.shape)


def top_call(diags, lows, ties):
    steps = len(lows) + 1
    count = diags[0].shape[0]
    size = steps * count
    padded = -(-size // LANES) * LANES
    return pl.pallas_call(
        functools.partial(top_kernel, steps),
        in_specs=[VMEM] * (2 * steps) + [ANY] * len(ties),
        out_specs=[VMEM, VMEM],
        out_shape=[
            jax.ShapeDtypeStruct((size, size), jnp.float32),
            jax.ShapeDtypeStruct((8, LANES), jnp.float32),
        ],
        scratch_shapes=[pltpu.VMEM((padded, padded), jnp.float32)],
        compiler_params=PARAMS,
    )(*diags, *lows, *ties)


def step_kernel(ties, weight_ref, moment_ref, rate_ref, *refs):
    stepped = weight_ref[...].astype(jnp.float32) - moment_ref[...] * rate_ref[:1, :1]
    stepped = stepped.astype(jnp.bfloat16)
    for i, out_ref in enumerate(refs[ties:]):
        width = out_ref.shape[1]
        first = 0 if i == 0 else (i - 1) * width
        out_ref[...] = stepped[:, first : first + width]


def step_call(weight, moment, rate, first, width, pieces, ties):
    depth = weight.shape[0]
    height = min(512, depth)
    block = pl.BlockSpec((height, width), lambda r: (r, first // width))
    sizes = [width] + [width // pieces] * (pieces if pieces > 1 else 0)
    return pl.pallas_call(
        functools.partial(step_kernel, len(ties)),
        grid=(depth // height,),
        in_specs=[block, block, VMEM] + [ANY] * len(ties),
        out_specs=[pl.BlockSpec((height, size), lambda r: (r, 0)) for size in sizes],
        out_shape=[jax.ShapeDtypeStruct((depth, size), jnp.bfloat16) for size in sizes],
        compiler_params=LARGE,
        cost_estimate=BRIEF,
    )(weight, moment, rate, *ties)


def project_kernel(far, pieces, layout, early, in_place, ties, first, order_ref, *refs):
    count = len(layout)
    tokens = refs[:pieces]
    refs = refs[pieces:]
    weights = []
    for parts in layout:
        weights.append(list(zip(refs, parts)))
        refs = refs[len(parts) :]
    if early:
        moments, rate_ref, refs = refs[:count], refs[count], refs[count + 1 :]
    refs = refs[ties + (1 if in_place else 0) :]
    if not far:
        refs[1][...] = jnp.zeros(refs[1].shape, jnp.float32)
        refs = refs[:1] + refs[2:]
    out_ref, tokens_buf, weight_buf, moment_buf, total_ref, result_ref, sems, out_sem = refs
    depth, width = weight_buf.shape[1:]
    copies = []
    for k in range(count):
        step = []
        for i in range(pieces):
            if far:
                rows = tokens[i].shape[0]
                source = tokens[i].at[:, k * depth : (k + 1) * depth]
                target = tokens_buf.at[k, pl.ds(pl.multiple_of(order_ref[i], 16), rows), :]
            else:
                source = tokens[i].at[:, pl.ds(pl.multiple_of(order_ref[k] * depth, LANES), depth)]
                target = tokens_buf.at[k]
            step.append(pltpu.make_async_copy(source, target, sems.at[k, i]))
        filled = 0
        for i, (part, (at, size)) in enumerate(weights[k]):
            target = weight_buf.at[k, :, filled : filled + size]
            step.append(pltpu.make_async_copy(part.at[:, at : at + size], target, sems.at[k, pieces + i]))
            filled += size
        if early:
            at, size = layout[k][0]
            step.append(
                pltpu.make_async_copy(
                    moments[k].at[:, at : at + size], moment_buf.at[k], sems.at[k, pieces + 1]
                )
            )
        for copy in step:
            copy.start()
        copies.append(step)
    for k in range(count):
        for copy in copies[k]:
            copy.wait()
        block = weight_buf[k]
        if early:
            stepped = block.astype(jnp.float32) - moment_buf[k].astype(jnp.float32) * rate_ref[:1, :1]
            block = stepped.astype(jnp.bfloat16)
        part = jnp.dot(tokens_buf[k], block, preferred_element_type=jnp.float32)
        total_ref[...] = part if k == 0 else total_ref[...] + part
    if far:
        result_ref[...] = total_ref[...].astype(result_ref.dtype)
        copy = pltpu.make_async_copy(result_ref, out_ref, out_sem)
    else:
        copy = pltpu.make_async_copy(total_ref, out_ref.at[:, first : first + width], out_sem)
    copy.start()
    copy.wait()


def project_call(far, order, tokens, first, width, weights, moments, rate, ties=(), out=None, cols=None):
    early = moments is not None
    layout = tuple(tuple((at, size) for _, at, size in parts) for parts in weights)
    count = len(weights)
    depth = weights[0][0][0].shape[0]
    num_rows = sum(at.shape[0] for at in tokens)
    operands = list(tokens) + [part for parts in weights for part, _, _ in parts]
    specs = [ANY] * len(operands)
    if early:
        operands += list(moments) + [rate]
        specs += [ANY] * count + [VMEM]
    operands += list(ties)
    specs += [ANY] * len(ties)
    aliases = {}
    if far:
        out_shape = jax.ShapeDtypeStruct((num_rows, width), jnp.bfloat16)
    else:
        out_shape = [
            jax.ShapeDtypeStruct((num_rows, cols), jnp.float32),
            jax.ShapeDtypeStruct((8, LANES), jnp.float32),
        ]
        if out is not None:
            operands.append(out)
            specs.append(ANY)
            aliases = {len(operands): 0}
    return pl.pallas_call(
        functools.partial(
            project_kernel, far, len(tokens), layout, early, bool(aliases), len(ties), first
        ),
        grid_spec=pltpu.PrefetchScalarGridSpec(
            num_scalar_prefetch=1,
            grid=(1,),
            in_specs=specs,
            out_specs=ANY if far else [ANY, VMEM],
            scratch_shapes=[
                pltpu.VMEM((count, num_rows, depth), jnp.bfloat16),
                pltpu.VMEM((count, depth, width), jnp.bfloat16),
                pltpu.VMEM((count, depth, width) if early else (8, LANES), jnp.bfloat16),
                pltpu.VMEM((num_rows, width), jnp.float32),
                pltpu.VMEM((num_rows, width) if far else (8, LANES), jnp.bfloat16),
                pltpu.SemaphoreType.DMA((count, len(tokens) + 2)),
                pltpu.SemaphoreType.DMA,
            ],
        ),
        out_shape=out_shape,
        input_output_aliases=aliases,
        compiler_params=LARGE,
        cost_estimate=BRIEF,
    )(order, *operands)


def add_kernel(old_ref, far_ref, out_ref):
    out_ref[...] = old_ref[...] + far_ref[...].astype(jnp.float32)


def add_call(out, far, first):
    num_rows, width = far.shape
    block = pl.BlockSpec((num_rows, UNIT), lambda c: (0, first // UNIT + c))
    return pl.pallas_call(
        add_kernel,
        grid=(width // UNIT,),
        in_specs=[block, pl.BlockSpec((num_rows, UNIT), lambda c: (0, c))],
        out_specs=block,
        out_shape=jax.ShapeDtypeStruct(out.shape, out.dtype),
        input_output_aliases={0: 0},
        compiler_params=LARGE,
        cost_estimate=BRIEF,
    )(out, far)


def swap(values, axis, size, bit):
    return lax.ppermute(values, axis, [(at, at ^ bit) for at in range(size)])


def butterfly(values, axis, size):
    bit = 1
    while 2 * bit < size:
        values = values + swap(values, axis, size, bit)
        bit *= 2
    return values, swap(values, axis, size, bit)


def offsets(count):
    found = [0]
    bit = count // 2
    while bit:
        found = found + [at ^ bit for at in found]
        bit //= 2
    return found


def spread(piece, axis, size):
    parts = [piece]
    bit = 1
    while bit < size:
        parts = parts + [swap(part, axis, size, bit) for part in parts]
        bit *= 2
    return parts


def local(rows_n, cols_n, tokens, weight, momentum, gradient, probes):
    half = rows_n // 2
    far_bit, near_bit = half // 2, half // 4
    place = lax.axis_index("fsdp")
    low_at = lax.rem(place, half)
    side = lax.div(place, half)
    column_at = lax.axis_index("tensor")
    num_rows = tokens.shape[0]
    depth, cols = weight.shape
    rows = num_rows // cols_n // PARTS
    unit = cols // (sum(EARLY) + sum(LATE))
    early_cols = sum(EARLY) * unit

    def fswap(values, bit):
        return swap(values, "fsdp", rows_n, bit)

    def complete(parts):
        bit = near_bit // 2
        while bit:
            parts = parts + [[(fswap(at, bit), first, size) for at, first, size in part] for part in parts]
            bit //= 2
        return parts

    def blocks(own, across, beside):
        parts = [own, across, beside, fswap(across, near_bit)]
        return [part[0][0] for part in complete([[(part, 0, part.shape[1])] for part in parts])]

    def sum_over_rows(pack, gates, ties):
        passed = {}
        bit = 1
        while bit < half:
            pack, *passed[bit] = gate_call(pack, fswap(pack, bit), gates.get(bit, ()), ties.get(bit, ()))
            bit *= 2
        return pack, fswap(pack, half), passed

    mixed = jnp.stack([low_at ^ at for at in offsets(half)]).astype(jnp.int32)
    near_order = side * half + mixed
    pick_order = jnp.concatenate([(column_at * PARTS)[None], (1 - side) * half + mixed])
    far_order = jnp.stack(
        [(column_at ^ i) * PARTS * rows + part * rows for part in range(PARTS) for i in range(cols_n)]
    ).astype(jnp.int32)

    sent_0, sent_1, weight_own = pick_call(pick_order, tokens, weight, rows, half, early_cols)
    moment, short_1, pack = start_call(momentum, gradient, probes, sent_0, early_cols)
    weight_beside = fswap(weight_own, near_bit)
    weight_across = fswap(weight_own, far_bit)
    tokens_0 = fswap(sent_0, half)

    own, recv = butterfly(pack, "tensor", cols_n)
    pack, basis_1, _ = images_call(own, recv, probes, moment, True)
    own, recv, passed = sum_over_rows(
        pack, {1: [short_1, tokens_0], 2: [weight_across]}, {2: [weight_beside]}
    )
    short_1, tokens_0 = passed[1]
    weight_across, = passed[2]
    weight_parts = blocks(weight_own, weight_across, weight_beside)
    moment_beside = fswap(short_1, near_bit)
    token_parts = spread(tokens_0, "tensor", cols_n)
    pack, residue, diag_1, short_2, sent_1 = reduced_call(
        own, recv, basis_1, None, None, moment, [sent_1], early_cols
    )
    moment_across = fswap(short_2, far_bit)
    tokens_1 = fswap(sent_1, half)

    own, recv = butterfly(pack, "tensor", cols_n)
    pack, basis_2, low_1 = images_call(own, recv, residue, moment, False, weight_parts[3:])
    own, recv, passed = sum_over_rows(
        pack,
        {1: [moment_across, tokens_1]},
        {1: [moment_beside], 2: token_parts[1:]},
    )
    moment_across, token_1 = passed[1]
    moment_parts = blocks(short_1, moment_across, moment_beside)
    token_1_beside = swap(token_1, "tensor", cols_n, 1)
    token_1_across = swap(token_1, "tensor", cols_n, 2)
    pack, _, diag_2 = reduced_call(own, recv, basis_2, basis_1, low_1, moment, [], early_cols)

    own, recv = butterfly(pack, "tensor", cols_n)
    diag_3, low_2, token_1_beside = last_call(
        own, recv, [token_1_beside], [token_1_across, *moment_parts[3:]]
    )
    token_parts += [token_1, token_1_beside, token_1_across, swap(token_1_beside, "tensor", cols_n, 2)]
    own, recv = butterfly(diag_3, "fsdp", rows_n)
    scaled, rate = top_call(
        [diag_1, diag_2, own, recv], [low_1, low_2], []
    )

    firsts, widths = [0], []
    for size in EARLY + LATE:
        widths.append(size * unit)
        firsts.append(firsts[-1] + size * unit)
    total = len(widths)
    partial, far = [], []

    def send(weights, first, width, *ties):
        partial.append(project_call(True, far_order, token_parts, first, width, *weights, ties=ties))
        far.append(fswap(partial[-1], half))

    def keep(weights, chunk, out, *ties):
        return project_call(
            False, near_order, [tokens], firsts[chunk], widths[chunk], *weights, ties=ties, out=out, cols=cols
        )

    def step(chunk, pieces, *ties):
        own = step_call(weight, moment, rate, firsts[chunk], widths[chunk], pieces, ties)
        return own[0], [fswap(at, far_bit) for at in (own[1:] or own)]

    def whole(array):
        return [(array, 0, array.shape[1])]

    early = ([[(part, firsts[0], widths[0])] for part in weight_parts], moment_parts, rate)
    own, across = step(1, widths[1] // unit, token_parts[-1])
    beside = fswap(own, near_bit)
    send(early, firsts[0], widths[0], own)
    passed = pass_call(across, [partial[0], beside])
    arrived = [fswap(at, near_bit) for at in passed]
    parts = [whole(own), [at for part in across for at in whole(part)], whole(beside)]
    parts.append([at for part in arrived for at in whole(part)])
    weights = (complete(parts), None, None)
    own, across = step(2, widths[2] // unit, passed[0])
    out, token = keep(early, 0, None, partial[0], own)
    for chunk in range(1, total):
        if chunk + 1 < total:
            width = widths[chunk + 1]
            split = width // unit if chunk + 2 == total else 1
            size = width // split
            merged = []
            for i in range(split):
                values = [(own, i * size, size)]
                if len(across) == 1:
                    values.append((across[0], i * size, size))
                else:
                    values += [at for part in across for at in whole(part)]
                ties = [*arrived, partial[-1], token, *merged]
                merged.append(merge_call(values, ties + far[:1] * (chunk == 1)))
            moved = [fswap(at, near_bit) for at in merged]
            send(weights, firsts[chunk], widths[chunk], merged[-1], far[chunk - 1])
            parts = [whole(own), [at for part in across for at in whole(part)]]
            parts += [[(at, first, size) for at in moved] for first in (0, size)]
            following = (complete(parts), None, None)
            if chunk + 2 < total:
                own, across = step(chunk + 2, 1, partial[-1])
            out = add_call(out, far[chunk - 1], firsts[chunk - 1])
            out, token = keep(weights, chunk, out, partial[-1], own)
            weights, arrived = following, moved
    for i in range(split):
        pieces = []
        for part in weights[0]:
            array, first, _ = part[i] if len(part) > 1 else part[0]
            pieces.append([(array, first if len(part) > 1 else i * size, size)])
        send((pieces, None, None), firsts[-2] + i * size, size, partial[-1], token)
    out = add_call(out, far[total - 2], firsts[total - 2])
    out, _ = keep(weights, total - 1, out, partial[-1])
    for i in range(split):
        out = add_call(out, far[total - 1 + i], firsts[total - 1] + i * size)
    return out, moment, scaled


def solution(mesh):
    return jax.shard_map(
        functools.partial(local, mesh.shape["fsdp"], mesh.shape["tensor"]),
        mesh=mesh,
        in_specs=(
            P("fsdp", None),
            P("fsdp", "tensor"),
            P("fsdp", "tensor"),
            P("fsdp", "tensor"),
            P(None, "tensor"),
        ),
        out_specs=(P("fsdp", "tensor"), P("fsdp", "tensor"), P()),
        check_vma=False,
    )
```

```python
import functools

import jax
import jax.numpy as jnp
from jax import lax
from jax.experimental import pallas as pl
from jax.experimental.pallas import tpu as pltpu
from jax.sharding import PartitionSpec as P

DECAY = 0.9
SQUARINGS = 5
LANES = 128
UNIT = 256
EARLY = (2,)
LATE = (2, 2, 2)
PARTS = 2

HIGHEST = lax.Precision.HIGHEST
LARGE = pltpu.CompilerParams(vmem_limit_bytes=53 * 1024 * 1024)
PARAMS = pltpu.CompilerParams(vmem_limit_bytes=24 * 1024 * 1024)
BRIEF = pl.CostEstimate(flops=0, bytes_accessed=0, transcendentals=0)
VMEM = pl.BlockSpec(memory_space=pltpu.VMEM)
ANY = pl.BlockSpec(memory_space=pl.ANY)


def fdot(left, right):
    return lax.dot_general(
        left, right, (((1,), (0,)), ((), ())), precision=HIGHEST, preferred_element_type=jnp.float32
    )


def fdot_t(left, right):
    return lax.dot_general(
        left, right, (((1,), (1,)), ((), ())), precision=HIGHEST, preferred_element_type=jnp.float32
    )


def halves(values):
    high = values.astype(jnp.bfloat16)
    return high, (values - high.astype(jnp.float32)).astype(jnp.bfloat16)


def split_dot(stacked, mat, contract):
    rows = stacked.shape[0] // 2
    mat_high, mat_low = halves(mat)
    dims = (((1,), (contract,)), ((), ()))
    first = lax.dot_general(stacked, mat_high, dims, preferred_element_type=jnp.float32)
    second = lax.dot_general(stacked[:rows], mat_low, dims, preferred_element_type=jnp.float32)
    return first[:rows] + first[rows:] + second


def eliminate(gram, count):
    rows = lax.broadcasted_iota(jnp.int32, (count, LANES), 0)
    lanes = lax.broadcasted_iota(jnp.int32, (count, LANES), 1)
    aug = jnp.where(lanes < count, gram, jnp.where(lanes - count == rows, 1.0, 0.0))
    for step in range(count):
        pivot = aug[step : step + 1, step : step + 1]
        factor = jnp.where(rows > step, aug[:, step : step + 1] * (1.0 / pivot), 0.0)
        aug = aug - factor * aug[step : step + 1, :]
    pivots = jnp.sum(jnp.where(lanes == rows, aug, 0.0), axis=1, keepdims=True)
    aug = aug * (1.0 / jnp.sqrt(pivots))
    low_t = jnp.where((lanes >= rows) & (lanes < count), aug, 0.0)
    return low_t, aug[:, count : 2 * count]


def pad_lanes(square):
    return jnp.concatenate(
        [square, jnp.zeros((square.shape[0], LANES - square.shape[1]), jnp.float32)], axis=1
    )


def pick_kernel(order_ref, token_0, token_1, weight_ref, sent_0, sent_1, early_ref):
    sent_0[...] = token_0[...]
    sent_1[...] = token_1[...]
    early_ref[...] = weight_ref[...]


def pick_call(order, tokens, weight, rows, count, early_cols):
    depth = weight.shape[0]
    height = depth // count
    sent = jax.ShapeDtypeStruct((rows, count * depth), tokens.dtype)
    weight_spec = pl.BlockSpec((height, early_cols), lambda i, order_ref: (i, 0))
    sent_spec = pl.BlockSpec((rows, depth), lambda i, order_ref: (0, i))
    return pl.pallas_call(
        pick_kernel,
        grid_spec=pltpu.PrefetchScalarGridSpec(
            num_scalar_prefetch=1,
            grid=(count,),
            in_specs=[
                pl.BlockSpec((rows, depth), lambda i, order_ref: (order_ref[0], order_ref[1 + i])),
                pl.BlockSpec((rows, depth), lambda i, order_ref: (order_ref[0] + 1, order_ref[1 + i])),
                weight_spec,
            ],
            out_specs=[sent_spec, sent_spec, weight_spec],
        ),
        out_shape=[sent, sent, jax.ShapeDtypeStruct((depth, early_cols), weight.dtype)],
        compiler_params=LARGE,
    )(order, tokens, tokens, weight)


def start_kernel(width, mom_ref, grad_ref, probes_ref, tie_ref, moment_ref, short_ref, pack_ref, stack_ref):
    at = pl.program_id(0)
    count = probes_ref.shape[0]
    height = mom_ref.shape[0]

    @pl.when(at == 0)
    def _():
        probes = probes_ref[...]
        high, low = halves(probes)
        stack_ref[:count] = high
        stack_ref[count:] = low
        pack_ref[:, width:] = pad_lanes(fdot_t(probes, probes))

    moment = DECAY * mom_ref[...] + grad_ref[...].astype(jnp.float32)
    moment_ref[...] = moment
    short_ref[...] = moment[:, : short_ref.shape[1]].astype(jnp.bfloat16)
    pack_ref[:, pl.ds(pl.multiple_of(at * height, height), height)] = split_dot(stack_ref[...], moment, 1)


def start_call(momentum, gradient, probes, tie, early_cols):
    depth, cols = momentum.shape
    count = probes.shape[0]
    height = min(256, depth)
    rows = pl.BlockSpec((height, cols), lambda i: (i, 0))
    return pl.pallas_call(
        functools.partial(start_kernel, depth),
        grid=(depth // height,),
        in_specs=[rows, rows, VMEM, ANY],
        out_specs=[rows, pl.BlockSpec((height, early_cols), lambda i: (i, 0)), VMEM],
        out_shape=[
            jax.ShapeDtypeStruct((depth, cols), jnp.float32),
            jax.ShapeDtypeStruct((depth, early_cols), jnp.bfloat16),
            jax.ShapeDtypeStruct((count, depth + LANES), jnp.float32),
        ],
        scratch_shapes=[pltpu.VMEM((2 * count, cols), jnp.bfloat16)],
        compiler_params=LARGE,
    )(momentum, gradient, probes, tie)


def gate_kernel(passed, own_ref, recv_ref, *refs):
    sum_ref = refs[-1 - passed]
    sum_ref[...] = own_ref[...] + recv_ref[...]


def gate_call(own, recv, gates=(), ties=()):
    shapes = [jax.ShapeDtypeStruct(at.shape, at.dtype) for at in (own, *gates)]
    first = 2 + len(ties)
    return pl.pallas_call(
        functools.partial(gate_kernel, len(gates)),
        in_specs=[VMEM, VMEM] + [ANY] * (len(gates) + len(ties)),
        out_specs=[VMEM] + [ANY] * len(gates),
        out_shape=shapes,
        input_output_aliases={first + i: 1 + i for i in range(len(gates))},
        compiler_params=PARAMS,
    )(own, recv, *ties, *gates)


def pass_kernel(*refs):
    pass


def pass_call(values, ties):
    return pl.pallas_call(
        pass_kernel,
        in_specs=[ANY] * (len(values) + len(ties)),
        out_specs=[ANY] * len(values),
        out_shape=[jax.ShapeDtypeStruct(at.shape, at.dtype) for at in values],
        input_output_aliases={i: i for i in range(len(values))},
        compiler_params=LARGE,
        cost_estimate=BRIEF,
    )(*values, *ties)


def merge_kernel(count, *refs):
    first = 0
    for value_ref in refs[:count]:
        width = value_ref.shape[1]
        refs[-1][:, first : first + width] = value_ref[...]
        first += width


def merge_call(values, ties):
    depth = values[0][0].shape[0]
    height = min(512, depth)
    cols = sum(width for _, _, width in values)

    def spec(first, width):
        return pl.BlockSpec((height, width), lambda r: (r, first // width))

    return pl.pallas_call(
        functools.partial(merge_kernel, len(values)),
        grid=(depth // height,),
        in_specs=[spec(first, width) for _, first, width in values] + [ANY] * len(ties),
        out_specs=spec(0, cols),
        out_shape=jax.ShapeDtypeStruct((depth, cols), values[0][0].dtype),
        compiler_params=LARGE,
        cost_estimate=BRIEF,
    )(*[array for array, _, _ in values], *ties)


def images_blocked(own_ref, recv_ref, block_ref, moment_ref, *refs):
    pack_ref, basis_ref, low_ref, stack_ref = refs[-4:]
    at = pl.program_id(0)
    count, cols = block_ref.shape
    depth = moment_ref.shape[0]
    width = moment_ref.shape[1]

    @pl.when(at == 0)
    def _():
        low_t, inverse = eliminate(own_ref[:, depth:] + recv_ref[:, depth:], count)
        low_ref[...] = low_t
        reduced = fdot(inverse, own_ref[:, :depth] + recv_ref[:, :depth])
        high, low = halves(reduced)
        stack_ref[:count] = high
        stack_ref[count:] = low
        pack_ref[:, cols:] = pad_lanes(fdot_t(reduced, reduced))
        basis_ref[...] = fdot(inverse, block_ref[...])

    pack_ref[:, pl.ds(pl.multiple_of(at * width, width), width)] = split_dot(stack_ref[...], moment_ref[...], 0)


def images_kernel(
    own_ref, recv_ref, block_ref, moment_ref, pack_ref, basis_ref, low_ref, held_ref, stack_ref, sems
):
    count, cols = block_ref.shape
    blocks, depth, width = held_ref.shape
    copies = [
        pltpu.make_async_copy(
            moment_ref.at[:, at * width : (at + 1) * width], held_ref.at[at], sems.at[at]
        )
        for at in range(blocks)
    ]
    for copy in copies:
        copy.start()
    low_t, inverse = eliminate(own_ref[:, depth:] + recv_ref[:, depth:], count)
    low_ref[...] = low_t
    reduced = fdot(inverse, own_ref[:, :depth] + recv_ref[:, :depth])
    high, low = halves(reduced)
    stack_ref[:count] = high
    stack_ref[count:] = low
    pack_ref[:, cols:] = pad_lanes(fdot_t(reduced, reduced))
    basis_ref[...] = fdot(inverse, block_ref[...])
    for at, copy in enumerate(copies):
        copy.wait()
        pack_ref[:, at * width : (at + 1) * width] = split_dot(stack_ref[...], held_ref[at], 0)


def images_call(own, recv, block, moment, fetch, ties=()):
    depth, cols = moment.shape
    count = block.shape[0]
    width = min(512, cols)
    stack = pltpu.VMEM((2 * count, depth), jnp.bfloat16)
    held = [
        pltpu.VMEM((cols // width, depth, width), jnp.float32),
        stack,
        pltpu.SemaphoreType.DMA((cols // width,)),
    ]
    return pl.pallas_call(
        images_kernel if fetch else images_blocked,
        grid=(1 if fetch else cols // width,),
        in_specs=[VMEM, VMEM, VMEM, ANY if fetch else pl.BlockSpec((depth, width), lambda i: (0, i))]
        + [ANY] * len(ties),
        out_specs=[VMEM, VMEM, VMEM],
        out_shape=[
            jax.ShapeDtypeStruct((count, cols + LANES), jnp.float32),
            jax.ShapeDtypeStruct((count, cols), jnp.float32),
            jax.ShapeDtypeStruct((count, LANES), jnp.float32),
        ],
        scratch_shapes=held if fetch else [stack],
        compiler_params=LARGE if fetch else PARAMS,
    )(own, recv, block, moment, *ties)


def reduced_kernel(has_prev, first, passed, width, *refs):
    names = 5 if has_prev else 3
    own_ref, recv_ref, basis_ref = refs[:3]
    prev_ref, low_ref = refs[3:5] if has_prev else (None, None)
    moment_ref = refs[names]
    outs = refs[names + 1 + passed :]
    pack_ref, residue_ref, diag_ref = outs[:3]
    stack_ref = refs[-1]
    at = pl.program_id(0)
    count, cols = basis_ref.shape
    height = moment_ref.shape[0]

    @pl.when(at == 0)
    def _():
        diag = (own_ref[:, cols:] + recv_ref[:, cols:])[:, :count]
        diag = 0.5 * (diag + diag.T)
        diag_ref[...] = pad_lanes(diag)
        residue = own_ref[:, :cols] + recv_ref[:, :cols] - fdot(diag, basis_ref[...])
        if has_prev:
            residue = residue - fdot(low_ref[:, :count], prev_ref[...])
        residue_ref[...] = residue
        high, low = halves(residue)
        stack_ref[:count] = high
        stack_ref[count:] = low
        pack_ref[:, width:] = pad_lanes(fdot_t(residue, residue))

    moment = moment_ref[...]
    if first:
        weight_ref, short_ref = refs[names + 1], outs[3]
        cols = weight_ref.shape[1]
        short_ref[:, :cols] = weight_ref[...]
        short_ref[:, cols:] = moment[:, first : first + cols].astype(jnp.bfloat16)
    else:
        short_ref = outs[3]
        short_ref[...] = moment[:, : short_ref.shape[1]].astype(jnp.bfloat16)
    pack_ref[:, pl.ds(pl.multiple_of(at * height, height), height)] = split_dot(stack_ref[...], moment, 1)


def reduced_call(own, recv, basis, prev, low, moment, gates, size, weight=None, first=0, ties=()):
    depth, cols = moment.shape
    count = basis.shape[0]
    height = min(256, depth)
    has_prev = prev is not None
    operands = (own, recv, basis) + ((prev, low) if has_prev else ()) + (moment,)
    specs = [VMEM] * (len(operands) - 1) + [pl.BlockSpec((height, cols), lambda i: (i, 0))]
    emitted = size
    if first:
        operands += (weight,)
        specs.append(pl.BlockSpec((height, size), lambda i: (i, first // size)))
        emitted = 2 * size
    return pl.pallas_call(
        functools.partial(reduced_kernel, has_prev, first, len(gates) + bool(first) + len(ties), depth),
        grid=(depth // height,),
        in_specs=specs + [ANY] * (len(gates) + len(ties)),
        out_specs=[VMEM, VMEM, VMEM, pl.BlockSpec((height, emitted), lambda i: (i, 0))] + [ANY] * len(gates),
        out_shape=[
            jax.ShapeDtypeStruct((count, depth + LANES), jnp.float32),
            jax.ShapeDtypeStruct((count, cols), jnp.float32),
            jax.ShapeDtypeStruct((count, LANES), jnp.float32),
            jax.ShapeDtypeStruct((depth, emitted), jnp.bfloat16),
        ]
        + [jax.ShapeDtypeStruct(at.shape, at.dtype) for at in gates],
        input_output_aliases={len(operands) + i: 4 + i for i in range(len(gates))},
        scratch_shapes=[pltpu.VMEM((2 * count, cols), jnp.bfloat16)],
        compiler_params=PARAMS,
    )(*operands, *gates, *ties)


def last_kernel(passed, own_ref, recv_ref, *refs):
    diag_ref, low_ref = refs[passed : passed + 2]
    count = own_ref.shape[0]
    depth = own_ref.shape[1] - LANES
    low_t, inverse = eliminate(own_ref[:, depth:] + recv_ref[:, depth:], count)
    low_ref[...] = low_t
    reduced = fdot(inverse, own_ref[:, :depth] + recv_ref[:, :depth])
    diag_ref[...] = pad_lanes(fdot_t(reduced, reduced))


def last_call(own, recv, gates, ties):
    shape = jax.ShapeDtypeStruct((own.shape[0], LANES), jnp.float32)
    return pl.pallas_call(
        functools.partial(last_kernel, len(gates) + len(ties)),
        in_specs=[VMEM, VMEM] + [ANY] * (len(gates) + len(ties)),
        out_specs=[VMEM, VMEM] + [ANY] * len(gates),
        out_shape=[shape, shape] + [jax.ShapeDtypeStruct(at.shape, at.dtype) for at in gates],
        input_output_aliases={2 + i: 2 + i for i in range(len(gates))},
        compiler_params=PARAMS,
    )(own, recv, *gates, *ties)


def top_kernel(steps, *refs):
    diag_refs = refs[: steps + 1]
    low_refs = refs[steps + 1 : 2 * steps]
    scaled_ref, rate_ref, krylov_ref = refs[-3:]
    count = diag_refs[0].shape[0]
    size = steps * count
    krylov_ref[...] = jnp.zeros_like(krylov_ref)
    for place in range(steps):
        first = place * count
        diag = diag_refs[place][:, :count]
        if place + 1 == steps:
            diag = diag + diag_refs[steps][:, :count]
        krylov_ref[first : first + count, first : first + count] = 0.5 * (diag + diag.T)
        if place + 1 < steps:
            second = first + count
            low_t = low_refs[place][:, :count]
            krylov_ref[second : second + count, first:second] = low_t
            krylov_ref[first:second, second : second + count] = low_t.T
    krylov = krylov_ref[...]
    power = krylov * (1.0 / jnp.max(jnp.abs(krylov), keepdims=True))
    for _ in range(SQUARINGS):
        power = fdot(power, power)
        power = power * (1.0 / jnp.max(jnp.abs(power), keepdims=True))
    tall = jnp.sum(power, axis=1, keepdims=True)
    wide = jnp.sum(power, axis=0, keepdims=True)
    tall = tall * (1.0 / jnp.sqrt(jnp.sum(tall * tall, keepdims=True)))
    wide = wide * (1.0 / jnp.sqrt(jnp.sum(wide * wide, keepdims=True)))
    top = jnp.sum(krylov * tall * wide, keepdims=True)
    scaled_ref[...] = krylov[:size, :size] / top
    rate_ref[...] = jnp.broadcast_to(1.0 / jnp.sqrt(top), rate_ref.shape)


def top_call(diags, lows, ties):
    steps = len(lows) + 1
    count = diags[0].shape[0]
    size = steps * count
    padded = -(-size // LANES) * LANES
    return pl.pallas_call(
        functools.partial(top_kernel, steps),
        in_specs=[VMEM] * (2 * steps) + [ANY] * len(ties),
        out_specs=[VMEM, VMEM],
        out_shape=[
            jax.ShapeDtypeStruct((size, size), jnp.float32),
            jax.ShapeDtypeStruct((8, LANES), jnp.float32),
        ],
        scratch_shapes=[pltpu.VMEM((padded, padded), jnp.float32)],
        compiler_params=PARAMS,
    )(*diags, *lows, *ties)


def step_kernel(ties, weight_ref, moment_ref, rate_ref, *refs):
    stepped = weight_ref[...].astype(jnp.float32) - moment_ref[...] * rate_ref[:1, :1]
    stepped = stepped.astype(jnp.bfloat16)
    for i, out_ref in enumerate(refs[ties:]):
        width = out_ref.shape[1]
        first = 0 if i == 0 else (i - 1) * width
        out_ref[...] = stepped[:, first : first + width]


def step_call(weight, moment, rate, first, width, pieces, ties):
    depth = weight.shape[0]
    height = min(512, depth)
    block = pl.BlockSpec((height, width), lambda r: (r, first // width))
    sizes = [width] + [width // pieces] * (pieces if pieces > 1 else 0)
    return pl.pallas_call(
        functools.partial(step_kernel, len(ties)),
        grid=(depth // height,),
        in_specs=[block, block, VMEM] + [ANY] * len(ties),
        out_specs=[pl.BlockSpec((height, size), lambda r: (r, 0)) for size in sizes],
        out_shape=[jax.ShapeDtypeStruct((depth, size), jnp.bfloat16) for size in sizes],
        compiler_params=LARGE,
        cost_estimate=BRIEF,
    )(weight, moment, rate, *ties)


def cross_kernel(pair_ref, rate_ref, tie_ref, out_ref):
    cols = out_ref.shape[1]
    stepped = pair_ref[:, :cols].astype(jnp.float32) - pair_ref[:, cols:].astype(jnp.float32) * rate_ref[:1, :1]
    out_ref[...] = stepped.astype(jnp.bfloat16)


def cross_call(pair, rate, tie):
    depth, cols = pair.shape
    height = min(512, depth)
    return pl.pallas_call(
        cross_kernel,
        grid=(depth // height,),
        in_specs=[pl.BlockSpec((height, cols), lambda r: (r, 0)), VMEM, ANY],
        out_specs=pl.BlockSpec((height, cols // 2), lambda r: (r, 0)),
        out_shape=jax.ShapeDtypeStruct((depth, cols // 2), jnp.bfloat16),
        compiler_params=LARGE,
        cost_estimate=BRIEF,
    )(pair, rate, tie)


def project_kernel(far, pieces, layout, early, in_place, ties, first, order_ref, *refs):
    count = len(layout)
    tokens = refs[:pieces]
    refs = refs[pieces:]
    weights = []
    for parts in layout:
        weights.append(list(zip(refs, parts)))
        refs = refs[len(parts) :]
    if early:
        moments, rate_ref, refs = refs[:count], refs[count], refs[count + 1 :]
    refs = refs[ties + (1 if in_place else 0) :]
    if not far:
        refs[1][...] = jnp.zeros(refs[1].shape, jnp.float32)
        refs = refs[:1] + refs[2:]
    out_ref, tokens_buf, weight_buf, moment_buf, total_ref, result_ref, sems, out_sem = refs
    depth, width = weight_buf.shape[1:]
    copies = []
    for k in range(count):
        step = []
        for i in range(pieces):
            if far:
                rows = tokens[i].shape[0]
                source = tokens[i].at[:, k * depth : (k + 1) * depth]
                target = tokens_buf.at[k, pl.ds(pl.multiple_of(order_ref[i], 16), rows), :]
            else:
                source = tokens[i].at[:, pl.ds(pl.multiple_of(order_ref[k] * depth, LANES), depth)]
                target = tokens_buf.at[k]
            step.append(pltpu.make_async_copy(source, target, sems.at[k, i]))
        filled = 0
        for i, (part, (at, size)) in enumerate(weights[k]):
            target = weight_buf.at[k, :, filled : filled + size]
            step.append(pltpu.make_async_copy(part.at[:, at : at + size], target, sems.at[k, pieces + i]))
            filled += size
        if early:
            at, size = layout[k][0]
            step.append(
                pltpu.make_async_copy(
                    moments[k].at[:, at : at + size], moment_buf.at[k], sems.at[k, pieces + 1]
                )
            )
        for copy in step:
            copy.start()
        copies.append(step)
    for k in range(count):
        for copy in copies[k]:
            copy.wait()
        block = weight_buf[k]
        if early:
            stepped = block.astype(jnp.float32) - moment_buf[k].astype(jnp.float32) * rate_ref[:1, :1]
            block = stepped.astype(jnp.bfloat16)
        part = jnp.dot(tokens_buf[k], block, preferred_element_type=jnp.float32)
        total_ref[...] = part if k == 0 else total_ref[...] + part
    if far:
        result_ref[...] = total_ref[...].astype(result_ref.dtype)
        copy = pltpu.make_async_copy(result_ref, out_ref, out_sem)
    else:
        copy = pltpu.make_async_copy(total_ref, out_ref.at[:, first : first + width], out_sem)
    copy.start()
    copy.wait()


def project_call(far, order, tokens, first, width, weights, moments, rate, ties=(), out=None, cols=None):
    early = moments is not None
    layout = tuple(tuple((at, size) for _, at, size in parts) for parts in weights)
    count = len(weights)
    depth = weights[0][0][0].shape[0]
    num_rows = sum(at.shape[0] for at in tokens)
    operands = list(tokens) + [part for parts in weights for part, _, _ in parts]
    specs = [ANY] * len(operands)
    if early:
        operands += list(moments) + [rate]
        specs += [ANY] * count + [VMEM]
    operands += list(ties)
    specs += [ANY] * len(ties)
    aliases = {}
    if far:
        out_shape = jax.ShapeDtypeStruct((num_rows, width), jnp.bfloat16)
    else:
        out_shape = [
            jax.ShapeDtypeStruct((num_rows, cols), jnp.float32),
            jax.ShapeDtypeStruct((8, LANES), jnp.float32),
        ]
        if out is not None:
            operands.append(out)
            specs.append(ANY)
            aliases = {len(operands): 0}
    return pl.pallas_call(
        functools.partial(
            project_kernel, far, len(tokens), layout, early, bool(aliases), len(ties), first
        ),
        grid_spec=pltpu.PrefetchScalarGridSpec(
            num_scalar_prefetch=1,
            grid=(1,),
            in_specs=specs,
            out_specs=ANY if far else [ANY, VMEM],
            scratch_shapes=[
                pltpu.VMEM((count, num_rows, depth), jnp.bfloat16),
                pltpu.VMEM((count, depth, width), jnp.bfloat16),
                pltpu.VMEM((count, depth, width) if early else (8, LANES), jnp.bfloat16),
                pltpu.VMEM((num_rows, width), jnp.float32),
                pltpu.VMEM((num_rows, width) if far else (8, LANES), jnp.bfloat16),
                pltpu.SemaphoreType.DMA((count, len(tokens) + 2)),
                pltpu.SemaphoreType.DMA,
            ],
        ),
        out_shape=out_shape,
        input_output_aliases=aliases,
        compiler_params=LARGE,
        cost_estimate=BRIEF,
    )(order, *operands)


def add_kernel(old_ref, far_ref, out_ref):
    out_ref[...] = old_ref[...] + far_ref[...].astype(jnp.float32)


def add_call(out, far, first):
    num_rows, width = far.shape
    block = pl.BlockSpec((num_rows, UNIT), lambda c: (0, first // UNIT + c))
    return pl.pallas_call(
        add_kernel,
        grid=(width // UNIT,),
        in_specs=[block, pl.BlockSpec((num_rows, UNIT), lambda c: (0, c))],
        out_specs=block,
        out_shape=jax.ShapeDtypeStruct(out.shape, out.dtype),
        input_output_aliases={0: 0},
        compiler_params=LARGE,
        cost_estimate=BRIEF,
    )(out, far)


def swap(values, axis, size, bit):
    return lax.ppermute(values, axis, [(at, at ^ bit) for at in range(size)])


def butterfly(values, axis, size):
    bit = 1
    while 2 * bit < size:
        values = values + swap(values, axis, size, bit)
        bit *= 2
    return values, swap(values, axis, size, bit)


def offsets(count):
    found = [0]
    bit = count // 2
    while bit:
        found = found + [at ^ bit for at in found]
        bit //= 2
    return found


def spread(piece, axis, size):
    parts = [piece]
    bit = 1
    while bit < size:
        parts = parts + [swap(part, axis, size, bit) for part in parts]
        bit *= 2
    return parts


def local(rows_n, cols_n, tokens, weight, momentum, gradient, probes):
    half = rows_n // 2
    far_bit, near_bit = half // 2, half // 4
    place = lax.axis_index("fsdp")
    low_at = lax.rem(place, half)
    side = lax.div(place, half)
    column_at = lax.axis_index("tensor")
    num_rows = tokens.shape[0]
    depth, cols = weight.shape
    rows = num_rows // cols_n // PARTS
    unit = cols // (sum(EARLY) + sum(LATE))
    early_cols = sum(EARLY) * unit

    def fswap(values, bit):
        return swap(values, "fsdp", rows_n, bit)

    def complete(parts):
        bit = near_bit // 2
        while bit:
            parts = parts + [[(fswap(at, bit), first, size) for at, first, size in part] for part in parts]
            bit //= 2
        return parts

    def blocks(own, across, beside):
        parts = [own, across, beside, fswap(across, near_bit)]
        return [part[0][0] for part in complete([[(part, 0, part.shape[1])] for part in parts])]

    def sum_over_rows(pack, gates, ties):
        passed = {}
        bit = 1
        while bit < half:
            pack, *passed[bit] = gate_call(pack, fswap(pack, bit), gates.get(bit, ()), ties.get(bit, ()))
            bit *= 2
        return pack, fswap(pack, half), passed

    mixed = jnp.stack([low_at ^ at for at in offsets(half)]).astype(jnp.int32)
    near_order = side * half + mixed
    pick_order = jnp.concatenate([(column_at * PARTS)[None], (1 - side) * half + mixed])
    far_order = jnp.stack(
        [(column_at ^ i) * PARTS * rows + part * rows for part in range(PARTS) for i in range(cols_n)]
    ).astype(jnp.int32)

    sent_0, sent_1, weight_own = pick_call(pick_order, tokens, weight, rows, half, early_cols)
    moment, short_1, pack = start_call(momentum, gradient, probes, sent_0, early_cols)
    weight_beside = fswap(weight_own, near_bit)
    weight_across = fswap(weight_own, far_bit)
    tokens_0 = fswap(sent_0, half)

    own, recv = butterfly(pack, "tensor", cols_n)
    pack, basis_1, _ = images_call(own, recv, probes, moment, True)
    own, recv, passed = sum_over_rows(
        pack, {1: [short_1, tokens_0], 2: [weight_across]}, {2: [weight_beside]}
    )
    short_1, tokens_0 = passed[1]
    weight_across, = passed[2]
    weight_parts = blocks(weight_own, weight_across, weight_beside)
    moment_beside = fswap(short_1, near_bit)
    token_parts = spread(tokens_0, "tensor", cols_n)
    pack, residue, diag_1, short_2, sent_1 = reduced_call(
        own, recv, basis_1, None, None, moment, [sent_1], early_cols
    )
    moment_across = fswap(short_2, far_bit)
    tokens_1 = fswap(sent_1, half)

    own, recv = butterfly(pack, "tensor", cols_n)
    pack, basis_2, low_1 = images_call(own, recv, residue, moment, False, weight_parts[3:])
    own, recv, passed = sum_over_rows(
        pack,
        {1: [moment_across, tokens_1]},
        {1: [moment_beside], 2: token_parts[1:]},
    )
    moment_across, token_1 = passed[1]
    moment_parts = blocks(short_1, moment_across, moment_beside)
    token_1_beside = swap(token_1, "tensor", cols_n, 1)
    token_1_across = swap(token_1, "tensor", cols_n, 2)
    pack, _, diag_2, pair = reduced_call(
        own, recv, basis_2, basis_1, low_1, moment, [], LATE[0] * unit, weight, early_cols, [token_1_across]
    )
    pair = fswap(pair, far_bit)

    own, recv = butterfly(pack, "tensor", cols_n)
    diag_3, low_2, token_1_beside = last_call(
        own, recv, [token_1_beside], []
    )
    token_parts += [token_1, token_1_beside, token_1_across, swap(token_1_beside, "tensor", cols_n, 2)]
    own, recv = butterfly(diag_3, "fsdp", rows_n)
    scaled, rate = top_call(
        [diag_1, diag_2, own, recv], [low_1, low_2], []
    )

    firsts, widths = [0], []
    for size in EARLY + LATE:
        widths.append(size * unit)
        firsts.append(firsts[-1] + size * unit)
    total = len(widths)
    partial, far = [], []

    def send(weights, first, width, *ties):
        partial.append(project_call(True, far_order, token_parts, first, width, *weights, ties=ties))
        far.append(fswap(partial[-1], half))

    def keep(weights, chunk, out, *ties):
        return project_call(
            False, near_order, [tokens], firsts[chunk], widths[chunk], *weights, ties=ties, out=out, cols=cols
        )

    def step(chunk, pieces, *ties):
        own = step_call(weight, moment, rate, firsts[chunk], widths[chunk], pieces, ties)
        return own[0], [fswap(at, far_bit) for at in (own[1:] or own)]

    def whole(array):
        return [(array, 0, array.shape[1])]

    early = ([[(part, firsts[0], widths[0])] for part in weight_parts], moment_parts, rate)
    own = step_call(weight, moment, rate, firsts[1], widths[1], 1, [token_parts[-1]])[0]
    beside = fswap(own, near_bit)
    following, across = step(2, 1, own)
    send(early, firsts[0], widths[0], following)
    passed = cross_call(pair, rate, partial[0])
    arrived = [beside, fswap(passed, near_bit)]
    weights = (complete([whole(at) for at in (own, passed, *arrived)]), None, None)
    own = following
    out, token = keep(early, 0, None, passed)
    for chunk in range(1, total):
        if chunk + 1 < total:
            width = widths[chunk + 1]
            split = width // unit if chunk + 2 == total else 1
            size = width // split
            merged = []
            for i in range(split):
                values = [(own, i * size, size)]
                if len(across) == 1:
                    values.append((across[0], i * size, size))
                else:
                    values += [at for part in across for at in whole(part)]
                ties = [*arrived, partial[-1], token, *merged]
                merged.append(merge_call(values, ties + far[:1] * (chunk == 1)))
            moved = [fswap(at, near_bit) for at in merged]
            send(weights, firsts[chunk], widths[chunk], merged[-1], far[chunk - 1])
            parts = [whole(own), [at for part in across for at in whole(part)]]
            parts += [[(at, first, size) for at in moved] for first in (0, size)]
            following = (complete(parts), None, None)
            if chunk + 2 < total:
                own, across = step(chunk + 2, 1, token)
            out = add_call(out, far[chunk - 1], firsts[chunk - 1])
            out, token = keep(weights, chunk, out, partial[-1], own)
            weights, arrived = following, moved
    for i in range(split):
        pieces = []
        for part in weights[0]:
            array, first, _ = part[i] if len(part) > 1 else part[0]
            pieces.append([(array, first if len(part) > 1 else i * size, size)])
        send((pieces, None, None), firsts[-2] + i * size, size, partial[-1], token)
    out = add_call(out, far[total - 2], firsts[total - 2])
    out, _ = keep(weights, total - 1, out, partial[-1])
    for i in range(split):
        out = add_call(out, far[total - 1 + i], firsts[total - 1] + i * size)
    return out, moment, scaled


def solution(mesh):
    return jax.shard_map(
        functools.partial(local, mesh.shape["fsdp"], mesh.shape["tensor"]),
        mesh=mesh,
        in_specs=(
            P("fsdp", None),
            P("fsdp", "tensor"),
            P("fsdp", "tensor"),
            P("fsdp", "tensor"),
            P(None, "tensor"),
        ),
        out_specs=(P("fsdp", "tensor"), P("fsdp", "tensor"), P()),
        check_vma=False,
    )
```

```python
import functools

import jax
import jax.numpy as jnp
from jax import lax
from jax.experimental import pallas as pl
from jax.experimental.pallas import tpu as pltpu
from jax.sharding import PartitionSpec as P

DECAY = 0.9
SQUARINGS = 5
LANES = 128
UNIT = 256
EARLY = (2,)
LATE = (2, 2, 2)
PARTS = 2

HIGHEST = lax.Precision.HIGHEST
LARGE = pltpu.CompilerParams(vmem_limit_bytes=53 * 1024 * 1024)
PARAMS = pltpu.CompilerParams(vmem_limit_bytes=24 * 1024 * 1024)
BRIEF = pl.CostEstimate(flops=0, bytes_accessed=0, transcendentals=0)
VMEM = pl.BlockSpec(memory_space=pltpu.VMEM)
ANY = pl.BlockSpec(memory_space=pl.ANY)


def fdot(left, right):
    return lax.dot_general(
        left, right, (((1,), (0,)), ((), ())), precision=HIGHEST, preferred_element_type=jnp.float32
    )


def fdot_t(left, right):
    return lax.dot_general(
        left, right, (((1,), (1,)), ((), ())), precision=HIGHEST, preferred_element_type=jnp.float32
    )


def halves(values):
    high = values.astype(jnp.bfloat16)
    return high, (values - high.astype(jnp.float32)).astype(jnp.bfloat16)


def split_dot(stacked, mat, contract):
    rows = stacked.shape[0] // 2
    mat_high, mat_low = halves(mat)
    dims = (((1,), (contract,)), ((), ()))
    first = lax.dot_general(stacked, mat_high, dims, preferred_element_type=jnp.float32)
    second = lax.dot_general(stacked[:rows], mat_low, dims, preferred_element_type=jnp.float32)
    return first[:rows] + first[rows:] + second


def eliminate(gram, count):
    rows = lax.broadcasted_iota(jnp.int32, (count, LANES), 0)
    lanes = lax.broadcasted_iota(jnp.int32, (count, LANES), 1)
    aug = jnp.where(lanes < count, gram, jnp.where(lanes - count == rows, 1.0, 0.0))
    for step in range(count):
        pivot = aug[step : step + 1, step : step + 1]
        factor = jnp.where(rows > step, aug[:, step : step + 1] * (1.0 / pivot), 0.0)
        aug = aug - factor * aug[step : step + 1, :]
    pivots = jnp.sum(jnp.where(lanes == rows, aug, 0.0), axis=1, keepdims=True)
    aug = aug * (1.0 / jnp.sqrt(pivots))
    low_t = jnp.where((lanes >= rows) & (lanes < count), aug, 0.0)
    return low_t, aug[:, count : 2 * count]


def pad_lanes(square):
    return jnp.concatenate(
        [square, jnp.zeros((square.shape[0], LANES - square.shape[1]), jnp.float32)], axis=1
    )


def pick_kernel(order_ref, token_0, token_1, weight_ref, sent_0, sent_1, early_ref):
    sent_0[...] = token_0[...]
    sent_1[...] = token_1[...]
    early_ref[...] = weight_ref[...]


def pick_call(order, tokens, weight, rows, count, early_cols):
    depth = weight.shape[0]
    height = depth // count
    sent = jax.ShapeDtypeStruct((rows, count * depth), tokens.dtype)
    weight_spec = pl.BlockSpec((height, early_cols), lambda i, order_ref: (i, 0))
    sent_spec = pl.BlockSpec((rows, depth), lambda i, order_ref: (0, i))
    return pl.pallas_call(
        pick_kernel,
        grid_spec=pltpu.PrefetchScalarGridSpec(
            num_scalar_prefetch=1,
            grid=(count,),
            in_specs=[
                pl.BlockSpec((rows, depth), lambda i, order_ref: (order_ref[0], order_ref[1 + i])),
                pl.BlockSpec((rows, depth), lambda i, order_ref: (order_ref[0] + 1, order_ref[1 + i])),
                weight_spec,
            ],
            out_specs=[sent_spec, sent_spec, weight_spec],
        ),
        out_shape=[sent, sent, jax.ShapeDtypeStruct((depth, early_cols), weight.dtype)],
        compiler_params=LARGE,
    )(order, tokens, tokens, weight)


def start_kernel(width, mom_ref, grad_ref, probes_ref, tie_ref, moment_ref, short_ref, pack_ref, stack_ref):
    at = pl.program_id(0)
    count = probes_ref.shape[0]
    height = mom_ref.shape[0]

    @pl.when(at == 0)
    def _():
        probes = probes_ref[...]
        high, low = halves(probes)
        stack_ref[:count] = high
        stack_ref[count:] = low
        pack_ref[:, width:] = pad_lanes(fdot_t(probes, probes))

    moment = DECAY * mom_ref[...] + grad_ref[...].astype(jnp.float32)
    moment_ref[...] = moment
    short_ref[...] = moment[:, : short_ref.shape[1]].astype(jnp.bfloat16)
    pack_ref[:, pl.ds(pl.multiple_of(at * height, height), height)] = split_dot(stack_ref[...], moment, 1)


def start_call(momentum, gradient, probes, tie, early_cols):
    depth, cols = momentum.shape
    count = probes.shape[0]
    height = min(256, depth)
    rows = pl.BlockSpec((height, cols), lambda i: (i, 0))
    return pl.pallas_call(
        functools.partial(start_kernel, depth),
        grid=(depth // height,),
        in_specs=[rows, rows, VMEM, ANY],
        out_specs=[rows, pl.BlockSpec((height, early_cols), lambda i: (i, 0)), VMEM],
        out_shape=[
            jax.ShapeDtypeStruct((depth, cols), jnp.float32),
            jax.ShapeDtypeStruct((depth, early_cols), jnp.bfloat16),
            jax.ShapeDtypeStruct((count, depth + LANES), jnp.float32),
        ],
        scratch_shapes=[pltpu.VMEM((2 * count, cols), jnp.bfloat16)],
        compiler_params=LARGE,
    )(momentum, gradient, probes, tie)


def gate_kernel(passed, own_ref, recv_ref, *refs):
    sum_ref = refs[-1 - passed]
    sum_ref[...] = own_ref[...] + recv_ref[...]


def gate_call(own, recv, gates=(), ties=()):
    shapes = [jax.ShapeDtypeStruct(at.shape, at.dtype) for at in (own, *gates)]
    first = 2 + len(ties)
    return pl.pallas_call(
        functools.partial(gate_kernel, len(gates)),
        in_specs=[VMEM, VMEM] + [ANY] * (len(gates) + len(ties)),
        out_specs=[VMEM] + [ANY] * len(gates),
        out_shape=shapes,
        input_output_aliases={first + i: 1 + i for i in range(len(gates))},
        compiler_params=PARAMS,
    )(own, recv, *ties, *gates)


def pass_kernel(*refs):
    pass


def pass_call(values, ties):
    return pl.pallas_call(
        pass_kernel,
        in_specs=[ANY] * (len(values) + len(ties)),
        out_specs=[ANY] * len(values),
        out_shape=[jax.ShapeDtypeStruct(at.shape, at.dtype) for at in values],
        input_output_aliases={i: i for i in range(len(values))},
        compiler_params=LARGE,
        cost_estimate=BRIEF,
    )(*values, *ties)


def merge_kernel(count, *refs):
    first = 0
    for value_ref in refs[:count]:
        width = value_ref.shape[1]
        refs[-1][:, first : first + width] = value_ref[...]
        first += width


def merge_call(values, ties):
    depth = values[0][0].shape[0]
    height = min(512, depth)
    cols = sum(width for _, _, width in values)

    def spec(first, width):
        return pl.BlockSpec((height, width), lambda r: (r, first // width))

    return pl.pallas_call(
        functools.partial(merge_kernel, len(values)),
        grid=(depth // height,),
        in_specs=[spec(first, width) for _, first, width in values] + [ANY] * len(ties),
        out_specs=spec(0, cols),
        out_shape=jax.ShapeDtypeStruct((depth, cols), values[0][0].dtype),
        compiler_params=LARGE,
        cost_estimate=BRIEF,
    )(*[array for array, _, _ in values], *ties)


def images_blocked(own_ref, recv_ref, block_ref, moment_ref, *refs):
    pack_ref, basis_ref, low_ref, stack_ref = refs[-4:]
    at = pl.program_id(0)
    count, cols = block_ref.shape
    depth = moment_ref.shape[0]
    width = moment_ref.shape[1]

    @pl.when(at == 0)
    def _():
        low_t, inverse = eliminate(own_ref[:, depth:] + recv_ref[:, depth:], count)
        low_ref[...] = low_t
        reduced = fdot(inverse, own_ref[:, :depth] + recv_ref[:, :depth])
        high, low = halves(reduced)
        stack_ref[:count] = high
        stack_ref[count:] = low
        pack_ref[:, cols:] = pad_lanes(fdot_t(reduced, reduced))
        basis_ref[...] = fdot(inverse, block_ref[...])

    pack_ref[:, pl.ds(pl.multiple_of(at * width, width), width)] = split_dot(stack_ref[...], moment_ref[...], 0)


def images_kernel(
    own_ref, recv_ref, block_ref, moment_ref, pack_ref, basis_ref, low_ref, held_ref, stack_ref, sems
):
    count, cols = block_ref.shape
    blocks, depth, width = held_ref.shape
    copies = [
        pltpu.make_async_copy(
            moment_ref.at[:, at * width : (at + 1) * width], held_ref.at[at], sems.at[at]
        )
        for at in range(blocks)
    ]
    for copy in copies:
        copy.start()
    low_t, inverse = eliminate(own_ref[:, depth:] + recv_ref[:, depth:], count)
    low_ref[...] = low_t
    reduced = fdot(inverse, own_ref[:, :depth] + recv_ref[:, :depth])
    high, low = halves(reduced)
    stack_ref[:count] = high
    stack_ref[count:] = low
    pack_ref[:, cols:] = pad_lanes(fdot_t(reduced, reduced))
    basis_ref[...] = fdot(inverse, block_ref[...])
    for at, copy in enumerate(copies):
        copy.wait()
        pack_ref[:, at * width : (at + 1) * width] = split_dot(stack_ref[...], held_ref[at], 0)


def images_call(own, recv, block, moment, fetch, ties=()):
    depth, cols = moment.shape
    count = block.shape[0]
    width = min(512, cols)
    stack = pltpu.VMEM((2 * count, depth), jnp.bfloat16)
    held = [
        pltpu.VMEM((cols // width, depth, width), jnp.float32),
        stack,
        pltpu.SemaphoreType.DMA((cols // width,)),
    ]
    return pl.pallas_call(
        images_kernel if fetch else images_blocked,
        grid=(1 if fetch else cols // width,),
        in_specs=[VMEM, VMEM, VMEM, ANY if fetch else pl.BlockSpec((depth, width), lambda i: (0, i))]
        + [ANY] * len(ties),
        out_specs=[VMEM, VMEM, VMEM],
        out_shape=[
            jax.ShapeDtypeStruct((count, cols + LANES), jnp.float32),
            jax.ShapeDtypeStruct((count, cols), jnp.float32),
            jax.ShapeDtypeStruct((count, LANES), jnp.float32),
        ],
        scratch_shapes=held if fetch else [stack],
        compiler_params=LARGE if fetch else PARAMS,
    )(own, recv, block, moment, *ties)


def reduced_kernel(has_prev, first, passed, width, *refs):
    names = 5 if has_prev else 3
    own_ref, recv_ref, basis_ref = refs[:3]
    prev_ref, low_ref = refs[3:5] if has_prev else (None, None)
    moment_ref = refs[names]
    outs = refs[names + 1 + passed :]
    pack_ref, residue_ref, diag_ref = outs[:3]
    stack_ref = refs[-1]
    at = pl.program_id(0)
    count, cols = basis_ref.shape
    height = moment_ref.shape[0]

    @pl.when(at == 0)
    def _():
        diag = (own_ref[:, cols:] + recv_ref[:, cols:])[:, :count]
        diag = 0.5 * (diag + diag.T)
        diag_ref[...] = pad_lanes(diag)
        residue = own_ref[:, :cols] + recv_ref[:, :cols] - fdot(diag, basis_ref[...])
        if has_prev:
            residue = residue - fdot(low_ref[:, :count], prev_ref[...])
        residue_ref[...] = residue
        high, low = halves(residue)
        stack_ref[:count] = high
        stack_ref[count:] = low
        pack_ref[:, width:] = pad_lanes(fdot_t(residue, residue))

    moment = moment_ref[...]
    if first:
        weight_ref, short_ref = refs[names + 1], outs[3]
        cols = weight_ref.shape[1]
        short_ref[:, :cols] = weight_ref[...]
        short_ref[:, cols:] = moment[:, first : first + cols].astype(jnp.bfloat16)
    else:
        short_ref = outs[3]
        short_ref[...] = moment[:, : short_ref.shape[1]].astype(jnp.bfloat16)
    pack_ref[:, pl.ds(pl.multiple_of(at * height, height), height)] = split_dot(stack_ref[...], moment, 1)


def reduced_call(own, recv, basis, prev, low, moment, gates, size, weight=None, first=0, ties=()):
    depth, cols = moment.shape
    count = basis.shape[0]
    height = min(256, depth)
    has_prev = prev is not None
    operands = (own, recv, basis) + ((prev, low) if has_prev else ()) + (moment,)
    specs = [VMEM] * (len(operands) - 1) + [pl.BlockSpec((height, cols), lambda i: (i, 0))]
    emitted = size
    if first:
        operands += (weight,)
        specs.append(pl.BlockSpec((height, size), lambda i: (i, first // size)))
        emitted = 2 * size
    return pl.pallas_call(
        functools.partial(reduced_kernel, has_prev, first, len(gates) + bool(first) + len(ties), depth),
        grid=(depth // height,),
        in_specs=specs + [ANY] * (len(gates) + len(ties)),
        out_specs=[VMEM, VMEM, VMEM, pl.BlockSpec((height, emitted), lambda i: (i, 0))] + [ANY] * len(gates),
        out_shape=[
            jax.ShapeDtypeStruct((count, depth + LANES), jnp.float32),
            jax.ShapeDtypeStruct((count, cols), jnp.float32),
            jax.ShapeDtypeStruct((count, LANES), jnp.float32),
            jax.ShapeDtypeStruct((depth, emitted), jnp.bfloat16),
        ]
        + [jax.ShapeDtypeStruct(at.shape, at.dtype) for at in gates],
        input_output_aliases={len(operands) + i: 4 + i for i in range(len(gates))},
        scratch_shapes=[pltpu.VMEM((2 * count, cols), jnp.bfloat16)],
        compiler_params=PARAMS,
    )(*operands, *gates, *ties)


def last_kernel(passed, own_ref, recv_ref, *refs):
    diag_ref, low_ref = refs[passed : passed + 2]
    count = own_ref.shape[0]
    depth = own_ref.shape[1] - LANES
    low_t, inverse = eliminate(own_ref[:, depth:] + recv_ref[:, depth:], count)
    low_ref[...] = low_t
    reduced = fdot(inverse, own_ref[:, :depth] + recv_ref[:, :depth])
    diag_ref[...] = pad_lanes(fdot_t(reduced, reduced))


def last_call(own, recv, gates, ties):
    shape = jax.ShapeDtypeStruct((own.shape[0], LANES), jnp.float32)
    return pl.pallas_call(
        functools.partial(last_kernel, len(gates) + len(ties)),
        in_specs=[VMEM, VMEM] + [ANY] * (len(gates) + len(ties)),
        out_specs=[VMEM, VMEM] + [ANY] * len(gates),
        out_shape=[shape, shape] + [jax.ShapeDtypeStruct(at.shape, at.dtype) for at in gates],
        input_output_aliases={2 + i: 2 + i for i in range(len(gates))},
        compiler_params=PARAMS,
    )(own, recv, *gates, *ties)


def top_kernel(steps, *refs):
    diag_refs = refs[: steps + 1]
    low_refs = refs[steps + 1 : 2 * steps]
    scaled_ref, rate_ref, krylov_ref = refs[-3:]
    count = diag_refs[0].shape[0]
    size = steps * count
    krylov_ref[...] = jnp.zeros_like(krylov_ref)
    for place in range(steps):
        first = place * count
        diag = diag_refs[place][:, :count]
        if place + 1 == steps:
            diag = diag + diag_refs[steps][:, :count]
        krylov_ref[first : first + count, first : first + count] = 0.5 * (diag + diag.T)
        if place + 1 < steps:
            second = first + count
            low_t = low_refs[place][:, :count]
            krylov_ref[second : second + count, first:second] = low_t
            krylov_ref[first:second, second : second + count] = low_t.T
    krylov = krylov_ref[...]
    power = krylov * (1.0 / jnp.max(jnp.abs(krylov), keepdims=True))
    for _ in range(SQUARINGS):
        power = fdot(power, power)
        power = power * (1.0 / jnp.max(jnp.abs(power), keepdims=True))
    tall = jnp.sum(power, axis=1, keepdims=True)
    wide = jnp.sum(power, axis=0, keepdims=True)
    tall = tall * (1.0 / jnp.sqrt(jnp.sum(tall * tall, keepdims=True)))
    wide = wide * (1.0 / jnp.sqrt(jnp.sum(wide * wide, keepdims=True)))
    top = jnp.sum(krylov * tall * wide, keepdims=True)
    scaled_ref[...] = krylov[:size, :size] / top
    rate_ref[...] = jnp.broadcast_to(1.0 / jnp.sqrt(top), rate_ref.shape)


def top_call(diags, lows, ties):
    steps = len(lows) + 1
    count = diags[0].shape[0]
    size = steps * count
    padded = -(-size // LANES) * LANES
    return pl.pallas_call(
        functools.partial(top_kernel, steps),
        in_specs=[VMEM] * (2 * steps) + [ANY] * len(ties),
        out_specs=[VMEM, VMEM],
        out_shape=[
            jax.ShapeDtypeStruct((size, size), jnp.float32),
            jax.ShapeDtypeStruct((8, LANES), jnp.float32),
        ],
        scratch_shapes=[pltpu.VMEM((padded, padded), jnp.float32)],
        compiler_params=PARAMS,
    )(*diags, *lows, *ties)


def step_kernel(ties, weight_ref, moment_ref, rate_ref, *refs):
    stepped = weight_ref[...].astype(jnp.float32) - moment_ref[...] * rate_ref[:1, :1]
    stepped = stepped.astype(jnp.bfloat16)
    for i, out_ref in enumerate(refs[ties:]):
        width = out_ref.shape[1]
        first = 0 if i == 0 else (i - 1) * width
        out_ref[...] = stepped[:, first : first + width]


def step_call(weight, moment, rate, first, width, pieces, ties):
    depth = weight.shape[0]
    height = min(512, depth)
    block = pl.BlockSpec((height, width), lambda r: (r, first // width))
    sizes = [width] + [width // pieces] * (pieces if pieces > 1 else 0)
    return pl.pallas_call(
        functools.partial(step_kernel, len(ties)),
        grid=(depth // height,),
        in_specs=[block, block, VMEM] + [ANY] * len(ties),
        out_specs=[pl.BlockSpec((height, size), lambda r: (r, 0)) for size in sizes],
        out_shape=[jax.ShapeDtypeStruct((depth, size), jnp.bfloat16) for size in sizes],
        compiler_params=LARGE,
        cost_estimate=BRIEF,
    )(weight, moment, rate, *ties)


def cross_kernel(pair_ref, rate_ref, tie_ref, out_ref):
    cols = out_ref.shape[1]
    stepped = pair_ref[:, :cols].astype(jnp.float32) - pair_ref[:, cols:].astype(jnp.float32) * rate_ref[:1, :1]
    out_ref[...] = stepped.astype(jnp.bfloat16)


def cross_call(pair, rate, tie):
    depth, cols = pair.shape
    height = min(512, depth)
    return pl.pallas_call(
        cross_kernel,
        grid=(depth // height,),
        in_specs=[pl.BlockSpec((height, cols), lambda r: (r, 0)), VMEM, ANY],
        out_specs=pl.BlockSpec((height, cols // 2), lambda r: (r, 0)),
        out_shape=jax.ShapeDtypeStruct((depth, cols // 2), jnp.bfloat16),
        compiler_params=LARGE,
        cost_estimate=BRIEF,
    )(pair, rate, tie)


def project_kernel(far, pieces, layout, early, in_place, ties, first, order_ref, *refs):
    count = len(layout)
    tokens = refs[:pieces]
    refs = refs[pieces:]
    weights = []
    for parts in layout:
        weights.append(list(zip(refs, parts)))
        refs = refs[len(parts) :]
    if early:
        moments, rate_ref, refs = refs[:count], refs[count], refs[count + 1 :]
    refs = refs[ties + (1 if in_place else 0) :]
    if not far:
        refs[1][...] = jnp.zeros(refs[1].shape, jnp.float32)
        refs = refs[:1] + refs[2:]
    out_ref, tokens_buf, weight_buf, moment_buf, total_ref, result_ref, sems, out_sem = refs
    depth, width = weight_buf.shape[1:]
    copies = []
    for k in range(count):
        step = []
        for i in range(pieces):
            if far:
                rows = tokens[i].shape[0]
                source = tokens[i].at[:, k * depth : (k + 1) * depth]
                target = tokens_buf.at[k, pl.ds(pl.multiple_of(order_ref[i], 16), rows), :]
            else:
                source = tokens[i].at[:, pl.ds(pl.multiple_of(order_ref[k] * depth, LANES), depth)]
                target = tokens_buf.at[k]
            step.append(pltpu.make_async_copy(source, target, sems.at[k, i]))
        filled = 0
        for i, (part, (at, size)) in enumerate(weights[k]):
            target = weight_buf.at[k, :, filled : filled + size]
            step.append(pltpu.make_async_copy(part.at[:, at : at + size], target, sems.at[k, pieces + i]))
            filled += size
        if early:
            at, size = layout[k][0]
            step.append(
                pltpu.make_async_copy(
                    moments[k].at[:, at : at + size], moment_buf.at[k], sems.at[k, pieces + 1]
                )
            )
        for copy in step:
            copy.start()
        copies.append(step)
    for k in range(count):
        for copy in copies[k]:
            copy.wait()
        block = weight_buf[k]
        if early:
            stepped = block.astype(jnp.float32) - moment_buf[k].astype(jnp.float32) * rate_ref[:1, :1]
            block = stepped.astype(jnp.bfloat16)
        part = jnp.dot(tokens_buf[k], block, preferred_element_type=jnp.float32)
        total_ref[...] = part if k == 0 else total_ref[...] + part
    if far:
        result_ref[...] = total_ref[...].astype(result_ref.dtype)
        copy = pltpu.make_async_copy(result_ref, out_ref, out_sem)
    else:
        copy = pltpu.make_async_copy(total_ref, out_ref.at[:, first : first + width], out_sem)
    copy.start()
    copy.wait()


def project_call(far, order, tokens, first, width, weights, moments, rate, ties=(), out=None, cols=None):
    early = moments is not None
    layout = tuple(tuple((at, size) for _, at, size in parts) for parts in weights)
    count = len(weights)
    depth = weights[0][0][0].shape[0]
    num_rows = sum(at.shape[0] for at in tokens)
    operands = list(tokens) + [part for parts in weights for part, _, _ in parts]
    specs = [ANY] * len(operands)
    if early:
        operands += list(moments) + [rate]
        specs += [ANY] * count + [VMEM]
    operands += list(ties)
    specs += [ANY] * len(ties)
    aliases = {}
    if far:
        out_shape = jax.ShapeDtypeStruct((num_rows, width), jnp.bfloat16)
    else:
        out_shape = [
            jax.ShapeDtypeStruct((num_rows, cols), jnp.float32),
            jax.ShapeDtypeStruct((8, LANES), jnp.float32),
        ]
        if out is not None:
            operands.append(out)
            specs.append(ANY)
            aliases = {len(operands): 0}
    return pl.pallas_call(
        functools.partial(
            project_kernel, far, len(tokens), layout, early, bool(aliases), len(ties), first
        ),
        grid_spec=pltpu.PrefetchScalarGridSpec(
            num_scalar_prefetch=1,
            grid=(1,),
            in_specs=specs,
            out_specs=ANY if far else [ANY, VMEM],
            scratch_shapes=[
                pltpu.VMEM((count, num_rows, depth), jnp.bfloat16),
                pltpu.VMEM((count, depth, width), jnp.bfloat16),
                pltpu.VMEM((count, depth, width) if early else (8, LANES), jnp.bfloat16),
                pltpu.VMEM((num_rows, width), jnp.float32),
                pltpu.VMEM((num_rows, width) if far else (8, LANES), jnp.bfloat16),
                pltpu.SemaphoreType.DMA((count, len(tokens) + 2)),
                pltpu.SemaphoreType.DMA,
            ],
        ),
        out_shape=out_shape,
        input_output_aliases=aliases,
        compiler_params=LARGE,
        cost_estimate=BRIEF,
    )(order, *operands)


def add_kernel(old_ref, far_ref, out_ref):
    out_ref[...] = old_ref[...] + far_ref[...].astype(jnp.float32)


def add_call(out, far, first):
    num_rows, width = far.shape
    block = pl.BlockSpec((num_rows, UNIT), lambda c: (0, first // UNIT + c))
    return pl.pallas_call(
        add_kernel,
        grid=(width // UNIT,),
        in_specs=[block, pl.BlockSpec((num_rows, UNIT), lambda c: (0, c))],
        out_specs=block,
        out_shape=jax.ShapeDtypeStruct(out.shape, out.dtype),
        input_output_aliases={0: 0},
        compiler_params=LARGE,
        cost_estimate=BRIEF,
    )(out, far)


def swap(values, axis, size, bit):
    return lax.ppermute(values, axis, [(at, at ^ bit) for at in range(size)])


def butterfly(values, axis, size):
    bit = 1
    while 2 * bit < size:
        values = values + swap(values, axis, size, bit)
        bit *= 2
    return values, swap(values, axis, size, bit)


def offsets(count):
    found = [0]
    bit = count // 2
    while bit:
        found = found + [at ^ bit for at in found]
        bit //= 2
    return found


def spread(piece, axis, size):
    parts = [piece]
    bit = 1
    while bit < size:
        parts = parts + [swap(part, axis, size, bit) for part in parts]
        bit *= 2
    return parts


def local(rows_n, cols_n, tokens, weight, momentum, gradient, probes):
    half = rows_n // 2
    far_bit, near_bit = half // 2, half // 4
    place = lax.axis_index("fsdp")
    low_at = lax.rem(place, half)
    side = lax.div(place, half)
    column_at = lax.axis_index("tensor")
    num_rows = tokens.shape[0]
    depth, cols = weight.shape
    rows = num_rows // cols_n // PARTS
    unit = cols // (sum(EARLY) + sum(LATE))
    early_cols = sum(EARLY) * unit

    def fswap(values, bit):
        return swap(values, "fsdp", rows_n, bit)

    def complete(parts):
        bit = near_bit // 2
        while bit:
            parts = parts + [[(fswap(at, bit), first, size) for at, first, size in part] for part in parts]
            bit //= 2
        return parts

    def blocks(own, across, beside):
        parts = [own, across, beside, fswap(across, near_bit)]
        return [part[0][0] for part in complete([[(part, 0, part.shape[1])] for part in parts])]

    def sum_over_rows(pack, gates, ties):
        passed = {}
        bit = 1
        while bit < half:
            pack, *passed[bit] = gate_call(pack, fswap(pack, bit), gates.get(bit, ()), ties.get(bit, ()))
            bit *= 2
        return pack, fswap(pack, half), passed

    mixed = jnp.stack([low_at ^ at for at in offsets(half)]).astype(jnp.int32)
    near_order = side * half + mixed
    pick_order = jnp.concatenate([(column_at * PARTS)[None], (1 - side) * half + mixed])
    far_order = jnp.stack(
        [(column_at ^ i) * PARTS * rows + part * rows for part in range(PARTS) for i in range(cols_n)]
    ).astype(jnp.int32)

    sent_0, sent_1, weight_own = pick_call(pick_order, tokens, weight, rows, half, early_cols)
    moment, short_1, pack = start_call(momentum, gradient, probes, sent_0, early_cols)
    weight_beside = fswap(weight_own, near_bit)
    weight_across = fswap(weight_own, far_bit)
    tokens_0 = fswap(sent_0, half)

    own, recv = butterfly(pack, "tensor", cols_n)
    pack, basis_1, _ = images_call(own, recv, probes, moment, True)
    own, recv, passed = sum_over_rows(
        pack, {1: [short_1, tokens_0], 2: [weight_across]}, {2: [weight_beside]}
    )
    short_1, tokens_0 = passed[1]
    weight_across, = passed[2]
    weight_parts = blocks(weight_own, weight_across, weight_beside)
    moment_beside = fswap(short_1, near_bit)
    token_parts = spread(tokens_0, "tensor", cols_n)
    pack, residue, diag_1, short_2, sent_1 = reduced_call(
        own, recv, basis_1, None, None, moment, [sent_1], early_cols
    )
    moment_across = fswap(short_2, far_bit)
    tokens_1 = fswap(sent_1, half)

    own, recv = butterfly(pack, "tensor", cols_n)
    pack, basis_2, low_1 = images_call(own, recv, residue, moment, False, weight_parts[3:])
    own, recv, passed = sum_over_rows(
        pack,
        {1: [moment_across, tokens_1]},
        {1: [moment_beside], 2: token_parts[1:]},
    )
    moment_across, token_1 = passed[1]
    moment_parts = blocks(short_1, moment_across, moment_beside)
    token_1_beside = swap(token_1, "tensor", cols_n, 1)
    token_1_across = swap(token_1, "tensor", cols_n, 2)
    pack, _, diag_2, pair = reduced_call(
        own, recv, basis_2, basis_1, low_1, moment, [], unit, weight, early_cols, [token_1_across]
    )
    pair = fswap(pair, far_bit)

    own, recv = butterfly(pack, "tensor", cols_n)
    diag_3, low_2, token_1_beside = last_call(
        own, recv, [token_1_beside], moment_parts[3:]
    )
    token_parts += [token_1, token_1_beside, token_1_across, swap(token_1_beside, "tensor", cols_n, 2)]
    own, recv, _ = sum_over_rows(diag_3, {}, {1: [pair]})
    scaled, rate = top_call(
        [diag_1, diag_2, own, recv], [low_1, low_2], []
    )

    firsts, widths = [0], []
    for size in EARLY + LATE:
        widths.append(size * unit)
        firsts.append(firsts[-1] + size * unit)
    total = len(widths)
    partial, far = [], []

    def send(weights, first, width, *ties):
        partial.append(project_call(True, far_order, token_parts, first, width, *weights, ties=ties))
        far.append(fswap(partial[-1], half))

    def keep(weights, chunk, out, *ties):
        return project_call(
            False, near_order, [tokens], firsts[chunk], widths[chunk], *weights, ties=ties, out=out, cols=cols
        )

    def step(chunk, pieces, *ties):
        own = step_call(weight, moment, rate, firsts[chunk], widths[chunk], pieces, ties)
        return own[0], [fswap(at, far_bit) for at in (own[1:] or own)]

    def whole(array):
        return [(array, 0, array.shape[1])]

    early = ([[(part, firsts[0], widths[0])] for part in weight_parts], moment_parts, rate)
    own, _, *rest = step_call(weight, moment, rate, firsts[1], widths[1], widths[1] // unit, [token_parts[-1]])
    across = [fswap(at, far_bit) for at in rest]
    beside = fswap(own, near_bit)
    following, later = step(2, 1, own)
    send(early, firsts[0], widths[0], following)
    passed = [cross_call(pair, rate, partial[0])]
    passed += pass_call(across, [passed[0]])
    moved = [fswap(at, near_bit) for at in passed]
    parts = [whole(own), [at for part in passed for at in whole(part)], whole(beside)]
    parts.append([at for part in moved for at in whole(part)])
    weights = (complete(parts), None, None)
    arrived = [beside, *moved]
    own, across = following, later
    out, token = keep(early, 0, None, passed[0])
    for chunk in range(1, total):
        if chunk + 1 < total:
            width = widths[chunk + 1]
            split = width // unit if chunk + 2 == total else 1
            size = width // split
            merged = []
            for i in range(split):
                values = [(own, i * size, size)]
                if len(across) == 1:
                    values.append((across[0], i * size, size))
                else:
                    values += [at for part in across for at in whole(part)]
                ties = [*arrived, partial[-1], token, *merged]
                merged.append(merge_call(values, ties + far[:1] * (chunk == 1)))
            moved = [fswap(at, near_bit) for at in merged]
            send(weights, firsts[chunk], widths[chunk], merged[-1], far[chunk - 1])
            parts = [whole(own), [at for part in across for at in whole(part)]]
            parts += [[(at, first, size) for at in moved] for first in (0, size)]
            following = (complete(parts), None, None)
            if chunk + 2 < total:
                own, across = step(chunk + 2, 1, token)
            out = add_call(out, far[chunk - 1], firsts[chunk - 1])
            out, token = keep(weights, chunk, out, partial[-1], own)
            weights, arrived = following, moved
    for i in range(split):
        pieces = []
        for part in weights[0]:
            array, first, _ = part[i] if len(part) > 1 else part[0]
            pieces.append([(array, first if len(part) > 1 else i * size, size)])
        send((pieces, None, None), firsts[-2] + i * size, size, partial[-1], token)
    out = add_call(out, far[total - 2], firsts[total - 2])
    out, _ = keep(weights, total - 1, out, partial[-1])
    for i in range(split):
        out = add_call(out, far[total - 1 + i], firsts[total - 1] + i * size)
    return out, moment, scaled


def solution(mesh):
    return jax.shard_map(
        functools.partial(local, mesh.shape["fsdp"], mesh.shape["tensor"]),
        mesh=mesh,
        in_specs=(
            P("fsdp", None),
            P("fsdp", "tensor"),
            P("fsdp", "tensor"),
            P("fsdp", "tensor"),
            P(None, "tensor"),
        ),
        out_specs=(P("fsdp", "tensor"), P("fsdp", "tensor"), P()),
        check_vma=False,
    )
```

```python
import functools

import jax
import jax.numpy as jnp
from jax import lax
from jax.experimental import pallas as pl
from jax.experimental.pallas import tpu as pltpu
from jax.sharding import PartitionSpec as P

DECAY = 0.9
SQUARINGS = 5
LANES = 128
UNIT = 256
EARLY = (2,)
EXTRA = 1
LATE = (2, 2, 1)
PARTS = 2

HIGHEST = lax.Precision.HIGHEST
LARGE = pltpu.CompilerParams(vmem_limit_bytes=53 * 1024 * 1024)
PARAMS = pltpu.CompilerParams(vmem_limit_bytes=24 * 1024 * 1024)
BRIEF = pl.CostEstimate(flops=0, bytes_accessed=0, transcendentals=0)
VMEM = pl.BlockSpec(memory_space=pltpu.VMEM)
ANY = pl.BlockSpec(memory_space=pl.ANY)


def fdot(left, right):
    return lax.dot_general(
        left, right, (((1,), (0,)), ((), ())), precision=HIGHEST, preferred_element_type=jnp.float32
    )


def fdot_t(left, right):
    return lax.dot_general(
        left, right, (((1,), (1,)), ((), ())), precision=HIGHEST, preferred_element_type=jnp.float32
    )


def halves(values):
    high = values.astype(jnp.bfloat16)
    return high, (values - high.astype(jnp.float32)).astype(jnp.bfloat16)


def split_dot(stacked, mat, contract):
    rows = stacked.shape[0] // 2
    mat_high, mat_low = halves(mat)
    dims = (((1,), (contract,)), ((), ()))
    first = lax.dot_general(stacked, mat_high, dims, preferred_element_type=jnp.float32)
    second = lax.dot_general(stacked[:rows], mat_low, dims, preferred_element_type=jnp.float32)
    return first[:rows] + first[rows:] + second


def eliminate(gram, count):
    rows = lax.broadcasted_iota(jnp.int32, (count, LANES), 0)
    lanes = lax.broadcasted_iota(jnp.int32, (count, LANES), 1)
    aug = jnp.where(lanes < count, gram, jnp.where(lanes - count == rows, 1.0, 0.0))
    for step in range(count):
        pivot = aug[step : step + 1, step : step + 1]
        factor = jnp.where(rows > step, aug[:, step : step + 1] * (1.0 / pivot), 0.0)
        aug = aug - factor * aug[step : step + 1, :]
    pivots = jnp.sum(jnp.where(lanes == rows, aug, 0.0), axis=1, keepdims=True)
    aug = aug * (1.0 / jnp.sqrt(pivots))
    low_t = jnp.where((lanes >= rows) & (lanes < count), aug, 0.0)
    return low_t, aug[:, count : 2 * count]


def pad_lanes(square):
    return jnp.concatenate(
        [square, jnp.zeros((square.shape[0], LANES - square.shape[1]), jnp.float32)], axis=1
    )


def pick_kernel(order_ref, token_0, token_1, weight_ref, sent_0, sent_1, early_ref):
    sent_0[...] = token_0[...]
    sent_1[...] = token_1[...]
    early_ref[...] = weight_ref[...]


def pick_call(order, tokens, weight, rows, count, early_cols):
    depth = weight.shape[0]
    height = depth // count
    sent = jax.ShapeDtypeStruct((rows, count * depth), tokens.dtype)
    weight_spec = pl.BlockSpec((height, early_cols), lambda i, order_ref: (i, 0))
    sent_spec = pl.BlockSpec((rows, depth), lambda i, order_ref: (0, i))
    return pl.pallas_call(
        pick_kernel,
        grid_spec=pltpu.PrefetchScalarGridSpec(
            num_scalar_prefetch=1,
            grid=(count,),
            in_specs=[
                pl.BlockSpec((rows, depth), lambda i, order_ref: (order_ref[0], order_ref[1 + i])),
                pl.BlockSpec((rows, depth), lambda i, order_ref: (order_ref[0] + 1, order_ref[1 + i])),
                weight_spec,
            ],
            out_specs=[sent_spec, sent_spec, weight_spec],
        ),
        out_shape=[sent, sent, jax.ShapeDtypeStruct((depth, early_cols), weight.dtype)],
        compiler_params=LARGE,
    )(order, tokens, tokens, weight)


def start_kernel(width, mom_ref, grad_ref, probes_ref, tie_ref, moment_ref, short_ref, pack_ref, stack_ref):
    at = pl.program_id(0)
    count = probes_ref.shape[0]
    height = mom_ref.shape[0]

    @pl.when(at == 0)
    def _():
        probes = probes_ref[...]
        high, low = halves(probes)
        stack_ref[:count] = high
        stack_ref[count:] = low
        pack_ref[:, width:] = pad_lanes(fdot_t(probes, probes))

    moment = DECAY * mom_ref[...] + grad_ref[...].astype(jnp.float32)
    moment_ref[...] = moment
    short_ref[...] = moment[:, : short_ref.shape[1]].astype(jnp.bfloat16)
    pack_ref[:, pl.ds(pl.multiple_of(at * height, height), height)] = split_dot(stack_ref[...], moment, 1)


def start_call(momentum, gradient, probes, tie, early_cols):
    depth, cols = momentum.shape
    count = probes.shape[0]
    height = min(256, depth)
    rows = pl.BlockSpec((height, cols), lambda i: (i, 0))
    return pl.pallas_call(
        functools.partial(start_kernel, depth),
        grid=(depth // height,),
        in_specs=[rows, rows, VMEM, ANY],
        out_specs=[rows, pl.BlockSpec((height, early_cols), lambda i: (i, 0)), VMEM],
        out_shape=[
            jax.ShapeDtypeStruct((depth, cols), jnp.float32),
            jax.ShapeDtypeStruct((depth, early_cols), jnp.bfloat16),
            jax.ShapeDtypeStruct((count, depth + LANES), jnp.float32),
        ],
        scratch_shapes=[pltpu.VMEM((2 * count, cols), jnp.bfloat16)],
        compiler_params=LARGE,
    )(momentum, gradient, probes, tie)


def gate_kernel(passed, own_ref, recv_ref, *refs):
    sum_ref = refs[-1 - passed]
    sum_ref[...] = own_ref[...] + recv_ref[...]


def gate_call(own, recv, gates=(), ties=()):
    shapes = [jax.ShapeDtypeStruct(at.shape, at.dtype) for at in (own, *gates)]
    first = 2 + len(ties)
    return pl.pallas_call(
        functools.partial(gate_kernel, len(gates)),
        in_specs=[VMEM, VMEM] + [ANY] * (len(gates) + len(ties)),
        out_specs=[VMEM] + [ANY] * len(gates),
        out_shape=shapes,
        input_output_aliases={first + i: 1 + i for i in range(len(gates))},
        compiler_params=PARAMS,
    )(own, recv, *ties, *gates)


def pass_kernel(*refs):
    pass


def pass_call(values, ties):
    return pl.pallas_call(
        pass_kernel,
        in_specs=[ANY] * (len(values) + len(ties)),
        out_specs=[ANY] * len(values),
        out_shape=[jax.ShapeDtypeStruct(at.shape, at.dtype) for at in values],
        input_output_aliases={i: i for i in range(len(values))},
        compiler_params=LARGE,
        cost_estimate=BRIEF,
    )(*values, *ties)


def merge_kernel(count, *refs):
    first = 0
    for value_ref in refs[:count]:
        width = value_ref.shape[1]
        refs[-1][:, first : first + width] = value_ref[...]
        first += width


def merge_call(values, ties):
    depth = values[0][0].shape[0]
    height = min(512, depth)
    cols = sum(width for _, _, width in values)

    def spec(first, width):
        return pl.BlockSpec((height, width), lambda r: (r, first // width))

    return pl.pallas_call(
        functools.partial(merge_kernel, len(values)),
        grid=(depth // height,),
        in_specs=[spec(first, width) for _, first, width in values] + [ANY] * len(ties),
        out_specs=spec(0, cols),
        out_shape=jax.ShapeDtypeStruct((depth, cols), values[0][0].dtype),
        compiler_params=LARGE,
        cost_estimate=BRIEF,
    )(*[array for array, _, _ in values], *ties)


def images_blocked(own_ref, recv_ref, block_ref, moment_ref, *refs):
    pack_ref, basis_ref, low_ref, stack_ref = refs[-4:]
    at = pl.program_id(0)
    count, cols = block_ref.shape
    depth = moment_ref.shape[0]
    width = moment_ref.shape[1]

    @pl.when(at == 0)
    def _():
        low_t, inverse = eliminate(own_ref[:, depth:] + recv_ref[:, depth:], count)
        low_ref[...] = low_t
        reduced = fdot(inverse, own_ref[:, :depth] + recv_ref[:, :depth])
        high, low = halves(reduced)
        stack_ref[:count] = high
        stack_ref[count:] = low
        pack_ref[:, cols:] = pad_lanes(fdot_t(reduced, reduced))
        basis_ref[...] = fdot(inverse, block_ref[...])

    pack_ref[:, pl.ds(pl.multiple_of(at * width, width), width)] = split_dot(stack_ref[...], moment_ref[...], 0)


def images_kernel(
    own_ref, recv_ref, block_ref, moment_ref, pack_ref, basis_ref, low_ref, held_ref, stack_ref, sems
):
    count, cols = block_ref.shape
    blocks, depth, width = held_ref.shape
    copies = [
        pltpu.make_async_copy(
            moment_ref.at[:, at * width : (at + 1) * width], held_ref.at[at], sems.at[at]
        )
        for at in range(blocks)
    ]
    for copy in copies:
        copy.start()
    low_t, inverse = eliminate(own_ref[:, depth:] + recv_ref[:, depth:], count)
    low_ref[...] = low_t
    reduced = fdot(inverse, own_ref[:, :depth] + recv_ref[:, :depth])
    high, low = halves(reduced)
    stack_ref[:count] = high
    stack_ref[count:] = low
    pack_ref[:, cols:] = pad_lanes(fdot_t(reduced, reduced))
    basis_ref[...] = fdot(inverse, block_ref[...])
    for at, copy in enumerate(copies):
        copy.wait()
        pack_ref[:, at * width : (at + 1) * width] = split_dot(stack_ref[...], held_ref[at], 0)


def images_call(own, recv, block, moment, fetch, ties=()):
    depth, cols = moment.shape
    count = block.shape[0]
    width = min(512, cols)
    stack = pltpu.VMEM((2 * count, depth), jnp.bfloat16)
    held = [
        pltpu.VMEM((cols // width, depth, width), jnp.float32),
        stack,
        pltpu.SemaphoreType.DMA((cols // width,)),
    ]
    return pl.pallas_call(
        images_kernel if fetch else images_blocked,
        grid=(1 if fetch else cols // width,),
        in_specs=[VMEM, VMEM, VMEM, ANY if fetch else pl.BlockSpec((depth, width), lambda i: (0, i))]
        + [ANY] * len(ties),
        out_specs=[VMEM, VMEM, VMEM],
        out_shape=[
            jax.ShapeDtypeStruct((count, cols + LANES), jnp.float32),
            jax.ShapeDtypeStruct((count, cols), jnp.float32),
            jax.ShapeDtypeStruct((count, LANES), jnp.float32),
        ],
        scratch_shapes=held if fetch else [stack],
        compiler_params=LARGE if fetch else PARAMS,
    )(own, recv, block, moment, *ties)


def reduced_kernel(has_prev, first, passed, width, *refs):
    names = 5 if has_prev else 3
    own_ref, recv_ref, basis_ref = refs[:3]
    prev_ref, low_ref = refs[3:5] if has_prev else (None, None)
    moment_ref = refs[names]
    outs = refs[names + 1 + passed :]
    pack_ref, residue_ref, diag_ref = outs[:3]
    stack_ref = refs[-1]
    at = pl.program_id(0)
    count, cols = basis_ref.shape
    height = moment_ref.shape[0]

    @pl.when(at == 0)
    def _():
        diag = (own_ref[:, cols:] + recv_ref[:, cols:])[:, :count]
        diag = 0.5 * (diag + diag.T)
        diag_ref[...] = pad_lanes(diag)
        residue = own_ref[:, :cols] + recv_ref[:, :cols] - fdot(diag, basis_ref[...])
        if has_prev:
            residue = residue - fdot(low_ref[:, :count], prev_ref[...])
        residue_ref[...] = residue
        high, low = halves(residue)
        stack_ref[:count] = high
        stack_ref[count:] = low
        pack_ref[:, width:] = pad_lanes(fdot_t(residue, residue))

    moment = moment_ref[...]
    if first:
        weight_ref, short_ref = refs[names + 1], outs[3]
        cols = weight_ref.shape[1]
        short_ref[:, :cols] = weight_ref[...]
        short_ref[:, cols:] = moment[:, first : first + cols].astype(jnp.bfloat16)
    else:
        short_ref = outs[3]
        short_ref[...] = moment[:, : short_ref.shape[1]].astype(jnp.bfloat16)
    pack_ref[:, pl.ds(pl.multiple_of(at * height, height), height)] = split_dot(stack_ref[...], moment, 1)


def reduced_call(own, recv, basis, prev, low, moment, gates, size, weight=None, first=0, ties=()):
    depth, cols = moment.shape
    count = basis.shape[0]
    height = min(256, depth)
    has_prev = prev is not None
    operands = (own, recv, basis) + ((prev, low) if has_prev else ()) + (moment,)
    specs = [VMEM] * (len(operands) - 1) + [pl.BlockSpec((height, cols), lambda i: (i, 0))]
    emitted = size
    if first:
        operands += (weight,)
        specs.append(pl.BlockSpec((height, size), lambda i: (i, first // size)))
        emitted = 2 * size
    return pl.pallas_call(
        functools.partial(reduced_kernel, has_prev, first, len(gates) + bool(first) + len(ties), depth),
        grid=(depth // height,),
        in_specs=specs + [ANY] * (len(gates) + len(ties)),
        out_specs=[VMEM, VMEM, VMEM, pl.BlockSpec((height, emitted), lambda i: (i, 0))] + [ANY] * len(gates),
        out_shape=[
            jax.ShapeDtypeStruct((count, depth + LANES), jnp.float32),
            jax.ShapeDtypeStruct((count, cols), jnp.float32),
            jax.ShapeDtypeStruct((count, LANES), jnp.float32),
            jax.ShapeDtypeStruct((depth, emitted), jnp.bfloat16),
        ]
        + [jax.ShapeDtypeStruct(at.shape, at.dtype) for at in gates],
        input_output_aliases={len(operands) + i: 4 + i for i in range(len(gates))},
        scratch_shapes=[pltpu.VMEM((2 * count, cols), jnp.bfloat16)],
        compiler_params=PARAMS,
    )(*operands, *gates, *ties)


def last_kernel(passed, own_ref, recv_ref, *refs):
    diag_ref, low_ref = refs[passed : passed + 2]
    count = own_ref.shape[0]
    depth = own_ref.shape[1] - LANES
    low_t, inverse = eliminate(own_ref[:, depth:] + recv_ref[:, depth:], count)
    low_ref[...] = low_t
    reduced = fdot(inverse, own_ref[:, :depth] + recv_ref[:, :depth])
    diag_ref[...] = pad_lanes(fdot_t(reduced, reduced))


def last_call(own, recv, gates, ties):
    shape = jax.ShapeDtypeStruct((own.shape[0], LANES), jnp.float32)
    return pl.pallas_call(
        functools.partial(last_kernel, len(gates) + len(ties)),
        in_specs=[VMEM, VMEM] + [ANY] * (len(gates) + len(ties)),
        out_specs=[VMEM, VMEM] + [ANY] * len(gates),
        out_shape=[shape, shape] + [jax.ShapeDtypeStruct(at.shape, at.dtype) for at in gates],
        input_output_aliases={2 + i: 2 + i for i in range(len(gates))},
        compiler_params=PARAMS,
    )(own, recv, *gates, *ties)


def top_kernel(steps, *refs):
    diag_refs = refs[: steps + 1]
    low_refs = refs[steps + 1 : 2 * steps]
    scaled_ref, rate_ref, krylov_ref = refs[-3:]
    count = diag_refs[0].shape[0]
    size = steps * count
    krylov_ref[...] = jnp.zeros_like(krylov_ref)
    for place in range(steps):
        first = place * count
        diag = diag_refs[place][:, :count]
        if place + 1 == steps:
            diag = diag + diag_refs[steps][:, :count]
        krylov_ref[first : first + count, first : first + count] = 0.5 * (diag + diag.T)
        if place + 1 < steps:
            second = first + count
            low_t = low_refs[place][:, :count]
            krylov_ref[second : second + count, first:second] = low_t
            krylov_ref[first:second, second : second + count] = low_t.T
    krylov = krylov_ref[...]
    power = krylov * (1.0 / jnp.max(jnp.abs(krylov), keepdims=True))
    for _ in range(SQUARINGS):
        power = fdot(power, power)
        power = power * (1.0 / jnp.max(jnp.abs(power), keepdims=True))
    tall = jnp.sum(power, axis=1, keepdims=True)
    wide = jnp.sum(power, axis=0, keepdims=True)
    tall = tall * (1.0 / jnp.sqrt(jnp.sum(tall * tall, keepdims=True)))
    wide = wide * (1.0 / jnp.sqrt(jnp.sum(wide * wide, keepdims=True)))
    top = jnp.sum(krylov * tall * wide, keepdims=True)
    scaled_ref[...] = krylov[:size, :size] / top
    rate_ref[...] = jnp.broadcast_to(1.0 / jnp.sqrt(top), rate_ref.shape)


def top_call(diags, lows, ties):
    steps = len(lows) + 1
    count = diags[0].shape[0]
    size = steps * count
    padded = -(-size // LANES) * LANES
    return pl.pallas_call(
        functools.partial(top_kernel, steps),
        in_specs=[VMEM] * (2 * steps) + [ANY] * len(ties),
        out_specs=[VMEM, VMEM],
        out_shape=[
            jax.ShapeDtypeStruct((size, size), jnp.float32),
            jax.ShapeDtypeStruct((8, LANES), jnp.float32),
        ],
        scratch_shapes=[pltpu.VMEM((padded, padded), jnp.float32)],
        compiler_params=PARAMS,
    )(*diags, *lows, *ties)


def step_kernel(units, ties, *refs):
    weights, moments, rate_ref, outs = refs[:units], refs[units : 2 * units], refs[2 * units], refs[2 * units + 1 + ties :]
    for i in range(units):
        stepped = weights[i][...].astype(jnp.float32) - moments[i][...] * rate_ref[:1, :1]
        stepped = stepped.astype(jnp.bfloat16)
        outs[0][:, i * UNIT : (i + 1) * UNIT] = stepped
        if len(outs) > 1:
            outs[1 + i][...] = stepped


def step_call(weight, moment, rate, first, width, pieces, ties):
    depth = weight.shape[0]
    height = min(512, depth)
    units = width // UNIT
    sizes = [width] + [UNIT] * (units if pieces else 0)

    def spec(i):
        return pl.BlockSpec((height, UNIT), lambda r: (r, first // UNIT + i))

    blocks = [spec(i) for i in range(units)]
    return pl.pallas_call(
        functools.partial(step_kernel, units, len(ties)),
        grid=(depth // height,),
        in_specs=blocks + blocks + [VMEM] + [ANY] * len(ties),
        out_specs=[pl.BlockSpec((height, size), lambda r: (r, 0)) for size in sizes],
        out_shape=[jax.ShapeDtypeStruct((depth, size), jnp.bfloat16) for size in sizes],
        compiler_params=LARGE,
        cost_estimate=BRIEF,
    )(*[weight] * units, *[moment] * units, rate, *ties)


def project_kernel(far, pieces, layout, early, in_place, ties, first, order_ref, *refs):
    count = len(layout)
    tokens = refs[:pieces]
    refs = refs[pieces:]
    weights = []
    for parts in layout:
        weights.append(list(zip(refs, parts)))
        refs = refs[len(parts) :]
    if early:
        moments = []
        for parts in early:
            moments.append(list(zip(refs, parts)))
            refs = refs[len(parts) :]
        rate_ref, refs = refs[0], refs[1:]
    refs = refs[ties + (1 if in_place else 0) :]
    if not far:
        refs[1][...] = jnp.zeros(refs[1].shape, jnp.float32)
        refs = refs[:1] + refs[2:]
    out_ref, tokens_buf, weight_buf, moment_buf, total_ref, result_ref, sems, out_sem = refs
    depth, width = weight_buf.shape[1:]
    copies = []
    for k in range(count):
        step = []
        for i in range(pieces):
            if far:
                rows = tokens[i].shape[0]
                source = tokens[i].at[:, k * depth : (k + 1) * depth]
                target = tokens_buf.at[k, pl.ds(pl.multiple_of(order_ref[i], 16), rows), :]
            else:
                source = tokens[i].at[:, pl.ds(pl.multiple_of(order_ref[k] * depth, LANES), depth)]
                target = tokens_buf.at[k]
            step.append(pltpu.make_async_copy(source, target, sems.at[k, i]))
        filled = 0
        for i, (part, (at, size)) in enumerate(weights[k]):
            target = weight_buf.at[k, :, filled : filled + size]
            step.append(pltpu.make_async_copy(part.at[:, at : at + size], target, sems.at[k, pieces + i]))
            filled += size
        filled = 0
        for i, (part, (at, size)) in enumerate(moments[k] if early else ()):
            target = moment_buf.at[k, :, filled : filled + size]
            slot = sems.at[k, pieces + len(weights[k]) + i]
            step.append(pltpu.make_async_copy(part.at[:, at : at + size], target, slot))
            filled += size
        for copy in step:
            copy.start()
        copies.append(step)
    for k in range(count):
        for copy in copies[k]:
            copy.wait()
        block = weight_buf[k]
        if early:
            stepped = block.astype(jnp.float32) - moment_buf[k].astype(jnp.float32) * rate_ref[:1, :1]
            block = stepped.astype(jnp.bfloat16)
        part = jnp.dot(tokens_buf[k], block, preferred_element_type=jnp.float32)
        total_ref[...] = part if k == 0 else total_ref[...] + part
    if far:
        result_ref[...] = total_ref[...].astype(result_ref.dtype)
        copy = pltpu.make_async_copy(result_ref, out_ref, out_sem)
    else:
        copy = pltpu.make_async_copy(total_ref, out_ref.at[:, first : first + width], out_sem)
    copy.start()
    copy.wait()


def project_call(far, order, tokens, first, width, weights, moments, rate, ties=(), out=None, cols=None):
    early = tuple(tuple((at, size) for _, at, size in parts) for parts in moments or ())
    layout = tuple(tuple((at, size) for _, at, size in parts) for parts in weights)
    count = len(weights)
    depth = weights[0][0][0].shape[0]
    num_rows = sum(at.shape[0] for at in tokens)
    operands = list(tokens) + [part for parts in weights for part, _, _ in parts]
    specs = [ANY] * len(operands)
    if early:
        operands += [part for parts in moments for part, _, _ in parts] + [rate]
        specs += [ANY] * sum(len(parts) for parts in moments) + [VMEM]
    operands += list(ties)
    specs += [ANY] * len(ties)
    aliases = {}
    if far:
        out_shape = jax.ShapeDtypeStruct((num_rows, width), jnp.bfloat16)
    else:
        out_shape = [
            jax.ShapeDtypeStruct((num_rows, cols), jnp.float32),
            jax.ShapeDtypeStruct((8, LANES), jnp.float32),
        ]
        if out is not None:
            operands.append(out)
            specs.append(ANY)
            aliases = {len(operands): 0}
    return pl.pallas_call(
        functools.partial(
            project_kernel, far, len(tokens), layout, early, bool(aliases), len(ties), first
        ),
        grid_spec=pltpu.PrefetchScalarGridSpec(
            num_scalar_prefetch=1,
            grid=(1,),
            in_specs=specs,
            out_specs=ANY if far else [ANY, VMEM],
            scratch_shapes=[
                pltpu.VMEM((count, num_rows, depth), jnp.bfloat16),
                pltpu.VMEM((count, depth, width), jnp.bfloat16),
                pltpu.VMEM((count, depth, width) if early else (8, LANES), jnp.bfloat16),
                pltpu.VMEM((num_rows, width), jnp.float32),
                pltpu.VMEM((num_rows, width) if far else (8, LANES), jnp.bfloat16),
                pltpu.SemaphoreType.DMA((count, len(tokens) + 4)),
                pltpu.SemaphoreType.DMA,
            ],
        ),
        out_shape=out_shape,
        input_output_aliases=aliases,
        compiler_params=LARGE,
        cost_estimate=BRIEF,
    )(order, *operands)


def add_kernel(old_ref, far_ref, out_ref):
    out_ref[...] = old_ref[...] + far_ref[...].astype(jnp.float32)


def add_call(out, far, first):
    num_rows, width = far.shape
    block = pl.BlockSpec((num_rows, UNIT), lambda c: (0, first // UNIT + c))
    return pl.pallas_call(
        add_kernel,
        grid=(width // UNIT,),
        in_specs=[block, pl.BlockSpec((num_rows, UNIT), lambda c: (0, c))],
        out_specs=block,
        out_shape=jax.ShapeDtypeStruct(out.shape, out.dtype),
        input_output_aliases={0: 0},
        compiler_params=LARGE,
        cost_estimate=BRIEF,
    )(out, far)


def swap(values, axis, size, bit):
    return lax.ppermute(values, axis, [(at, at ^ bit) for at in range(size)])


def butterfly(values, axis, size):
    bit = 1
    while 2 * bit < size:
        values = values + swap(values, axis, size, bit)
        bit *= 2
    return values, swap(values, axis, size, bit)


def offsets(count):
    found = [0]
    bit = count // 2
    while bit:
        found = found + [at ^ bit for at in found]
        bit //= 2
    return found


def spread(piece, axis, size):
    parts = [piece]
    bit = 1
    while bit < size:
        parts = parts + [swap(part, axis, size, bit) for part in parts]
        bit *= 2
    return parts


def local(rows_n, cols_n, tokens, weight, momentum, gradient, probes):
    half = rows_n // 2
    far_bit, near_bit = half // 2, half // 4
    place = lax.axis_index("fsdp")
    low_at = lax.rem(place, half)
    side = lax.div(place, half)
    column_at = lax.axis_index("tensor")
    num_rows = tokens.shape[0]
    depth, cols = weight.shape
    rows = num_rows // cols_n // PARTS
    unit = cols // (sum(EARLY) + EXTRA + sum(LATE))
    early_cols = sum(EARLY) * unit

    def fswap(values, bit):
        return swap(values, "fsdp", rows_n, bit)

    def complete(parts):
        bit = near_bit // 2
        while bit:
            parts = parts + [[(fswap(at, bit), first, size) for at, first, size in part] for part in parts]
            bit //= 2
        return parts

    def blocks(own, across, beside):
        parts = [own, across, beside, fswap(across, near_bit)]
        return [part[0][0] for part in complete([[(part, 0, part.shape[1])] for part in parts])]

    def sum_over_rows(pack, gates, ties):
        passed = {}
        bit = 1
        while bit < half:
            pack, *passed[bit] = gate_call(pack, fswap(pack, bit), gates.get(bit, ()), ties.get(bit, ()))
            bit *= 2
        return pack, fswap(pack, half), passed

    mixed = jnp.stack([low_at ^ at for at in offsets(half)]).astype(jnp.int32)
    near_order = side * half + mixed
    pick_order = jnp.concatenate([(column_at * PARTS)[None], (1 - side) * half + mixed])
    far_order = jnp.stack(
        [(column_at ^ i) * PARTS * rows + part * rows for part in range(PARTS) for i in range(cols_n)]
    ).astype(jnp.int32)

    sent_0, sent_1, weight_own = pick_call(pick_order, tokens, weight, rows, half, early_cols)
    moment, short_1, pack = start_call(momentum, gradient, probes, sent_0, early_cols)
    weight_beside = fswap(weight_own, near_bit)
    weight_across = fswap(weight_own, far_bit)
    tokens_0 = fswap(sent_0, half)

    own, recv = butterfly(pack, "tensor", cols_n)
    pack, basis_1, _ = images_call(own, recv, probes, moment, True)
    own, recv, passed = sum_over_rows(
        pack, {1: [short_1, tokens_0], 2: [weight_across]}, {2: [weight_beside]}
    )
    short_1, tokens_0 = passed[1]
    weight_across, = passed[2]
    weight_parts = blocks(weight_own, weight_across, weight_beside)
    moment_beside = fswap(short_1, near_bit)
    token_parts = spread(tokens_0, "tensor", cols_n)
    pack, residue, diag_1, short_2, sent_1 = reduced_call(
        own, recv, basis_1, None, None, moment, [sent_1], early_cols
    )
    moment_across = fswap(short_2, far_bit)
    tokens_1 = fswap(sent_1, half)

    own, recv = butterfly(pack, "tensor", cols_n)
    pack, basis_2, low_1 = images_call(own, recv, residue, moment, False, weight_parts[3:])
    own, recv, passed = sum_over_rows(
        pack,
        {1: [moment_across, tokens_1]},
        {1: [moment_beside], 2: token_parts[1:]},
    )
    moment_across, token_1 = passed[1]
    moment_parts = blocks(short_1, moment_across, moment_beside)
    token_1_beside = swap(token_1, "tensor", cols_n, 1)
    token_1_across = swap(token_1, "tensor", cols_n, 2)
    pack, _, diag_2, pair = reduced_call(
        own, recv, basis_2, basis_1, low_1, moment, [], EXTRA * unit, weight, early_cols, [token_1_across]
    )
    pair_across, pair_beside = fswap(pair, far_bit), fswap(pair, near_bit)

    own, recv = butterfly(pack, "tensor", cols_n)
    diag_3, low_2, token_1_beside = last_call(
        own, recv, [token_1_beside], moment_parts[3:]
    )
    token_parts += [token_1, token_1_beside, token_1_across, swap(token_1_beside, "tensor", cols_n, 2)]
    own, recv, passed = sum_over_rows(diag_3, {1: [pair_across]}, {1: [pair_beside]})
    pairs = blocks(pair, passed[1][0], pair_beside)
    scaled, rate = top_call(
        [diag_1, diag_2, own, recv], [low_1, low_2], []
    )

    firsts, widths = [0], []
    for size in (sum(EARLY) + EXTRA, *LATE):
        widths.append(size * unit)
        firsts.append(firsts[-1] + size * unit)
    total = len(widths)
    partial, far = [], []

    def send(weights, first, width, *ties):
        partial.append(project_call(True, far_order, token_parts, first, width, *weights, ties=ties))
        far.append(fswap(partial[-1], half))

    def keep(weights, chunk, out, *ties):
        return project_call(
            False, near_order, [tokens], firsts[chunk], widths[chunk], *weights, ties=ties, out=out, cols=cols
        )

    def step(chunk, pieces, *ties):
        own = step_call(weight, moment, rate, firsts[chunk], widths[chunk], pieces, ties)
        return own[0], [fswap(at, far_bit) for at in (own[1:] or own)]

    def whole(array):
        return [(array, 0, array.shape[1])]

    extra = widths[0] - early_cols
    early = (
        [[(part, 0, early_cols), (pair, 0, extra)] for part, pair in zip(weight_parts, pairs)],
        [[(part, 0, early_cols), (pair, extra, extra)] for part, pair in zip(moment_parts, pairs)],
        rate,
    )
    own, across = step(1, False, token_parts[-1])
    beside = fswap(own, near_bit)
    send(early, firsts[0], widths[0], own)
    passed = pass_call(across, [partial[0], beside])
    arrived = [fswap(at, near_bit) for at in passed]
    parts = [whole(own), [at for part in across for at in whole(part)], whole(beside)]
    parts.append([at for part in arrived for at in whole(part)])
    weights = (complete(parts), None, None)
    own, across = step(2, True, passed[0])
    out, token = keep(early, 0, None, partial[0], own)
    for chunk in range(1, total):
        if chunk + 1 < total:
            width = widths[chunk + 1]
            split = width // unit if chunk + 2 == total else 1
            size = width // split
            merged = []
            for i in range(split):
                values = [(own, i * size, size)]
                if len(across) == 1:
                    values.append((across[0], i * size, size))
                else:
                    values += [at for part in across for at in whole(part)]
                ties = [*arrived, partial[-1], token, *merged]
                merged.append(merge_call(values, ties + far[:1] * (chunk == 1)))
            moved = [fswap(at, near_bit) for at in merged]
            send(weights, firsts[chunk], widths[chunk], merged[-1], far[chunk - 1])
            parts = [whole(own), [at for part in across for at in whole(part)]]
            parts += [[(at, first, size) for at in moved] for first in (0, size)]
            following = (complete(parts), None, None)
            if chunk + 2 < total:
                own, across = step(chunk + 2, False, token)
            out = add_call(out, far[chunk - 1], firsts[chunk - 1])
            out, token = keep(weights, chunk, out, partial[-1], own)
            weights, arrived = following, moved
    for i in range(split):
        pieces = []
        for part in weights[0]:
            array, first, _ = part[i] if len(part) > 1 else part[0]
            pieces.append([(array, first if len(part) > 1 else first + i * size, size)])
        send((pieces, None, None), firsts[-2] + i * size, size, partial[-1], token)
    out = add_call(out, far[total - 2], firsts[total - 2])
    out, _ = keep(weights, total - 1, out, partial[-1])
    for i in range(split):
        out = add_call(out, far[total - 1 + i], firsts[total - 1] + i * size)
    return out, moment, scaled


def solution(mesh):
    return jax.shard_map(
        functools.partial(local, mesh.shape["fsdp"], mesh.shape["tensor"]),
        mesh=mesh,
        in_specs=(
            P("fsdp", None),
            P("fsdp", "tensor"),
            P("fsdp", "tensor"),
            P("fsdp", "tensor"),
            P(None, "tensor"),
        ),
        out_specs=(P("fsdp", "tensor"), P("fsdp", "tensor"), P()),
        check_vma=False,
    )
```

```python
import functools

import jax
import jax.numpy as jnp
from jax import lax
from jax.experimental import pallas as pl
from jax.experimental.pallas import tpu as pltpu
from jax.sharding import PartitionSpec as P

DECAY = 0.9
SQUARINGS = 5
LANES = 128
UNIT = 256
EARLY = (2,)
LATE = (2, 2, 2)
PARTS = 2

HIGHEST = lax.Precision.HIGHEST
LARGE = pltpu.CompilerParams(vmem_limit_bytes=53 * 1024 * 1024)
PARAMS = pltpu.CompilerParams(vmem_limit_bytes=24 * 1024 * 1024)
BRIEF = pl.CostEstimate(flops=0, bytes_accessed=0, transcendentals=0)
VMEM = pl.BlockSpec(memory_space=pltpu.VMEM)
ANY = pl.BlockSpec(memory_space=pl.ANY)


def fdot(left, right):
    return lax.dot_general(
        left, right, (((1,), (0,)), ((), ())), precision=HIGHEST, preferred_element_type=jnp.float32
    )


def fdot_t(left, right):
    return lax.dot_general(
        left, right, (((1,), (1,)), ((), ())), precision=HIGHEST, preferred_element_type=jnp.float32
    )


def halves(values):
    high = values.astype(jnp.bfloat16)
    return high, (values - high.astype(jnp.float32)).astype(jnp.bfloat16)


def split_dot(stacked, mat, contract):
    rows = stacked.shape[0] // 2
    mat_high, mat_low = halves(mat)
    dims = (((1,), (contract,)), ((), ()))
    first = lax.dot_general(stacked, mat_high, dims, preferred_element_type=jnp.float32)
    second = lax.dot_general(stacked[:rows], mat_low, dims, preferred_element_type=jnp.float32)
    return first[:rows] + first[rows:] + second


def eliminate(gram, count):
    rows = lax.broadcasted_iota(jnp.int32, (count, LANES), 0)
    lanes = lax.broadcasted_iota(jnp.int32, (count, LANES), 1)
    aug = jnp.where(lanes < count, gram, jnp.where(lanes - count == rows, 1.0, 0.0))
    for step in range(count):
        pivot = aug[step : step + 1, step : step + 1]
        factor = jnp.where(rows > step, aug[:, step : step + 1] * (1.0 / pivot), 0.0)
        aug = aug - factor * aug[step : step + 1, :]
    pivots = jnp.sum(jnp.where(lanes == rows, aug, 0.0), axis=1, keepdims=True)
    aug = aug * (1.0 / jnp.sqrt(pivots))
    low_t = jnp.where((lanes >= rows) & (lanes < count), aug, 0.0)
    return low_t, aug[:, count : 2 * count]


def pad_lanes(square):
    return jnp.concatenate(
        [square, jnp.zeros((square.shape[0], LANES - square.shape[1]), jnp.float32)], axis=1
    )


def pick_kernel(order_ref, token_0, token_1, weight_ref, sent_0, sent_1, early_ref):
    sent_0[...] = token_0[...]
    sent_1[...] = token_1[...]
    early_ref[...] = weight_ref[...]


def pick_call(order, tokens, weight, rows, count, early_cols):
    depth = weight.shape[0]
    height = depth // count
    sent = jax.ShapeDtypeStruct((rows, count * depth), tokens.dtype)
    weight_spec = pl.BlockSpec((height, early_cols), lambda i, order_ref: (i, 0))
    sent_spec = pl.BlockSpec((rows, depth), lambda i, order_ref: (0, i))
    return pl.pallas_call(
        pick_kernel,
        grid_spec=pltpu.PrefetchScalarGridSpec(
            num_scalar_prefetch=1,
            grid=(count,),
            in_specs=[
                pl.BlockSpec((rows, depth), lambda i, order_ref: (order_ref[0], order_ref[1 + i])),
                pl.BlockSpec((rows, depth), lambda i, order_ref: (order_ref[0] + 1, order_ref[1 + i])),
                weight_spec,
            ],
            out_specs=[sent_spec, sent_spec, weight_spec],
        ),
        out_shape=[sent, sent, jax.ShapeDtypeStruct((depth, early_cols), weight.dtype)],
        compiler_params=LARGE,
    )(order, tokens, tokens, weight)


def start_kernel(width, mom_ref, grad_ref, probes_ref, tie_ref, moment_ref, short_ref, pack_ref, stack_ref):
    at = pl.program_id(0)
    count = probes_ref.shape[0]
    height = mom_ref.shape[0]

    @pl.when(at == 0)
    def _():
        probes = probes_ref[...]
        high, low = halves(probes)
        stack_ref[:count] = high
        stack_ref[count:] = low
        pack_ref[:, width:] = pad_lanes(fdot_t(probes, probes))

    moment = DECAY * mom_ref[...] + grad_ref[...].astype(jnp.float32)
    moment_ref[...] = moment
    short_ref[...] = moment[:, : short_ref.shape[1]].astype(jnp.bfloat16)
    pack_ref[:, pl.ds(pl.multiple_of(at * height, height), height)] = split_dot(stack_ref[...], moment, 1)


def start_call(momentum, gradient, probes, tie, early_cols):
    depth, cols = momentum.shape
    count = probes.shape[0]
    height = min(256, depth)
    rows = pl.BlockSpec((height, cols), lambda i: (i, 0))
    return pl.pallas_call(
        functools.partial(start_kernel, depth),
        grid=(depth // height,),
        in_specs=[rows, rows, VMEM, ANY],
        out_specs=[rows, pl.BlockSpec((height, early_cols), lambda i: (i, 0)), VMEM],
        out_shape=[
            jax.ShapeDtypeStruct((depth, cols), jnp.float32),
            jax.ShapeDtypeStruct((depth, early_cols), jnp.bfloat16),
            jax.ShapeDtypeStruct((count, depth + LANES), jnp.float32),
        ],
        scratch_shapes=[pltpu.VMEM((2 * count, cols), jnp.bfloat16)],
        compiler_params=LARGE,
    )(momentum, gradient, probes, tie)


def gate_kernel(passed, own_ref, recv_ref, *refs):
    sum_ref = refs[-1 - passed]
    sum_ref[...] = own_ref[...] + recv_ref[...]


def gate_call(own, recv, gates=(), ties=()):
    shapes = [jax.ShapeDtypeStruct(at.shape, at.dtype) for at in (own, *gates)]
    first = 2 + len(ties)
    return pl.pallas_call(
        functools.partial(gate_kernel, len(gates)),
        in_specs=[VMEM, VMEM] + [ANY] * (len(gates) + len(ties)),
        out_specs=[VMEM] + [ANY] * len(gates),
        out_shape=shapes,
        input_output_aliases={first + i: 1 + i for i in range(len(gates))},
        compiler_params=PARAMS,
    )(own, recv, *ties, *gates)


def pass_kernel(*refs):
    pass


def pass_call(values, ties):
    return pl.pallas_call(
        pass_kernel,
        in_specs=[ANY] * (len(values) + len(ties)),
        out_specs=[ANY] * len(values),
        out_shape=[jax.ShapeDtypeStruct(at.shape, at.dtype) for at in values],
        input_output_aliases={i: i for i in range(len(values))},
        compiler_params=LARGE,
        cost_estimate=BRIEF,
    )(*values, *ties)


def images_blocked(own_ref, recv_ref, block_ref, moment_ref, *refs):
    pack_ref, basis_ref, low_ref, stack_ref = refs[-4:]
    at = pl.program_id(0)
    count, cols = block_ref.shape
    depth = moment_ref.shape[0]
    width = moment_ref.shape[1]

    @pl.when(at == 0)
    def _():
        low_t, inverse = eliminate(own_ref[:, depth:] + recv_ref[:, depth:], count)
        low_ref[...] = low_t
        reduced = fdot(inverse, own_ref[:, :depth] + recv_ref[:, :depth])
        high, low = halves(reduced)
        stack_ref[:count] = high
        stack_ref[count:] = low
        pack_ref[:, cols:] = pad_lanes(fdot_t(reduced, reduced))
        basis_ref[...] = fdot(inverse, block_ref[...])

    pack_ref[:, pl.ds(pl.multiple_of(at * width, width), width)] = split_dot(stack_ref[...], moment_ref[...], 0)


def images_kernel(
    own_ref, recv_ref, block_ref, moment_ref, pack_ref, basis_ref, low_ref, held_ref, stack_ref, sems
):
    count, cols = block_ref.shape
    blocks, depth, width = held_ref.shape
    copies = [
        pltpu.make_async_copy(
            moment_ref.at[:, at * width : (at + 1) * width], held_ref.at[at], sems.at[at]
        )
        for at in range(blocks)
    ]
    for copy in copies:
        copy.start()
    low_t, inverse = eliminate(own_ref[:, depth:] + recv_ref[:, depth:], count)
    low_ref[...] = low_t
    reduced = fdot(inverse, own_ref[:, :depth] + recv_ref[:, :depth])
    high, low = halves(reduced)
    stack_ref[:count] = high
    stack_ref[count:] = low
    pack_ref[:, cols:] = pad_lanes(fdot_t(reduced, reduced))
    basis_ref[...] = fdot(inverse, block_ref[...])
    for at, copy in enumerate(copies):
        copy.wait()
        pack_ref[:, at * width : (at + 1) * width] = split_dot(stack_ref[...], held_ref[at], 0)


def images_call(own, recv, block, moment, fetch, ties=()):
    depth, cols = moment.shape
    count = block.shape[0]
    width = min(512, cols)
    stack = pltpu.VMEM((2 * count, depth), jnp.bfloat16)
    held = [
        pltpu.VMEM((cols // width, depth, width), jnp.float32),
        stack,
        pltpu.SemaphoreType.DMA((cols // width,)),
    ]
    return pl.pallas_call(
        images_kernel if fetch else images_blocked,
        grid=(1 if fetch else cols // width,),
        in_specs=[VMEM, VMEM, VMEM, ANY if fetch else pl.BlockSpec((depth, width), lambda i: (0, i))]
        + [ANY] * len(ties),
        out_specs=[VMEM, VMEM, VMEM],
        out_shape=[
            jax.ShapeDtypeStruct((count, cols + LANES), jnp.float32),
            jax.ShapeDtypeStruct((count, cols), jnp.float32),
            jax.ShapeDtypeStruct((count, LANES), jnp.float32),
        ],
        scratch_shapes=held if fetch else [stack],
        compiler_params=LARGE if fetch else PARAMS,
    )(own, recv, block, moment, *ties)


def reduced_kernel(has_prev, passed, width, *refs):
    names = 5 if has_prev else 3
    own_ref, recv_ref, basis_ref = refs[:3]
    prev_ref, low_ref = refs[3:5] if has_prev else (None, None)
    moment_ref = refs[names]
    outs = refs[names + 1 + passed :]
    pack_ref, residue_ref, diag_ref = outs[:3]
    stack_ref = refs[-1]
    at = pl.program_id(0)
    count, cols = basis_ref.shape
    height = moment_ref.shape[0]

    @pl.when(at == 0)
    def _():
        diag = (own_ref[:, cols:] + recv_ref[:, cols:])[:, :count]
        diag = 0.5 * (diag + diag.T)
        diag_ref[...] = pad_lanes(diag)
        residue = own_ref[:, :cols] + recv_ref[:, :cols] - fdot(diag, basis_ref[...])
        if has_prev:
            residue = residue - fdot(low_ref[:, :count], prev_ref[...])
        residue_ref[...] = residue
        high, low = halves(residue)
        stack_ref[:count] = high
        stack_ref[count:] = low
        pack_ref[:, width:] = pad_lanes(fdot_t(residue, residue))

    moment = moment_ref[...]
    if passed:
        short_ref = outs[3]
        short_ref[...] = moment[:, : short_ref.shape[1]].astype(jnp.bfloat16)
    pack_ref[:, pl.ds(pl.multiple_of(at * height, height), height)] = split_dot(stack_ref[...], moment, 1)


def reduced_call(own, recv, basis, prev, low, moment, gates, early_cols):
    depth, cols = moment.shape
    count = basis.shape[0]
    height = min(256, depth)
    has_prev = prev is not None
    operands = (own, recv, basis) + ((prev, low) if has_prev else ()) + (moment,)
    out_specs = [VMEM, VMEM, VMEM]
    out_shape = [
        jax.ShapeDtypeStruct((count, depth + LANES), jnp.float32),
        jax.ShapeDtypeStruct((count, cols), jnp.float32),
        jax.ShapeDtypeStruct((count, LANES), jnp.float32),
    ]
    if gates:
        out_specs += [pl.BlockSpec((height, early_cols), lambda i: (i, 0))] + [ANY] * len(gates)
        out_shape += [jax.ShapeDtypeStruct((depth, early_cols), jnp.bfloat16)]
        out_shape += [jax.ShapeDtypeStruct(at.shape, at.dtype) for at in gates]
    return pl.pallas_call(
        functools.partial(reduced_kernel, has_prev, len(gates), depth),
        grid=(depth // height,),
        in_specs=[VMEM] * (len(operands) - 1)
        + [pl.BlockSpec((height, cols), lambda i: (i, 0))]
        + [ANY] * len(gates),
        out_specs=out_specs,
        out_shape=out_shape,
        input_output_aliases={len(operands) + i: 4 + i for i in range(len(gates))},
        scratch_shapes=[pltpu.VMEM((2 * count, cols), jnp.bfloat16)],
        compiler_params=PARAMS,
    )(*operands, *gates)


def last_kernel(passed, own_ref, recv_ref, *refs):
    diag_ref, low_ref = refs[passed : passed + 2]
    count = own_ref.shape[0]
    depth = own_ref.shape[1] - LANES
    low_t, inverse = eliminate(own_ref[:, depth:] + recv_ref[:, depth:], count)
    low_ref[...] = low_t
    reduced = fdot(inverse, own_ref[:, :depth] + recv_ref[:, :depth])
    diag_ref[...] = pad_lanes(fdot_t(reduced, reduced))


def last_call(own, recv, gates, ties):
    shape = jax.ShapeDtypeStruct((own.shape[0], LANES), jnp.float32)
    return pl.pallas_call(
        functools.partial(last_kernel, len(gates) + len(ties)),
        in_specs=[VMEM, VMEM] + [ANY] * (len(gates) + len(ties)),
        out_specs=[VMEM, VMEM] + [ANY] * len(gates),
        out_shape=[shape, shape] + [jax.ShapeDtypeStruct(at.shape, at.dtype) for at in gates],
        input_output_aliases={2 + i: 2 + i for i in range(len(gates))},
        compiler_params=PARAMS,
    )(own, recv, *gates, *ties)


def top_kernel(steps, *refs):
    diag_refs = refs[: steps + 1]
    low_refs = refs[steps + 1 : 2 * steps]
    scaled_ref, rate_ref, krylov_ref = refs[-3:]
    count = diag_refs[0].shape[0]
    size = steps * count
    krylov_ref[...] = jnp.zeros_like(krylov_ref)
    for place in range(steps):
        first = place * count
        diag = diag_refs[place][:, :count]
        if place + 1 == steps:
            diag = diag + diag_refs[steps][:, :count]
        krylov_ref[first : first + count, first : first + count] = 0.5 * (diag + diag.T)
        if place + 1 < steps:
            second = first + count
            low_t = low_refs[place][:, :count]
            krylov_ref[second : second + count, first:second] = low_t
            krylov_ref[first:second, second : second + count] = low_t.T
    krylov = krylov_ref[...]
    power = krylov * (1.0 / jnp.max(jnp.abs(krylov), keepdims=True))
    for _ in range(SQUARINGS):
        power = fdot(power, power)
        power = power * (1.0 / jnp.max(jnp.abs(power), keepdims=True))
    tall = jnp.sum(power, axis=1, keepdims=True)
    wide = jnp.sum(power, axis=0, keepdims=True)
    tall = tall * (1.0 / jnp.sqrt(jnp.sum(tall * tall, keepdims=True)))
    wide = wide * (1.0 / jnp.sqrt(jnp.sum(wide * wide, keepdims=True)))
    top = jnp.sum(krylov * tall * wide, keepdims=True)
    scaled_ref[...] = krylov[:size, :size] / top
    rate_ref[...] = jnp.broadcast_to(1.0 / jnp.sqrt(top), rate_ref.shape)


def top_call(diags, lows, ties):
    steps = len(lows) + 1
    count = diags[0].shape[0]
    size = steps * count
    padded = -(-size // LANES) * LANES
    return pl.pallas_call(
        functools.partial(top_kernel, steps),
        in_specs=[VMEM] * (2 * steps) + [ANY] * len(ties),
        out_specs=[VMEM, VMEM],
        out_shape=[
            jax.ShapeDtypeStruct((size, size), jnp.float32),
            jax.ShapeDtypeStruct((8, LANES), jnp.float32),
        ],
        scratch_shapes=[pltpu.VMEM((padded, padded), jnp.float32)],
        compiler_params=PARAMS,
    )(*diags, *lows, *ties)


def step_kernel(ties, weight_ref, moment_ref, rate_ref, *refs):
    stepped = weight_ref[...].astype(jnp.float32) - moment_ref[...] * rate_ref[:1, :1]
    for i, out_ref in enumerate(refs[ties:]):
        out_ref[...] = stepped[:, i * UNIT : (i + 1) * UNIT].astype(jnp.bfloat16)


def step_call(weight, moment, rate, first, width, ties):
    depth = weight.shape[0]
    height = min(512, depth)
    block = pl.BlockSpec((height, width), lambda r: (r, first // width))
    return pl.pallas_call(
        functools.partial(step_kernel, len(ties)),
        grid=(depth // height,),
        in_specs=[block, block, VMEM] + [ANY] * len(ties),
        out_specs=[pl.BlockSpec((height, UNIT), lambda r: (r, 0))] * (width // UNIT),
        out_shape=[jax.ShapeDtypeStruct((depth, UNIT), jnp.bfloat16)] * (width // UNIT),
        compiler_params=LARGE,
        cost_estimate=BRIEF,
    )(weight, moment, rate, *ties)


def project_kernel(far, pieces, count, split, early, in_place, ties, first, order_ref, *refs):
    tokens = refs[:pieces]
    refs = refs[pieces:]
    weights, refs = refs[: split * count], refs[split * count :]
    if early:
        moments, rate_ref, refs = refs[:count], refs[count], refs[count + 1 :]
    refs = refs[ties + (1 if in_place else 0) :]
    if not far:
        refs[1][...] = jnp.zeros(refs[1].shape, jnp.float32)
        refs = refs[:1] + refs[2:]
    out_ref, tokens_buf, weight_buf, moment_buf, total_ref, result_ref, sems, out_sem = refs
    depth, width = weight_buf.shape[1:]
    copies = []
    for k in range(count):
        step = []
        for i in range(pieces):
            if far:
                rows = tokens[i].shape[0]
                source = tokens[i].at[:, k * depth : (k + 1) * depth]
                target = tokens_buf.at[k, pl.ds(pl.multiple_of(order_ref[i], 16), rows), :]
            else:
                source = tokens[i].at[:, pl.ds(pl.multiple_of(order_ref[k] * depth, LANES), depth)]
                target = tokens_buf.at[k]
            step.append(pltpu.make_async_copy(source, target, sems.at[k, i]))
        if early:
            at = slice(first, first + width)
            step.append(pltpu.make_async_copy(weights[k].at[:, at], weight_buf.at[k], sems.at[k, pieces]))
            step.append(
                pltpu.make_async_copy(moments[k].at[:, at], moment_buf.at[k], sems.at[k, pieces + 1])
            )
        else:
            for i in range(split):
                target = weight_buf.at[k, :, i * UNIT : (i + 1) * UNIT]
                step.append(
                    pltpu.make_async_copy(weights[k * split + i], target, sems.at[k, pieces + i])
                )
        for copy in step:
            copy.start()
        copies.append(step)
    for k in range(count):
        for copy in copies[k]:
            copy.wait()
        block = weight_buf[k]
        if early:
            stepped = block.astype(jnp.float32) - moment_buf[k].astype(jnp.float32) * rate_ref[:1, :1]
            block = stepped.astype(jnp.bfloat16)
        part = jnp.dot(tokens_buf[k], block, preferred_element_type=jnp.float32)
        total_ref[...] = part if k == 0 else total_ref[...] + part
    if far:
        result_ref[...] = total_ref[...].astype(result_ref.dtype)
        copy = pltpu.make_async_copy(result_ref, out_ref, out_sem)
    else:
        copy = pltpu.make_async_copy(total_ref, out_ref.at[:, first : first + width], out_sem)
    copy.start()
    copy.wait()


def project_call(far, order, tokens, first, width, weights, moments, rate, ties=(), out=None, cols=None):
    early = moments is not None
    split = 1 if early else width // UNIT
    count = len(weights) // split
    depth = weights[0].shape[0]
    num_rows = sum(at.shape[0] for at in tokens)
    operands = list(tokens) + list(weights)
    specs = [ANY] * len(operands)
    if early:
        operands += list(moments) + [rate]
        specs += [ANY] * count + [VMEM]
    operands += list(ties)
    specs += [ANY] * len(ties)
    aliases = {}
    if far:
        out_shape = jax.ShapeDtypeStruct((num_rows, width), jnp.bfloat16)
    else:
        out_shape = [
            jax.ShapeDtypeStruct((num_rows, cols), jnp.float32),
            jax.ShapeDtypeStruct((8, LANES), jnp.float32),
        ]
        if out is not None:
            operands.append(out)
            specs.append(ANY)
            aliases = {len(operands): 0}
    return pl.pallas_call(
        functools.partial(
            project_kernel, far, len(tokens), count, split, early, bool(aliases), len(ties), first
        ),
        grid_spec=pltpu.PrefetchScalarGridSpec(
            num_scalar_prefetch=1,
            grid=(1,),
            in_specs=specs,
            out_specs=ANY if far else [ANY, VMEM],
            scratch_shapes=[
                pltpu.VMEM((count, num_rows, depth), jnp.bfloat16),
                pltpu.VMEM((count, depth, width), jnp.bfloat16),
                pltpu.VMEM((count, depth, width) if early else (8, LANES), jnp.bfloat16),
                pltpu.VMEM((num_rows, width), jnp.float32),
                pltpu.VMEM((num_rows, width) if far else (8, LANES), jnp.bfloat16),
                pltpu.SemaphoreType.DMA((count, len(tokens) + max(2, split))),
                pltpu.SemaphoreType.DMA,
            ],
        ),
        out_shape=out_shape,
        input_output_aliases=aliases,
        compiler_params=LARGE,
        cost_estimate=BRIEF,
    )(order, *operands)


def add_kernel(old_ref, far_ref, out_ref):
    out_ref[...] = old_ref[...] + far_ref[...].astype(jnp.float32)


def add_call(out, far, first):
    num_rows, width = far.shape
    block = pl.BlockSpec((num_rows, UNIT), lambda c: (0, first // UNIT + c))
    return pl.pallas_call(
        add_kernel,
        grid=(width // UNIT,),
        in_specs=[block, pl.BlockSpec((num_rows, UNIT), lambda c: (0, c))],
        out_specs=block,
        out_shape=jax.ShapeDtypeStruct(out.shape, out.dtype),
        input_output_aliases={0: 0},
        compiler_params=LARGE,
        cost_estimate=BRIEF,
    )(out, far)


def swap(values, axis, size, bit):
    return lax.ppermute(values, axis, [(at, at ^ bit) for at in range(size)])


def butterfly(values, axis, size):
    bit = 1
    while 2 * bit < size:
        values = values + swap(values, axis, size, bit)
        bit *= 2
    return values, swap(values, axis, size, bit)


def offsets(count):
    found = [0]
    bit = count // 2
    while bit:
        found = found + [at ^ bit for at in found]
        bit //= 2
    return found


def spread(piece, axis, size):
    parts = [piece]
    bit = 1
    while bit < size:
        parts = parts + [swap(part, axis, size, bit) for part in parts]
        bit *= 2
    return parts


def local(rows_n, cols_n, tokens, weight, momentum, gradient, probes):
    half = rows_n // 2
    far_bit, near_bit = half // 2, half // 4
    place = lax.axis_index("fsdp")
    low_at = lax.rem(place, half)
    side = lax.div(place, half)
    column_at = lax.axis_index("tensor")
    num_rows = tokens.shape[0]
    depth, cols = weight.shape
    rows = num_rows // cols_n // PARTS
    unit = cols // (sum(EARLY) + sum(LATE))
    early_cols = sum(EARLY) * unit

    def fswap(values, bit):
        return swap(values, "fsdp", rows_n, bit)

    def complete(own, across, beside):
        parts = [own, across, beside, fswap(across, near_bit)]
        bit = near_bit // 2
        while bit:
            parts = parts + [fswap(part, bit) for part in parts]
            bit //= 2
        return parts

    def sum_over_rows(pack, gates, ties):
        passed = {}
        bit = 1
        while bit < half:
            pack, *passed[bit] = gate_call(pack, fswap(pack, bit), gates.get(bit, ()), ties.get(bit, ()))
            bit *= 2
        return pack, fswap(pack, half), passed

    mixed = jnp.stack([low_at ^ at for at in offsets(half)]).astype(jnp.int32)
    near_order = side * half + mixed
    pick_order = jnp.concatenate([(column_at * PARTS)[None], (1 - side) * half + mixed])
    far_order = jnp.stack(
        [(column_at ^ i) * PARTS * rows + part * rows for part in range(PARTS) for i in range(cols_n)]
    ).astype(jnp.int32)

    sent_0, sent_1, weight_own = pick_call(pick_order, tokens, weight, rows, half, early_cols)
    moment, short_1, pack = start_call(momentum, gradient, probes, sent_0, early_cols)
    weight_beside = fswap(weight_own, near_bit)
    weight_across = fswap(weight_own, far_bit)
    tokens_0 = fswap(sent_0, half)

    own, recv = butterfly(pack, "tensor", cols_n)
    pack, basis_1, _ = images_call(own, recv, probes, moment, True)
    own, recv, passed = sum_over_rows(
        pack, {1: [short_1, tokens_0], 2: [weight_across]}, {2: [weight_beside]}
    )
    short_1, tokens_0 = passed[1]
    weight_across, = passed[2]
    weight_parts = complete(weight_own, weight_across, weight_beside)
    moment_beside = fswap(short_1, near_bit)
    token_parts = spread(tokens_0, "tensor", cols_n)
    pack, residue, diag_1, short_2, sent_1 = reduced_call(
        own, recv, basis_1, None, None, moment, [sent_1], early_cols
    )
    moment_across = fswap(short_2, far_bit)
    tokens_1 = fswap(sent_1, half)

    own, recv = butterfly(pack, "tensor", cols_n)
    pack, basis_2, low_1 = images_call(
        own, recv, residue, moment, False, [weight_parts[3], moment_beside]
    )
    own, recv, passed = sum_over_rows(
        pack,
        {1: [moment_across], 2: [tokens_1]},
        {2: token_parts[1:3]},
    )
    moment_across, = passed[1]
    token_1, = passed[2]
    moment_parts = complete(short_1, moment_across, moment_beside)
    token_1_beside = swap(token_1, "tensor", cols_n, 1)
    token_1_across = swap(token_1, "tensor", cols_n, 2)
    pack, _, diag_2 = reduced_call(own, recv, basis_2, basis_1, low_1, moment, [], early_cols)

    own, recv = butterfly(pack, "tensor", cols_n)
    diag_3, low_2, token_1_beside = last_call(
        own, recv, [token_1_beside], [token_1_across, *moment_parts[3:], token_parts[3]]
    )
    token_parts += [token_1, token_1_beside, token_1_across, swap(token_1_beside, "tensor", cols_n, 2)]
    own, recv = butterfly(diag_3, "fsdp", rows_n)
    scaled, rate = top_call(
        [diag_1, diag_2, own, recv], [low_1, low_2], []
    )

    firsts, widths = [0], []
    for size in EARLY + LATE:
        widths.append(size * unit)
        firsts.append(firsts[-1] + size * unit)
    num_early = len(EARLY)
    gathered = [(weight_parts, moment_parts, rate)] * num_early
    out, partial, far = None, [], []

    def send(weights, first, width, *ties):
        partial.append(project_call(True, far_order, token_parts, first, width, *weights, ties=ties))
        far.append(fswap(partial[-1], half))

    def keep(chunk, out, tie):
        return project_call(
            False,
            near_order,
            [tokens],
            firsts[chunk],
            widths[chunk],
            *gathered[chunk],
            ties=[tie],
            out=out,
            cols=cols,
        )

    total = len(widths)
    own, across, beside = {}, {}, {}

    def step(chunk, *ties):
        own[chunk] = step_call(weight, moment, rate, firsts[chunk], widths[chunk], ties)
        across[chunk] = [fswap(at, far_bit) for at in own[chunk]]
        beside[chunk] = [fswap(at, near_bit) for at in own[chunk]]

    step(num_early, rate)
    tie = own[num_early][0]
    for chunk in range(num_early):
        send(gathered[chunk], firsts[chunk], widths[chunk], tie)
        tie = partial[-1]
    kept = []
    for chunk in range(num_early):
        out, token = keep(chunk, out, kept[-1] if kept else partial[-1])
        kept.append(token)
    for chunk in range(num_early, total):
        late = far[max(chunk - 2, 0) : chunk - 1]
        passed = pass_call(across[chunk], [partial[-1], *beside[chunk], *late])
        pieces = [complete(*at) for at in zip(own[chunk], passed, beside[chunk])]
        gathered.append(([piece[k] for k in range(half) for piece in pieces], None, None))
        if chunk + 1 < total:
            step(chunk + 1, kept[-1], passed[0])
            send(gathered[chunk], firsts[chunk], widths[chunk], partial[-1], own[chunk + 1][0])
            out = add_call(out, far[chunk - 1], firsts[chunk - 1])
            out, token = keep(chunk, out, partial[-1])
            kept.append(token)
    last_sent = partial[-1]
    for i, piece in enumerate(pieces):
        ties = [last_sent, kept[-1]] + far[total - 2 : total - 1] * (i > 0)
        send((piece, None, None), firsts[total - 1] + i * unit, unit, *ties)
    out = add_call(out, far[total - 2], firsts[total - 2])
    out, _ = keep(total - 1, out, partial[-1])
    for i in range(len(pieces)):
        out = add_call(out, far[total - 1 + i], firsts[total - 1] + i * unit)
    return out, moment, scaled


def solution(mesh):
    return jax.shard_map(
        functools.partial(local, mesh.shape["fsdp"], mesh.shape["tensor"]),
        mesh=mesh,
        in_specs=(
            P("fsdp", None),
            P("fsdp", "tensor"),
            P("fsdp", "tensor"),
            P("fsdp", "tensor"),
            P(None, "tensor"),
        ),
        out_specs=(P("fsdp", "tensor"), P("fsdp", "tensor"), P()),
        check_vma=False,
    )
```

```python
import functools

import jax
import jax.numpy as jnp
from jax import lax
from jax.experimental import pallas as pl
from jax.experimental.pallas import tpu as pltpu
from jax.sharding import PartitionSpec as P

DECAY = 0.9
SQUARINGS = 5
LANES = 128
UNIT = 256
EARLY = (2,)
LATE = (2, 2, 2)
PARTS = 2

HIGHEST = lax.Precision.HIGHEST
LARGE = pltpu.CompilerParams(vmem_limit_bytes=53 * 1024 * 1024)
PARAMS = pltpu.CompilerParams(vmem_limit_bytes=24 * 1024 * 1024)
BRIEF = pl.CostEstimate(flops=0, bytes_accessed=0, transcendentals=0)
VMEM = pl.BlockSpec(memory_space=pltpu.VMEM)
ANY = pl.BlockSpec(memory_space=pl.ANY)


def fdot(left, right):
    return lax.dot_general(
        left, right, (((1,), (0,)), ((), ())), precision=HIGHEST, preferred_element_type=jnp.float32
    )


def fdot_t(left, right):
    return lax.dot_general(
        left, right, (((1,), (1,)), ((), ())), precision=HIGHEST, preferred_element_type=jnp.float32
    )


def halves(values):
    high = values.astype(jnp.bfloat16)
    return high, (values - high.astype(jnp.float32)).astype(jnp.bfloat16)


def split_dot(stacked, mat, contract):
    rows = stacked.shape[0] // 2
    mat_high, mat_low = halves(mat)
    dims = (((1,), (contract,)), ((), ()))
    first = lax.dot_general(stacked, mat_high, dims, preferred_element_type=jnp.float32)
    second = lax.dot_general(stacked[:rows], mat_low, dims, preferred_element_type=jnp.float32)
    return first[:rows] + first[rows:] + second


def eliminate(gram, count):
    rows = lax.broadcasted_iota(jnp.int32, (count, LANES), 0)
    lanes = lax.broadcasted_iota(jnp.int32, (count, LANES), 1)
    aug = jnp.where(lanes < count, gram, jnp.where(lanes - count == rows, 1.0, 0.0))
    for step in range(count):
        pivot = aug[step : step + 1, step : step + 1]
        factor = jnp.where(rows > step, aug[:, step : step + 1] * (1.0 / pivot), 0.0)
        aug = aug - factor * aug[step : step + 1, :]
    pivots = jnp.sum(jnp.where(lanes == rows, aug, 0.0), axis=1, keepdims=True)
    aug = aug * (1.0 / jnp.sqrt(pivots))
    low_t = jnp.where((lanes >= rows) & (lanes < count), aug, 0.0)
    return low_t, aug[:, count : 2 * count]


def pad_lanes(square):
    return jnp.concatenate(
        [square, jnp.zeros((square.shape[0], LANES - square.shape[1]), jnp.float32)], axis=1
    )


def pick_kernel(order_ref, token_0, token_1, weight_ref, sent_0, sent_1, early_ref):
    sent_0[...] = token_0[...]
    sent_1[...] = token_1[...]
    early_ref[...] = weight_ref[...]


def pick_call(order, tokens, weight, rows, count, early_cols):
    depth = weight.shape[0]
    height = depth // count
    sent = jax.ShapeDtypeStruct((rows, count * depth), tokens.dtype)
    weight_spec = pl.BlockSpec((height, early_cols), lambda i, order_ref: (i, 0))
    sent_spec = pl.BlockSpec((rows, depth), lambda i, order_ref: (0, i))
    return pl.pallas_call(
        pick_kernel,
        grid_spec=pltpu.PrefetchScalarGridSpec(
            num_scalar_prefetch=1,
            grid=(count,),
            in_specs=[
                pl.BlockSpec((rows, depth), lambda i, order_ref: (order_ref[0], order_ref[1 + i])),
                pl.BlockSpec((rows, depth), lambda i, order_ref: (order_ref[0] + 1, order_ref[1 + i])),
                weight_spec,
            ],
            out_specs=[sent_spec, sent_spec, weight_spec],
        ),
        out_shape=[sent, sent, jax.ShapeDtypeStruct((depth, early_cols), weight.dtype)],
        compiler_params=LARGE,
    )(order, tokens, tokens, weight)


def start_kernel(width, mom_ref, grad_ref, probes_ref, tie_ref, moment_ref, short_ref, pack_ref, stack_ref):
    at = pl.program_id(0)
    count = probes_ref.shape[0]
    height = mom_ref.shape[0]

    @pl.when(at == 0)
    def _():
        probes = probes_ref[...]
        high, low = halves(probes)
        stack_ref[:count] = high
        stack_ref[count:] = low
        pack_ref[:, width:] = pad_lanes(fdot_t(probes, probes))

    moment = DECAY * mom_ref[...] + grad_ref[...].astype(jnp.float32)
    moment_ref[...] = moment
    short_ref[...] = moment[:, : short_ref.shape[1]].astype(jnp.bfloat16)
    pack_ref[:, pl.ds(pl.multiple_of(at * height, height), height)] = split_dot(stack_ref[...], moment, 1)


def start_call(momentum, gradient, probes, tie, early_cols):
    depth, cols = momentum.shape
    count = probes.shape[0]
    height = min(256, depth)
    rows = pl.BlockSpec((height, cols), lambda i: (i, 0))
    return pl.pallas_call(
        functools.partial(start_kernel, depth),
        grid=(depth // height,),
        in_specs=[rows, rows, VMEM, ANY],
        out_specs=[rows, pl.BlockSpec((height, early_cols), lambda i: (i, 0)), VMEM],
        out_shape=[
            jax.ShapeDtypeStruct((depth, cols), jnp.float32),
            jax.ShapeDtypeStruct((depth, early_cols), jnp.bfloat16),
            jax.ShapeDtypeStruct((count, depth + LANES), jnp.float32),
        ],
        scratch_shapes=[pltpu.VMEM((2 * count, cols), jnp.bfloat16)],
        compiler_params=LARGE,
    )(momentum, gradient, probes, tie)


def gate_kernel(passed, own_ref, recv_ref, *refs):
    sum_ref = refs[-1 - passed]
    sum_ref[...] = own_ref[...] + recv_ref[...]


def gate_call(own, recv, gates=(), ties=()):
    shapes = [jax.ShapeDtypeStruct(at.shape, at.dtype) for at in (own, *gates)]
    first = 2 + len(ties)
    return pl.pallas_call(
        functools.partial(gate_kernel, len(gates)),
        in_specs=[VMEM, VMEM] + [ANY] * (len(gates) + len(ties)),
        out_specs=[VMEM] + [ANY] * len(gates),
        out_shape=shapes,
        input_output_aliases={first + i: 1 + i for i in range(len(gates))},
        compiler_params=PARAMS,
    )(own, recv, *ties, *gates)


def pass_kernel(*refs):
    pass


def pass_call(values, ties):
    return pl.pallas_call(
        pass_kernel,
        in_specs=[ANY] * (len(values) + len(ties)),
        out_specs=[ANY] * len(values),
        out_shape=[jax.ShapeDtypeStruct(at.shape, at.dtype) for at in values],
        input_output_aliases={i: i for i in range(len(values))},
        compiler_params=LARGE,
        cost_estimate=BRIEF,
    )(*values, *ties)


def images_blocked(own_ref, recv_ref, block_ref, moment_ref, *refs):
    pack_ref, basis_ref, low_ref, stack_ref = refs[-4:]
    at = pl.program_id(0)
    count, cols = block_ref.shape
    depth = moment_ref.shape[0]
    width = moment_ref.shape[1]

    @pl.when(at == 0)
    def _():
        low_t, inverse = eliminate(own_ref[:, depth:] + recv_ref[:, depth:], count)
        low_ref[...] = low_t
        reduced = fdot(inverse, own_ref[:, :depth] + recv_ref[:, :depth])
        high, low = halves(reduced)
        stack_ref[:count] = high
        stack_ref[count:] = low
        pack_ref[:, cols:] = pad_lanes(fdot_t(reduced, reduced))
        basis_ref[...] = fdot(inverse, block_ref[...])

    pack_ref[:, pl.ds(pl.multiple_of(at * width, width), width)] = split_dot(stack_ref[...], moment_ref[...], 0)


def images_kernel(
    own_ref, recv_ref, block_ref, moment_ref, pack_ref, basis_ref, low_ref, held_ref, stack_ref, sems
):
    count, cols = block_ref.shape
    blocks, depth, width = held_ref.shape
    copies = [
        pltpu.make_async_copy(
            moment_ref.at[:, at * width : (at + 1) * width], held_ref.at[at], sems.at[at]
        )
        for at in range(blocks)
    ]
    for copy in copies:
        copy.start()
    low_t, inverse = eliminate(own_ref[:, depth:] + recv_ref[:, depth:], count)
    low_ref[...] = low_t
    reduced = fdot(inverse, own_ref[:, :depth] + recv_ref[:, :depth])
    high, low = halves(reduced)
    stack_ref[:count] = high
    stack_ref[count:] = low
    pack_ref[:, cols:] = pad_lanes(fdot_t(reduced, reduced))
    basis_ref[...] = fdot(inverse, block_ref[...])
    for at, copy in enumerate(copies):
        copy.wait()
        pack_ref[:, at * width : (at + 1) * width] = split_dot(stack_ref[...], held_ref[at], 0)


def images_call(own, recv, block, moment, fetch, ties=()):
    depth, cols = moment.shape
    count = block.shape[0]
    width = min(512, cols)
    stack = pltpu.VMEM((2 * count, depth), jnp.bfloat16)
    held = [
        pltpu.VMEM((cols // width, depth, width), jnp.float32),
        stack,
        pltpu.SemaphoreType.DMA((cols // width,)),
    ]
    return pl.pallas_call(
        images_kernel if fetch else images_blocked,
        grid=(1 if fetch else cols // width,),
        in_specs=[VMEM, VMEM, VMEM, ANY if fetch else pl.BlockSpec((depth, width), lambda i: (0, i))]
        + [ANY] * len(ties),
        out_specs=[VMEM, VMEM, VMEM],
        out_shape=[
            jax.ShapeDtypeStruct((count, cols + LANES), jnp.float32),
            jax.ShapeDtypeStruct((count, cols), jnp.float32),
            jax.ShapeDtypeStruct((count, LANES), jnp.float32),
        ],
        scratch_shapes=held if fetch else [stack],
        compiler_params=LARGE if fetch else PARAMS,
    )(own, recv, block, moment, *ties)


def reduced_kernel(has_prev, passed, width, *refs):
    names = 5 if has_prev else 3
    own_ref, recv_ref, basis_ref = refs[:3]
    prev_ref, low_ref = refs[3:5] if has_prev else (None, None)
    moment_ref = refs[names]
    outs = refs[names + 1 + passed :]
    pack_ref, residue_ref, diag_ref = outs[:3]
    stack_ref = refs[-1]
    at = pl.program_id(0)
    count, cols = basis_ref.shape
    height = moment_ref.shape[0]

    @pl.when(at == 0)
    def _():
        diag = (own_ref[:, cols:] + recv_ref[:, cols:])[:, :count]
        diag = 0.5 * (diag + diag.T)
        diag_ref[...] = pad_lanes(diag)
        residue = own_ref[:, :cols] + recv_ref[:, :cols] - fdot(diag, basis_ref[...])
        if has_prev:
            residue = residue - fdot(low_ref[:, :count], prev_ref[...])
        residue_ref[...] = residue
        high, low = halves(residue)
        stack_ref[:count] = high
        stack_ref[count:] = low
        pack_ref[:, width:] = pad_lanes(fdot_t(residue, residue))

    moment = moment_ref[...]
    if passed:
        short_ref = outs[3]
        short_ref[...] = moment[:, : short_ref.shape[1]].astype(jnp.bfloat16)
    pack_ref[:, pl.ds(pl.multiple_of(at * height, height), height)] = split_dot(stack_ref[...], moment, 1)


def reduced_call(own, recv, basis, prev, low, moment, gates, early_cols):
    depth, cols = moment.shape
    count = basis.shape[0]
    height = min(256, depth)
    has_prev = prev is not None
    operands = (own, recv, basis) + ((prev, low) if has_prev else ()) + (moment,)
    out_specs = [VMEM, VMEM, VMEM]
    out_shape = [
        jax.ShapeDtypeStruct((count, depth + LANES), jnp.float32),
        jax.ShapeDtypeStruct((count, cols), jnp.float32),
        jax.ShapeDtypeStruct((count, LANES), jnp.float32),
    ]
    if gates:
        out_specs += [pl.BlockSpec((height, early_cols), lambda i: (i, 0))] + [ANY] * len(gates)
        out_shape += [jax.ShapeDtypeStruct((depth, early_cols), jnp.bfloat16)]
        out_shape += [jax.ShapeDtypeStruct(at.shape, at.dtype) for at in gates]
    return pl.pallas_call(
        functools.partial(reduced_kernel, has_prev, len(gates), depth),
        grid=(depth // height,),
        in_specs=[VMEM] * (len(operands) - 1)
        + [pl.BlockSpec((height, cols), lambda i: (i, 0))]
        + [ANY] * len(gates),
        out_specs=out_specs,
        out_shape=out_shape,
        input_output_aliases={len(operands) + i: 4 + i for i in range(len(gates))},
        scratch_shapes=[pltpu.VMEM((2 * count, cols), jnp.bfloat16)],
        compiler_params=PARAMS,
    )(*operands, *gates)


def last_kernel(passed, own_ref, recv_ref, *refs):
    diag_ref, low_ref = refs[passed : passed + 2]
    count = own_ref.shape[0]
    depth = own_ref.shape[1] - LANES
    low_t, inverse = eliminate(own_ref[:, depth:] + recv_ref[:, depth:], count)
    low_ref[...] = low_t
    reduced = fdot(inverse, own_ref[:, :depth] + recv_ref[:, :depth])
    diag_ref[...] = pad_lanes(fdot_t(reduced, reduced))


def last_call(own, recv, gates, ties):
    shape = jax.ShapeDtypeStruct((own.shape[0], LANES), jnp.float32)
    return pl.pallas_call(
        functools.partial(last_kernel, len(gates) + len(ties)),
        in_specs=[VMEM, VMEM] + [ANY] * (len(gates) + len(ties)),
        out_specs=[VMEM, VMEM] + [ANY] * len(gates),
        out_shape=[shape, shape] + [jax.ShapeDtypeStruct(at.shape, at.dtype) for at in gates],
        input_output_aliases={2 + i: 2 + i for i in range(len(gates))},
        compiler_params=PARAMS,
    )(own, recv, *gates, *ties)


def top_kernel(steps, *refs):
    diag_refs = refs[: steps + 1]
    low_refs = refs[steps + 1 : 2 * steps]
    scaled_ref, rate_ref, krylov_ref = refs[-3:]
    count = diag_refs[0].shape[0]
    size = steps * count
    krylov_ref[...] = jnp.zeros_like(krylov_ref)
    for place in range(steps):
        first = place * count
        diag = diag_refs[place][:, :count]
        if place + 1 == steps:
            diag = diag + diag_refs[steps][:, :count]
        krylov_ref[first : first + count, first : first + count] = 0.5 * (diag + diag.T)
        if place + 1 < steps:
            second = first + count
            low_t = low_refs[place][:, :count]
            krylov_ref[second : second + count, first:second] = low_t
            krylov_ref[first:second, second : second + count] = low_t.T
    krylov = krylov_ref[...]
    power = krylov * (1.0 / jnp.max(jnp.abs(krylov), keepdims=True))
    for _ in range(SQUARINGS):
        power = fdot(power, power)
        power = power * (1.0 / jnp.max(jnp.abs(power), keepdims=True))
    tall = jnp.sum(power, axis=1, keepdims=True)
    wide = jnp.sum(power, axis=0, keepdims=True)
    tall = tall * (1.0 / jnp.sqrt(jnp.sum(tall * tall, keepdims=True)))
    wide = wide * (1.0 / jnp.sqrt(jnp.sum(wide * wide, keepdims=True)))
    top = jnp.sum(krylov * tall * wide, keepdims=True)
    scaled_ref[...] = krylov[:size, :size] / top
    rate_ref[...] = jnp.broadcast_to(1.0 / jnp.sqrt(top), rate_ref.shape)


def top_call(diags, lows, ties):
    steps = len(lows) + 1
    count = diags[0].shape[0]
    size = steps * count
    padded = -(-size // LANES) * LANES
    return pl.pallas_call(
        functools.partial(top_kernel, steps),
        in_specs=[VMEM] * (2 * steps) + [ANY] * len(ties),
        out_specs=[VMEM, VMEM],
        out_shape=[
            jax.ShapeDtypeStruct((size, size), jnp.float32),
            jax.ShapeDtypeStruct((8, LANES), jnp.float32),
        ],
        scratch_shapes=[pltpu.VMEM((padded, padded), jnp.float32)],
        compiler_params=PARAMS,
    )(*diags, *lows, *ties)


def step_kernel(ties, weight_ref, moment_ref, rate_ref, *refs):
    stepped = weight_ref[...].astype(jnp.float32) - moment_ref[...] * rate_ref[:1, :1]
    for i, out_ref in enumerate(refs[ties:]):
        out_ref[...] = stepped[:, i * UNIT : (i + 1) * UNIT].astype(jnp.bfloat16)


def step_call(weight, moment, rate, first, width, ties):
    depth = weight.shape[0]
    height = min(512, depth)
    block = pl.BlockSpec((height, width), lambda r: (r, first // width))
    return pl.pallas_call(
        functools.partial(step_kernel, len(ties)),
        grid=(depth // height,),
        in_specs=[block, block, VMEM] + [ANY] * len(ties),
        out_specs=[pl.BlockSpec((height, UNIT), lambda r: (r, 0))] * (width // UNIT),
        out_shape=[jax.ShapeDtypeStruct((depth, UNIT), jnp.bfloat16)] * (width // UNIT),
        compiler_params=LARGE,
        cost_estimate=BRIEF,
    )(weight, moment, rate, *ties)


def project_kernel(far, pieces, count, split, early, in_place, ties, first, order_ref, *refs):
    tokens = refs[:pieces]
    refs = refs[pieces:]
    weights, refs = refs[: split * count], refs[split * count :]
    if early:
        moments, rate_ref, refs = refs[:count], refs[count], refs[count + 1 :]
    refs = refs[ties + (1 if in_place else 0) :]
    if not far:
        refs[1][...] = jnp.zeros(refs[1].shape, jnp.float32)
        refs = refs[:1] + refs[2:]
    out_ref, tokens_buf, weight_buf, moment_buf, total_ref, result_ref, sems, out_sem = refs
    depth, width = weight_buf.shape[1:]
    copies = []
    for k in range(count):
        step = []
        for i in range(pieces):
            if far:
                rows = tokens[i].shape[0]
                source = tokens[i].at[:, k * depth : (k + 1) * depth]
                target = tokens_buf.at[k, pl.ds(pl.multiple_of(order_ref[i], 16), rows), :]
            else:
                source = tokens[i].at[:, pl.ds(pl.multiple_of(order_ref[k] * depth, LANES), depth)]
                target = tokens_buf.at[k]
            step.append(pltpu.make_async_copy(source, target, sems.at[k, i]))
        if early:
            at = slice(first, first + width)
            step.append(pltpu.make_async_copy(weights[k].at[:, at], weight_buf.at[k], sems.at[k, pieces]))
            step.append(
                pltpu.make_async_copy(moments[k].at[:, at], moment_buf.at[k], sems.at[k, pieces + 1])
            )
        else:
            for i in range(split):
                target = weight_buf.at[k, :, i * UNIT : (i + 1) * UNIT]
                step.append(
                    pltpu.make_async_copy(weights[k * split + i], target, sems.at[k, pieces + i])
                )
        for copy in step:
            copy.start()
        copies.append(step)
    for k in range(count):
        for copy in copies[k]:
            copy.wait()
        block = weight_buf[k]
        if early:
            stepped = block.astype(jnp.float32) - moment_buf[k].astype(jnp.float32) * rate_ref[:1, :1]
            block = stepped.astype(jnp.bfloat16)
        part = jnp.dot(tokens_buf[k], block, preferred_element_type=jnp.float32)
        total_ref[...] = part if k == 0 else total_ref[...] + part
    if far:
        result_ref[...] = total_ref[...].astype(result_ref.dtype)
        copy = pltpu.make_async_copy(result_ref, out_ref, out_sem)
    else:
        copy = pltpu.make_async_copy(total_ref, out_ref.at[:, first : first + width], out_sem)
    copy.start()
    copy.wait()


def project_call(far, order, tokens, first, width, weights, moments, rate, ties=(), out=None, cols=None):
    early = moments is not None
    split = 1 if early else width // UNIT
    count = len(weights) // split
    depth = weights[0].shape[0]
    num_rows = sum(at.shape[0] for at in tokens)
    operands = list(tokens) + list(weights)
    specs = [ANY] * len(operands)
    if early:
        operands += list(moments) + [rate]
        specs += [ANY] * count + [VMEM]
    operands += list(ties)
    specs += [ANY] * len(ties)
    aliases = {}
    if far:
        out_shape = jax.ShapeDtypeStruct((num_rows, width), jnp.bfloat16)
    else:
        out_shape = [
            jax.ShapeDtypeStruct((num_rows, cols), jnp.float32),
            jax.ShapeDtypeStruct((8, LANES), jnp.float32),
        ]
        if out is not None:
            operands.append(out)
            specs.append(ANY)
            aliases = {len(operands): 0}
    return pl.pallas_call(
        functools.partial(
            project_kernel, far, len(tokens), count, split, early, bool(aliases), len(ties), first
        ),
        grid_spec=pltpu.PrefetchScalarGridSpec(
            num_scalar_prefetch=1,
            grid=(1,),
            in_specs=specs,
            out_specs=ANY if far else [ANY, VMEM],
            scratch_shapes=[
                pltpu.VMEM((count, num_rows, depth), jnp.bfloat16),
                pltpu.VMEM((count, depth, width), jnp.bfloat16),
                pltpu.VMEM((count, depth, width) if early else (8, LANES), jnp.bfloat16),
                pltpu.VMEM((num_rows, width), jnp.float32),
                pltpu.VMEM((num_rows, width) if far else (8, LANES), jnp.bfloat16),
                pltpu.SemaphoreType.DMA((count, len(tokens) + max(2, split))),
                pltpu.SemaphoreType.DMA,
            ],
        ),
        out_shape=out_shape,
        input_output_aliases=aliases,
        compiler_params=LARGE,
        cost_estimate=BRIEF,
    )(order, *operands)


def add_kernel(old_ref, far_ref, out_ref):
    out_ref[...] = old_ref[...] + far_ref[...].astype(jnp.float32)


def add_call(out, far, first):
    num_rows, width = far.shape
    block = pl.BlockSpec((num_rows, UNIT), lambda c: (0, first // UNIT + c))
    return pl.pallas_call(
        add_kernel,
        grid=(width // UNIT,),
        in_specs=[block, pl.BlockSpec((num_rows, UNIT), lambda c: (0, c))],
        out_specs=block,
        out_shape=jax.ShapeDtypeStruct(out.shape, out.dtype),
        input_output_aliases={0: 0},
        compiler_params=LARGE,
        cost_estimate=BRIEF,
    )(out, far)


def swap(values, axis, size, bit):
    return lax.ppermute(values, axis, [(at, at ^ bit) for at in range(size)])


def butterfly(values, axis, size):
    bit = 1
    while 2 * bit < size:
        values = values + swap(values, axis, size, bit)
        bit *= 2
    return values, swap(values, axis, size, bit)


def offsets(count):
    found = [0]
    bit = count // 2
    while bit:
        found = found + [at ^ bit for at in found]
        bit //= 2
    return found


def spread(piece, axis, size):
    parts = [piece]
    bit = 1
    while bit < size:
        parts = parts + [swap(part, axis, size, bit) for part in parts]
        bit *= 2
    return parts


def local(rows_n, cols_n, tokens, weight, momentum, gradient, probes):
    half = rows_n // 2
    far_bit, near_bit = half // 2, half // 4
    place = lax.axis_index("fsdp")
    low_at = lax.rem(place, half)
    side = lax.div(place, half)
    column_at = lax.axis_index("tensor")
    num_rows = tokens.shape[0]
    depth, cols = weight.shape
    rows = num_rows // cols_n // PARTS
    unit = cols // (sum(EARLY) + sum(LATE))
    early_cols = sum(EARLY) * unit

    def fswap(values, bit):
        return swap(values, "fsdp", rows_n, bit)

    def complete(own, across, beside):
        parts = [own, across, beside, fswap(across, near_bit)]
        bit = near_bit // 2
        while bit:
            parts = parts + [fswap(part, bit) for part in parts]
            bit //= 2
        return parts

    def sum_over_rows(pack, gates, ties):
        passed = {}
        bit = 1
        while bit < half:
            pack, *passed[bit] = gate_call(pack, fswap(pack, bit), gates.get(bit, ()), ties.get(bit, ()))
            bit *= 2
        return pack, fswap(pack, half), passed

    mixed = jnp.stack([low_at ^ at for at in offsets(half)]).astype(jnp.int32)
    near_order = side * half + mixed
    pick_order = jnp.concatenate([(column_at * PARTS)[None], (1 - side) * half + mixed])
    far_order = jnp.stack(
        [(column_at ^ i) * PARTS * rows + part * rows for part in range(PARTS) for i in range(cols_n)]
    ).astype(jnp.int32)

    sent_0, sent_1, weight_own = pick_call(pick_order, tokens, weight, rows, half, early_cols)
    moment, short_1, pack = start_call(momentum, gradient, probes, sent_0, early_cols)
    weight_beside = fswap(weight_own, near_bit)
    weight_across = fswap(weight_own, far_bit)
    tokens_0 = fswap(sent_0, half)

    own, recv = butterfly(pack, "tensor", cols_n)
    pack, basis_1, _ = images_call(own, recv, probes, moment, True)
    own, recv, passed = sum_over_rows(
        pack, {1: [short_1, tokens_0], 2: [weight_across]}, {2: [weight_beside]}
    )
    short_1, tokens_0 = passed[1]
    weight_across, = passed[2]
    weight_parts = complete(weight_own, weight_across, weight_beside)
    moment_beside = fswap(short_1, near_bit)
    token_parts = spread(tokens_0, "tensor", cols_n)
    pack, residue, diag_1, short_2, sent_1 = reduced_call(
        own, recv, basis_1, None, None, moment, [sent_1], early_cols
    )
    moment_across = fswap(short_2, far_bit)
    tokens_1 = fswap(sent_1, half)

    own, recv = butterfly(pack, "tensor", cols_n)
    pack, basis_2, low_1 = images_call(
        own, recv, residue, moment, False, [weight_parts[3], moment_beside]
    )
    own, recv, passed = sum_over_rows(
        pack,
        {1: [moment_across], 2: [tokens_1]},
        {2: token_parts[1:3]},
    )
    moment_across, = passed[1]
    token_1, = passed[2]
    moment_parts = complete(short_1, moment_across, moment_beside)
    token_1_beside = swap(token_1, "tensor", cols_n, 1)
    token_1_across = swap(token_1, "tensor", cols_n, 2)
    pack, _, diag_2 = reduced_call(own, recv, basis_2, basis_1, low_1, moment, [], early_cols)

    own, recv = butterfly(pack, "tensor", cols_n)
    diag_3, low_2, token_1_beside = last_call(
        own, recv, [token_1_beside], [token_1_across, *moment_parts[3:], token_parts[3]]
    )
    token_parts += [token_1, token_1_beside, token_1_across, swap(token_1_beside, "tensor", cols_n, 2)]
    own, recv = butterfly(diag_3, "fsdp", rows_n)
    scaled, rate = top_call(
        [diag_1, diag_2, own, recv], [low_1, low_2], []
    )

    firsts, widths = [0], []
    for size in EARLY + LATE:
        widths.append(size * unit)
        firsts.append(firsts[-1] + size * unit)
    num_early = len(EARLY)
    gathered = [(weight_parts, moment_parts, rate)] * num_early
    out, partial, far = None, [], []

    def send(weights, first, width, *ties):
        partial.append(project_call(True, far_order, token_parts, first, width, *weights, ties=ties))
        far.append(fswap(partial[-1], half))

    def keep(chunk, out, tie):
        return project_call(
            False,
            near_order,
            [tokens],
            firsts[chunk],
            widths[chunk],
            *gathered[chunk],
            ties=[tie],
            out=out,
            cols=cols,
        )

    total = len(widths)
    own, across, beside = {}, {}, {}

    def step(chunk, *ties):
        own[chunk] = step_call(weight, moment, rate, firsts[chunk], widths[chunk], ties)
        across[chunk] = [fswap(at, far_bit) for at in own[chunk]]
        beside[chunk] = [fswap(at, near_bit) for at in own[chunk]]

    step(num_early, rate)
    tie = own[num_early][0]
    for chunk in range(num_early):
        send(gathered[chunk], firsts[chunk], widths[chunk], tie)
        tie = partial[-1]
    kept = []
    for chunk in range(num_early):
        out, token = keep(chunk, out, kept[-1] if kept else partial[-1])
        kept.append(token)
    for chunk in range(num_early, total):
        late = far[max(chunk - 2, 0) : chunk - 1]
        passed = pass_call(across[chunk], [partial[-1], *(beside[chunk] if chunk == num_early else beside[chunk][:1]), *late])
        pieces = [complete(*at) for at in zip(own[chunk], passed, beside[chunk])]
        gathered.append(([piece[k] for k in range(half) for piece in pieces], None, None))
        if chunk + 1 < total:
            step(chunk + 1, kept[-1], passed[0])
            send(gathered[chunk], firsts[chunk], widths[chunk], partial[-1], own[chunk + 1][0])
            out = add_call(out, far[chunk - 1], firsts[chunk - 1])
            out, token = keep(chunk, out, partial[-1])
            kept.append(token)
    last_sent = partial[-1]
    for i, piece in enumerate(pieces):
        ties = [last_sent, kept[-1]] + far[total - 2 : total - 1] * (i > 0)
        send((piece, None, None), firsts[total - 1] + i * unit, unit, *ties)
    out = add_call(out, far[total - 2], firsts[total - 2])
    out, _ = keep(total - 1, out, partial[-1])
    for i in range(len(pieces)):
        out = add_call(out, far[total - 1 + i], firsts[total - 1] + i * unit)
    return out, moment, scaled


def solution(mesh):
    return jax.shard_map(
        functools.partial(local, mesh.shape["fsdp"], mesh.shape["tensor"]),
        mesh=mesh,
        in_specs=(
            P("fsdp", None),
            P("fsdp", "tensor"),
            P("fsdp", "tensor"),
            P("fsdp", "tensor"),
            P(None, "tensor"),
        ),
        out_specs=(P("fsdp", "tensor"), P("fsdp", "tensor"), P()),
        check_vma=False,
    )
```

```python
import functools

import jax
import jax.numpy as jnp
from jax import lax
from jax.experimental import pallas as pl
from jax.experimental.pallas import tpu as pltpu
from jax.sharding import PartitionSpec as P

DECAY = 0.9
SQUARINGS = 5
LANES = 128
UNIT = 256
EARLY = (2,)
LATE = (2, 2, 2)
PARTS = 2

HIGHEST = lax.Precision.HIGHEST
LARGE = pltpu.CompilerParams(vmem_limit_bytes=53 * 1024 * 1024)
PARAMS = pltpu.CompilerParams(vmem_limit_bytes=24 * 1024 * 1024)
BRIEF = pl.CostEstimate(flops=0, bytes_accessed=0, transcendentals=0)
VMEM = pl.BlockSpec(memory_space=pltpu.VMEM)
ANY = pl.BlockSpec(memory_space=pl.ANY)


def fdot(left, right):
    return lax.dot_general(
        left, right, (((1,), (0,)), ((), ())), precision=HIGHEST, preferred_element_type=jnp.float32
    )


def fdot_t(left, right):
    return lax.dot_general(
        left, right, (((1,), (1,)), ((), ())), precision=HIGHEST, preferred_element_type=jnp.float32
    )


def halves(values):
    high = values.astype(jnp.bfloat16)
    return high, (values - high.astype(jnp.float32)).astype(jnp.bfloat16)


def split_dot(stacked, mat, contract):
    rows = stacked.shape[0] // 2
    mat_high, mat_low = halves(mat)
    dims = (((1,), (contract,)), ((), ()))
    first = lax.dot_general(stacked, mat_high, dims, preferred_element_type=jnp.float32)
    second = lax.dot_general(stacked[:rows], mat_low, dims, preferred_element_type=jnp.float32)
    return first[:rows] + first[rows:] + second


def eliminate(gram, count):
    rows = lax.broadcasted_iota(jnp.int32, (count, LANES), 0)
    lanes = lax.broadcasted_iota(jnp.int32, (count, LANES), 1)
    aug = jnp.where(lanes < count, gram, jnp.where(lanes - count == rows, 1.0, 0.0))
    for step in range(count):
        pivot = aug[step : step + 1, step : step + 1]
        factor = jnp.where(rows > step, aug[:, step : step + 1] * (1.0 / pivot), 0.0)
        aug = aug - factor * aug[step : step + 1, :]
    pivots = jnp.sum(jnp.where(lanes == rows, aug, 0.0), axis=1, keepdims=True)
    aug = aug * (1.0 / jnp.sqrt(pivots))
    low_t = jnp.where((lanes >= rows) & (lanes < count), aug, 0.0)
    return low_t, aug[:, count : 2 * count]


def pad_lanes(square):
    return jnp.concatenate(
        [square, jnp.zeros((square.shape[0], LANES - square.shape[1]), jnp.float32)], axis=1
    )


def pick_kernel(order_ref, token_0, token_1, weight_ref, sent_0, sent_1, early_ref):
    sent_0[...] = token_0[...]
    sent_1[...] = token_1[...]
    early_ref[...] = weight_ref[...]


def pick_call(order, tokens, weight, rows, count, early_cols):
    depth = weight.shape[0]
    height = depth // count
    sent = jax.ShapeDtypeStruct((rows, count * depth), tokens.dtype)
    weight_spec = pl.BlockSpec((height, early_cols), lambda i, order_ref: (i, 0))
    sent_spec = pl.BlockSpec((rows, depth), lambda i, order_ref: (0, i))
    return pl.pallas_call(
        pick_kernel,
        grid_spec=pltpu.PrefetchScalarGridSpec(
            num_scalar_prefetch=1,
            grid=(count,),
            in_specs=[
                pl.BlockSpec((rows, depth), lambda i, order_ref: (order_ref[0], order_ref[1 + i])),
                pl.BlockSpec((rows, depth), lambda i, order_ref: (order_ref[0] + 1, order_ref[1 + i])),
                weight_spec,
            ],
            out_specs=[sent_spec, sent_spec, weight_spec],
        ),
        out_shape=[sent, sent, jax.ShapeDtypeStruct((depth, early_cols), weight.dtype)],
        compiler_params=LARGE,
    )(order, tokens, tokens, weight)


def start_kernel(width, mom_ref, grad_ref, probes_ref, tie_ref, moment_ref, short_ref, pack_ref, stack_ref):
    at = pl.program_id(0)
    count = probes_ref.shape[0]
    height = mom_ref.shape[0]

    @pl.when(at == 0)
    def _():
        probes = probes_ref[...]
        high, low = halves(probes)
        stack_ref[:count] = high
        stack_ref[count:] = low
        pack_ref[:, width:] = pad_lanes(fdot_t(probes, probes))

    moment = DECAY * mom_ref[...] + grad_ref[...].astype(jnp.float32)
    moment_ref[...] = moment
    short_ref[...] = moment[:, : short_ref.shape[1]].astype(jnp.bfloat16)
    pack_ref[:, pl.ds(pl.multiple_of(at * height, height), height)] = split_dot(stack_ref[...], moment, 1)


def start_call(momentum, gradient, probes, tie, early_cols):
    depth, cols = momentum.shape
    count = probes.shape[0]
    height = min(256, depth)
    rows = pl.BlockSpec((height, cols), lambda i: (i, 0))
    return pl.pallas_call(
        functools.partial(start_kernel, depth),
        grid=(depth // height,),
        in_specs=[rows, rows, VMEM, ANY],
        out_specs=[rows, pl.BlockSpec((height, early_cols), lambda i: (i, 0)), VMEM],
        out_shape=[
            jax.ShapeDtypeStruct((depth, cols), jnp.float32),
            jax.ShapeDtypeStruct((depth, early_cols), jnp.bfloat16),
            jax.ShapeDtypeStruct((count, depth + LANES), jnp.float32),
        ],
        scratch_shapes=[pltpu.VMEM((2 * count, cols), jnp.bfloat16)],
        compiler_params=LARGE,
    )(momentum, gradient, probes, tie)


def gate_kernel(passed, own_ref, recv_ref, *refs):
    sum_ref = refs[-1 - passed]
    sum_ref[...] = own_ref[...] + recv_ref[...]


def gate_call(own, recv, gates=(), ties=()):
    shapes = [jax.ShapeDtypeStruct(at.shape, at.dtype) for at in (own, *gates)]
    first = 2 + len(ties)
    return pl.pallas_call(
        functools.partial(gate_kernel, len(gates)),
        in_specs=[VMEM, VMEM] + [ANY] * (len(gates) + len(ties)),
        out_specs=[VMEM] + [ANY] * len(gates),
        out_shape=shapes,
        input_output_aliases={first + i: 1 + i for i in range(len(gates))},
        compiler_params=PARAMS,
    )(own, recv, *ties, *gates)


def pass_kernel(*refs):
    pass


def pass_call(values, ties):
    return pl.pallas_call(
        pass_kernel,
        in_specs=[ANY] * (len(values) + len(ties)),
        out_specs=[ANY] * len(values),
        out_shape=[jax.ShapeDtypeStruct(at.shape, at.dtype) for at in values],
        input_output_aliases={i: i for i in range(len(values))},
        compiler_params=LARGE,
        cost_estimate=BRIEF,
    )(*values, *ties)


def images_blocked(own_ref, recv_ref, block_ref, moment_ref, *refs):
    pack_ref, basis_ref, low_ref, stack_ref = refs[-4:]
    at = pl.program_id(0)
    count, cols = block_ref.shape
    depth = moment_ref.shape[0]
    width = moment_ref.shape[1]

    @pl.when(at == 0)
    def _():
        low_t, inverse = eliminate(own_ref[:, depth:] + recv_ref[:, depth:], count)
        low_ref[...] = low_t
        reduced = fdot(inverse, own_ref[:, :depth] + recv_ref[:, :depth])
        high, low = halves(reduced)
        stack_ref[:count] = high
        stack_ref[count:] = low
        pack_ref[:, cols:] = pad_lanes(fdot_t(reduced, reduced))
        basis_ref[...] = fdot(inverse, block_ref[...])

    pack_ref[:, pl.ds(pl.multiple_of(at * width, width), width)] = split_dot(stack_ref[...], moment_ref[...], 0)


def images_kernel(
    own_ref, recv_ref, block_ref, moment_ref, pack_ref, basis_ref, low_ref, held_ref, stack_ref, sems
):
    count, cols = block_ref.shape
    blocks, depth, width = held_ref.shape
    copies = [
        pltpu.make_async_copy(
            moment_ref.at[:, at * width : (at + 1) * width], held_ref.at[at], sems.at[at]
        )
        for at in range(blocks)
    ]
    for copy in copies:
        copy.start()
    low_t, inverse = eliminate(own_ref[:, depth:] + recv_ref[:, depth:], count)
    low_ref[...] = low_t
    reduced = fdot(inverse, own_ref[:, :depth] + recv_ref[:, :depth])
    high, low = halves(reduced)
    stack_ref[:count] = high
    stack_ref[count:] = low
    pack_ref[:, cols:] = pad_lanes(fdot_t(reduced, reduced))
    basis_ref[...] = fdot(inverse, block_ref[...])
    for at, copy in enumerate(copies):
        copy.wait()
        pack_ref[:, at * width : (at + 1) * width] = split_dot(stack_ref[...], held_ref[at], 0)


def images_call(own, recv, block, moment, fetch, ties=()):
    depth, cols = moment.shape
    count = block.shape[0]
    width = min(512, cols)
    stack = pltpu.VMEM((2 * count, depth), jnp.bfloat16)
    held = [
        pltpu.VMEM((cols // width, depth, width), jnp.float32),
        stack,
        pltpu.SemaphoreType.DMA((cols // width,)),
    ]
    return pl.pallas_call(
        images_kernel if fetch else images_blocked,
        grid=(1 if fetch else cols // width,),
        in_specs=[VMEM, VMEM, VMEM, ANY if fetch else pl.BlockSpec((depth, width), lambda i: (0, i))]
        + [ANY] * len(ties),
        out_specs=[VMEM, VMEM, VMEM],
        out_shape=[
            jax.ShapeDtypeStruct((count, cols + LANES), jnp.float32),
            jax.ShapeDtypeStruct((count, cols), jnp.float32),
            jax.ShapeDtypeStruct((count, LANES), jnp.float32),
        ],
        scratch_shapes=held if fetch else [stack],
        compiler_params=LARGE if fetch else PARAMS,
    )(own, recv, block, moment, *ties)


def reduced_kernel(has_prev, passed, width, *refs):
    names = 5 if has_prev else 3
    own_ref, recv_ref, basis_ref = refs[:3]
    prev_ref, low_ref = refs[3:5] if has_prev else (None, None)
    moment_ref = refs[names]
    outs = refs[names + 1 + passed :]
    pack_ref, residue_ref, diag_ref = outs[:3]
    stack_ref = refs[-1]
    at = pl.program_id(0)
    count, cols = basis_ref.shape
    height = moment_ref.shape[0]

    @pl.when(at == 0)
    def _():
        diag = (own_ref[:, cols:] + recv_ref[:, cols:])[:, :count]
        diag = 0.5 * (diag + diag.T)
        diag_ref[...] = pad_lanes(diag)
        residue = own_ref[:, :cols] + recv_ref[:, :cols] - fdot(diag, basis_ref[...])
        if has_prev:
            residue = residue - fdot(low_ref[:, :count], prev_ref[...])
        residue_ref[...] = residue
        high, low = halves(residue)
        stack_ref[:count] = high
        stack_ref[count:] = low
        pack_ref[:, width:] = pad_lanes(fdot_t(residue, residue))

    moment = moment_ref[...]
    if passed:
        short_ref = outs[3]
        short_ref[...] = moment[:, : short_ref.shape[1]].astype(jnp.bfloat16)
    pack_ref[:, pl.ds(pl.multiple_of(at * height, height), height)] = split_dot(stack_ref[...], moment, 1)


def reduced_call(own, recv, basis, prev, low, moment, gates, early_cols):
    depth, cols = moment.shape
    count = basis.shape[0]
    height = min(256, depth)
    has_prev = prev is not None
    operands = (own, recv, basis) + ((prev, low) if has_prev else ()) + (moment,)
    out_specs = [VMEM, VMEM, VMEM]
    out_shape = [
        jax.ShapeDtypeStruct((count, depth + LANES), jnp.float32),
        jax.ShapeDtypeStruct((count, cols), jnp.float32),
        jax.ShapeDtypeStruct((count, LANES), jnp.float32),
    ]
    if gates:
        out_specs += [pl.BlockSpec((height, early_cols), lambda i: (i, 0))] + [ANY] * len(gates)
        out_shape += [jax.ShapeDtypeStruct((depth, early_cols), jnp.bfloat16)]
        out_shape += [jax.ShapeDtypeStruct(at.shape, at.dtype) for at in gates]
    return pl.pallas_call(
        functools.partial(reduced_kernel, has_prev, len(gates), depth),
        grid=(depth // height,),
        in_specs=[VMEM] * (len(operands) - 1)
        + [pl.BlockSpec((height, cols), lambda i: (i, 0))]
        + [ANY] * len(gates),
        out_specs=out_specs,
        out_shape=out_shape,
        input_output_aliases={len(operands) + i: 4 + i for i in range(len(gates))},
        scratch_shapes=[pltpu.VMEM((2 * count, cols), jnp.bfloat16)],
        compiler_params=PARAMS,
    )(*operands, *gates)


def last_kernel(passed, own_ref, recv_ref, *refs):
    diag_ref, low_ref = refs[passed : passed + 2]
    count = own_ref.shape[0]
    depth = own_ref.shape[1] - LANES
    low_t, inverse = eliminate(own_ref[:, depth:] + recv_ref[:, depth:], count)
    low_ref[...] = low_t
    reduced = fdot(inverse, own_ref[:, :depth] + recv_ref[:, :depth])
    diag_ref[...] = pad_lanes(fdot_t(reduced, reduced))


def last_call(own, recv, gates, ties):
    shape = jax.ShapeDtypeStruct((own.shape[0], LANES), jnp.float32)
    return pl.pallas_call(
        functools.partial(last_kernel, len(gates) + len(ties)),
        in_specs=[VMEM, VMEM] + [ANY] * (len(gates) + len(ties)),
        out_specs=[VMEM, VMEM] + [ANY] * len(gates),
        out_shape=[shape, shape] + [jax.ShapeDtypeStruct(at.shape, at.dtype) for at in gates],
        input_output_aliases={2 + i: 2 + i for i in range(len(gates))},
        compiler_params=PARAMS,
    )(own, recv, *gates, *ties)


def top_kernel(steps, *refs):
    diag_refs = refs[: steps + 1]
    low_refs = refs[steps + 1 : 2 * steps]
    scaled_ref, rate_ref, krylov_ref = refs[-3:]
    count = diag_refs[0].shape[0]
    size = steps * count
    krylov_ref[...] = jnp.zeros_like(krylov_ref)
    for place in range(steps):
        first = place * count
        diag = diag_refs[place][:, :count]
        if place + 1 == steps:
            diag = diag + diag_refs[steps][:, :count]
        krylov_ref[first : first + count, first : first + count] = 0.5 * (diag + diag.T)
        if place + 1 < steps:
            second = first + count
            low_t = low_refs[place][:, :count]
            krylov_ref[second : second + count, first:second] = low_t
            krylov_ref[first:second, second : second + count] = low_t.T
    krylov = krylov_ref[...]
    power = krylov * (1.0 / jnp.max(jnp.abs(krylov), keepdims=True))
    for _ in range(SQUARINGS):
        power = fdot(power, power)
        power = power * (1.0 / jnp.max(jnp.abs(power), keepdims=True))
    tall = jnp.sum(power, axis=1, keepdims=True)
    wide = jnp.sum(power, axis=0, keepdims=True)
    tall = tall * (1.0 / jnp.sqrt(jnp.sum(tall * tall, keepdims=True)))
    wide = wide * (1.0 / jnp.sqrt(jnp.sum(wide * wide, keepdims=True)))
    top = jnp.sum(krylov * tall * wide, keepdims=True)
    scaled_ref[...] = krylov[:size, :size] / top
    rate_ref[...] = jnp.broadcast_to(1.0 / jnp.sqrt(top), rate_ref.shape)


def top_call(diags, lows, ties):
    steps = len(lows) + 1
    count = diags[0].shape[0]
    size = steps * count
    padded = -(-size // LANES) * LANES
    return pl.pallas_call(
        functools.partial(top_kernel, steps),
        in_specs=[VMEM] * (2 * steps) + [ANY] * len(ties),
        out_specs=[VMEM, VMEM],
        out_shape=[
            jax.ShapeDtypeStruct((size, size), jnp.float32),
            jax.ShapeDtypeStruct((8, LANES), jnp.float32),
        ],
        scratch_shapes=[pltpu.VMEM((padded, padded), jnp.float32)],
        compiler_params=PARAMS,
    )(*diags, *lows, *ties)


def step_kernel(ties, weight_ref, moment_ref, rate_ref, *refs):
    stepped = weight_ref[...].astype(jnp.float32) - moment_ref[...] * rate_ref[:1, :1]
    for i, out_ref in enumerate(refs[ties:]):
        out_ref[...] = stepped[:, i * UNIT : (i + 1) * UNIT].astype(jnp.bfloat16)


def step_call(weight, moment, rate, first, width, ties):
    depth = weight.shape[0]
    height = min(512, depth)
    block = pl.BlockSpec((height, width), lambda r: (r, first // width))
    return pl.pallas_call(
        functools.partial(step_kernel, len(ties)),
        grid=(depth // height,),
        in_specs=[block, block, VMEM] + [ANY] * len(ties),
        out_specs=[pl.BlockSpec((height, UNIT), lambda r: (r, 0))] * (width // UNIT),
        out_shape=[jax.ShapeDtypeStruct((depth, UNIT), jnp.bfloat16)] * (width // UNIT),
        compiler_params=LARGE,
        cost_estimate=BRIEF,
    )(weight, moment, rate, *ties)


def project_kernel(far, pieces, count, split, early, in_place, ties, first, order_ref, *refs):
    tokens = refs[:pieces]
    refs = refs[pieces:]
    weights, refs = refs[: split * count], refs[split * count :]
    if early:
        moments, rate_ref, refs = refs[:count], refs[count], refs[count + 1 :]
    refs = refs[ties + (1 if in_place else 0) :]
    if not far:
        refs[1][...] = jnp.zeros(refs[1].shape, jnp.float32)
        refs = refs[:1] + refs[2:]
    out_ref, tokens_buf, weight_buf, moment_buf, total_ref, result_ref, sems, out_sem = refs
    depth, width = weight_buf.shape[1:]
    copies = []
    for k in range(count):
        step = []
        for i in range(pieces):
            if far:
                rows = tokens[i].shape[0]
                source = tokens[i].at[:, k * depth : (k + 1) * depth]
                target = tokens_buf.at[k, pl.ds(pl.multiple_of(order_ref[i], 16), rows), :]
            else:
                source = tokens[i].at[:, pl.ds(pl.multiple_of(order_ref[k] * depth, LANES), depth)]
                target = tokens_buf.at[k]
            step.append(pltpu.make_async_copy(source, target, sems.at[k, i]))
        if early:
            at = slice(first, first + width)
            step.append(pltpu.make_async_copy(weights[k].at[:, at], weight_buf.at[k], sems.at[k, pieces]))
            step.append(
                pltpu.make_async_copy(moments[k].at[:, at], moment_buf.at[k], sems.at[k, pieces + 1])
            )
        else:
            for i in range(split):
                target = weight_buf.at[k, :, i * UNIT : (i + 1) * UNIT]
                step.append(
                    pltpu.make_async_copy(weights[k * split + i], target, sems.at[k, pieces + i])
                )
        for copy in step:
            copy.start()
        copies.append(step)
    for k in range(count):
        for copy in copies[k]:
            copy.wait()
        block = weight_buf[k]
        if early:
            stepped = block.astype(jnp.float32) - moment_buf[k].astype(jnp.float32) * rate_ref[:1, :1]
            block = stepped.astype(jnp.bfloat16)
        part = jnp.dot(tokens_buf[k], block, preferred_element_type=jnp.float32)
        total_ref[...] = part if k == 0 else total_ref[...] + part
    if far:
        result_ref[...] = total_ref[...].astype(result_ref.dtype)
        copy = pltpu.make_async_copy(result_ref, out_ref, out_sem)
    else:
        copy = pltpu.make_async_copy(total_ref, out_ref.at[:, first : first + width], out_sem)
    copy.start()
    copy.wait()


def project_call(far, order, tokens, first, width, weights, moments, rate, ties=(), out=None, cols=None):
    early = moments is not None
    split = 1 if early else width // UNIT
    count = len(weights) // split
    depth = weights[0].shape[0]
    num_rows = sum(at.shape[0] for at in tokens)
    operands = list(tokens) + list(weights)
    specs = [ANY] * len(operands)
    if early:
        operands += list(moments) + [rate]
        specs += [ANY] * count + [VMEM]
    operands += list(ties)
    specs += [ANY] * len(ties)
    aliases = {}
    if far:
        out_shape = jax.ShapeDtypeStruct((num_rows, width), jnp.bfloat16)
    else:
        out_shape = [
            jax.ShapeDtypeStruct((num_rows, cols), jnp.float32),
            jax.ShapeDtypeStruct((8, LANES), jnp.float32),
        ]
        if out is not None:
            operands.append(out)
            specs.append(ANY)
            aliases = {len(operands): 0}
    return pl.pallas_call(
        functools.partial(
            project_kernel, far, len(tokens), count, split, early, bool(aliases), len(ties), first
        ),
        grid_spec=pltpu.PrefetchScalarGridSpec(
            num_scalar_prefetch=1,
            grid=(1,),
            in_specs=specs,
            out_specs=ANY if far else [ANY, VMEM],
            scratch_shapes=[
                pltpu.VMEM((count, num_rows, depth), jnp.bfloat16),
                pltpu.VMEM((count, depth, width), jnp.bfloat16),
                pltpu.VMEM((count, depth, width) if early else (8, LANES), jnp.bfloat16),
                pltpu.VMEM((num_rows, width), jnp.float32),
                pltpu.VMEM((num_rows, width) if far else (8, LANES), jnp.bfloat16),
                pltpu.SemaphoreType.DMA((count, len(tokens) + max(2, split))),
                pltpu.SemaphoreType.DMA,
            ],
        ),
        out_shape=out_shape,
        input_output_aliases=aliases,
        compiler_params=LARGE,
        cost_estimate=BRIEF,
    )(order, *operands)


def add_kernel(old_ref, far_ref, out_ref):
    out_ref[...] = old_ref[...] + far_ref[...].astype(jnp.float32)


def add_call(out, far, first):
    num_rows, width = far.shape
    block = pl.BlockSpec((num_rows, UNIT), lambda c: (0, first // UNIT + c))
    return pl.pallas_call(
        add_kernel,
        grid=(width // UNIT,),
        in_specs=[block, pl.BlockSpec((num_rows, UNIT), lambda c: (0, c))],
        out_specs=block,
        out_shape=jax.ShapeDtypeStruct(out.shape, out.dtype),
        input_output_aliases={0: 0},
        compiler_params=LARGE,
        cost_estimate=BRIEF,
    )(out, far)


def swap(values, axis, size, bit):
    return lax.ppermute(values, axis, [(at, at ^ bit) for at in range(size)])


def butterfly(values, axis, size):
    bit = 1
    while 2 * bit < size:
        values = values + swap(values, axis, size, bit)
        bit *= 2
    return values, swap(values, axis, size, bit)


def offsets(count):
    found = [0]
    bit = count // 2
    while bit:
        found = found + [at ^ bit for at in found]
        bit //= 2
    return found


def spread(piece, axis, size):
    parts = [piece]
    bit = 1
    while bit < size:
        parts = parts + [swap(part, axis, size, bit) for part in parts]
        bit *= 2
    return parts


def local(rows_n, cols_n, tokens, weight, momentum, gradient, probes):
    half = rows_n // 2
    far_bit, near_bit = half // 2, half // 4
    place = lax.axis_index("fsdp")
    low_at = lax.rem(place, half)
    side = lax.div(place, half)
    column_at = lax.axis_index("tensor")
    num_rows = tokens.shape[0]
    depth, cols = weight.shape
    rows = num_rows // cols_n // PARTS
    unit = cols // (sum(EARLY) + sum(LATE))
    early_cols = sum(EARLY) * unit

    def fswap(values, bit):
        return swap(values, "fsdp", rows_n, bit)

    def complete(own, across, beside):
        parts = [own, across, beside, fswap(across, near_bit)]
        bit = near_bit // 2
        while bit:
            parts = parts + [fswap(part, bit) for part in parts]
            bit //= 2
        return parts

    def sum_over_rows(pack, gates, ties):
        passed = {}
        bit = 1
        while bit < half:
            pack, *passed[bit] = gate_call(pack, fswap(pack, bit), gates.get(bit, ()), ties.get(bit, ()))
            bit *= 2
        return pack, fswap(pack, half), passed

    mixed = jnp.stack([low_at ^ at for at in offsets(half)]).astype(jnp.int32)
    near_order = side * half + mixed
    pick_order = jnp.concatenate([(column_at * PARTS)[None], (1 - side) * half + mixed])
    far_order = jnp.stack(
        [(column_at ^ i) * PARTS * rows + part * rows for part in range(PARTS) for i in range(cols_n)]
    ).astype(jnp.int32)

    sent_0, sent_1, weight_own = pick_call(pick_order, tokens, weight, rows, half, early_cols)
    moment, short_1, pack = start_call(momentum, gradient, probes, sent_0, early_cols)
    weight_beside = fswap(weight_own, near_bit)
    weight_across = fswap(weight_own, far_bit)
    tokens_0 = fswap(sent_0, half)

    own, recv = butterfly(pack, "tensor", cols_n)
    pack, basis_1, _ = images_call(own, recv, probes, moment, True)
    own, recv, passed = sum_over_rows(
        pack, {1: [short_1, tokens_0], 2: [weight_across]}, {2: [weight_beside]}
    )
    short_1, tokens_0 = passed[1]
    weight_across, = passed[2]
    weight_parts = complete(weight_own, weight_across, weight_beside)
    moment_beside = fswap(short_1, near_bit)
    token_parts = spread(tokens_0, "tensor", cols_n)
    pack, residue, diag_1, short_2, sent_1 = reduced_call(
        own, recv, basis_1, None, None, moment, [sent_1], early_cols
    )
    moment_across = fswap(short_2, far_bit)
    tokens_1 = fswap(sent_1, half)

    own, recv = butterfly(pack, "tensor", cols_n)
    pack, basis_2, low_1 = images_call(
        own, recv, residue, moment, False, [weight_parts[3], moment_beside]
    )
    own, recv, passed = sum_over_rows(
        pack,
        {1: [moment_across], 2: [tokens_1]},
        {2: token_parts[1:3]},
    )
    moment_across, = passed[1]
    token_1, = passed[2]
    moment_parts = complete(short_1, moment_across, moment_beside)
    token_1_beside = swap(token_1, "tensor", cols_n, 1)
    token_1_across = swap(token_1, "tensor", cols_n, 2)
    pack, _, diag_2 = reduced_call(own, recv, basis_2, basis_1, low_1, moment, [], early_cols)

    own, recv = butterfly(pack, "tensor", cols_n)
    diag_3, low_2, token_1_beside = last_call(
        own, recv, [token_1_beside], [token_1_across, *moment_parts[3:], token_parts[3]]
    )
    token_parts += [token_1, token_1_beside, token_1_across, swap(token_1_beside, "tensor", cols_n, 2)]
    own, recv = butterfly(diag_3, "fsdp", rows_n)
    scaled, rate = top_call(
        [diag_1, diag_2, own, recv], [low_1, low_2], []
    )

    firsts, widths = [0], []
    for size in EARLY + LATE:
        widths.append(size * unit)
        firsts.append(firsts[-1] + size * unit)
    num_early = len(EARLY)
    gathered = [(weight_parts, moment_parts, rate)] * num_early
    out, partial, far = None, [], []

    def send(weights, first, width, *ties):
        partial.append(project_call(True, far_order, token_parts, first, width, *weights, ties=ties))
        far.append(fswap(partial[-1], half))

    def keep(chunk, out, tie):
        return project_call(
            False,
            near_order,
            [tokens],
            firsts[chunk],
            widths[chunk],
            *gathered[chunk],
            ties=[tie],
            out=out,
            cols=cols,
        )

    total = len(widths)
    own, across, beside = {}, {}, {}

    def step(chunk, *ties):
        own[chunk] = step_call(weight, moment, rate, firsts[chunk], widths[chunk], ties)
        across[chunk] = [fswap(at, far_bit) for at in own[chunk]]
        beside[chunk] = [fswap(at, near_bit) for at in own[chunk]]

    step(num_early, rate)
    tie = own[num_early][0]
    for chunk in range(num_early):
        send(gathered[chunk], firsts[chunk], widths[chunk], tie)
        tie = partial[-1]
    kept = []
    for chunk in range(num_early):
        out, token = keep(chunk, out, kept[-1] if kept else partial[-1])
        kept.append(token)
    for chunk in range(num_early, total):
        late = far[max(chunk - 2, 0) : chunk - 1]
        passed = pass_call(across[chunk], [partial[-1], *beside[chunk], *late])
        pieces = [complete(*at) for at in zip(own[chunk], passed, beside[chunk])]
        gathered.append(([piece[k] for k in range(half) for piece in pieces], None, None))
        if chunk + 1 < total:
            if chunk == num_early:
                for ahead in range(chunk + 1, total):
                    step(ahead, kept[-1], passed[0])
            send(gathered[chunk], firsts[chunk], widths[chunk], partial[-1], own[total - 1][0])
            out = add_call(out, far[chunk - 1], firsts[chunk - 1])
            out, token = keep(chunk, out, partial[-1])
            kept.append(token)
    last_sent = partial[-1]
    for i, piece in enumerate(pieces):
        ties = [last_sent, kept[-1]] + far[total - 2 : total - 1] * (i > 0)
        send((piece, None, None), firsts[total - 1] + i * unit, unit, *ties)
    out = add_call(out, far[total - 2], firsts[total - 2])
    out, _ = keep(total - 1, out, partial[-1])
    for i in range(len(pieces)):
        out = add_call(out, far[total - 1 + i], firsts[total - 1] + i * unit)
    return out, moment, scaled


def solution(mesh):
    return jax.shard_map(
        functools.partial(local, mesh.shape["fsdp"], mesh.shape["tensor"]),
        mesh=mesh,
        in_specs=(
            P("fsdp", None),
            P("fsdp", "tensor"),
            P("fsdp", "tensor"),
            P("fsdp", "tensor"),
            P(None, "tensor"),
        ),
        out_specs=(P("fsdp", "tensor"), P("fsdp", "tensor"), P()),
        check_vma=False,
    )
```
